32 devices in a mesh: seq: 4 (over z), head: 8 (over y, x, core).
Axes of the slice: x: 2, y: 2, z: 4, core: 2. Of those that a mesh axis runs over, the one named last changes fastest.
Arguments:
- tokens: bfloat16 [12288, 2048], P(('seq', 'head')), may hold values from -6 to 6
- segment: int32 [12288], P('seq'), may hold values from 0 to 32, as said below
- attn_gain: float32 [2048], replicated, may hold values from 0.1 to 1.9
- query_weight: bfloat16 [2048, 2048], P('seq', 'head'), may hold values from -0.125 to 0.125
- key_weight: bfloat16 [2048, 2048], P('seq', 'head'), may hold values from -0.125 to 0.125
- value_weight: bfloat16 [2048, 2048], P('seq', 'head'), may hold values from -0.125 to 0.125
- out_weight: bfloat16 [2048, 2048], P('head', 'seq'), may hold values from -1 to 1
- ffn_gain: float32 [2048], replicated, may hold values from 0.1 to 1.9
- gate_weight: bfloat16 [2048, 5504], P('seq', 'head'), may hold values from -0.125 to 0.125
- up_weight: bfloat16 [2048, 5504], P('seq', 'head'), may hold values from -0.125 to 0.125
- down_weight: bfloat16 [5504, 2048], P('head', 'seq'), may hold values from -0.078125 to 0.078125
- cotangent: bfloat16 [12288, 2048], P(('seq', 'head'))
Outputs:
- output: bfloat16 [12288, 2048], P(('seq', 'head'))
- input_grad: float32 [12288, 2048], P(('seq', 'head'))
- attn_gain_grad: float32 [2048], P(('seq', 'head'))
- query_grad: float32 [2048, 2048], P('seq', 'head')
- key_grad: float32 [2048, 2048], P('seq', 'head')
- value_grad: float32 [2048, 2048], P('seq', 'head')
- out_grad: float32 [2048, 2048], P('head', 'seq')
- ffn_gain_grad: float32 [2048], P(('seq', 'head'))
- gate_grad: float32 [2048, 5504], P('seq', 'head')
- up_grad: float32 [2048, 5504], P('seq', 'head')
- down_grad: float32 [5504, 2048], P('head', 'seq')
The draws below stay inside these ranges and needn't reach their ends.
Inputs may be any that keep to these rules, and one draw needn't show every extreme that they name: segment ids never fall along the tokens, no document starts within the first 768 tokens of an aligned block of 3072 tokens, and the last token's id is always the largest allowed.
All inputs are finite; a program needn't handle non-finite values.
Results may differ from the reference program's by a relative error of at most 0.018.
Values may be sent and summed in bfloat16 or wider, within the bound.
A program may use at most 320 MiB of HBM per device.

```python
import jax
import jax.numpy as jnp
from jax import lax

D = 2048
HEADS = 16
HEAD_DIM = 128
FF = 5504
WINDOW = 1024
GROUP = 3072
TOKENS = 12288


def draw_segment(key, part):
    key = jax.random.fold_in(key, 7)
    first, second, third = jax.random.split(key, 3)
    blocks = TOKENS // GROUP
    spots = jax.random.randint(first, (blocks, 8), GROUP // 4, GROUP)
    counts = jax.random.randint(second, (blocks, 1), 0, 9) * jax.random.randint(third, (blocks, 1), 0, 2)
    live = (jnp.arange(8)[None, :] < counts).astype(jnp.int32)
    rows = jnp.broadcast_to(jnp.arange(blocks)[:, None], (blocks, 8))
    starts = jnp.zeros((blocks, GROUP), jnp.int32).at[rows, spots].max(live)
    ids = jnp.cumsum(starts.reshape(-1)).astype(jnp.int32)
    return (ids + (8 * blocks - ids[-1])).astype(jnp.int32)


def draw_cotangent(key, part):
    key = jax.random.fold_in(key, 5)
    place = jnp.arange(TOKENS, dtype=jnp.float32)[:, None] / TOKENS
    base = jnp.clip(jax.random.normal(key, (TOKENS, D), jnp.float32), -5.0, 5.0)
    return (base * (1.0 + 2.0 * place)).astype(jnp.bfloat16)


def block_scale(own_key, shape, pieces, smallest, high):
    level, own = 1.0, jax.random.fold_in(own_key, 6)
    for position, shards_of in pieces:
        steps = jnp.exp(jax.random.uniform(jax.random.fold_in(own, position), (shards_of,), jnp.float32, smallest / len(pieces), high / len(pieces)))
        level = level * jnp.repeat(steps, shape[position] // shards_of).reshape([-1 if axis == position else 1 for axis in range(len(shape))])
    return level


def noise(stream_key, shape, deviation, reach, pieces=(), kind=jnp.bfloat16):
    level = block_scale(stream_key, shape, pieces, -0.22, 0.18) if pieces else 1.0
    entries = jax.random.normal(stream_key, shape, jnp.float32) * deviation * level
    return jnp.minimum(jnp.maximum(entries, -reach), reach).astype(kind)


def setup_inputs(seed: int = 0) -> dict:
    splits = jax.random.split(jax.random.key(seed), 13)
    tokens = noise(splits[0], (TOKENS, D), 1.0, 6.0, ((0, 32),))
    segment = draw_segment(jax.random.fold_in(splits[12], 71), 0)
    attn_gain = jnp.clip(1.0 + 0.18 * jax.random.normal(splits[2], (D,), jnp.float32), 0.1, 1.9)
    query_weight = noise(splits[3], (D, D), D ** -0.5, 0.125, ((0, 4), (1, 8)))
    key_weight = noise(splits[4], (D, D), D ** -0.5, 0.125, ((0, 4), (1, 8)))
    value_weight = noise(splits[5], (D, D), D ** -0.5, 0.125, ((0, 4), (1, 8)))
    out_weight = noise(splits[6], (D, D), (D // 64) ** -0.5, 1.0, ((0, 8), (1, 4)))
    ffn_gain = jnp.clip(1.0 + 0.18 * jax.random.normal(splits[7], (D,), jnp.float32), 0.1, 1.9)
    gate_weight = noise(splits[8], (D, FF), D ** -0.5, 0.125, ((0, 4), (1, 8)))
    up_weight = noise(splits[9], (D, FF), D ** -0.5, 0.125, ((0, 4), (1, 8)))
    down_weight = noise(splits[10], (FF, D), FF ** -0.5, 0.078125, ((0, 8), (1, 4)))
    cotangent = draw_cotangent(jax.random.fold_in(splits[12], 71), 0)
    return {"tokens": tokens, "segment": segment, "attn_gain": attn_gain, "query_weight": query_weight, "key_weight": key_weight, "value_weight": value_weight, "out_weight": out_weight, "ffn_gain": ffn_gain, "gate_weight": gate_weight, "up_weight": up_weight, "down_weight": down_weight, "cotangent": cotangent}


@jax.custom_vjp
def low(v):
    return lax.optimization_barrier(v.astype(jnp.bfloat16)).astype(jnp.float32)

@jax.custom_vjp
def low_back(v):
    return v

def low_keep(v):
    return (low(v), None)

def low_pass(kept, grad):
    return (grad,)

def back_keep(v):
    return (v, None)

def back_low(kept, grad):
    return (low(grad),)
low.defvjp(low_keep, low_pass)
low_back.defvjp(back_keep, back_low)
EPS = 1e-06

def product(left, right):
    return jnp.dot(left, right, precision=lax.Precision.HIGHEST, preferred_element_type=jnp.float32)

def rms_scale(rows, gain):
    return rows * lax.rsqrt(lax.optimization_barrier(jnp.mean(rows * rows, axis=-1, keepdims=True)) + EPS) * gain

def attend(queries, keys, values, segment):
    block = min(512, TOKENS)
    count = TOKENS // block
    query_heads = queries.reshape(TOKENS, HEADS, HEAD_DIM)
    padding = jnp.zeros((WINDOW, D), jnp.float32)
    key_heads = jnp.concatenate([padding, keys], axis=0).reshape(WINDOW + TOKENS, HEADS, HEAD_DIM)
    value_heads = jnp.concatenate([padding, values], axis=0).reshape(WINDOW + TOKENS, HEADS, HEAD_DIM)
    seg_padded = jnp.concatenate([jnp.full((WINDOW,), -1, jnp.int32), segment.astype(jnp.int32)])
    scale = HEAD_DIM ** (-0.5)

    def one_block(index):
        start = (index * block).astype(jnp.int32)
        query_part = lax.dynamic_slice_in_dim(query_heads, start, block, 0)
        key_part = lax.dynamic_slice_in_dim(key_heads, start, block + WINDOW, 0)
        value_part = lax.dynamic_slice_in_dim(value_heads, start, block + WINDOW, 0)
        seg_query = lax.dynamic_slice_in_dim(segment.astype(jnp.int32), start, block, 0)
        seg_keys = lax.dynamic_slice_in_dim(seg_padded, start, block + WINDOW, 0)
        scores = jnp.einsum('qhd,khd->hqk', query_part, key_part, precision=lax.Precision.HIGHEST) * scale
        scores = low_back(scores)
        rows = jnp.arange(block)[:, None] + WINDOW
        cols = jnp.arange(block + WINDOW)[None, :]
        distance = rows - cols
        visible = (distance >= 0) & (distance <= WINDOW) & (seg_query[:, None] == seg_keys[None, :])
        scores = jnp.where(visible[None], scores, -1e+30)
        highest = lax.optimization_barrier(jnp.max(scores, axis=-1, keepdims=True))
        weights = jnp.exp(scores - highest)
        probs = low(weights / lax.optimization_barrier(jnp.sum(weights, axis=-1, keepdims=True)))
        return jnp.einsum('hqk,khd->qhd', probs, value_part, precision=lax.Precision.HIGHEST)
    blocks = lax.map(jax.checkpoint(one_block), jnp.arange(count).astype(jnp.int32))
    return blocks.reshape(TOKENS, D)

def layer(tokens, attn_gain, query_weight, key_weight, value_weight, out_weight, ffn_gain, gate_weight, up_weight, down_weight, segment):
    normed_one = low(rms_scale(tokens, attn_gain))
    queries = low_back(low(product(normed_one, query_weight)))
    keys = low_back(low(product(normed_one, key_weight)))
    values = low_back(low(product(normed_one, value_weight)))
    attended = low_back(low(attend(queries, keys, values, segment)))
    branch = low_back(product(attended, out_weight))
    middle = tokens + branch
    normed_two = low(rms_scale(middle, ffn_gain))
    gate = low_back(product(normed_two, gate_weight))
    up = low_back(product(normed_two, up_weight))
    hidden = low(jax.nn.silu(gate) * up)
    return middle + product(hidden, down_weight)

def reference(tokens, segment, attn_gain, query_weight, key_weight, value_weight, out_weight, ffn_gain, gate_weight, up_weight, down_weight, cotangent):
    inputs = (tokens.astype(jnp.float32), attn_gain.astype(jnp.float32), query_weight.astype(jnp.float32), key_weight.astype(jnp.float32), value_weight.astype(jnp.float32), out_weight.astype(jnp.float32), ffn_gain.astype(jnp.float32), gate_weight.astype(jnp.float32), up_weight.astype(jnp.float32), down_weight.astype(jnp.float32))

    def forward(*values):
        return layer(*values, segment)
    result, pullback = jax.vjp(forward, *inputs)
    grads = pullback(cotangent.astype(jnp.float32))
    return (result.astype(jnp.bfloat16), grads[0], grads[1], grads[2], grads[3], grads[4], grads[5], grads[6], grads[7], grads[8], grads[9])
```

```python
import functools

import jax
import jax.numpy as jnp
from jax import lax
from jax.experimental import pallas as pl
from jax.experimental.pallas import tpu as pltpu
from jax.sharding import PartitionSpec as P

HEAD_DIM = 128
WINDOW = 1024


EPS = 1e-06
NEG = -1e30


def from_behind(value, axis, by):
    count = lax.axis_size(axis)
    pairs = [(i, i + by) for i in range(count) if 0 <= i + by < count]
    return lax.ppermute(value, axis, pairs)


def product(left, right):
    return jnp.dot(left, right, preferred_element_type=jnp.float32)


def product_tn(left, right):
    return lax.dot_general(
        left, right, (((0,), (0,)), ((), ())), preferred_element_type=jnp.float32
    )


def product_nt(left, right):
    return lax.dot_general(
        left, right, (((1,), (1,)), ((), ())), preferred_element_type=jnp.float32
    )


def normalize(rows):
    inverse = lax.rsqrt(jnp.mean(rows * rows, axis=-1, keepdims=True) + EPS)
    return (rows * inverse, inverse)


def norm_back(unit, inverse, gain, grad):
    scaled = grad * gain
    return inverse * (scaled - unit * jnp.mean(scaled * unit, axis=-1, keepdims=True))


def gather_rows(rows):
    return lax.all_gather(rows, "head", axis=0, tiled=True)


def block_scores(query_heads, key_heads, seg_query, seg_keys, valid, start, block):
    query_part = query_heads[start : start + block]
    key_part = key_heads[start : start + block + WINDOW]
    scores = jnp.einsum(
        "qhd,khd->hqk", query_part, key_part, preferred_element_type=jnp.float32
    ) * HEAD_DIM ** (-0.5)
    rows = jnp.arange(block)[:, None] + WINDOW
    cols = jnp.arange(block + WINDOW)[None, :]
    distance = rows - cols
    same_doc = (
        seg_query[start : start + block][:, None]
        == seg_keys[start : start + block + WINDOW][None, :]
    )
    visible = (
        (distance >= 0)
        & (distance <= WINDOW)
        & same_doc
        & valid[start : start + block + WINDOW][None, :]
    )
    return jnp.where(visible[None], scores, NEG)


def local(
    tokens,
    segment,
    attn_gain,
    query_weight,
    key_weight,
    value_weight,
    out_weight,
    ffn_gain,
    gate_weight,
    up_weight,
    down_weight,
    cotangent,
):
    own_rows = tokens.shape[0]
    group = own_rows * lax.axis_size("head")
    heads_here = query_weight.shape[1] // HEAD_DIM
    offset = lax.axis_index("head") * own_rows
    seq_index = lax.axis_index("seq")
    block = min(512, group)
    scale = HEAD_DIM ** (-0.5)
    w_query, w_key, w_value, w_out, w_gate, w_up, w_down = (
        lax.all_gather(query_weight, "seq", axis=0, tiled=True),
        lax.all_gather(key_weight, "seq", axis=0, tiled=True),
        lax.all_gather(value_weight, "seq", axis=0, tiled=True),
        lax.all_gather(out_weight, "seq", axis=1, tiled=True),
        lax.all_gather(gate_weight, "seq", axis=0, tiled=True),
        lax.all_gather(up_weight, "seq", axis=0, tiled=True),
        lax.all_gather(down_weight, "seq", axis=1, tiled=True),
    )
    inputs = tokens.astype(jnp.float32)
    unit_one, inverse_one = normalize(inputs)
    normed_full = gather_rows((unit_one * attn_gain).astype(jnp.bfloat16))
    queries = product(normed_full, w_query).astype(jnp.bfloat16)
    keys = product(normed_full, w_key).astype(jnp.bfloat16)
    values = product(normed_full, w_value).astype(jnp.bfloat16)
    halo_keys, halo_values, halo_segs = ([], [], [])
    hop = 1
    take = min(group, WINDOW - (hop - 1) * group)
    got_keys, got_values, got_segs = from_behind(
        (keys[group - take :], values[group - take :], segment[group - take :]), "seq", hop
    )
    halo_keys.append(got_keys)
    halo_values.append(got_values)
    halo_segs.append(got_segs)
    keys_ext = jnp.concatenate(halo_keys + [keys], axis=0)
    values_ext = jnp.concatenate(halo_values + [values], axis=0)
    segs_ext = jnp.concatenate(halo_segs + [segment], axis=0)
    positions = seq_index * group - WINDOW + jnp.arange(WINDOW + group)
    valid = positions >= 0
    query_heads = queries.reshape(group, heads_here, HEAD_DIM)
    key_heads = keys_ext.reshape(WINDOW + group, heads_here, HEAD_DIM)
    value_heads = values_ext.reshape(WINDOW + group, heads_here, HEAD_DIM)
    outputs, logsums = ([], [])
    for start in range(0, group, block):
        scores = block_scores(query_heads, key_heads, segment, segs_ext, valid, start, block)
        highest = jnp.max(scores, axis=-1, keepdims=True)
        weights = jnp.exp(scores - highest)
        total = jnp.sum(weights, axis=-1, keepdims=True)
        probs = (weights / total).astype(jnp.bfloat16)
        outputs.append(
            jnp.einsum(
                "hqk,khd->qhd",
                probs,
                value_heads[start : start + block + WINDOW],
                preferred_element_type=jnp.float32,
            )
        )
        logsums.append(highest + jnp.log(total))
    attended = (
        jnp.concatenate(outputs, axis=0).reshape(group, heads_here * HEAD_DIM).astype(jnp.bfloat16)
    )
    partial_out = product(attended, w_out)
    own_part = lax.dynamic_slice_in_dim(partial_out, offset, own_rows, 0)
    placed = lax.dynamic_update_slice_in_dim(partial_out, own_part + inputs, offset, 0)
    middle_full = lax.psum(placed, "head")
    middle = lax.dynamic_slice_in_dim(middle_full, offset, own_rows, 0)
    unit_full, inverse_full = normalize(middle_full)
    normed_two_full = (unit_full * ffn_gain).astype(jnp.bfloat16)
    unit_two, inverse_two = normalize(middle)
    gate = product(normed_two_full, w_gate)
    up = product(normed_two_full, w_up)
    sigmoid = jax.nn.sigmoid(gate)
    activated = gate * sigmoid
    hidden = (activated * up).astype(jnp.bfloat16)
    ffn_out = lax.psum_scatter(
        product(hidden, w_down).astype(jnp.bfloat16), "head", scatter_dimension=0, tiled=True
    ).astype(jnp.float32)
    result = middle + ffn_out
    grad_out = lax.all_gather(cotangent, "head", axis=0, tiled=True)
    grad_hidden = product_nt(grad_out, w_down)
    grad_gate = (grad_hidden * up * sigmoid * (1.0 + gate * (1.0 - sigmoid))).astype(jnp.bfloat16)
    grad_up = (grad_hidden * activated).astype(jnp.bfloat16)
    down_grad = product_tn(hidden, grad_out)
    gate_grad = product_tn(normed_two_full, grad_gate)
    up_grad = product_tn(normed_two_full, grad_up)
    grad_normed_two = lax.psum_scatter(
        (product_nt(grad_gate, w_gate) + product_nt(grad_up, w_up)).astype(jnp.bfloat16),
        "head",
        scatter_dimension=0,
        tiled=True,
    ).astype(jnp.float32)
    ffn_gain_part = jnp.sum(grad_normed_two * unit_two, axis=0)
    grad_middle = cotangent.astype(jnp.float32) + norm_back(
        unit_two, inverse_two, ffn_gain, grad_normed_two
    )
    grad_branch = lax.all_gather(grad_middle.astype(jnp.bfloat16), "head", axis=0, tiled=True)
    out_grad = product_tn(attended, grad_branch)
    grad_attended = product_nt(grad_branch, w_out).astype(jnp.bfloat16)
    grad_heads = grad_attended.reshape(group, heads_here, HEAD_DIM)
    grad_query_list = []
    grad_keys_ext = jnp.zeros((WINDOW + group, heads_here, HEAD_DIM), jnp.float32)
    grad_values_ext = jnp.zeros((WINDOW + group, heads_here, HEAD_DIM), jnp.float32)
    for number, start in enumerate(range(0, group, block)):
        scores = block_scores(query_heads, key_heads, segment, segs_ext, valid, start, block)
        probs = jnp.exp(scores - logsums[number])
        probs_low = probs.astype(jnp.bfloat16)
        key_part = key_heads[start : start + block + WINDOW]
        value_part = value_heads[start : start + block + WINDOW]
        query_part = query_heads[start : start + block]
        grad_part = grad_heads[start : start + block]
        grad_probs = jnp.einsum(
            "qhd,khd->hqk", grad_part, value_part, preferred_element_type=jnp.float32
        )
        inner = jnp.sum(probs * grad_probs, axis=-1, keepdims=True)
        grad_scores = (probs * (grad_probs - inner)).astype(jnp.bfloat16)
        grad_query_list.append(
            jnp.einsum("hqk,khd->qhd", grad_scores, key_part, preferred_element_type=jnp.float32)
            * scale
        )
        key_term = (
            jnp.einsum("hqk,qhd->khd", grad_scores, query_part, preferred_element_type=jnp.float32)
            * scale
        )
        value_term = jnp.einsum(
            "hqk,qhd->khd", probs_low, grad_part, preferred_element_type=jnp.float32
        )
        grad_keys_ext = grad_keys_ext.at[start : start + block + WINDOW].add(key_term)
        grad_values_ext = grad_values_ext.at[start : start + block + WINDOW].add(value_term)
    grad_keys_ext = grad_keys_ext.reshape(WINDOW + group, heads_here * HEAD_DIM)
    grad_values_ext = grad_values_ext.reshape(WINDOW + group, heads_here * HEAD_DIM)
    grad_keys = grad_keys_ext[WINDOW:]
    grad_values = grad_values_ext[WINDOW:]
    cursor = 0
    hop = 1
    take = min(group, WINDOW - (hop - 1) * group)
    back_keys = from_behind(
        grad_keys_ext[cursor : cursor + take].astype(jnp.bfloat16), "seq", -hop
    ).astype(jnp.float32)
    back_values = from_behind(
        grad_values_ext[cursor : cursor + take].astype(jnp.bfloat16), "seq", -hop
    ).astype(jnp.float32)
    grad_keys = grad_keys.at[group - take :].add(back_keys)
    grad_values = grad_values.at[group - take :].add(back_values)
    grad_queries = (
        jnp.concatenate(grad_query_list, axis=0)
        .reshape(group, heads_here * HEAD_DIM)
        .astype(jnp.bfloat16)
    )
    grad_keys = grad_keys.astype(jnp.bfloat16)
    grad_values = grad_values.astype(jnp.bfloat16)
    query_grad = product_tn(normed_full, grad_queries)
    key_grad = product_tn(normed_full, grad_keys)
    value_grad = product_tn(normed_full, grad_values)
    grad_normed_one = lax.psum_scatter(
        (
            product_nt(grad_queries, w_query)
            + product_nt(grad_keys, w_key)
            + product_nt(grad_values, w_value)
        ).astype(jnp.bfloat16),
        "head",
        scatter_dimension=0,
        tiled=True,
    ).astype(jnp.float32)
    attn_gain_part = jnp.sum(grad_normed_one * unit_one, axis=0)
    input_grad = grad_middle + norm_back(unit_one, inverse_one, attn_gain, grad_normed_one)
    summed = (
        lax.psum_scatter(
            query_grad.astype(jnp.bfloat16), "seq", scatter_dimension=0, tiled=True
        ).astype(jnp.float32),
        lax.psum_scatter(
            key_grad.astype(jnp.bfloat16), "seq", scatter_dimension=0, tiled=True
        ).astype(jnp.float32),
        lax.psum_scatter(
            value_grad.astype(jnp.bfloat16), "seq", scatter_dimension=0, tiled=True
        ).astype(jnp.float32),
        lax.psum_scatter(
            out_grad.astype(jnp.bfloat16), "seq", scatter_dimension=1, tiled=True
        ).astype(jnp.float32),
        lax.psum_scatter(
            gate_grad.astype(jnp.bfloat16), "seq", scatter_dimension=0, tiled=True
        ).astype(jnp.float32),
        lax.psum_scatter(
            up_grad.astype(jnp.bfloat16), "seq", scatter_dimension=0, tiled=True
        ).astype(jnp.float32),
        lax.psum_scatter(
            down_grad.astype(jnp.bfloat16), "seq", scatter_dimension=1, tiled=True
        ).astype(jnp.float32),
    )
    gain_grads = (
        lax.psum_scatter(attn_gain_part, ("seq", "head"), scatter_dimension=0, tiled=True),
        lax.psum_scatter(ffn_gain_part, ("seq", "head"), scatter_dimension=0, tiled=True),
    )
    return (
        result.astype(jnp.bfloat16),
        input_grad,
        gain_grads[0],
        summed[0],
        summed[1],
        summed[2],
        summed[3],
        gain_grads[1],
        summed[4],
        summed[5],
        summed[6],
    )


MESH = pl.DeviceIdType.MESH
BF16 = jnp.bfloat16
F32 = jnp.float32
MIB = 2**20


def remote(src, dst, send_sem, recv_sem, where):
    return pltpu.make_async_remote_copy(
        src_ref=src,
        dst_ref=dst,
        send_sem=send_sem,
        recv_sem=recv_sem,
        device_id=where,
        device_id_type=MESH,
    )


class Place:
    def __init__(self, line):
        s, h = lax.axis_index("seq"), lax.axis_index("head")
        core = lax.rem(h, 2)
        x = lax.rem(lax.div(h, 2), 2)
        y = lax.div(h, 4)
        self.s, self.h, self.line = s, h, line
        self.turn = 1 - 2 * core
        self.core = h + self.turn
        over_x, over_y = 2 - 4 * x, 4 - 8 * y
        self.first = h + over_x * (1 - core) + over_y * core
        self.second = h + over_y * (1 - core) + over_x * core
        self.across = h + over_x + over_y

    def at(self, head):
        return (self.s, head)

    def greet(self, along_seq=True):
        barrier = pltpu.get_barrier_semaphore()
        for head in (self.core, self.first, self.second):
            pl.semaphore_signal(barrier, inc=1, device_id=self.at(head), device_id_type=MESH)
        if along_seq:

            @pl.when(self.s > 0)
            def _():
                pl.semaphore_signal(
                    barrier, inc=1, device_id=(self.s - 1, self.h), device_id_type=MESH
                )

            @pl.when(self.s < self.line - 1)
            def _():
                pl.semaphore_signal(
                    barrier, inc=1, device_id=(self.s + 1, self.h), device_id_type=MESH
                )

            @pl.when((self.s > 0) & (self.s < self.line - 1))
            def _():
                pl.semaphore_wait(barrier, 5)

            @pl.when((self.s == 0) | (self.s == self.line - 1))
            def _():
                pl.semaphore_wait(barrier, 4)
        else:
            pl.semaphore_wait(barrier, 3)


class HeadGather:
    SEMS = 7

    def __init__(self, place, block, send, recv):
        p = place
        self.p = p
        plan = (
            (p.h, p.first, p.first),
            (p.h, p.second, p.second),
            (p.h, p.core, p.core),
            (p.first, p.second, p.across),
            (p.first, p.core, p.second + p.turn),
            (p.second, p.core, p.first + p.turn),
            (p.across, p.core, p.across + p.turn),
        )
        self.out = [
            remote(block(j), block(j), send.at[i], recv.at[i], p.at(to))
            for i, (j, to, _) in enumerate(plan)
        ]
        self.come = [
            remote(block(j), block(j), send.at[i], recv.at[i], p.at(to))
            for i, (_, to, j) in enumerate(plan)
        ]

    def start(self):
        for i in (0, 1, 2):
            self.out[i].start()

    def got_first(self):
        self.come[0].wait_recv()
        self.out[3].start()
        self.out[4].start()

    def got_second(self):
        self.come[1].wait_recv()
        self.out[5].start()

    def got_across(self):
        self.come[3].wait_recv()
        self.out[6].start()

    def got_core(self):
        self.come[2].wait_recv()

    def got_core_second(self):
        self.come[4].wait_recv()

    def got_core_first(self):
        self.come[5].wait_recv()

    def got_core_across(self):
        self.come[6].wait_recv()

    def finish(self):
        for copy in self.out:
            copy.wait_send()


class LineGather:
    def __init__(self, place, piece, up_send, up_recv, down_send, down_recv):
        self.p, self.piece = place, piece
        self.up = (up_send, up_recv)
        self.down = (down_send, down_recv)

    def _up(self, owner, t):
        p = self.p
        return remote(
            self.piece(owner), self.piece(owner), self.up[0].at[t], self.up[1].at[t], (p.s + 1, p.h)
        )

    def _down(self, owner, t):
        p = self.p
        return remote(
            self.piece(owner),
            self.piece(owner),
            self.down[0].at[t],
            self.down[1].at[t],
            (p.s - 1, p.h),
        )

    def start(self, t):
        p = self.p

        @pl.when((p.s < p.line - 1) & (p.s >= t))
        def _():
            self._up(p.s - t, t).start()

        @pl.when((p.s > 0) & (p.s + t < p.line))
        def _():
            self._down(p.s + t, t).start()

    def got(self, t):
        p = self.p

        @pl.when(p.s >= t + 1)
        def _():
            self._up(p.s - 1 - t, t).wait_recv()

        @pl.when(p.s + 1 + t < p.line)
        def _():
            self._down(p.s + 1 + t, t).wait_recv()

    def step(self, t):
        self.got(t)
        if t + 1 < self.p.line - 1:
            self.start(t + 1)

    def finish(self):
        p = self.p
        for t in range(p.line - 1):

            @pl.when((p.s < p.line - 1) & (p.s >= t))
            def _():
                self._up(p.s - t, t).wait_send()

            @pl.when((p.s > 0) & (p.s + t < p.line))
            def _():
                self._down(p.s + t, t).wait_send()


def line_sems(line, tensors=1):
    return [pltpu.SemaphoreType.DMA((line - 1,)) for _ in range(4 * tensors)]


def norm_rows(rows, gain):
    inverse = lax.rsqrt(jnp.mean(rows * rows, axis=-1, keepdims=True) + EPS)
    return rows * inverse * gain


def project_kernel(
    line,
    tokens,
    gain,
    wq,
    wk,
    wv,
    normed_out,
    qkv_out,
    weight_out,
    normed,
    weight,
    g_send,
    g_recv,
    us,
    ur,
    ds,
    dr,
    keep,
):
    p = Place(line)
    rows, width = tokens.shape
    slab, part = wq.shape
    weight_own = weight.at[pl.ds(pl.multiple_of(p.s * slab, slab), slab)]
    weight_own[:, 0:part] = wq[...]
    weight_own[:, part : 2 * part] = wk[...]
    weight_own[:, 2 * part : 3 * part] = wv[...]
    block = lambda j: normed.at[pl.ds(pl.multiple_of(j * rows, rows), rows)]
    home = lambda j: normed_out.at[pl.ds(pl.multiple_of(j * rows, rows), rows)]
    piece = lambda d: weight.at[pl.ds(pl.multiple_of(d * slab, slab), slab)]
    gather = HeadGather(p, block, g_send, g_recv)
    line_gather = LineGather(p, piece, us, ur, ds, dr)
    p.greet()
    line_gather.start(0)
    mine = block(p.h)
    step = 32

    @pl.loop(0, rows // step)
    def _(i):
        at = pl.ds(pl.multiple_of(i * step, step), step)
        mine[at] = norm_rows(tokens[at].astype(F32), gain[...]).astype(BF16)

    gather.start()

    def multiply(j):
        start = pl.multiple_of(j * rows, rows)

        @pl.loop(0, 3)
        def _(n):
            cols = pl.ds(pl.multiple_of(n * part, part), part)
            qkv_out[pl.ds(start, rows), cols] = jnp.dot(
                normed[pl.ds(start, rows), :], weight[:, cols], preferred_element_type=F32
            ).astype(BF16)

    saved = []

    def save(j):
        copy = pltpu.make_async_copy(block(j), home(j), keep.at[len(saved)])
        copy.start()
        saved.append(copy)

    save(p.h)
    gather.got_core()
    save(p.core)
    line_gather.step(0)
    gather.got_first()
    gather.got_second()
    save(p.first)
    save(p.second)
    line_gather.step(1)
    gather.got_core_second()
    gather.got_core_first()
    save(p.second + p.turn)
    save(p.first + p.turn)
    line_gather.step(2)
    out_copy = pltpu.make_async_copy(weight, weight_out, keep.at[8])
    out_copy.start()
    for j in (p.h, p.core, p.first, p.second):
        multiply(j)
    gather.got_across()
    save(p.across)
    for j in (p.second + p.turn, p.first + p.turn, p.across):
        multiply(j)
    gather.got_core_across()
    save(p.across + p.turn)
    multiply(p.across + p.turn)
    gather.finish()
    line_gather.finish()
    for copy in saved:
        copy.wait()
    out_copy.wait()


def any_spec():
    return pl.BlockSpec(memory_space=pl.ANY)


def vmem_spec():
    return pl.BlockSpec(memory_space=pltpu.VMEM)


def project(line, tokens, gain, wq, wk, wv):
    rows, width = tokens.shape
    slab, part = wq.shape
    full = rows * 8
    return pl.pallas_call(
        functools.partial(project_kernel, line),
        out_shape=(
            jax.ShapeDtypeStruct((full, width), BF16),
            jax.ShapeDtypeStruct((full, 3 * part), BF16),
            jax.ShapeDtypeStruct((slab * line, 3 * part), BF16),
        ),
        in_specs=[vmem_spec()] * 5,
        out_specs=(any_spec(), vmem_spec(), any_spec()),
        scratch_shapes=[
            pltpu.VMEM((full, width), BF16),
            pltpu.VMEM((slab * line, 3 * part), BF16),
            pltpu.SemaphoreType.DMA((7,)),
            pltpu.SemaphoreType.DMA((7,)),
            *line_sems(line),
            pltpu.SemaphoreType.DMA((9,)),
        ],
        compiler_params=pltpu.CompilerParams(
            collective_id=1, has_side_effects=True, vmem_limit_bytes=48 * MIB
        ),
        cost_estimate=pl.CostEstimate(
            flops=2 * full * width * 3 * part, bytes_accessed=40 * MIB, transcendentals=0
        ),
    )(tokens, gain.reshape(1, width), wq, wk, wv)


def fused(
    tokens,
    segment,
    attn_gain,
    query_weight,
    key_weight,
    value_weight,
    out_weight,
    ffn_gain,
    gate_weight,
    up_weight,
    down_weight,
    cotangent,
):
    own_rows = tokens.shape[0]
    group = own_rows * lax.axis_size("head")
    heads_here = query_weight.shape[1] // HEAD_DIM
    offset = lax.axis_index("head") * own_rows
    seq_index = lax.axis_index("seq")
    block = min(512, group)
    scale = HEAD_DIM ** (-0.5)
    line = lax.axis_size("seq")
    part = query_weight.shape[1]
    normed_full, qkv, w_qkv = project(
        line, tokens, attn_gain, query_weight, key_weight, value_weight
    )
    w_query, w_key, w_value = (w_qkv[:, i * part : (i + 1) * part] for i in range(3))
    queries, keys, values = (qkv[:, i * part : (i + 1) * part] for i in range(3))
    w_out, w_gate, w_up, w_down = (
        lax.all_gather(out_weight, "seq", axis=1, tiled=True),
        lax.all_gather(gate_weight, "seq", axis=0, tiled=True),
        lax.all_gather(up_weight, "seq", axis=0, tiled=True),
        lax.all_gather(down_weight, "seq", axis=1, tiled=True),
    )
    inputs = tokens.astype(jnp.float32)
    unit_one, inverse_one = normalize(inputs)
    halo_keys, halo_values, halo_segs = ([], [], [])
    hop = 1
    take = min(group, WINDOW - (hop - 1) * group)
    got_keys, got_values, got_segs = from_behind(
        (keys[group - take :], values[group - take :], segment[group - take :]), "seq", hop
    )
    halo_keys.append(got_keys)
    halo_values.append(got_values)
    halo_segs.append(got_segs)
    keys_ext = jnp.concatenate(halo_keys + [keys], axis=0)
    values_ext = jnp.concatenate(halo_values + [values], axis=0)
    segs_ext = jnp.concatenate(halo_segs + [segment], axis=0)
    positions = seq_index * group - WINDOW + jnp.arange(WINDOW + group)
    valid = positions >= 0
    query_heads = queries.reshape(group, heads_here, HEAD_DIM)
    key_heads = keys_ext.reshape(WINDOW + group, heads_here, HEAD_DIM)
    value_heads = values_ext.reshape(WINDOW + group, heads_here, HEAD_DIM)
    outputs, logsums = ([], [])
    for start in range(0, group, block):
        scores = block_scores(query_heads, key_heads, segment, segs_ext, valid, start, block)
        highest = jnp.max(scores, axis=-1, keepdims=True)
        weights = jnp.exp(scores - highest)
        total = jnp.sum(weights, axis=-1, keepdims=True)
        probs = (weights / total).astype(jnp.bfloat16)
        outputs.append(
            jnp.einsum(
                "hqk,khd->qhd",
                probs,
                value_heads[start : start + block + WINDOW],
                preferred_element_type=jnp.float32,
            )
        )
        logsums.append(highest + jnp.log(total))
    attended = (
        jnp.concatenate(outputs, axis=0).reshape(group, heads_here * HEAD_DIM).astype(jnp.bfloat16)
    )
    partial_out = product(attended, w_out)
    own_part = lax.dynamic_slice_in_dim(partial_out, offset, own_rows, 0)
    placed = lax.dynamic_update_slice_in_dim(partial_out, own_part + inputs, offset, 0)
    middle_full = lax.psum(placed, "head")
    middle = lax.dynamic_slice_in_dim(middle_full, offset, own_rows, 0)
    unit_full, inverse_full = normalize(middle_full)
    normed_two_full = (unit_full * ffn_gain).astype(jnp.bfloat16)
    unit_two, inverse_two = normalize(middle)
    gate = product(normed_two_full, w_gate)
    up = product(normed_two_full, w_up)
    sigmoid = jax.nn.sigmoid(gate)
    activated = gate * sigmoid
    hidden = (activated * up).astype(jnp.bfloat16)
    ffn_out = lax.psum_scatter(
        product(hidden, w_down).astype(jnp.bfloat16), "head", scatter_dimension=0, tiled=True
    ).astype(jnp.float32)
    result = middle + ffn_out
    grad_out = lax.all_gather(cotangent, "head", axis=0, tiled=True)
    grad_hidden = product_nt(grad_out, w_down)
    grad_gate = (grad_hidden * up * sigmoid * (1.0 + gate * (1.0 - sigmoid))).astype(jnp.bfloat16)
    grad_up = (grad_hidden * activated).astype(jnp.bfloat16)
    down_grad = product_tn(hidden, grad_out)
    gate_grad = product_tn(normed_two_full, grad_gate)
    up_grad = product_tn(normed_two_full, grad_up)
    grad_normed_two = lax.psum_scatter(
        (product_nt(grad_gate, w_gate) + product_nt(grad_up, w_up)).astype(jnp.bfloat16),
        "head",
        scatter_dimension=0,
        tiled=True,
    ).astype(jnp.float32)
    ffn_gain_part = jnp.sum(grad_normed_two * unit_two, axis=0)
    grad_middle = cotangent.astype(jnp.float32) + norm_back(
        unit_two, inverse_two, ffn_gain, grad_normed_two
    )
    grad_branch = lax.all_gather(grad_middle.astype(jnp.bfloat16), "head", axis=0, tiled=True)
    out_grad = product_tn(attended, grad_branch)
    grad_attended = product_nt(grad_branch, w_out).astype(jnp.bfloat16)
    grad_heads = grad_attended.reshape(group, heads_here, HEAD_DIM)
    grad_query_list = []
    grad_keys_ext = jnp.zeros((WINDOW + group, heads_here, HEAD_DIM), jnp.float32)
    grad_values_ext = jnp.zeros((WINDOW + group, heads_here, HEAD_DIM), jnp.float32)
    for number, start in enumerate(range(0, group, block)):
        scores = block_scores(query_heads, key_heads, segment, segs_ext, valid, start, block)
        probs = jnp.exp(scores - logsums[number])
        probs_low = probs.astype(jnp.bfloat16)
        key_part = key_heads[start : start + block + WINDOW]
        value_part = value_heads[start : start + block + WINDOW]
        query_part = query_heads[start : start + block]
        grad_part = grad_heads[start : start + block]
        grad_probs = jnp.einsum(
            "qhd,khd->hqk", grad_part, value_part, preferred_element_type=jnp.float32
        )
        inner = jnp.sum(probs * grad_probs, axis=-1, keepdims=True)
        grad_scores = (probs * (grad_probs - inner)).astype(jnp.bfloat16)
        grad_query_list.append(
            jnp.einsum("hqk,khd->qhd", grad_scores, key_part, preferred_element_type=jnp.float32)
            * scale
        )
        key_term = (
            jnp.einsum("hqk,qhd->khd", grad_scores, query_part, preferred_element_type=jnp.float32)
            * scale
        )
        value_term = jnp.einsum(
            "hqk,qhd->khd", probs_low, grad_part, preferred_element_type=jnp.float32
        )
        grad_keys_ext = grad_keys_ext.at[start : start + block + WINDOW].add(key_term)
        grad_values_ext = grad_values_ext.at[start : start + block + WINDOW].add(value_term)
    grad_keys_ext = grad_keys_ext.reshape(WINDOW + group, heads_here * HEAD_DIM)
    grad_values_ext = grad_values_ext.reshape(WINDOW + group, heads_here * HEAD_DIM)
    grad_keys = grad_keys_ext[WINDOW:]
    grad_values = grad_values_ext[WINDOW:]
    cursor = 0
    hop = 1
    take = min(group, WINDOW - (hop - 1) * group)
    back_keys = from_behind(
        grad_keys_ext[cursor : cursor + take].astype(jnp.bfloat16), "seq", -hop
    ).astype(jnp.float32)
    back_values = from_behind(
        grad_values_ext[cursor : cursor + take].astype(jnp.bfloat16), "seq", -hop
    ).astype(jnp.float32)
    grad_keys = grad_keys.at[group - take :].add(back_keys)
    grad_values = grad_values.at[group - take :].add(back_values)
    grad_queries = (
        jnp.concatenate(grad_query_list, axis=0)
        .reshape(group, heads_here * HEAD_DIM)
        .astype(jnp.bfloat16)
    )
    grad_keys = grad_keys.astype(jnp.bfloat16)
    grad_values = grad_values.astype(jnp.bfloat16)
    query_grad = product_tn(normed_full, grad_queries)
    key_grad = product_tn(normed_full, grad_keys)
    value_grad = product_tn(normed_full, grad_values)
    grad_normed_one = lax.psum_scatter(
        (
            product_nt(grad_queries, w_query)
            + product_nt(grad_keys, w_key)
            + product_nt(grad_values, w_value)
        ).astype(jnp.bfloat16),
        "head",
        scatter_dimension=0,
        tiled=True,
    ).astype(jnp.float32)
    attn_gain_part = jnp.sum(grad_normed_one * unit_one, axis=0)
    input_grad = grad_middle + norm_back(unit_one, inverse_one, attn_gain, grad_normed_one)
    summed = (
        lax.psum_scatter(
            query_grad.astype(jnp.bfloat16), "seq", scatter_dimension=0, tiled=True
        ).astype(jnp.float32),
        lax.psum_scatter(
            key_grad.astype(jnp.bfloat16), "seq", scatter_dimension=0, tiled=True
        ).astype(jnp.float32),
        lax.psum_scatter(
            value_grad.astype(jnp.bfloat16), "seq", scatter_dimension=0, tiled=True
        ).astype(jnp.float32),
        lax.psum_scatter(
            out_grad.astype(jnp.bfloat16), "seq", scatter_dimension=1, tiled=True
        ).astype(jnp.float32),
        lax.psum_scatter(
            gate_grad.astype(jnp.bfloat16), "seq", scatter_dimension=0, tiled=True
        ).astype(jnp.float32),
        lax.psum_scatter(
            up_grad.astype(jnp.bfloat16), "seq", scatter_dimension=0, tiled=True
        ).astype(jnp.float32),
        lax.psum_scatter(
            down_grad.astype(jnp.bfloat16), "seq", scatter_dimension=1, tiled=True
        ).astype(jnp.float32),
    )
    gain_grads = (
        lax.psum_scatter(attn_gain_part, ("seq", "head"), scatter_dimension=0, tiled=True),
        lax.psum_scatter(ffn_gain_part, ("seq", "head"), scatter_dimension=0, tiled=True),
    )
    return (
        result.astype(jnp.bfloat16),
        input_grad,
        gain_grads[0],
        summed[0],
        summed[1],
        summed[2],
        summed[3],
        gain_grads[1],
        summed[4],
        summed[5],
        summed[6],
    )


def solution(mesh):
    placed = (
        P(("seq", "head"), None),
        P("seq"),
        P(),
        P("seq", "head"),
        P("seq", "head"),
        P("seq", "head"),
        P("head", "seq"),
        P(),
        P("seq", "head"),
        P("seq", "head"),
        P("head", "seq"),
        P(("seq", "head"), None),
    )
    body = fused if mesh.shape["head"] == 8 else local
    return jax.shard_map(
        body,
        mesh=mesh,
        in_specs=placed,
        out_specs=(
            P(("seq", "head"), None),
            P(("seq", "head"), None),
            P(("seq", "head")),
            P("seq", "head"),
            P("seq", "head"),
            P("seq", "head"),
            P("head", "seq"),
            P(("seq", "head")),
            P("seq", "head"),
            P("seq", "head"),
            P("head", "seq"),
        ),
        check_vma=False,
    )
```

```python
import functools

import jax
import jax.numpy as jnp
from jax import lax
from jax.experimental import pallas as pl
from jax.experimental.pallas import tpu as pltpu
from jax.sharding import PartitionSpec as P

HEAD_DIM = 128
WINDOW = 1024


EPS = 1e-06
NEG = -1e30


def from_behind(value, axis, by):
    count = lax.axis_size(axis)
    pairs = [(i, i + by) for i in range(count) if 0 <= i + by < count]
    return lax.ppermute(value, axis, pairs)


def product(left, right):
    return jnp.dot(left, right, preferred_element_type=jnp.float32)


def product_tn(left, right):
    return lax.dot_general(
        left, right, (((0,), (0,)), ((), ())), preferred_element_type=jnp.float32
    )


def product_nt(left, right):
    return lax.dot_general(
        left, right, (((1,), (1,)), ((), ())), preferred_element_type=jnp.float32
    )


def normalize(rows):
    inverse = lax.rsqrt(jnp.mean(rows * rows, axis=-1, keepdims=True) + EPS)
    return (rows * inverse, inverse)


def norm_back(unit, inverse, gain, grad):
    scaled = grad * gain
    return inverse * (scaled - unit * jnp.mean(scaled * unit, axis=-1, keepdims=True))


def gather_rows(rows):
    return lax.all_gather(rows, "head", axis=0, tiled=True)


def block_scores(query_heads, key_heads, seg_query, seg_keys, valid, start, block):
    query_part = query_heads[start : start + block]
    key_part = key_heads[start : start + block + WINDOW]
    scores = jnp.einsum(
        "qhd,khd->hqk", query_part, key_part, preferred_element_type=jnp.float32
    ) * HEAD_DIM ** (-0.5)
    rows = jnp.arange(block)[:, None] + WINDOW
    cols = jnp.arange(block + WINDOW)[None, :]
    distance = rows - cols
    same_doc = (
        seg_query[start : start + block][:, None]
        == seg_keys[start : start + block + WINDOW][None, :]
    )
    visible = (
        (distance >= 0)
        & (distance <= WINDOW)
        & same_doc
        & valid[start : start + block + WINDOW][None, :]
    )
    return jnp.where(visible[None], scores, NEG)


def local(
    tokens,
    segment,
    attn_gain,
    query_weight,
    key_weight,
    value_weight,
    out_weight,
    ffn_gain,
    gate_weight,
    up_weight,
    down_weight,
    cotangent,
):
    own_rows = tokens.shape[0]
    group = own_rows * lax.axis_size("head")
    heads_here = query_weight.shape[1] // HEAD_DIM
    offset = lax.axis_index("head") * own_rows
    seq_index = lax.axis_index("seq")
    block = min(512, group)
    scale = HEAD_DIM ** (-0.5)
    w_query, w_key, w_value, w_out, w_gate, w_up, w_down = (
        lax.all_gather(query_weight, "seq", axis=0, tiled=True),
        lax.all_gather(key_weight, "seq", axis=0, tiled=True),
        lax.all_gather(value_weight, "seq", axis=0, tiled=True),
        lax.all_gather(out_weight, "seq", axis=1, tiled=True),
        lax.all_gather(gate_weight, "seq", axis=0, tiled=True),
        lax.all_gather(up_weight, "seq", axis=0, tiled=True),
        lax.all_gather(down_weight, "seq", axis=1, tiled=True),
    )
    inputs = tokens.astype(jnp.float32)
    unit_one, inverse_one = normalize(inputs)
    normed_full = gather_rows((unit_one * attn_gain).astype(jnp.bfloat16))
    queries = product(normed_full, w_query).astype(jnp.bfloat16)
    keys = product(normed_full, w_key).astype(jnp.bfloat16)
    values = product(normed_full, w_value).astype(jnp.bfloat16)
    halo_keys, halo_values, halo_segs = ([], [], [])
    hop = 1
    take = min(group, WINDOW - (hop - 1) * group)
    got_keys, got_values, got_segs = from_behind(
        (keys[group - take :], values[group - take :], segment[group - take :]), "seq", hop
    )
    halo_keys.append(got_keys)
    halo_values.append(got_values)
    halo_segs.append(got_segs)
    keys_ext = jnp.concatenate(halo_keys + [keys], axis=0)
    values_ext = jnp.concatenate(halo_values + [values], axis=0)
    segs_ext = jnp.concatenate(halo_segs + [segment], axis=0)
    positions = seq_index * group - WINDOW + jnp.arange(WINDOW + group)
    valid = positions >= 0
    query_heads = queries.reshape(group, heads_here, HEAD_DIM)
    key_heads = keys_ext.reshape(WINDOW + group, heads_here, HEAD_DIM)
    value_heads = values_ext.reshape(WINDOW + group, heads_here, HEAD_DIM)
    outputs, logsums = ([], [])
    for start in range(0, group, block):
        scores = block_scores(query_heads, key_heads, segment, segs_ext, valid, start, block)
        highest = jnp.max(scores, axis=-1, keepdims=True)
        weights = jnp.exp(scores - highest)
        total = jnp.sum(weights, axis=-1, keepdims=True)
        probs = (weights / total).astype(jnp.bfloat16)
        outputs.append(
            jnp.einsum(
                "hqk,khd->qhd",
                probs,
                value_heads[start : start + block + WINDOW],
                preferred_element_type=jnp.float32,
            )
        )
        logsums.append(highest + jnp.log(total))
    attended = (
        jnp.concatenate(outputs, axis=0).reshape(group, heads_here * HEAD_DIM).astype(jnp.bfloat16)
    )
    partial_out = product(attended, w_out)
    own_part = lax.dynamic_slice_in_dim(partial_out, offset, own_rows, 0)
    placed = lax.dynamic_update_slice_in_dim(partial_out, own_part + inputs, offset, 0)
    middle_full = lax.psum(placed, "head")
    middle = lax.dynamic_slice_in_dim(middle_full, offset, own_rows, 0)
    unit_full, inverse_full = normalize(middle_full)
    normed_two_full = (unit_full * ffn_gain).astype(jnp.bfloat16)
    unit_two, inverse_two = normalize(middle)
    gate = product(normed_two_full, w_gate)
    up = product(normed_two_full, w_up)
    sigmoid = jax.nn.sigmoid(gate)
    activated = gate * sigmoid
    hidden = (activated * up).astype(jnp.bfloat16)
    ffn_out = lax.psum_scatter(
        product(hidden, w_down).astype(jnp.bfloat16), "head", scatter_dimension=0, tiled=True
    ).astype(jnp.float32)
    result = middle + ffn_out
    grad_out = lax.all_gather(cotangent, "head", axis=0, tiled=True)
    grad_hidden = product_nt(grad_out, w_down)
    grad_gate = (grad_hidden * up * sigmoid * (1.0 + gate * (1.0 - sigmoid))).astype(jnp.bfloat16)
    grad_up = (grad_hidden * activated).astype(jnp.bfloat16)
    down_grad = product_tn(hidden, grad_out)
    gate_grad = product_tn(normed_two_full, grad_gate)
    up_grad = product_tn(normed_two_full, grad_up)
    grad_normed_two = lax.psum_scatter(
        (product_nt(grad_gate, w_gate) + product_nt(grad_up, w_up)).astype(jnp.bfloat16),
        "head",
        scatter_dimension=0,
        tiled=True,
    ).astype(jnp.float32)
    ffn_gain_part = jnp.sum(grad_normed_two * unit_two, axis=0)
    grad_middle = cotangent.astype(jnp.float32) + norm_back(
        unit_two, inverse_two, ffn_gain, grad_normed_two
    )
    grad_branch = lax.all_gather(grad_middle.astype(jnp.bfloat16), "head", axis=0, tiled=True)
    out_grad = product_tn(attended, grad_branch)
    grad_attended = product_nt(grad_branch, w_out).astype(jnp.bfloat16)
    grad_heads = grad_attended.reshape(group, heads_here, HEAD_DIM)
    grad_query_list = []
    grad_keys_ext = jnp.zeros((WINDOW + group, heads_here, HEAD_DIM), jnp.float32)
    grad_values_ext = jnp.zeros((WINDOW + group, heads_here, HEAD_DIM), jnp.float32)
    for number, start in enumerate(range(0, group, block)):
        scores = block_scores(query_heads, key_heads, segment, segs_ext, valid, start, block)
        probs = jnp.exp(scores - logsums[number])
        probs_low = probs.astype(jnp.bfloat16)
        key_part = key_heads[start : start + block + WINDOW]
        value_part = value_heads[start : start + block + WINDOW]
        query_part = query_heads[start : start + block]
        grad_part = grad_heads[start : start + block]
        grad_probs = jnp.einsum(
            "qhd,khd->hqk", grad_part, value_part, preferred_element_type=jnp.float32
        )
        inner = jnp.sum(probs * grad_probs, axis=-1, keepdims=True)
        grad_scores = (probs * (grad_probs - inner)).astype(jnp.bfloat16)
        grad_query_list.append(
            jnp.einsum("hqk,khd->qhd", grad_scores, key_part, preferred_element_type=jnp.float32)
            * scale
        )
        key_term = (
            jnp.einsum("hqk,qhd->khd", grad_scores, query_part, preferred_element_type=jnp.float32)
            * scale
        )
        value_term = jnp.einsum(
            "hqk,qhd->khd", probs_low, grad_part, preferred_element_type=jnp.float32
        )
        grad_keys_ext = grad_keys_ext.at[start : start + block + WINDOW].add(key_term)
        grad_values_ext = grad_values_ext.at[start : start + block + WINDOW].add(value_term)
    grad_keys_ext = grad_keys_ext.reshape(WINDOW + group, heads_here * HEAD_DIM)
    grad_values_ext = grad_values_ext.reshape(WINDOW + group, heads_here * HEAD_DIM)
    grad_keys = grad_keys_ext[WINDOW:]
    grad_values = grad_values_ext[WINDOW:]
    cursor = 0
    hop = 1
    take = min(group, WINDOW - (hop - 1) * group)
    back_keys = from_behind(
        grad_keys_ext[cursor : cursor + take].astype(jnp.bfloat16), "seq", -hop
    ).astype(jnp.float32)
    back_values = from_behind(
        grad_values_ext[cursor : cursor + take].astype(jnp.bfloat16), "seq", -hop
    ).astype(jnp.float32)
    grad_keys = grad_keys.at[group - take :].add(back_keys)
    grad_values = grad_values.at[group - take :].add(back_values)
    grad_queries = (
        jnp.concatenate(grad_query_list, axis=0)
        .reshape(group, heads_here * HEAD_DIM)
        .astype(jnp.bfloat16)
    )
    grad_keys = grad_keys.astype(jnp.bfloat16)
    grad_values = grad_values.astype(jnp.bfloat16)
    query_grad = product_tn(normed_full, grad_queries)
    key_grad = product_tn(normed_full, grad_keys)
    value_grad = product_tn(normed_full, grad_values)
    grad_normed_one = lax.psum_scatter(
        (
            product_nt(grad_queries, w_query)
            + product_nt(grad_keys, w_key)
            + product_nt(grad_values, w_value)
        ).astype(jnp.bfloat16),
        "head",
        scatter_dimension=0,
        tiled=True,
    ).astype(jnp.float32)
    attn_gain_part = jnp.sum(grad_normed_one * unit_one, axis=0)
    input_grad = grad_middle + norm_back(unit_one, inverse_one, attn_gain, grad_normed_one)
    summed = (
        lax.psum_scatter(
            query_grad.astype(jnp.bfloat16), "seq", scatter_dimension=0, tiled=True
        ).astype(jnp.float32),
        lax.psum_scatter(
            key_grad.astype(jnp.bfloat16), "seq", scatter_dimension=0, tiled=True
        ).astype(jnp.float32),
        lax.psum_scatter(
            value_grad.astype(jnp.bfloat16), "seq", scatter_dimension=0, tiled=True
        ).astype(jnp.float32),
        lax.psum_scatter(
            out_grad.astype(jnp.bfloat16), "seq", scatter_dimension=1, tiled=True
        ).astype(jnp.float32),
        lax.psum_scatter(
            gate_grad.astype(jnp.bfloat16), "seq", scatter_dimension=0, tiled=True
        ).astype(jnp.float32),
        lax.psum_scatter(
            up_grad.astype(jnp.bfloat16), "seq", scatter_dimension=0, tiled=True
        ).astype(jnp.float32),
        lax.psum_scatter(
            down_grad.astype(jnp.bfloat16), "seq", scatter_dimension=1, tiled=True
        ).astype(jnp.float32),
    )
    gain_grads = (
        lax.psum_scatter(attn_gain_part, ("seq", "head"), scatter_dimension=0, tiled=True),
        lax.psum_scatter(ffn_gain_part, ("seq", "head"), scatter_dimension=0, tiled=True),
    )
    return (
        result.astype(jnp.bfloat16),
        input_grad,
        gain_grads[0],
        summed[0],
        summed[1],
        summed[2],
        summed[3],
        gain_grads[1],
        summed[4],
        summed[5],
        summed[6],
    )


MESH = pl.DeviceIdType.MESH
BF16 = jnp.bfloat16
F32 = jnp.float32
MIB = 2**20


def remote(src, dst, send_sem, recv_sem, where):
    return pltpu.make_async_remote_copy(
        src_ref=src,
        dst_ref=dst,
        send_sem=send_sem,
        recv_sem=recv_sem,
        device_id=where,
        device_id_type=MESH,
    )


class Place:
    def __init__(self, line):
        s, h = lax.axis_index("seq"), lax.axis_index("head")
        core = lax.rem(h, 2)
        x = lax.rem(lax.div(h, 2), 2)
        y = lax.div(h, 4)
        self.s, self.h, self.line = s, h, line
        self.turn = 1 - 2 * core
        self.core = h + self.turn
        over_x, over_y = 2 - 4 * x, 4 - 8 * y
        self.first = h + over_x * (1 - core) + over_y * core
        self.second = h + over_y * (1 - core) + over_x * core
        self.across = h + over_x + over_y

    def at(self, head):
        return (self.s, head)

    def greet(self, along_seq=True):
        barrier = pltpu.get_barrier_semaphore()
        for head in (self.core, self.first, self.second):
            pl.semaphore_signal(barrier, inc=1, device_id=self.at(head), device_id_type=MESH)
        if along_seq:

            @pl.when(self.s > 0)
            def _():
                pl.semaphore_signal(
                    barrier, inc=1, device_id=(self.s - 1, self.h), device_id_type=MESH
                )

            @pl.when(self.s < self.line - 1)
            def _():
                pl.semaphore_signal(
                    barrier, inc=1, device_id=(self.s + 1, self.h), device_id_type=MESH
                )

            @pl.when((self.s > 0) & (self.s < self.line - 1))
            def _():
                pl.semaphore_wait(barrier, 5)

            @pl.when((self.s == 0) | (self.s == self.line - 1))
            def _():
                pl.semaphore_wait(barrier, 4)
        else:
            pl.semaphore_wait(barrier, 3)


class HeadGather:
    SEMS = 7

    def __init__(self, place, block, send, recv, own=None):
        p = place
        self.p = p
        plan = (
            (p.h, p.first, p.first),
            (p.h, p.second, p.second),
            (p.h, p.core, p.core),
            (p.first, p.second, p.across),
            (p.first, p.core, p.second + p.turn),
            (p.second, p.core, p.first + p.turn),
            (p.across, p.core, p.across + p.turn),
        )
        self.out = [
            remote(
                block(j) if own is None or i > 2 else own,
                block(j),
                send.at[i],
                recv.at[i],
                p.at(to),
            )
            for i, (j, to, _) in enumerate(plan)
        ]
        self.come = [
            remote(block(j), block(j), send.at[i], recv.at[i], p.at(to))
            for i, (_, to, j) in enumerate(plan)
        ]

    def start(self):
        for i in (0, 1, 2):
            self.out[i].start()

    def got_first(self):
        self.come[0].wait_recv()
        self.out[3].start()
        self.out[4].start()

    def got_second(self):
        self.come[1].wait_recv()
        self.out[5].start()

    def got_across(self):
        self.come[3].wait_recv()
        self.out[6].start()

    def got_core(self):
        self.come[2].wait_recv()

    def got_core_second(self):
        self.come[4].wait_recv()

    def got_core_first(self):
        self.come[5].wait_recv()

    def got_core_across(self):
        self.come[6].wait_recv()

    def finish(self):
        for copy in self.out:
            copy.wait_send()


class LineGather:
    def __init__(self, place, piece, up_send, up_recv, down_send, down_recv, own=None):
        self.p, self.piece, self.own = place, piece, own
        self.up = (up_send, up_recv)
        self.down = (down_send, down_recv)

    def _up(self, owner, t):
        p = self.p
        source = self.own if t == 0 and self.own is not None else self.piece(owner)
        return remote(
            source, self.piece(owner), self.up[0].at[t], self.up[1].at[t], (p.s + 1, p.h)
        )

    def _down(self, owner, t):
        p = self.p
        source = self.own if t == 0 and self.own is not None else self.piece(owner)
        return remote(
            source,
            self.piece(owner),
            self.down[0].at[t],
            self.down[1].at[t],
            (p.s - 1, p.h),
        )

    def start(self, t):
        p = self.p

        @pl.when((p.s < p.line - 1) & (p.s >= t))
        def _():
            self._up(p.s - t, t).start()

        @pl.when((p.s > 0) & (p.s + t < p.line))
        def _():
            self._down(p.s + t, t).start()

    def got(self, t):
        p = self.p

        @pl.when(p.s >= t + 1)
        def _():
            self._up(p.s - 1 - t, t).wait_recv()

        @pl.when(p.s + 1 + t < p.line)
        def _():
            self._down(p.s + 1 + t, t).wait_recv()

    def step(self, t):
        self.got(t)
        if t + 1 < self.p.line - 1:
            self.start(t + 1)

    def finish(self):
        p = self.p
        for t in range(p.line - 1):

            @pl.when((p.s < p.line - 1) & (p.s >= t))
            def _():
                self._up(p.s - t, t).wait_send()

            @pl.when((p.s > 0) & (p.s + t < p.line))
            def _():
                self._down(p.s + t, t).wait_send()


def line_sems(line, tensors=1):
    return [pltpu.SemaphoreType.DMA((line - 1,)) for _ in range(4 * tensors)]


def norm_rows(rows, gain):
    inverse = lax.rsqrt(jnp.mean(rows * rows, axis=-1, keepdims=True) + EPS)
    return rows * inverse * gain


def own_starts(segment):
    count = segment.shape[1]
    ids = segment[...]
    place = lax.broadcasted_iota(jnp.int32, (1, count), 1)
    starts = jnp.where((place > 0) & (ids != pltpu.roll(ids, 1, 1)), place, -1)
    shift = 1
    while shift < count:
        earlier = jnp.where(place >= shift, pltpu.roll(starts, shift, 1), -1)
        starts = jnp.maximum(starts, earlier)
        shift *= 2
    return starts


def turned_over(source, target):
    width = source.shape[1]
    for start in range(0, width, 128):
        stop = min(start + 128, width)
        target[start:stop, :] = source[:, start:stop].T


def project_kernel(
    line,
    tokens,
    gain,
    wq,
    wk,
    wv,
    segment,
    w_gate,
    w_up,
    normed_out,
    qkv_out,
    weight_out,
    floor_out,
    gate_out,
    up_out,
    normed,
    weight,
    g_send,
    g_recv,
    us,
    ur,
    ds,
    dr,
    keep,
    seg_halo,
    seg_sems,
):
    p = Place(line)
    rows, width = tokens.shape
    slab, part = wq.shape
    count = segment.shape[1]
    seg_copy = remote(
        segment.at[:, pl.ds(count - WINDOW, WINDOW)],
        seg_halo,
        seg_sems.at[0],
        seg_sems.at[1],
        (p.s + 1, p.h),
    )
    weight_own = weight.at[pl.ds(pl.multiple_of(p.s * slab, slab), slab)]
    weight_own[:, 0:part] = wq[...]
    weight_own[:, part : 2 * part] = wk[...]
    weight_own[:, 2 * part : 3 * part] = wv[...]
    block = lambda j: normed.at[pl.ds(pl.multiple_of(j * rows, rows), rows)]
    home = lambda j: normed_out.at[pl.ds(pl.multiple_of(j * rows, rows), rows)]
    piece = lambda d: weight.at[pl.ds(pl.multiple_of(d * slab, slab), slab)]
    gather = HeadGather(p, block, g_send, g_recv)
    line_gather = LineGather(p, piece, us, ur, ds, dr)
    p.greet()
    line_gather.start(0)

    @pl.when(p.s < line - 1)
    def _():
        seg_copy.start()

    mine = block(p.h)
    step = 32

    @pl.loop(0, rows // step)
    def _(i):
        at = pl.ds(pl.multiple_of(i * step, step), step)
        mine[at] = norm_rows(tokens[at].astype(F32), gain[...]).astype(BF16)

    gather.start()

    def multiply(j):
        start = pl.multiple_of(j * rows, rows)

        @pl.loop(0, 3)
        def _(n):
            cols = pl.ds(pl.multiple_of(n * part, part), part)
            qkv_out[pl.ds(start, rows), cols] = jnp.dot(
                normed[pl.ds(start, rows), :], weight[:, cols], preferred_element_type=F32
            ).astype(BF16)

    saved = []

    def save(j):
        copy = pltpu.make_async_copy(block(j), home(j), keep.at[len(saved)])
        copy.start()
        saved.append(copy)

    save(p.h)
    starts = own_starts(segment)
    for source, target in ((w_gate, gate_out), (w_up, up_out)):
        turned_over(source, target)

    @pl.when(p.s > 0)
    def _():
        seg_copy.wait_recv()

    before = jnp.sum(
        (seg_halo[...] == segment[:, 0:1]).astype(jnp.int32), axis=1, keepdims=True
    )
    before = jnp.where(p.s > 0, before, 0)
    floor_out[...] = jnp.maximum(
        lax.broadcasted_iota(jnp.int32, (1, count), 1),
        jnp.where(starts >= 0, starts + WINDOW, WINDOW - before),
    )
    gather.got_core()
    save(p.core)
    line_gather.step(0)
    gather.got_first()
    gather.got_second()
    save(p.first)
    save(p.second)
    line_gather.step(1)
    gather.got_core_second()
    gather.got_core_first()
    save(p.second + p.turn)
    save(p.first + p.turn)
    line_gather.step(2)
    out_copy = pltpu.make_async_copy(weight, weight_out, keep.at[8])
    out_copy.start()
    for j in (p.h, p.core, p.first, p.second):
        multiply(j)
    gather.got_across()
    save(p.across)
    for j in (p.second + p.turn, p.first + p.turn, p.across):
        multiply(j)
    gather.got_core_across()
    save(p.across + p.turn)
    multiply(p.across + p.turn)
    gather.finish()
    line_gather.finish()

    @pl.when(p.s < line - 1)
    def _():
        seg_copy.wait_send()

    for copy in saved:
        copy.wait()
    out_copy.wait()


def any_spec():
    return pl.BlockSpec(memory_space=pl.ANY)


def vmem_spec():
    return pl.BlockSpec(memory_space=pltpu.VMEM)


def project(line, tokens, gain, wq, wk, wv, segment, w_gate, w_up):
    rows, width = tokens.shape
    slab, part = wq.shape
    full = rows * 8
    return pl.pallas_call(
        functools.partial(project_kernel, line),
        out_shape=(
            jax.ShapeDtypeStruct((full, width), BF16),
            jax.ShapeDtypeStruct((full, 3 * part), BF16),
            jax.ShapeDtypeStruct((slab * line, 3 * part), BF16),
            jax.ShapeDtypeStruct((1, full), jnp.int32),
            jax.ShapeDtypeStruct((w_gate.shape[1], slab), BF16),
            jax.ShapeDtypeStruct((w_gate.shape[1], slab), BF16),
        ),
        in_specs=[vmem_spec()] * 8,
        out_specs=(any_spec(), vmem_spec(), any_spec(), vmem_spec(), vmem_spec(), vmem_spec()),
        scratch_shapes=[
            pltpu.VMEM((full, width), BF16),
            pltpu.VMEM((slab * line, 3 * part), BF16),
            pltpu.SemaphoreType.DMA((7,)),
            pltpu.SemaphoreType.DMA((7,)),
            *line_sems(line),
            pltpu.SemaphoreType.DMA((9,)),
            pltpu.VMEM((1, WINDOW), jnp.int32),
            pltpu.SemaphoreType.DMA((2,)),
        ],
        compiler_params=pltpu.CompilerParams(
            collective_id=1, has_side_effects=True, vmem_limit_bytes=48 * MIB
        ),
        cost_estimate=pl.CostEstimate(
            flops=2 * full * width * 3 * part, bytes_accessed=40 * MIB, transcendentals=0
        ),
    )(tokens, gain.reshape(1, width), wq, wk, wv, segment.reshape(1, full), w_gate, w_up)


LOG2E = 1.4426950408889634
TILE = 256
CHUNKS = WINDOW // TILE + 1


def tile_scores(tile, head, q, k_ext, floor):
    start = pl.multiple_of(tile * TILE, TILE)
    cols = slice(head * HEAD_DIM, (head + 1) * HEAD_DIM)
    queries = q[pl.ds(start, TILE), cols]
    row = lax.broadcasted_iota(jnp.int32, (TILE, TILE), 0)
    lane = lax.broadcasted_iota(jnp.int32, (TILE, TILE), 1)
    lowest = floor[:, pl.ds(start, TILE)] - start
    found = []
    for i in range(CHUNKS):
        keys = k_ext[pl.ds(start + i * TILE, TILE), cols]
        scores = product_nt(keys, queries)
        visible = row >= lowest - i * TILE
        if i == CHUNKS - 1:
            visible = visible & (row <= lane)
        found.append((scores, visible))
    return found


def forward_tile(tile, q, k_ext, v_t, floor, attended, logs):
    start = pl.multiple_of(tile * TILE, TILE)
    sharp = HEAD_DIM ** (-0.5) * LOG2E
    for head in range(q.shape[1] // HEAD_DIM):
        cols = slice(head * HEAD_DIM, (head + 1) * HEAD_DIM)
        found = [
            jnp.where(visible, scores, NEG)
            for scores, visible in tile_scores(tile, head, q, k_ext, floor)
        ]
        highest = functools.reduce(
            jnp.maximum, [jnp.max(scores, axis=0, keepdims=True) for scores in found]
        )
        total = jnp.zeros((1, TILE), F32)
        mixed = jnp.zeros((HEAD_DIM, TILE), F32)
        for i, scores in enumerate(found):
            weights = jnp.exp2((scores - highest) * sharp)
            total = total + jnp.sum(weights, axis=0, keepdims=True)
            mixed = mixed + product(
                v_t[cols, pl.ds(start + i * TILE, TILE)], weights.astype(BF16)
            )
        attended[pl.ds(start, TILE), cols] = (mixed / total).astype(BF16).T
        logs[head : head + 1, pl.ds(start, TILE)] = highest * sharp + jnp.log2(total)


def attend_kernel(
    line,
    qkv,
    floor,
    cot,
    w_out,
    gate_a,
    attended,
    logs,
    halo_out,
    cot_out,
    w_out_full,
    gate_full,
    q,
    k_ext,
    v_ext,
    v_t,
    g_send,
    g_recv,
    *sems,
):
    p = Place(line)
    out_sems, gate_sems, halo_send, halo_recv, keep = sems[0:4], sems[4:8], *sems[8:11]
    rows = cot.shape[0]
    count, part = q.shape
    p.greet()
    block = lambda j: cot_out.at[pl.ds(pl.multiple_of(j * rows, rows), rows)]
    gather = HeadGather(p, block, g_send, g_recv, own=cot)
    halo = [
        remote(
            qkv.at[pl.ds(count - WINDOW, WINDOW), pl.ds((1 + i) * part, part)],
            ext.at[pl.ds(0, WINDOW)],
            halo_send.at[i],
            halo_recv.at[i],
            (p.s + 1, p.h),
        )
        for i, ext in enumerate((k_ext, v_ext))
    ]

    @pl.when(p.s < line - 1)
    def _():
        halo[0].start()
        halo[1].start()

    gather.start()
    loads = [
        pltpu.make_async_copy(qkv.at[:, pl.ds(0, part)], q, keep.at[0]),
        pltpu.make_async_copy(
            qkv.at[:, pl.ds(part, part)], k_ext.at[pl.ds(WINDOW, count)], keep.at[1]
        ),
        pltpu.make_async_copy(
            qkv.at[:, pl.ds(2 * part, part)], v_ext.at[pl.ds(WINDOW, count)], keep.at[2]
        ),
    ]
    for copy in loads:
        copy.start()
    out_gather = LineGather(p, lambda d: w_out_full.at[d], *out_sems, own=w_out)
    gate_gather = LineGather(p, lambda d: gate_full.at[d], *gate_sems, own=gate_a)
    out_gather.start(0)
    own = [
        pltpu.make_async_copy(cot, block(p.h), keep.at[3]),
        pltpu.make_async_copy(w_out, w_out_full.at[p.s], keep.at[4]),
        pltpu.make_async_copy(gate_a, gate_full.at[p.s], keep.at[5]),
    ]
    for copy in own:
        copy.start()

    @pl.when(p.s == 0)
    def _():
        k_ext[0:WINDOW, :] = jnp.zeros((WINDOW, part), BF16)
        v_ext[0:WINDOW, :] = jnp.zeros((WINDOW, part), BF16)

    for copy in loads:
        copy.wait()

    def turn(first, last):
        @pl.loop(first, last)
        def _(i):
            at = pl.ds(pl.multiple_of(i * TILE, TILE), TILE)
            v_t[:, at] = v_ext[at, :].T

    def tiles(first, last):
        @pl.loop(first, last)
        def _(tile):
            forward_tile(tile, q, k_ext, v_t, floor, attended, logs)

    ahead = WINDOW // TILE
    turn(ahead, ahead + count // TILE)
    tiles(ahead, count // TILE)
    out_gather.step(0)
    gate_gather.start(0)

    @pl.when(p.s > 0)
    def _():
        halo[0].wait_recv()
        halo[1].wait_recv()

    turn(0, ahead)
    tiles(0, ahead)
    saves = [
        pltpu.make_async_copy(ext.at[pl.ds(0, WINDOW)], halo_out.at[i], keep.at[6 + i])
        for i, ext in enumerate((k_ext, v_ext))
    ]
    for copy in saves:
        copy.start()
    out_gather.step(1)
    gate_gather.step(0)
    gather.got_core()
    gather.got_first()
    gather.got_second()
    gather.got_core_second()
    gather.got_core_first()
    out_gather.step(2)
    gate_gather.step(1)
    gather.got_across()
    gather.got_core_across()
    gate_gather.step(2)
    gather.finish()
    out_gather.finish()
    gate_gather.finish()

    @pl.when(p.s < line - 1)
    def _():
        halo[0].wait_send()
        halo[1].wait_send()

    for copy in own + saves:
        copy.wait()


def attend(line, qkv, floor, cot, w_out, gate_a):
    count = qkv.shape[0]
    part = qkv.shape[1] // 3
    heads = part // HEAD_DIM
    rows, width = cot.shape
    return pl.pallas_call(
        functools.partial(attend_kernel, line),
        out_shape=(
            jax.ShapeDtypeStruct((count, part), BF16),
            jax.ShapeDtypeStruct((heads, count), F32),
            jax.ShapeDtypeStruct((2, WINDOW, part), BF16),
            jax.ShapeDtypeStruct((rows * 8, width), BF16),
            jax.ShapeDtypeStruct((line, *w_out.shape), BF16),
            jax.ShapeDtypeStruct((line, *gate_a.shape), BF16),
        ),
        in_specs=[any_spec(), vmem_spec(), any_spec(), any_spec(), any_spec()],
        out_specs=(vmem_spec(), vmem_spec(), any_spec(), any_spec(), any_spec(), any_spec()),
        scratch_shapes=[
            pltpu.VMEM((count, part), BF16),
            pltpu.VMEM((WINDOW + count, part), BF16),
            pltpu.VMEM((WINDOW + count, part), BF16),
            pltpu.VMEM((part, WINDOW + count), BF16),
            pltpu.SemaphoreType.DMA((7,)),
            pltpu.SemaphoreType.DMA((7,)),
            *line_sems(line, 2),
            pltpu.SemaphoreType.DMA((2,)),
            pltpu.SemaphoreType.DMA((2,)),
            pltpu.SemaphoreType.DMA((8,)),
        ],
        compiler_params=pltpu.CompilerParams(
            collective_id=2, has_side_effects=True, vmem_limit_bytes=48 * MIB
        ),
        cost_estimate=pl.CostEstimate(
            flops=5 * 2**31, bytes_accessed=40 * MIB, transcendentals=0
        ),
    )(qkv, floor, cot, w_out, gate_a)


class HeadReduce:
    def __init__(self, place, out, into, send, recv):
        p = place
        self.p, self.out, self.into = p, out, into
        goes = (p.core, p.core, p.core, p.core, p.first, p.first, p.second)
        self.copies = [
            remote(out.at[i], into.at[i], send.at[i], recv.at[i], p.at(to))
            for i, to in enumerate(goes)
        ]
        self.for_core = (p.second + p.turn, p.across + p.turn, p.first + p.turn, p.core)
        self.mine = (p.first, p.across, p.second, p.h)

    def send(self, i):
        self.copies[i].start()

    def got(self, i):
        self.copies[i].wait_recv()

    def finish(self):
        for copy in self.copies:
            copy.wait_send()


def reduce_scratch(rows, width):
    return [
        pltpu.VMEM((7, rows, width), BF16),
        pltpu.VMEM((7, rows, width), BF16),
        pltpu.SemaphoreType.DMA((7,)),
        pltpu.SemaphoreType.DMA((7,)),
    ]


def branch_kernel(
    line,
    attended,
    w_out,
    tokens,
    gate_b,
    up,
    middle,
    gate_full,
    up_full,
    out,
    into,
    r_send,
    r_recv,
    *sems,
):
    p = Place(line)
    gate_sems, up_sems, keep = sems[0:4], sems[4:8], sems[8]
    rows, width = tokens.shape
    slab = w_out.shape[2]
    p.greet()
    gate_gather = LineGather(p, lambda d: gate_full.at[d], *gate_sems, own=gate_b)
    up_gather = LineGather(p, lambda d: up_full.at[d], *up_sems, own=up)
    gate_gather.start(0)
    own = [
        pltpu.make_async_copy(gate_b, gate_full.at[p.s], keep.at[0]),
        pltpu.make_async_copy(up, up_full.at[p.s], keep.at[1]),
    ]
    for copy in own:
        copy.start()
    reduce = HeadReduce(p, out, into, r_send, r_recv)

    def emit(j, target, *more):
        start = pl.multiple_of(j * rows, rows)

        @pl.loop(0, line)
        def _(n):
            cols = pl.ds(pl.multiple_of(n * slab, slab), slab)
            value = product(attended[pl.ds(start, rows), :], w_out[n])
            for other in more:
                value = value + other[:, cols].astype(F32)
            target[:, cols] = value.astype(target.dtype)

    for i in range(4):
        emit(reduce.for_core[i], out.at[i])
        reduce.send(i)
    for i in range(2):
        reduce.got(i)
        emit(reduce.mine[i], out.at[4 + i], into.at[i])
        reduce.send(4 + i)
    reduce.got(3)
    emit(p.h, middle, into.at[3], tokens)
    reduce.got(2)
    gate_gather.step(0)
    up_gather.start(0)
    gate_gather.step(1)
    reduce.got(5)
    emit(p.second, out.at[6], into.at[2], into.at[5])
    reduce.send(6)
    gate_gather.step(2)
    up_gather.step(0)
    reduce.got(4)
    up_gather.step(1)
    reduce.got(6)

    @pl.loop(0, line)
    def _(n):
        cols = pl.ds(pl.multiple_of(n * slab, slab), slab)
        middle[:, cols] += into[4, :, cols].astype(F32) + into[6, :, cols].astype(F32)

    up_gather.step(2)
    reduce.finish()
    gate_gather.finish()
    up_gather.finish()
    for copy in own:
        copy.wait()


def branch(line, attended, w_out, tokens, gate_b, up):
    rows, width = tokens.shape
    return pl.pallas_call(
        functools.partial(branch_kernel, line),
        out_shape=(
            jax.ShapeDtypeStruct((rows, width), F32),
            jax.ShapeDtypeStruct((line, *gate_b.shape), BF16),
            jax.ShapeDtypeStruct((line, *up.shape), BF16),
        ),
        in_specs=[vmem_spec(), vmem_spec(), vmem_spec(), any_spec(), any_spec()],
        out_specs=(vmem_spec(), any_spec(), any_spec()),
        scratch_shapes=[
            *reduce_scratch(rows, width),
            *line_sems(line, 2),
            pltpu.SemaphoreType.DMA((2,)),
        ],
        compiler_params=pltpu.CompilerParams(
            collective_id=3, has_side_effects=True, vmem_limit_bytes=48 * MIB
        ),
        cost_estimate=pl.CostEstimate(
            flops=3 * 2**30, bytes_accessed=40 * MIB, transcendentals=0
        ),
    )(attended, w_out, tokens, gate_b, up)


def strips(width, most=256):
    return [(start, min(start + most, width)) for start in range(0, width, most)]


def feed_kernel(
    line,
    middle,
    gain,
    cot,
    gate_a,
    gate_b,
    up,
    down,
    normed_out,
    hidden_out,
    grad_gate_out,
    grad_up_out,
    grad_out,
    down_out,
    normed,
    w_gate,
    w_up,
    w_down,
    gates,
    ups,
    cot_block,
    hidden,
    grad_gate,
    grad_up,
    out,
    into,
    r_send,
    r_recv,
    g_send,
    g_recv,
    *sems,
):
    p = Place(line)
    down_sems, loads, saves, stage = sems[0:4], sems[4], sems[5], sems[6]
    rows, width = grad_out.shape
    units = w_down.shape[1]
    slab = w_down.shape[2]
    cut = gate_a.shape[1]
    block = lambda j: normed.at[pl.ds(pl.multiple_of(j * rows, rows), rows)]
    rows_of = lambda ref, j: ref.at[pl.ds(pl.multiple_of(j * rows, rows), rows)]
    gather = HeadGather(p, block, g_send, g_recv)
    down_gather = LineGather(p, lambda d: w_down.at[d], *down_sems, own=down)
    p.greet()
    down_gather.start(0)
    started = [
        pltpu.make_async_copy(middle, grad_out, loads.at[0]),
        pltpu.make_async_copy(gate_a, w_gate.at[:, pl.ds(0, cut)], loads.at[1]),
        pltpu.make_async_copy(gate_b, w_gate.at[:, pl.ds(cut, units - cut)], loads.at[2]),
        pltpu.make_async_copy(up, w_up, loads.at[3]),
        pltpu.make_async_copy(down, w_down.at[p.s], loads.at[4]),
    ]
    for copy in started:
        copy.start()
    started[0].wait()
    mine = block(p.h)
    step = 32

    @pl.loop(0, rows // step)
    def _(i):
        at = pl.ds(pl.multiple_of(i * step, step), step)
        mine[at] = norm_rows(grad_out[at], gain[...]).astype(BF16)

    gather.start()
    saved = []

    def save(j):
        copy = pltpu.make_async_copy(block(j), rows_of(normed_out, j), saves.at[len(saved)])
        copy.start()
        saved.append(copy)

    def open_up(j, slot):
        rows_in = normed.at[pl.ds(pl.multiple_of(j * rows, rows), rows)]
        for weight, kept in ((w_gate, gates), (w_up, ups)):
            for first, last in strips(units):
                value = product_nt(rows_in[:, 0:slab], weight[0, first:last, :])
                for d in range(1, line):
                    value = value + product_nt(
                        rows_in[:, d * slab : (d + 1) * slab], weight[d, first:last, :]
                    )
                kept[slot, :, first:last] = value

    order = (
        p.second + p.turn,
        p.first,
        p.across + p.turn,
        p.across,
        p.first + p.turn,
        p.second,
        p.core,
        p.h,
    )
    fetches = [
        pltpu.make_async_copy(rows_of(cot, j), cot_block, stage.at[6]) for j in order
    ]
    stores = [
        [
            pltpu.make_async_copy(held.at[n % 2], rows_of(home, j), stage.at[3 * (n % 2) + i])
            for i, (held, home) in enumerate(
                ((hidden, hidden_out), (grad_gate, grad_gate_out), (grad_up, grad_up_out))
            )
        ]
        for n, j in enumerate(order)
    ]

    def close(n, slot):
        fetches[n].wait()
        if n > 1:
            for copy in stores[n - 2]:
                copy.wait()
        turn = n % 2
        for first, last in strips(units):
            grad = product_nt(cot_block[:, 0:slab], w_down[0, first:last, :])
            for d in range(1, line):
                grad = grad + product_nt(
                    cot_block[:, d * slab : (d + 1) * slab], w_down[d, first:last, :]
                )
            gate = gates[slot, :, first:last]
            lift = ups[slot, :, first:last]
            sigmoid = jax.nn.sigmoid(gate)
            active = gate * sigmoid
            hidden[turn, :, first:last] = (active * lift).astype(BF16)
            grad_up[turn, :, first:last] = (grad * active).astype(BF16)
            grad_gate[turn, :, first:last] = (
                grad * lift * (sigmoid * (1.0 + gate * (1.0 - sigmoid)))
            ).astype(BF16)
        if n + 1 < len(order):
            fetches[n + 1].start()
        for copy in stores[n]:
            copy.start()

    def back(n, target, *more):
        turn = n % 2

        @pl.loop(0, line)
        def _(d):
            cols = pl.ds(pl.multiple_of(d * slab, slab), slab)
            value = product(grad_gate[turn], w_gate[d]) + product(grad_up[turn], w_up[d])
            for other in more:
                value = value + other[:, cols].astype(F32)
            target[:, cols] = value.astype(target.dtype)

    goes = (p.core, p.core, p.core, p.core, p.first, p.first, p.second)
    slots = (0, 1, 0, 1, 2, 3, 4)
    copies = [
        remote(out.at[slots[i]], into.at[i], r_send.at[i], r_recv.at[i], p.at(to))
        for i, to in enumerate(goes)
    ]
    fetches[0].start()
    for copy in started[1:4]:
        copy.wait()
    save(p.h)
    open_up(p.h, 0)
    gather.got_core()
    save(p.core)
    open_up(p.core, 1)
    down_gather.step(0)
    gather.got_first()
    gather.got_second()
    save(p.first)
    save(p.second)
    down_gather.step(1)
    open_up(p.first, 2)
    gather.got_core_second()
    gather.got_core_first()
    save(p.second + p.turn)
    save(p.first + p.turn)
    open_up(p.second + p.turn, 3)
    down_gather.step(2)
    started[4].wait()
    down_save = pltpu.make_async_copy(w_down, down_out, loads.at[5])
    down_save.start()
    close(0, 3)
    back(0, out.at[0])
    copies[0].start()
    gather.got_across()
    save(p.across)
    close(1, 2)
    copies[0].wait_recv()
    back(1, out.at[2], into.at[0])
    copies[4].start()
    gather.got_core_across()
    save(p.across + p.turn)
    open_up(p.across + p.turn, 3)
    close(2, 3)
    back(2, out.at[1])
    copies[1].start()
    open_up(p.across, 3)
    close(3, 3)
    copies[1].wait_recv()
    back(3, out.at[3], into.at[1])
    copies[5].start()
    open_up(p.first + p.turn, 3)
    close(4, 3)
    copies[0].wait_send()
    back(4, out.at[0])
    copies[2].start()
    open_up(p.second, 3)
    close(5, 3)
    copies[2].wait_recv()
    copies[5].wait_recv()
    back(5, out.at[4], into.at[2], into.at[5])
    copies[6].start()
    close(6, 1)
    copies[1].wait_send()
    back(6, out.at[1])
    copies[3].start()
    close(7, 0)
    copies[3].wait_recv()
    back(7, grad_out, into.at[3])
    copies[4].wait_recv()
    copies[6].wait_recv()

    @pl.loop(0, line)
    def _(d):
        cols = pl.ds(pl.multiple_of(d * slab, slab), slab)
        grad_out[:, cols] += into[4, :, cols].astype(F32) + into[6, :, cols].astype(F32)

    for i in range(2, 7):
        copies[i].wait_send()
    gather.finish()
    down_gather.finish()
    for copy in saved:
        copy.wait()
    for copy in stores[6] + stores[7]:
        copy.wait()
    down_save.wait()


def feed(line, middle, gain, cot, gate_a, gate_b, up, down):
    rows, width = middle.shape
    units, slab = down.shape
    full = rows * 8
    return pl.pallas_call(
        functools.partial(feed_kernel, line),
        out_shape=(
            jax.ShapeDtypeStruct((full, width), BF16),
            jax.ShapeDtypeStruct((full, units), BF16),
            jax.ShapeDtypeStruct((full, units), BF16),
            jax.ShapeDtypeStruct((full, units), BF16),
            jax.ShapeDtypeStruct((rows, width), F32),
            jax.ShapeDtypeStruct((line, units, slab), BF16),
        ),
        in_specs=[any_spec(), vmem_spec()] + [any_spec()] * 5,
        out_specs=(any_spec(), any_spec(), any_spec(), any_spec(), vmem_spec(), any_spec()),
        scratch_shapes=[
            pltpu.VMEM((full, width), BF16),
            pltpu.VMEM((line, units, slab), BF16),
            pltpu.VMEM((line, units, slab), BF16),
            pltpu.VMEM((line, units, slab), BF16),
            pltpu.VMEM((4, rows, units), F32),
            pltpu.VMEM((4, rows, units), F32),
            pltpu.VMEM((rows, width), BF16),
            pltpu.VMEM((2, rows, units), BF16),
            pltpu.VMEM((2, rows, units), BF16),
            pltpu.VMEM((2, rows, units), BF16),
            pltpu.VMEM((5, rows, width), BF16),
            pltpu.VMEM((7, rows, width), BF16),
            pltpu.SemaphoreType.DMA((7,)),
            pltpu.SemaphoreType.DMA((7,)),
            pltpu.SemaphoreType.DMA((7,)),
            pltpu.SemaphoreType.DMA((7,)),
            *line_sems(line),
            pltpu.SemaphoreType.DMA((6,)),
            pltpu.SemaphoreType.DMA((8,)),
            pltpu.SemaphoreType.DMA((7,)),
        ],
        compiler_params=pltpu.CompilerParams(
            collective_id=4, has_side_effects=True, vmem_limit_bytes=60 * MIB
        ),
        cost_estimate=pl.CostEstimate(
            flops=50 * 2**30, bytes_accessed=80 * MIB, transcendentals=0
        ),
    )(middle, gain.reshape(1, width), cot, gate_a, gate_b, up, down)


def fused(
    tokens,
    segment,
    attn_gain,
    query_weight,
    key_weight,
    value_weight,
    out_weight,
    ffn_gain,
    gate_weight,
    up_weight,
    down_weight,
    cotangent,
):
    own_rows = tokens.shape[0]
    group = own_rows * lax.axis_size("head")
    heads_here = query_weight.shape[1] // HEAD_DIM
    offset = lax.axis_index("head") * own_rows
    seq_index = lax.axis_index("seq")
    block = min(512, group)
    scale = HEAD_DIM ** (-0.5)
    line = lax.axis_size("seq")
    part = query_weight.shape[1]
    normed_full, qkv, w_qkv, floor, gate_t, up_t = project(
        line,
        tokens,
        attn_gain,
        query_weight,
        key_weight,
        value_weight,
        segment,
        gate_weight,
        up_weight,
    )
    cut = gate_t.shape[0] // 32 * 16 + 16
    attended, logs, halo_kv, grad_out, w_out_parts, gate_a = attend(
        line, qkv, floor, cotangent, out_weight, gate_t[:cut]
    )
    middle, gate_b, up_all = branch(line, attended, w_out_parts, tokens, gate_t[cut:], up_t)
    normed_two_full, hidden, grad_gate, grad_up, grad_normed_two, down_parts = feed(
        line, middle, ffn_gain, grad_out, gate_a, gate_b, up_all, down_weight
    )
    w_down = down_parts.transpose(1, 0, 2).reshape(down_weight.shape[0], -1)
    w_out = w_out_parts.transpose(1, 0, 2).reshape(part, -1)
    w_query, w_key, w_value = (w_qkv[:, i * part : (i + 1) * part] for i in range(3))
    queries, keys, values = (qkv[:, i * part : (i + 1) * part] for i in range(3))
    inputs = tokens.astype(jnp.float32)
    unit_one, inverse_one = normalize(inputs)
    halo_keys, halo_values, halo_segs = ([], [], [])
    hop = 1
    take = min(group, WINDOW - (hop - 1) * group)
    got_keys, got_values, got_segs = from_behind(
        (keys[group - take :], values[group - take :], segment[group - take :]), "seq", hop
    )
    halo_keys.append(got_keys)
    halo_values.append(got_values)
    halo_segs.append(got_segs)
    keys_ext = jnp.concatenate(halo_keys + [keys], axis=0)
    values_ext = jnp.concatenate(halo_values + [values], axis=0)
    segs_ext = jnp.concatenate(halo_segs + [segment], axis=0)
    positions = seq_index * group - WINDOW + jnp.arange(WINDOW + group)
    valid = positions >= 0
    query_heads = queries.reshape(group, heads_here, HEAD_DIM)
    key_heads = keys_ext.reshape(WINDOW + group, heads_here, HEAD_DIM)
    value_heads = values_ext.reshape(WINDOW + group, heads_here, HEAD_DIM)
    logsums = [
        logs[:, start : start + block, None] * 0.6931471805599453
        for start in range(0, group, block)
    ]
    unit_two, inverse_two = normalize(middle)
    ffn_out = lax.psum_scatter(
        product(hidden, w_down).astype(jnp.bfloat16), "head", scatter_dimension=0, tiled=True
    ).astype(jnp.float32)
    result = middle + ffn_out
    down_grad = product_tn(hidden, grad_out)
    gate_grad = product_tn(normed_two_full, grad_gate)
    up_grad = product_tn(normed_two_full, grad_up)
    ffn_gain_part = jnp.sum(grad_normed_two * unit_two, axis=0)
    grad_middle = cotangent.astype(jnp.float32) + norm_back(
        unit_two, inverse_two, ffn_gain, grad_normed_two
    )
    grad_branch = lax.all_gather(grad_middle.astype(jnp.bfloat16), "head", axis=0, tiled=True)
    out_grad = product_tn(attended, grad_branch)
    grad_attended = product_nt(grad_branch, w_out).astype(jnp.bfloat16)
    grad_heads = grad_attended.reshape(group, heads_here, HEAD_DIM)
    grad_query_list = []
    grad_keys_ext = jnp.zeros((WINDOW + group, heads_here, HEAD_DIM), jnp.float32)
    grad_values_ext = jnp.zeros((WINDOW + group, heads_here, HEAD_DIM), jnp.float32)
    for number, start in enumerate(range(0, group, block)):
        scores = block_scores(query_heads, key_heads, segment, segs_ext, valid, start, block)
        probs = jnp.exp(scores - logsums[number])
        probs_low = probs.astype(jnp.bfloat16)
        key_part = key_heads[start : start + block + WINDOW]
        value_part = value_heads[start : start + block + WINDOW]
        query_part = query_heads[start : start + block]
        grad_part = grad_heads[start : start + block]
        grad_probs = jnp.einsum(
            "qhd,khd->hqk", grad_part, value_part, preferred_element_type=jnp.float32
        )
        inner = jnp.sum(probs * grad_probs, axis=-1, keepdims=True)
        grad_scores = (probs * (grad_probs - inner)).astype(jnp.bfloat16)
        grad_query_list.append(
            jnp.einsum("hqk,khd->qhd", grad_scores, key_part, preferred_element_type=jnp.float32)
            * scale
        )
        key_term = (
            jnp.einsum("hqk,qhd->khd", grad_scores, query_part, preferred_element_type=jnp.float32)
            * scale
        )
        value_term = jnp.einsum(
            "hqk,qhd->khd", probs_low, grad_part, preferred_element_type=jnp.float32
        )
        grad_keys_ext = grad_keys_ext.at[start : start + block + WINDOW].add(key_term)
        grad_values_ext = grad_values_ext.at[start : start + block + WINDOW].add(value_term)
    grad_keys_ext = grad_keys_ext.reshape(WINDOW + group, heads_here * HEAD_DIM)
    grad_values_ext = grad_values_ext.reshape(WINDOW + group, heads_here * HEAD_DIM)
    grad_keys = grad_keys_ext[WINDOW:]
    grad_values = grad_values_ext[WINDOW:]
    cursor = 0
    hop = 1
    take = min(group, WINDOW - (hop - 1) * group)
    back_keys = from_behind(
        grad_keys_ext[cursor : cursor + take].astype(jnp.bfloat16), "seq", -hop
    ).astype(jnp.float32)
    back_values = from_behind(
        grad_values_ext[cursor : cursor + take].astype(jnp.bfloat16), "seq", -hop
    ).astype(jnp.float32)
    grad_keys = grad_keys.at[group - take :].add(back_keys)
    grad_values = grad_values.at[group - take :].add(back_values)
    grad_queries = (
        jnp.concatenate(grad_query_list, axis=0)
        .reshape(group, heads_here * HEAD_DIM)
        .astype(jnp.bfloat16)
    )
    grad_keys = grad_keys.astype(jnp.bfloat16)
    grad_values = grad_values.astype(jnp.bfloat16)
    query_grad = product_tn(normed_full, grad_queries)
    key_grad = product_tn(normed_full, grad_keys)
    value_grad = product_tn(normed_full, grad_values)
    grad_normed_one = lax.psum_scatter(
        (
            product_nt(grad_queries, w_query)
            + product_nt(grad_keys, w_key)
            + product_nt(grad_values, w_value)
        ).astype(jnp.bfloat16),
        "head",
        scatter_dimension=0,
        tiled=True,
    ).astype(jnp.float32)
    attn_gain_part = jnp.sum(grad_normed_one * unit_one, axis=0)
    input_grad = grad_middle + norm_back(unit_one, inverse_one, attn_gain, grad_normed_one)
    summed = (
        lax.psum_scatter(
            query_grad.astype(jnp.bfloat16), "seq", scatter_dimension=0, tiled=True
        ).astype(jnp.float32),
        lax.psum_scatter(
            key_grad.astype(jnp.bfloat16), "seq", scatter_dimension=0, tiled=True
        ).astype(jnp.float32),
        lax.psum_scatter(
            value_grad.astype(jnp.bfloat16), "seq", scatter_dimension=0, tiled=True
        ).astype(jnp.float32),
        lax.psum_scatter(
            out_grad.astype(jnp.bfloat16), "seq", scatter_dimension=1, tiled=True
        ).astype(jnp.float32),
        lax.psum_scatter(
            gate_grad.astype(jnp.bfloat16), "seq", scatter_dimension=0, tiled=True
        ).astype(jnp.float32),
        lax.psum_scatter(
            up_grad.astype(jnp.bfloat16), "seq", scatter_dimension=0, tiled=True
        ).astype(jnp.float32),
        lax.psum_scatter(
            down_grad.astype(jnp.bfloat16), "seq", scatter_dimension=1, tiled=True
        ).astype(jnp.float32),
    )
    gain_grads = (
        lax.psum_scatter(attn_gain_part, ("seq", "head"), scatter_dimension=0, tiled=True),
        lax.psum_scatter(ffn_gain_part, ("seq", "head"), scatter_dimension=0, tiled=True),
    )
    return (
        result.astype(jnp.bfloat16),
        input_grad,
        gain_grads[0],
        summed[0],
        summed[1],
        summed[2],
        summed[3],
        gain_grads[1],
        summed[4],
        summed[5],
        summed[6],
    )


def solution(mesh):
    placed = (
        P(("seq", "head"), None),
        P("seq"),
        P(),
        P("seq", "head"),
        P("seq", "head"),
        P("seq", "head"),
        P("head", "seq"),
        P(),
        P("seq", "head"),
        P("seq", "head"),
        P("head", "seq"),
        P(("seq", "head"), None),
    )
    body = fused if mesh.shape["head"] == 8 else local
    return jax.shard_map(
        body,
        mesh=mesh,
        in_specs=placed,
        out_specs=(
            P(("seq", "head"), None),
            P(("seq", "head"), None),
            P(("seq", "head")),
            P("seq", "head"),
            P("seq", "head"),
            P("seq", "head"),
            P("head", "seq"),
            P(("seq", "head")),
            P("seq", "head"),
            P("seq", "head"),
            P("head", "seq"),
        ),
        check_vma=False,
    )
```

```python
import functools

import jax
import jax.numpy as jnp
from jax import lax
from jax.experimental import pallas as pl
from jax.experimental.pallas import tpu as pltpu
from jax.sharding import PartitionSpec as P

HEAD_DIM = 128
WINDOW = 1024


EPS = 1e-06
NEG = -1e30


def from_behind(value, axis, by):
    count = lax.axis_size(axis)
    pairs = [(i, i + by) for i in range(count) if 0 <= i + by < count]
    return lax.ppermute(value, axis, pairs)


def product(left, right):
    return jnp.dot(left, right, preferred_element_type=jnp.float32)


def product_tn(left, right):
    return lax.dot_general(
        left, right, (((0,), (0,)), ((), ())), preferred_element_type=jnp.float32
    )


def product_nt(left, right):
    return lax.dot_general(
        left, right, (((1,), (1,)), ((), ())), preferred_element_type=jnp.float32
    )


def normalize(rows):
    inverse = lax.rsqrt(jnp.mean(rows * rows, axis=-1, keepdims=True) + EPS)
    return (rows * inverse, inverse)


def norm_back(unit, inverse, gain, grad):
    scaled = grad * gain
    return inverse * (scaled - unit * jnp.mean(scaled * unit, axis=-1, keepdims=True))


def gather_rows(rows):
    return lax.all_gather(rows, "head", axis=0, tiled=True)


def block_scores(query_heads, key_heads, seg_query, seg_keys, valid, start, block):
    query_part = query_heads[start : start + block]
    key_part = key_heads[start : start + block + WINDOW]
    scores = jnp.einsum(
        "qhd,khd->hqk", query_part, key_part, preferred_element_type=jnp.float32
    ) * HEAD_DIM ** (-0.5)
    rows = jnp.arange(block)[:, None] + WINDOW
    cols = jnp.arange(block + WINDOW)[None, :]
    distance = rows - cols
    same_doc = (
        seg_query[start : start + block][:, None]
        == seg_keys[start : start + block + WINDOW][None, :]
    )
    visible = (
        (distance >= 0)
        & (distance <= WINDOW)
        & same_doc
        & valid[start : start + block + WINDOW][None, :]
    )
    return jnp.where(visible[None], scores, NEG)


def local(
    tokens,
    segment,
    attn_gain,
    query_weight,
    key_weight,
    value_weight,
    out_weight,
    ffn_gain,
    gate_weight,
    up_weight,
    down_weight,
    cotangent,
):
    own_rows = tokens.shape[0]
    group = own_rows * lax.axis_size("head")
    heads_here = query_weight.shape[1] // HEAD_DIM
    offset = lax.axis_index("head") * own_rows
    seq_index = lax.axis_index("seq")
    block = min(512, group)
    scale = HEAD_DIM ** (-0.5)
    w_query, w_key, w_value, w_out, w_gate, w_up, w_down = (
        lax.all_gather(query_weight, "seq", axis=0, tiled=True),
        lax.all_gather(key_weight, "seq", axis=0, tiled=True),
        lax.all_gather(value_weight, "seq", axis=0, tiled=True),
        lax.all_gather(out_weight, "seq", axis=1, tiled=True),
        lax.all_gather(gate_weight, "seq", axis=0, tiled=True),
        lax.all_gather(up_weight, "seq", axis=0, tiled=True),
        lax.all_gather(down_weight, "seq", axis=1, tiled=True),
    )
    inputs = tokens.astype(jnp.float32)
    unit_one, inverse_one = normalize(inputs)
    normed_full = gather_rows((unit_one * attn_gain).astype(jnp.bfloat16))
    queries = product(normed_full, w_query).astype(jnp.bfloat16)
    keys = product(normed_full, w_key).astype(jnp.bfloat16)
    values = product(normed_full, w_value).astype(jnp.bfloat16)
    halo_keys, halo_values, halo_segs = ([], [], [])
    hop = 1
    take = min(group, WINDOW - (hop - 1) * group)
    got_keys, got_values, got_segs = from_behind(
        (keys[group - take :], values[group - take :], segment[group - take :]), "seq", hop
    )
    halo_keys.append(got_keys)
    halo_values.append(got_values)
    halo_segs.append(got_segs)
    keys_ext = jnp.concatenate(halo_keys + [keys], axis=0)
    values_ext = jnp.concatenate(halo_values + [values], axis=0)
    segs_ext = jnp.concatenate(halo_segs + [segment], axis=0)
    positions = seq_index * group - WINDOW + jnp.arange(WINDOW + group)
    valid = positions >= 0
    query_heads = queries.reshape(group, heads_here, HEAD_DIM)
    key_heads = keys_ext.reshape(WINDOW + group, heads_here, HEAD_DIM)
    value_heads = values_ext.reshape(WINDOW + group, heads_here, HEAD_DIM)
    outputs, logsums = ([], [])
    for start in range(0, group, block):
        scores = block_scores(query_heads, key_heads, segment, segs_ext, valid, start, block)
        highest = jnp.max(scores, axis=-1, keepdims=True)
        weights = jnp.exp(scores - highest)
        total = jnp.sum(weights, axis=-1, keepdims=True)
        probs = (weights / total).astype(jnp.bfloat16)
        outputs.append(
            jnp.einsum(
                "hqk,khd->qhd",
                probs,
                value_heads[start : start + block + WINDOW],
                preferred_element_type=jnp.float32,
            )
        )
        logsums.append(highest + jnp.log(total))
    attended = (
        jnp.concatenate(outputs, axis=0).reshape(group, heads_here * HEAD_DIM).astype(jnp.bfloat16)
    )
    partial_out = product(attended, w_out)
    own_part = lax.dynamic_slice_in_dim(partial_out, offset, own_rows, 0)
    placed = lax.dynamic_update_slice_in_dim(partial_out, own_part + inputs, offset, 0)
    middle_full = lax.psum(placed, "head")
    middle = lax.dynamic_slice_in_dim(middle_full, offset, own_rows, 0)
    unit_full, inverse_full = normalize(middle_full)
    normed_two_full = (unit_full * ffn_gain).astype(jnp.bfloat16)
    unit_two, inverse_two = normalize(middle)
    gate = product(normed_two_full, w_gate)
    up = product(normed_two_full, w_up)
    sigmoid = jax.nn.sigmoid(gate)
    activated = gate * sigmoid
    hidden = (activated * up).astype(jnp.bfloat16)
    ffn_out = lax.psum_scatter(
        product(hidden, w_down).astype(jnp.bfloat16), "head", scatter_dimension=0, tiled=True
    ).astype(jnp.float32)
    result = middle + ffn_out
    grad_out = lax.all_gather(cotangent, "head", axis=0, tiled=True)
    grad_hidden = product_nt(grad_out, w_down)
    grad_gate = (grad_hidden * up * sigmoid * (1.0 + gate * (1.0 - sigmoid))).astype(jnp.bfloat16)
    grad_up = (grad_hidden * activated).astype(jnp.bfloat16)
    down_grad = product_tn(hidden, grad_out)
    gate_grad = product_tn(normed_two_full, grad_gate)
    up_grad = product_tn(normed_two_full, grad_up)
    grad_normed_two = lax.psum_scatter(
        (product_nt(grad_gate, w_gate) + product_nt(grad_up, w_up)).astype(jnp.bfloat16),
        "head",
        scatter_dimension=0,
        tiled=True,
    ).astype(jnp.float32)
    ffn_gain_part = jnp.sum(grad_normed_two * unit_two, axis=0)
    grad_middle = cotangent.astype(jnp.float32) + norm_back(
        unit_two, inverse_two, ffn_gain, grad_normed_two
    )
    grad_branch = lax.all_gather(grad_middle.astype(jnp.bfloat16), "head", axis=0, tiled=True)
    out_grad = product_tn(attended, grad_branch)
    grad_attended = product_nt(grad_branch, w_out).astype(jnp.bfloat16)
    grad_heads = grad_attended.reshape(group, heads_here, HEAD_DIM)
    grad_query_list = []
    grad_keys_ext = jnp.zeros((WINDOW + group, heads_here, HEAD_DIM), jnp.float32)
    grad_values_ext = jnp.zeros((WINDOW + group, heads_here, HEAD_DIM), jnp.float32)
    for number, start in enumerate(range(0, group, block)):
        scores = block_scores(query_heads, key_heads, segment, segs_ext, valid, start, block)
        probs = jnp.exp(scores - logsums[number])
        probs_low = probs.astype(jnp.bfloat16)
        key_part = key_heads[start : start + block + WINDOW]
        value_part = value_heads[start : start + block + WINDOW]
        query_part = query_heads[start : start + block]
        grad_part = grad_heads[start : start + block]
        grad_probs = jnp.einsum(
            "qhd,khd->hqk", grad_part, value_part, preferred_element_type=jnp.float32
        )
        inner = jnp.sum(probs * grad_probs, axis=-1, keepdims=True)
        grad_scores = (probs * (grad_probs - inner)).astype(jnp.bfloat16)
        grad_query_list.append(
            jnp.einsum("hqk,khd->qhd", grad_scores, key_part, preferred_element_type=jnp.float32)
            * scale
        )
        key_term = (
            jnp.einsum("hqk,qhd->khd", grad_scores, query_part, preferred_element_type=jnp.float32)
            * scale
        )
        value_term = jnp.einsum(
            "hqk,qhd->khd", probs_low, grad_part, preferred_element_type=jnp.float32
        )
        grad_keys_ext = grad_keys_ext.at[start : start + block + WINDOW].add(key_term)
        grad_values_ext = grad_values_ext.at[start : start + block + WINDOW].add(value_term)
    grad_keys_ext = grad_keys_ext.reshape(WINDOW + group, heads_here * HEAD_DIM)
    grad_values_ext = grad_values_ext.reshape(WINDOW + group, heads_here * HEAD_DIM)
    grad_keys = grad_keys_ext[WINDOW:]
    grad_values = grad_values_ext[WINDOW:]
    cursor = 0
    hop = 1
    take = min(group, WINDOW - (hop - 1) * group)
    back_keys = from_behind(
        grad_keys_ext[cursor : cursor + take].astype(jnp.bfloat16), "seq", -hop
    ).astype(jnp.float32)
    back_values = from_behind(
        grad_values_ext[cursor : cursor + take].astype(jnp.bfloat16), "seq", -hop
    ).astype(jnp.float32)
    grad_keys = grad_keys.at[group - take :].add(back_keys)
    grad_values = grad_values.at[group - take :].add(back_values)
    grad_queries = (
        jnp.concatenate(grad_query_list, axis=0)
        .reshape(group, heads_here * HEAD_DIM)
        .astype(jnp.bfloat16)
    )
    grad_keys = grad_keys.astype(jnp.bfloat16)
    grad_values = grad_values.astype(jnp.bfloat16)
    query_grad = product_tn(normed_full, grad_queries)
    key_grad = product_tn(normed_full, grad_keys)
    value_grad = product_tn(normed_full, grad_values)
    grad_normed_one = lax.psum_scatter(
        (
            product_nt(grad_queries, w_query)
            + product_nt(grad_keys, w_key)
            + product_nt(grad_values, w_value)
        ).astype(jnp.bfloat16),
        "head",
        scatter_dimension=0,
        tiled=True,
    ).astype(jnp.float32)
    attn_gain_part = jnp.sum(grad_normed_one * unit_one, axis=0)
    input_grad = grad_middle + norm_back(unit_one, inverse_one, attn_gain, grad_normed_one)
    summed = (
        lax.psum_scatter(
            query_grad.astype(jnp.bfloat16), "seq", scatter_dimension=0, tiled=True
        ).astype(jnp.float32),
        lax.psum_scatter(
            key_grad.astype(jnp.bfloat16), "seq", scatter_dimension=0, tiled=True
        ).astype(jnp.float32),
        lax.psum_scatter(
            value_grad.astype(jnp.bfloat16), "seq", scatter_dimension=0, tiled=True
        ).astype(jnp.float32),
        lax.psum_scatter(
            out_grad.astype(jnp.bfloat16), "seq", scatter_dimension=1, tiled=True
        ).astype(jnp.float32),
        lax.psum_scatter(
            gate_grad.astype(jnp.bfloat16), "seq", scatter_dimension=0, tiled=True
        ).astype(jnp.float32),
        lax.psum_scatter(
            up_grad.astype(jnp.bfloat16), "seq", scatter_dimension=0, tiled=True
        ).astype(jnp.float32),
        lax.psum_scatter(
            down_grad.astype(jnp.bfloat16), "seq", scatter_dimension=1, tiled=True
        ).astype(jnp.float32),
    )
    gain_grads = (
        lax.psum_scatter(attn_gain_part, ("seq", "head"), scatter_dimension=0, tiled=True),
        lax.psum_scatter(ffn_gain_part, ("seq", "head"), scatter_dimension=0, tiled=True),
    )
    return (
        result.astype(jnp.bfloat16),
        input_grad,
        gain_grads[0],
        summed[0],
        summed[1],
        summed[2],
        summed[3],
        gain_grads[1],
        summed[4],
        summed[5],
        summed[6],
    )


MESH = pl.DeviceIdType.MESH
BF16 = jnp.bfloat16
F32 = jnp.float32
MIB = 2**20


def remote(src, dst, send_sem, recv_sem, where):
    return pltpu.make_async_remote_copy(
        src_ref=src,
        dst_ref=dst,
        send_sem=send_sem,
        recv_sem=recv_sem,
        device_id=where,
        device_id_type=MESH,
    )


class Place:
    def __init__(self, line):
        s, h = lax.axis_index("seq"), lax.axis_index("head")
        core = lax.rem(h, 2)
        x = lax.rem(lax.div(h, 2), 2)
        y = lax.div(h, 4)
        self.s, self.h, self.line = s, h, line
        self.turn = 1 - 2 * core
        self.core = h + self.turn
        over_x, over_y = 2 - 4 * x, 4 - 8 * y
        self.first = h + over_x * (1 - core) + over_y * core
        self.second = h + over_y * (1 - core) + over_x * core
        self.across = h + over_x + over_y

    def at(self, head):
        return (self.s, head)

    def greet(self, along_seq=True):
        barrier = pltpu.get_barrier_semaphore()
        for head in (self.core, self.first, self.second):
            pl.semaphore_signal(barrier, inc=1, device_id=self.at(head), device_id_type=MESH)
        if along_seq:

            @pl.when(self.s > 0)
            def _():
                pl.semaphore_signal(
                    barrier, inc=1, device_id=(self.s - 1, self.h), device_id_type=MESH
                )

            @pl.when(self.s < self.line - 1)
            def _():
                pl.semaphore_signal(
                    barrier, inc=1, device_id=(self.s + 1, self.h), device_id_type=MESH
                )

            @pl.when((self.s > 0) & (self.s < self.line - 1))
            def _():
                pl.semaphore_wait(barrier, 5)

            @pl.when((self.s == 0) | (self.s == self.line - 1))
            def _():
                pl.semaphore_wait(barrier, 4)
        else:
            pl.semaphore_wait(barrier, 3)


class HeadGather:
    SEMS = 7

    def __init__(self, place, block, send, recv, own=None):
        p = place
        self.p = p
        plan = (
            (p.h, p.first, p.first),
            (p.h, p.second, p.second),
            (p.h, p.core, p.core),
            (p.first, p.second, p.across),
            (p.first, p.core, p.second + p.turn),
            (p.second, p.core, p.first + p.turn),
            (p.across, p.core, p.across + p.turn),
        )
        self.out = [
            remote(
                block(j) if own is None or i > 2 else own,
                block(j),
                send.at[i],
                recv.at[i],
                p.at(to),
            )
            for i, (j, to, _) in enumerate(plan)
        ]
        self.come = [
            remote(block(j), block(j), send.at[i], recv.at[i], p.at(to))
            for i, (_, to, j) in enumerate(plan)
        ]

    def start(self):
        for i in (0, 1, 2):
            self.out[i].start()

    def got_first(self):
        self.come[0].wait_recv()
        self.out[3].start()
        self.out[4].start()

    def got_second(self):
        self.come[1].wait_recv()
        self.out[5].start()

    def got_across(self):
        self.come[3].wait_recv()
        self.out[6].start()

    def got_core(self):
        self.come[2].wait_recv()

    def got_core_second(self):
        self.come[4].wait_recv()

    def got_core_first(self):
        self.come[5].wait_recv()

    def got_core_across(self):
        self.come[6].wait_recv()

    def finish(self):
        for copy in self.out:
            copy.wait_send()


class LineGather:
    def __init__(self, place, piece, up_send, up_recv, down_send, down_recv, own=None):
        self.p, self.piece, self.own = place, piece, own
        self.up = (up_send, up_recv)
        self.down = (down_send, down_recv)

    def _up(self, owner, t):
        p = self.p
        source = self.own if t == 0 and self.own is not None else self.piece(owner)
        return remote(
            source, self.piece(owner), self.up[0].at[t], self.up[1].at[t], (p.s + 1, p.h)
        )

    def _down(self, owner, t):
        p = self.p
        source = self.own if t == 0 and self.own is not None else self.piece(owner)
        return remote(
            source,
            self.piece(owner),
            self.down[0].at[t],
            self.down[1].at[t],
            (p.s - 1, p.h),
        )

    def start(self, t):
        p = self.p

        @pl.when((p.s < p.line - 1) & (p.s >= t))
        def _():
            self._up(p.s - t, t).start()

        @pl.when((p.s > 0) & (p.s + t < p.line))
        def _():
            self._down(p.s + t, t).start()

    def got(self, t):
        p = self.p

        @pl.when(p.s >= t + 1)
        def _():
            self._up(p.s - 1 - t, t).wait_recv()

        @pl.when(p.s + 1 + t < p.line)
        def _():
            self._down(p.s + 1 + t, t).wait_recv()

    def step(self, t):
        self.got(t)
        if t + 1 < self.p.line - 1:
            self.start(t + 1)

    def finish(self):
        p = self.p
        for t in range(p.line - 1):

            @pl.when((p.s < p.line - 1) & (p.s >= t))
            def _():
                self._up(p.s - t, t).wait_send()

            @pl.when((p.s > 0) & (p.s + t < p.line))
            def _():
                self._down(p.s + t, t).wait_send()


def line_sems(line, tensors=1):
    return [pltpu.SemaphoreType.DMA((line - 1,)) for _ in range(4 * tensors)]


def norm_rows(rows, gain):
    inverse = lax.rsqrt(jnp.mean(rows * rows, axis=-1, keepdims=True) + EPS)
    return rows * inverse * gain


def own_starts(segment):
    count = segment.shape[1]
    ids = segment[...]
    place = lax.broadcasted_iota(jnp.int32, (1, count), 1)
    starts = jnp.where((place > 0) & (ids != pltpu.roll(ids, 1, 1)), place, -1)
    shift = 1
    while shift < count:
        earlier = jnp.where(place >= shift, pltpu.roll(starts, shift, 1), -1)
        starts = jnp.maximum(starts, earlier)
        shift *= 2
    return starts


def turned_over(source, target):
    width = source.shape[1]
    for start in range(0, width, 128):
        stop = min(start + 128, width)
        target[start:stop, :] = source[:, start:stop].T


def project_kernel(
    line,
    tokens,
    gain,
    wq,
    wk,
    wv,
    segment,
    w_gate,
    w_up,
    normed_out,
    qkv_out,
    weight_out,
    floor_out,
    gate_out,
    up_out,
    normed,
    weight,
    g_send,
    g_recv,
    us,
    ur,
    ds,
    dr,
    keep,
    seg_halo,
    seg_sems,
):
    p = Place(line)
    rows, width = tokens.shape
    slab, part = wq.shape
    count = segment.shape[1]
    seg_copy = remote(
        segment.at[:, pl.ds(count - WINDOW, WINDOW)],
        seg_halo,
        seg_sems.at[0],
        seg_sems.at[1],
        (p.s + 1, p.h),
    )
    weight_own = weight.at[pl.ds(pl.multiple_of(p.s * slab, slab), slab)]
    weight_own[:, 0:part] = wq[...]
    weight_own[:, part : 2 * part] = wk[...]
    weight_own[:, 2 * part : 3 * part] = wv[...]
    block = lambda j: normed.at[pl.ds(pl.multiple_of(j * rows, rows), rows)]
    home = lambda j: normed_out.at[pl.ds(pl.multiple_of(j * rows, rows), rows)]
    piece = lambda d: weight.at[pl.ds(pl.multiple_of(d * slab, slab), slab)]
    gather = HeadGather(p, block, g_send, g_recv)
    line_gather = LineGather(p, piece, us, ur, ds, dr)
    p.greet()
    line_gather.start(0)

    @pl.when(p.s < line - 1)
    def _():
        seg_copy.start()

    mine = block(p.h)
    step = 32

    @pl.loop(0, rows // step)
    def _(i):
        at = pl.ds(pl.multiple_of(i * step, step), step)
        mine[at] = norm_rows(tokens[at].astype(F32), gain[...]).astype(BF16)

    gather.start()

    def multiply(j):
        start = pl.multiple_of(j * rows, rows)

        @pl.loop(0, 3)
        def _(n):
            cols = pl.ds(pl.multiple_of(n * part, part), part)
            qkv_out[pl.ds(start, rows), cols] = jnp.dot(
                normed[pl.ds(start, rows), :], weight[:, cols], preferred_element_type=F32
            ).astype(BF16)

    saved = []

    def save(j):
        copy = pltpu.make_async_copy(block(j), home(j), keep.at[len(saved)])
        copy.start()
        saved.append(copy)

    save(p.h)
    starts = own_starts(segment)
    for source, target in ((w_gate, gate_out), (w_up, up_out)):
        turned_over(source, target)

    @pl.when(p.s > 0)
    def _():
        seg_copy.wait_recv()

    before = jnp.sum(
        (seg_halo[...] == segment[:, 0:1]).astype(jnp.int32), axis=1, keepdims=True
    )
    before = jnp.where(p.s > 0, before, 0)
    floor_out[...] = jnp.maximum(
        lax.broadcasted_iota(jnp.int32, (1, count), 1),
        jnp.where(starts >= 0, starts + WINDOW, WINDOW - before),
    )
    gather.got_core()
    save(p.core)
    line_gather.step(0)
    gather.got_first()
    gather.got_second()
    save(p.first)
    save(p.second)
    line_gather.step(1)
    gather.got_core_second()
    gather.got_core_first()
    save(p.second + p.turn)
    save(p.first + p.turn)
    line_gather.step(2)
    out_copy = pltpu.make_async_copy(weight, weight_out, keep.at[8])
    out_copy.start()
    for j in (p.h, p.core, p.first, p.second):
        multiply(j)
    gather.got_across()
    save(p.across)
    for j in (p.second + p.turn, p.first + p.turn, p.across):
        multiply(j)
    gather.got_core_across()
    save(p.across + p.turn)
    multiply(p.across + p.turn)
    gather.finish()
    line_gather.finish()

    @pl.when(p.s < line - 1)
    def _():
        seg_copy.wait_send()

    for copy in saved:
        copy.wait()
    out_copy.wait()


def any_spec():
    return pl.BlockSpec(memory_space=pl.ANY)


def vmem_spec():
    return pl.BlockSpec(memory_space=pltpu.VMEM)


def project(line, tokens, gain, wq, wk, wv, segment, w_gate, w_up):
    rows, width = tokens.shape
    slab, part = wq.shape
    full = rows * 8
    return pl.pallas_call(
        functools.partial(project_kernel, line),
        out_shape=(
            jax.ShapeDtypeStruct((full, width), BF16),
            jax.ShapeDtypeStruct((full, 3 * part), BF16),
            jax.ShapeDtypeStruct((slab * line, 3 * part), BF16),
            jax.ShapeDtypeStruct((1, full), jnp.int32),
            jax.ShapeDtypeStruct((w_gate.shape[1], slab), BF16),
            jax.ShapeDtypeStruct((w_gate.shape[1], slab), BF16),
        ),
        in_specs=[vmem_spec()] * 8,
        out_specs=(any_spec(), vmem_spec(), any_spec(), vmem_spec(), vmem_spec(), vmem_spec()),
        scratch_shapes=[
            pltpu.VMEM((full, width), BF16),
            pltpu.VMEM((slab * line, 3 * part), BF16),
            pltpu.SemaphoreType.DMA((7,)),
            pltpu.SemaphoreType.DMA((7,)),
            *line_sems(line),
            pltpu.SemaphoreType.DMA((9,)),
            pltpu.VMEM((1, WINDOW), jnp.int32),
            pltpu.SemaphoreType.DMA((2,)),
        ],
        compiler_params=pltpu.CompilerParams(
            collective_id=1, has_side_effects=True, vmem_limit_bytes=48 * MIB
        ),
        cost_estimate=pl.CostEstimate(
            flops=2 * full * width * 3 * part, bytes_accessed=40 * MIB, transcendentals=0
        ),
    )(tokens, gain.reshape(1, width), wq, wk, wv, segment.reshape(1, full), w_gate, w_up)


LOG2E = 1.4426950408889634
TILE = 256
CHUNKS = WINDOW // TILE + 1


def tile_scores(tile, head, q, k_ext, floor):
    start = pl.multiple_of(tile * TILE, TILE)
    cols = slice(head * HEAD_DIM, (head + 1) * HEAD_DIM)
    queries = q[pl.ds(start, TILE), cols]
    row = lax.broadcasted_iota(jnp.int32, (TILE, TILE), 0)
    lane = lax.broadcasted_iota(jnp.int32, (TILE, TILE), 1)
    lowest = floor[:, pl.ds(start, TILE)] - start
    found = []
    for i in range(CHUNKS):
        keys = k_ext[pl.ds(start + i * TILE, TILE), cols]
        scores = product_nt(keys, queries)
        visible = row >= lowest - i * TILE
        if i == CHUNKS - 1:
            visible = visible & (row <= lane)
        found.append((scores, visible))
    return found


def forward_tile(tile, q, k_ext, v_t, floor, attended, logs):
    start = pl.multiple_of(tile * TILE, TILE)
    sharp = HEAD_DIM ** (-0.5) * LOG2E
    for head in range(q.shape[1] // HEAD_DIM):
        cols = slice(head * HEAD_DIM, (head + 1) * HEAD_DIM)
        found = [
            jnp.where(visible, scores, NEG)
            for scores, visible in tile_scores(tile, head, q, k_ext, floor)
        ]
        highest = functools.reduce(
            jnp.maximum, [jnp.max(scores, axis=0, keepdims=True) for scores in found]
        )
        total = jnp.zeros((1, TILE), F32)
        mixed = jnp.zeros((HEAD_DIM, TILE), F32)
        for i, scores in enumerate(found):
            weights = jnp.exp2((scores - highest) * sharp)
            total = total + jnp.sum(weights, axis=0, keepdims=True)
            mixed = mixed + product(
                v_t[cols, pl.ds(start + i * TILE, TILE)], weights.astype(BF16)
            )
        attended[pl.ds(start, TILE), cols] = (mixed / total).astype(BF16).T
        logs[head : head + 1, pl.ds(start, TILE)] = highest * sharp + jnp.log2(total)


def attend_kernel(
    line,
    qkv,
    floor,
    cot,
    w_out,
    gate_a,
    attended,
    logs,
    halo_out,
    cot_out,
    w_out_full,
    gate_full,
    q,
    k_ext,
    v_ext,
    v_t,
    g_send,
    g_recv,
    *sems,
):
    p = Place(line)
    out_sems, gate_sems, halo_send, halo_recv, keep = sems[0:4], sems[4:8], *sems[8:11]
    rows = cot.shape[0]
    count, part = q.shape
    p.greet()
    block = lambda j: cot_out.at[pl.ds(pl.multiple_of(j * rows, rows), rows)]
    gather = HeadGather(p, block, g_send, g_recv, own=cot)
    halo = [
        remote(
            qkv.at[pl.ds(count - WINDOW, WINDOW), pl.ds((1 + i) * part, part)],
            ext.at[pl.ds(0, WINDOW)],
            halo_send.at[i],
            halo_recv.at[i],
            (p.s + 1, p.h),
        )
        for i, ext in enumerate((k_ext, v_ext))
    ]

    @pl.when(p.s < line - 1)
    def _():
        halo[0].start()
        halo[1].start()

    gather.start()
    loads = [
        pltpu.make_async_copy(qkv.at[:, pl.ds(0, part)], q, keep.at[0]),
        pltpu.make_async_copy(
            qkv.at[:, pl.ds(part, part)], k_ext.at[pl.ds(WINDOW, count)], keep.at[1]
        ),
        pltpu.make_async_copy(
            qkv.at[:, pl.ds(2 * part, part)], v_ext.at[pl.ds(WINDOW, count)], keep.at[2]
        ),
    ]
    for copy in loads:
        copy.start()
    out_gather = LineGather(p, lambda d: w_out_full.at[d], *out_sems, own=w_out)
    gate_gather = LineGather(p, lambda d: gate_full.at[d], *gate_sems, own=gate_a)
    out_gather.start(0)
    own = [
        pltpu.make_async_copy(cot, block(p.h), keep.at[3]),
        pltpu.make_async_copy(w_out, w_out_full.at[p.s], keep.at[4]),
        pltpu.make_async_copy(gate_a, gate_full.at[p.s], keep.at[5]),
    ]
    for copy in own:
        copy.start()

    @pl.when(p.s == 0)
    def _():
        k_ext[0:WINDOW, :] = jnp.zeros((WINDOW, part), BF16)
        v_ext[0:WINDOW, :] = jnp.zeros((WINDOW, part), BF16)

    for copy in loads:
        copy.wait()

    def turn(first, last):
        @pl.loop(first, last)
        def _(i):
            at = pl.ds(pl.multiple_of(i * TILE, TILE), TILE)
            v_t[:, at] = v_ext[at, :].T

    def tiles(first, last):
        @pl.loop(first, last)
        def _(tile):
            forward_tile(tile, q, k_ext, v_t, floor, attended, logs)

    ahead = WINDOW // TILE
    turn(ahead, ahead + count // TILE)
    tiles(ahead, count // TILE)
    out_gather.step(0)
    gate_gather.start(0)

    @pl.when(p.s > 0)
    def _():
        halo[0].wait_recv()
        halo[1].wait_recv()

    turn(0, ahead)
    tiles(0, ahead)
    saves = [
        pltpu.make_async_copy(ext.at[pl.ds(0, WINDOW)], halo_out.at[i], keep.at[6 + i])
        for i, ext in enumerate((k_ext, v_ext))
    ]
    for copy in saves:
        copy.start()
    out_gather.step(1)
    gate_gather.step(0)
    gather.got_core()
    gather.got_first()
    gather.got_second()
    gather.got_core_second()
    gather.got_core_first()
    out_gather.step(2)
    gate_gather.step(1)
    gather.got_across()
    gather.got_core_across()
    gate_gather.step(2)
    gather.finish()
    out_gather.finish()
    gate_gather.finish()

    @pl.when(p.s < line - 1)
    def _():
        halo[0].wait_send()
        halo[1].wait_send()

    for copy in own + saves:
        copy.wait()


def attend(line, qkv, floor, cot, w_out, gate_a):
    count = qkv.shape[0]
    part = qkv.shape[1] // 3
    heads = part // HEAD_DIM
    rows, width = cot.shape
    return pl.pallas_call(
        functools.partial(attend_kernel, line),
        out_shape=(
            jax.ShapeDtypeStruct((count, part), BF16),
            jax.ShapeDtypeStruct((heads, count), F32),
            jax.ShapeDtypeStruct((2, WINDOW, part), BF16),
            jax.ShapeDtypeStruct((rows * 8, width), BF16),
            jax.ShapeDtypeStruct((line, *w_out.shape), BF16),
            jax.ShapeDtypeStruct((line, *gate_a.shape), BF16),
        ),
        in_specs=[any_spec(), vmem_spec(), any_spec(), any_spec(), any_spec()],
        out_specs=(vmem_spec(), vmem_spec(), any_spec(), any_spec(), any_spec(), any_spec()),
        scratch_shapes=[
            pltpu.VMEM((count, part), BF16),
            pltpu.VMEM((WINDOW + count, part), BF16),
            pltpu.VMEM((WINDOW + count, part), BF16),
            pltpu.VMEM((part, WINDOW + count), BF16),
            pltpu.SemaphoreType.DMA((7,)),
            pltpu.SemaphoreType.DMA((7,)),
            *line_sems(line, 2),
            pltpu.SemaphoreType.DMA((2,)),
            pltpu.SemaphoreType.DMA((2,)),
            pltpu.SemaphoreType.DMA((8,)),
        ],
        compiler_params=pltpu.CompilerParams(
            collective_id=2, has_side_effects=True, vmem_limit_bytes=48 * MIB
        ),
        cost_estimate=pl.CostEstimate(
            flops=5 * 2**31, bytes_accessed=40 * MIB, transcendentals=0
        ),
    )(qkv, floor, cot, w_out, gate_a)


class HeadReduce:
    def __init__(self, place, out, into, send, recv):
        p = place
        self.p, self.out, self.into = p, out, into
        goes = (p.core, p.core, p.core, p.core, p.first, p.first, p.second)
        self.copies = [
            remote(out.at[i], into.at[i], send.at[i], recv.at[i], p.at(to))
            for i, to in enumerate(goes)
        ]
        self.for_core = (p.second + p.turn, p.across + p.turn, p.first + p.turn, p.core)
        self.mine = (p.first, p.across, p.second, p.h)

    def send(self, i):
        self.copies[i].start()

    def got(self, i):
        self.copies[i].wait_recv()

    def finish(self):
        for copy in self.copies:
            copy.wait_send()


def reduce_scratch(rows, width):
    return [
        pltpu.VMEM((7, rows, width), BF16),
        pltpu.VMEM((7, rows, width), BF16),
        pltpu.SemaphoreType.DMA((7,)),
        pltpu.SemaphoreType.DMA((7,)),
    ]


def branch_kernel(
    line,
    attended,
    w_out,
    tokens,
    gate_b,
    up,
    middle,
    gate_full,
    up_full,
    out,
    into,
    r_send,
    r_recv,
    *sems,
):
    p = Place(line)
    gate_sems, up_sems, keep = sems[0:4], sems[4:8], sems[8]
    rows, width = tokens.shape
    slab = w_out.shape[2]
    p.greet()
    gate_gather = LineGather(p, lambda d: gate_full.at[d], *gate_sems, own=gate_b)
    up_gather = LineGather(p, lambda d: up_full.at[d], *up_sems, own=up)
    gate_gather.start(0)
    own = [
        pltpu.make_async_copy(gate_b, gate_full.at[p.s], keep.at[0]),
        pltpu.make_async_copy(up, up_full.at[p.s], keep.at[1]),
    ]
    for copy in own:
        copy.start()
    reduce = HeadReduce(p, out, into, r_send, r_recv)

    def emit(j, target, *more):
        start = pl.multiple_of(j * rows, rows)

        @pl.loop(0, line)
        def _(n):
            cols = pl.ds(pl.multiple_of(n * slab, slab), slab)
            value = product(attended[pl.ds(start, rows), :], w_out[n])
            for other in more:
                value = value + other[:, cols].astype(F32)
            target[:, cols] = value.astype(target.dtype)

    for i in range(4):
        emit(reduce.for_core[i], out.at[i])
        reduce.send(i)
    for i in range(2):
        reduce.got(i)
        emit(reduce.mine[i], out.at[4 + i], into.at[i])
        reduce.send(4 + i)
    reduce.got(3)
    emit(p.h, middle, into.at[3], tokens)
    reduce.got(2)
    gate_gather.step(0)
    up_gather.start(0)
    gate_gather.step(1)
    reduce.got(5)
    emit(p.second, out.at[6], into.at[2], into.at[5])
    reduce.send(6)
    gate_gather.step(2)
    up_gather.step(0)
    reduce.got(4)
    up_gather.step(1)
    reduce.got(6)

    @pl.loop(0, line)
    def _(n):
        cols = pl.ds(pl.multiple_of(n * slab, slab), slab)
        middle[:, cols] += into[4, :, cols].astype(F32) + into[6, :, cols].astype(F32)

    up_gather.step(2)
    reduce.finish()
    gate_gather.finish()
    up_gather.finish()
    for copy in own:
        copy.wait()


def branch(line, attended, w_out, tokens, gate_b, up):
    rows, width = tokens.shape
    return pl.pallas_call(
        functools.partial(branch_kernel, line),
        out_shape=(
            jax.ShapeDtypeStruct((rows, width), F32),
            jax.ShapeDtypeStruct((line, *gate_b.shape), BF16),
            jax.ShapeDtypeStruct((line, *up.shape), BF16),
        ),
        in_specs=[vmem_spec(), vmem_spec(), vmem_spec(), any_spec(), any_spec()],
        out_specs=(vmem_spec(), any_spec(), any_spec()),
        scratch_shapes=[
            *reduce_scratch(rows, width),
            *line_sems(line, 2),
            pltpu.SemaphoreType.DMA((2,)),
        ],
        compiler_params=pltpu.CompilerParams(
            collective_id=3, has_side_effects=True, vmem_limit_bytes=48 * MIB
        ),
        cost_estimate=pl.CostEstimate(
            flops=3 * 2**30, bytes_accessed=40 * MIB, transcendentals=0
        ),
    )(attended, w_out, tokens, gate_b, up)


def strips(width, most=256):
    return [(start, min(start + most, width)) for start in range(0, width, most)]


def feed_kernel(
    line,
    middle,
    gain,
    cot,
    gate_a,
    gate_b,
    up,
    down,
    normed_out,
    hidden_out,
    grad_gate_out,
    grad_up_out,
    grad_out,
    down_out,
    normed,
    w_gate,
    w_up,
    w_down,
    gates,
    ups,
    cot_block,
    hidden,
    grad_gate,
    grad_up,
    out,
    into,
    r_send,
    r_recv,
    g_send,
    g_recv,
    *sems,
):
    p = Place(line)
    down_sems, loads, saves, stage = sems[0:4], sems[4], sems[5], sems[6]
    rows, width = grad_out.shape
    units = w_down.shape[1]
    slab = w_down.shape[2]
    cut = gate_a.shape[1]
    block = lambda j: normed.at[pl.ds(pl.multiple_of(j * rows, rows), rows)]
    rows_of = lambda ref, j: ref.at[pl.ds(pl.multiple_of(j * rows, rows), rows)]
    gather = HeadGather(p, block, g_send, g_recv)
    down_gather = LineGather(p, lambda d: w_down.at[d], *down_sems, own=down)
    p.greet()
    down_gather.start(0)
    started = [
        pltpu.make_async_copy(middle, grad_out, loads.at[0]),
        pltpu.make_async_copy(gate_a, w_gate.at[:, pl.ds(0, cut)], loads.at[1]),
        pltpu.make_async_copy(gate_b, w_gate.at[:, pl.ds(cut, units - cut)], loads.at[2]),
        pltpu.make_async_copy(up, w_up, loads.at[3]),
        pltpu.make_async_copy(down, w_down.at[p.s], loads.at[4]),
    ]
    for copy in started:
        copy.start()
    started[0].wait()
    mine = block(p.h)
    step = 32

    @pl.loop(0, rows // step)
    def _(i):
        at = pl.ds(pl.multiple_of(i * step, step), step)
        mine[at] = norm_rows(grad_out[at], gain[...]).astype(BF16)

    gather.start()
    saved = []

    def save(j):
        copy = pltpu.make_async_copy(block(j), rows_of(normed_out, j), saves.at[len(saved)])
        copy.start()
        saved.append(copy)

    def open_up(j, slot):
        rows_in = normed.at[pl.ds(pl.multiple_of(j * rows, rows), rows)]
        for weight, kept in ((w_gate, gates), (w_up, ups)):
            for first, last in strips(units):
                value = product_nt(rows_in[:, 0:slab], weight[0, first:last, :])
                for d in range(1, line):
                    value = value + product_nt(
                        rows_in[:, d * slab : (d + 1) * slab], weight[d, first:last, :]
                    )
                kept[slot, :, first:last] = value

    order = (
        p.second + p.turn,
        p.first,
        p.across + p.turn,
        p.across,
        p.first + p.turn,
        p.second,
        p.core,
        p.h,
    )
    fetches = [
        pltpu.make_async_copy(rows_of(cot, j), cot_block, stage.at[6]) for j in order
    ]
    stores = [
        [
            pltpu.make_async_copy(held.at[n % 2], rows_of(home, j), stage.at[3 * (n % 2) + i])
            for i, (held, home) in enumerate(
                ((hidden, hidden_out), (grad_gate, grad_gate_out), (grad_up, grad_up_out))
            )
        ]
        for n, j in enumerate(order)
    ]

    def close(n, slot):
        fetches[n].wait()
        if n > 1:
            for copy in stores[n - 2]:
                copy.wait()
        turn = n % 2
        for first, last in strips(units):
            grad = product_nt(cot_block[:, 0:slab], w_down[0, first:last, :])
            for d in range(1, line):
                grad = grad + product_nt(
                    cot_block[:, d * slab : (d + 1) * slab], w_down[d, first:last, :]
                )
            gate = gates[slot, :, first:last]
            lift = ups[slot, :, first:last]
            sigmoid = jax.nn.sigmoid(gate)
            active = gate * sigmoid
            hidden[turn, :, first:last] = (active * lift).astype(BF16)
            grad_up[turn, :, first:last] = (grad * active).astype(BF16)
            grad_gate[turn, :, first:last] = (
                grad * lift * (sigmoid * (1.0 + gate * (1.0 - sigmoid)))
            ).astype(BF16)
        if n + 1 < len(order):
            fetches[n + 1].start()
        for copy in stores[n]:
            copy.start()

    def back(n, target, *more):
        turn = n % 2

        @pl.loop(0, line)
        def _(d):
            cols = pl.ds(pl.multiple_of(d * slab, slab), slab)
            value = product(grad_gate[turn], w_gate[d]) + product(grad_up[turn], w_up[d])
            for other in more:
                value = value + other[:, cols].astype(F32)
            target[:, cols] = value.astype(target.dtype)

    goes = (p.core, p.core, p.core, p.core, p.first, p.first, p.second)
    slots = (0, 1, 0, 1, 2, 3, 4)
    copies = [
        remote(out.at[slots[i]], into.at[i], r_send.at[i], r_recv.at[i], p.at(to))
        for i, to in enumerate(goes)
    ]
    fetches[0].start()
    for copy in started[1:4]:
        copy.wait()
    save(p.h)
    open_up(p.h, 0)
    gather.got_core()
    save(p.core)
    open_up(p.core, 1)
    down_gather.step(0)
    gather.got_first()
    gather.got_second()
    save(p.first)
    save(p.second)
    down_gather.step(1)
    open_up(p.first, 2)
    gather.got_core_second()
    gather.got_core_first()
    save(p.second + p.turn)
    save(p.first + p.turn)
    open_up(p.second + p.turn, 3)
    down_gather.step(2)
    started[4].wait()
    down_save = pltpu.make_async_copy(w_down, down_out, loads.at[5])
    down_save.start()
    close(0, 3)
    back(0, out.at[0])
    copies[0].start()
    gather.got_across()
    save(p.across)
    close(1, 2)
    copies[0].wait_recv()
    back(1, out.at[2], into.at[0])
    copies[4].start()
    gather.got_core_across()
    save(p.across + p.turn)
    open_up(p.across + p.turn, 3)
    close(2, 3)
    back(2, out.at[1])
    copies[1].start()
    open_up(p.across, 3)
    close(3, 3)
    copies[1].wait_recv()
    back(3, out.at[3], into.at[1])
    copies[5].start()
    open_up(p.first + p.turn, 3)
    close(4, 3)
    copies[0].wait_send()
    back(4, out.at[0])
    copies[2].start()
    open_up(p.second, 3)
    close(5, 3)
    copies[2].wait_recv()
    copies[5].wait_recv()
    back(5, out.at[4], into.at[2], into.at[5])
    copies[6].start()
    close(6, 1)
    copies[1].wait_send()
    back(6, out.at[1])
    copies[3].start()
    close(7, 0)
    copies[3].wait_recv()
    back(7, grad_out, into.at[3])
    copies[4].wait_recv()
    copies[6].wait_recv()

    @pl.loop(0, line)
    def _(d):
        cols = pl.ds(pl.multiple_of(d * slab, slab), slab)
        grad_out[:, cols] += into[4, :, cols].astype(F32) + into[6, :, cols].astype(F32)

    for i in range(2, 7):
        copies[i].wait_send()
    gather.finish()
    down_gather.finish()
    for copy in saved:
        copy.wait()
    for copy in stores[6] + stores[7]:
        copy.wait()
    down_save.wait()


def feed(line, middle, gain, cot, gate_a, gate_b, up, down):
    rows, width = middle.shape
    units, slab = down.shape
    full = rows * 8
    return pl.pallas_call(
        functools.partial(feed_kernel, line),
        out_shape=(
            jax.ShapeDtypeStruct((full, width), BF16),
            jax.ShapeDtypeStruct((full, units), BF16),
            jax.ShapeDtypeStruct((full, units), BF16),
            jax.ShapeDtypeStruct((full, units), BF16),
            jax.ShapeDtypeStruct((rows, width), F32),
            jax.ShapeDtypeStruct((line, units, slab), BF16),
        ),
        in_specs=[any_spec(), vmem_spec()] + [any_spec()] * 5,
        out_specs=(any_spec(), any_spec(), any_spec(), any_spec(), vmem_spec(), any_spec()),
        scratch_shapes=[
            pltpu.VMEM((full, width), BF16),
            pltpu.VMEM((line, units, slab), BF16),
            pltpu.VMEM((line, units, slab), BF16),
            pltpu.VMEM((line, units, slab), BF16),
            pltpu.VMEM((4, rows, units), F32),
            pltpu.VMEM((4, rows, units), F32),
            pltpu.VMEM((rows, width), BF16),
            pltpu.VMEM((2, rows, units), BF16),
            pltpu.VMEM((2, rows, units), BF16),
            pltpu.VMEM((2, rows, units), BF16),
            pltpu.VMEM((5, rows, width), BF16),
            pltpu.VMEM((7, rows, width), BF16),
            pltpu.SemaphoreType.DMA((7,)),
            pltpu.SemaphoreType.DMA((7,)),
            pltpu.SemaphoreType.DMA((7,)),
            pltpu.SemaphoreType.DMA((7,)),
            *line_sems(line),
            pltpu.SemaphoreType.DMA((6,)),
            pltpu.SemaphoreType.DMA((8,)),
            pltpu.SemaphoreType.DMA((7,)),
        ],
        compiler_params=pltpu.CompilerParams(
            collective_id=4, has_side_effects=True, vmem_limit_bytes=60 * MIB
        ),
        cost_estimate=pl.CostEstimate(
            flops=50 * 2**30, bytes_accessed=80 * MIB, transcendentals=0
        ),
    )(middle, gain.reshape(1, width), cot, gate_a, gate_b, up, down)


class LineReduce:
    def __init__(self, place, part, up_in, down_in, up_send, up_recv, down_send, down_recv):
        self.p, self.part = place, part
        self.up_in, self.down_in = up_in, down_in
        self.up = (up_send, up_recv)
        self.down = (down_send, down_recv)

    def _up(self, d, t):
        p = self.p
        return remote(
            self.part(d), self.up_in.at[t], self.up[0].at[t], self.up[1].at[t], (p.s + 1, p.h)
        )

    def _down(self, d, t):
        p = self.p
        return remote(
            self.part(d),
            self.down_in.at[t],
            self.down[0].at[t],
            self.down[1].at[t],
            (p.s - 1, p.h),
        )

    def _sends(self, t):
        p, last = self.p, self.p.line - 1
        return (
            ((p.s <= t) & (p.s < last), self._up, last - t + p.s),
            ((last - p.s <= t) & (p.s > 0), self._down, t - last + p.s),
        )

    def start(self, t):
        p, last = self.p, self.p.line - 1
        for number, (goes, copy, d) in enumerate(self._sends(t)):
            came = (self.up_in, self.down_in)[number]

            @pl.when(goes)
            def _():
                if t > 0:
                    inner = p.s > 0 if number == 0 else p.s < last

                    @pl.when(inner)
                    def _():
                        add_rows(self.part(d), came.at[t - 1])

                copy(d, t).start()

    def got(self, t):
        p, last = self.p, self.p.line - 1

        @pl.when((p.s >= 1) & (t >= p.s - 1))
        def _():
            self._up(0, t).wait_recv()

        @pl.when((p.s < last) & (t >= last - p.s - 1))
        def _():
            self._down(0, t).wait_recv()

    def step(self, t):
        self.got(t)
        if t + 1 < self.p.line - 1:
            self.start(t + 1)

    def end(self):
        p, last = self.p, self.p.line - 1

        @pl.when(p.s >= 1)
        def _():
            add_rows(self.part(p.s), self.up_in.at[last - 1])

        @pl.when(p.s < last)
        def _():
            add_rows(self.part(p.s), self.down_in.at[last - 1])

    def total(self, rows):
        p, last = self.p, self.p.line - 1
        value = self.part(p.s)[rows, :].astype(F32)
        value = value + jnp.where(p.s >= 1, self.up_in[last - 1, rows, :].astype(F32), 0.0)
        return value + jnp.where(p.s < last, self.down_in[last - 1, rows, :].astype(F32), 0.0)

    def finish(self):
        for t in range(self.p.line - 1):
            for goes, copy, d in self._sends(t):

                @pl.when(goes)
                def _():
                    copy(d, t).wait_send()


def add_rows(target, other):
    step = 16

    @pl.loop(0, target.shape[0] // step)
    def _(i):
        at = pl.ds(pl.multiple_of(i * step, step), step)
        target[at, :] = (target[at, :].astype(F32) + other[at, :].astype(F32)).astype(BF16)


def clear_last(reduce):
    p, last = reduce.p, reduce.p.line - 1

    @pl.when(p.s == 0)
    def _():
        reduce.up_in[last - 1] = jnp.zeros(reduce.up_in.shape[1:], BF16)

    @pl.when(p.s == last)
    def _():
        reduce.down_in[last - 1] = jnp.zeros(reduce.down_in.shape[1:], BF16)


def weight_product(turned, source, piece, strip, sems):
    depth = turned.shape[1]
    wide = strip.shape[2]
    slab = piece(0).shape[1]
    count = source.shape[1] // wide
    each = slab // wide

    def fetch(n):
        cols = pl.ds(pl.multiple_of(n * wide, wide), wide)
        return pltpu.make_async_copy(
            source.at[:, cols], strip.at[lax.rem(n, 2)], sems.at[lax.rem(n, 2)]
        )

    fetch(0).start()

    @pl.loop(0, count)
    def _(n):
        @pl.when(n + 1 < count)
        def _():
            fetch(n + 1).start()

        fetch(n).wait()
        cols = pl.ds(pl.multiple_of(lax.rem(n, each) * wide, wide), wide)
        piece(lax.div(n, each))[:, cols] = product(
            turned[...], strip[lax.rem(n, 2)]
        ).astype(BF16)


def turn_rows(source, target):
    step = 256

    @pl.loop(0, source.shape[0] // step)
    def _(i):
        at = pl.ds(pl.multiple_of(i * step, step), step)
        for first, last in strips(source.shape[1], 128):
            target[first:last, at] = source[at, first:last].T


def return_kernel(
    line,
    cut,
    grad_normed,
    middle,
    cot_own,
    gain,
    attended,
    w_out,
    hidden,
    grad_gate,
    grad_up,
    cot,
    normed,
    grad_middle,
    gain_part,
    grad_attended,
    inner,
    down_grad,
    up_low,
    up_high,
    gate_parts,
    out_parts,
    branch,
    units_in,
    turned,
    strip,
    down_parts,
    up_parts,
    other_parts,
    down_up_in,
    down_down_in,
    up_up_in,
    up_down_in,
    att_turned,
    out_sum,
    g_send,
    g_recv,
    *sems,
):
    p = Place(line)
    down_sems, up_sems, loads, strips_sem, saves = sems[0:4], sems[4:8], *sems[8:11]
    rows, width = grad_normed.shape
    slab = w_out.shape[2]
    part = attended.shape[1]
    block = lambda j: branch.at[pl.ds(pl.multiple_of(j * rows, rows), rows)]
    gather = HeadGather(p, block, g_send, g_recv)
    down_reduce = LineReduce(
        p, lambda d: down_parts.at[d], down_up_in, down_down_in, *down_sems
    )
    up_reduce = LineReduce(
        p, lambda d: up_parts.at[d, pl.ds(0, cut)], up_up_in, up_down_in, *up_sems
    )
    load = [
        pltpu.make_async_copy(source, units_in, loads.at[i])
        for i, source in enumerate((hidden, grad_up, grad_gate))
    ]
    load[0].start()
    p.greet()
    mine = block(p.h)
    gain_part[...] = jnp.zeros_like(gain_part)
    step = 32

    @pl.loop(0, rows // step)
    def _(i):
        at = pl.ds(pl.multiple_of(i * step, step), step)
        value = middle[at]
        inverse = lax.rsqrt(jnp.mean(value * value, axis=-1, keepdims=True) + EPS)
        unit = value * inverse
        grad = grad_normed[at]
        gain_part[...] += jnp.sum(grad * unit, axis=0, keepdims=True)
        result = cot_own[at].astype(F32) + norm_back(unit, inverse, gain[...], grad)
        grad_middle[at] = result
        mine[at] = result.astype(BF16)

    gather.start()
    clear_last(down_reduce)
    clear_last(up_reduce)
    load[0].wait()
    turn_rows(units_in, turned)
    load[1].start()
    weight_product(turned, cot, lambda d: down_parts.at[d], strip, strips_sem)
    down_reduce.start(0)
    load[1].wait()
    turn_rows(units_in, turned)
    load[2].start()
    gather.got_core()
    weight_product(turned, normed, lambda d: up_parts.at[d], strip, strips_sem)
    up_reduce.start(0)
    down_reduce.step(0)
    gather.got_first()
    gather.got_second()
    save_up = pltpu.make_async_copy(
        up_parts.at[:, pl.ds(cut, up_parts.shape[1] - cut)], up_high, saves.at[0]
    )
    save_up.start()
    load[2].wait()
    turn_rows(units_in, turned)
    weight_product(turned, normed, lambda d: other_parts.at[d], strip, strips_sem)
    save_gate = pltpu.make_async_copy(other_parts, gate_parts, saves.at[1])
    save_gate.start()
    turn_rows(attended, att_turned)
    down_reduce.step(1)
    gather.got_core_second()
    gather.got_core_first()
    out_sum[...] = jnp.zeros_like(out_sum)

    def take(j):
        start = pl.multiple_of(j * rows, rows)
        at = pl.ds(start, rows)
        total = product_nt(branch[at, 0:slab], w_out[0])
        for d in range(1, line):
            total = total + product_nt(branch[at, d * slab : (d + 1) * slab], w_out[d])
        low = total.astype(BF16)
        grad_attended[at, :] = low
        for head in range(part // HEAD_DIM):
            cols = slice(head * HEAD_DIM, (head + 1) * HEAD_DIM)
            both = low[:, cols].astype(F32) * attended[at, cols].astype(F32)
            inner[head : head + 1, at] = jnp.sum(both.T, axis=0, keepdims=True)

        @pl.loop(0, line)
        def _(d):
            cols = pl.ds(pl.multiple_of(d * slab, slab), slab)
            out_sum[d] += product(att_turned[:, at], branch[at, cols])

    for j in (p.h, p.core, p.first, p.second):
        take(j)
    up_reduce.step(0)
    for j in (p.second + p.turn, p.first + p.turn):
        take(j)
    gather.got_across()
    take(p.across)
    gather.got_core_across()
    take(p.across + p.turn)
    for d in range(line):
        out_parts[d] = out_sum[d].astype(BF16)
    down_reduce.step(2)
    for first, last in strips(down_grad.shape[0], 128):
        down_grad[first:last, :] = down_reduce.total(slice(first, last))
    up_reduce.step(1)
    up_reduce.step(2)
    for first, last in strips(cut, 128):
        up_low[:, first:last] = up_reduce.total(slice(first, last)).T
    gather.finish()
    down_reduce.finish()
    up_reduce.finish()
    save_up.wait()
    save_gate.wait()


def give_back(line, cut, grad_normed, middle, cot_own, gain, attended, w_out, hidden, grad_gate, grad_up, cot, normed):
    rows, width = middle.shape
    full, units = hidden.shape
    part = attended.shape[1]
    slab = w_out.shape[2]
    heads = part // HEAD_DIM
    return pl.pallas_call(
        functools.partial(return_kernel, line, cut),
        out_shape=(
            jax.ShapeDtypeStruct((rows, width), F32),
            jax.ShapeDtypeStruct((1, width), F32),
            jax.ShapeDtypeStruct((full, part), BF16),
            jax.ShapeDtypeStruct((heads, full), F32),
            jax.ShapeDtypeStruct((units, slab), F32),
            jax.ShapeDtypeStruct((slab, cut), F32),
            jax.ShapeDtypeStruct((line, units - cut, slab), BF16),
            jax.ShapeDtypeStruct((line, units, slab), BF16),
            jax.ShapeDtypeStruct((line, part, slab), BF16),
        ),
        in_specs=[vmem_spec()] * 6 + [any_spec()] * 5,
        out_specs=(
            vmem_spec(),
            vmem_spec(),
            vmem_spec(),
            vmem_spec(),
            vmem_spec(),
            vmem_spec(),
            any_spec(),
            any_spec(),
            vmem_spec(),
        ),
        scratch_shapes=[
            pltpu.VMEM((full, width), BF16),
            pltpu.VMEM((full, units), BF16),
            pltpu.VMEM((units, full), BF16),
            pltpu.VMEM((2, full, 256), BF16),
            pltpu.VMEM((line, units, slab), BF16),
            pltpu.VMEM((line, units, slab), BF16),
            pltpu.VMEM((line, units, slab), BF16),
            pltpu.VMEM((line - 1, units, slab), BF16),
            pltpu.VMEM((line - 1, units, slab), BF16),
            pltpu.VMEM((line - 1, cut, slab), BF16),
            pltpu.VMEM((line - 1, cut, slab), BF16),
            pltpu.VMEM((part, full), BF16),
            pltpu.VMEM((line, part, slab), F32),
            pltpu.SemaphoreType.DMA((7,)),
            pltpu.SemaphoreType.DMA((7,)),
            *line_sems(line, 2),
            pltpu.SemaphoreType.DMA((3,)),
            pltpu.SemaphoreType.DMA((2,)),
            pltpu.SemaphoreType.DMA((2,)),
        ],
        compiler_params=pltpu.CompilerParams(
            collective_id=5, has_side_effects=True, vmem_limit_bytes=62 * MIB
        ),
        cost_estimate=pl.CostEstimate(
            flops=35 * 2**30, bytes_accessed=80 * MIB, transcendentals=0
        ),
    )(
        grad_normed,
        middle,
        cot_own,
        gain.reshape(1, width),
        attended,
        w_out,
        hidden,
        grad_gate,
        grad_up,
        cot,
        normed,
    )


def backward_tile(tile, q, k_ext, v_ext, k_t, floor, logs, inner, grad, key_sum, value_sum):
    start = pl.multiple_of(tile * TILE, TILE)
    mine = pl.ds(start, TILE)
    scale = HEAD_DIM ** (-0.5)
    for head in range(q.shape[1] // HEAD_DIM):
        cols = slice(head * HEAD_DIM, (head + 1) * HEAD_DIM)
        queries = q[mine, cols]
        grads = grad[mine, cols]
        log = logs[head : head + 1, mine]
        middle = inner[head : head + 1, mine]
        turned = jnp.zeros((HEAD_DIM, TILE), F32)
        for i, (scores, visible) in enumerate(tile_scores(tile, head, q, k_ext, floor)):
            at = pl.ds(start + i * TILE, TILE)
            probs = jnp.where(visible, jnp.exp2(scores * (scale * LOG2E) - log), 0.0)
            grad_probs = product_nt(v_ext[at, cols], grads)
            grad_scores = (probs * (grad_probs - middle)).astype(BF16)
            value_sum[at, cols] += product(probs.astype(BF16), grads)
            key_sum[at, cols] += product(grad_scores, queries)
            turned = turned + product(k_t[cols, at], grad_scores)
        q[mine, cols] = (turned * scale).astype(BF16).T


def block_reduce(place, out, into, r_send, r_recv):
    p = place
    goes = (p.core, p.core, p.core, p.core, p.first, p.first, p.second)
    slots = (0, 1, 0, 1, 2, 3, 4)
    return [
        remote(out.at[slots[i]], into.at[i], r_send.at[i], r_recv.at[i], p.at(to))
        for i, to in enumerate(goes)
    ]


def attend_back_kernel(
    line,
    qkv,
    halo_kv,
    floor,
    logs,
    grad,
    inner,
    hidden,
    w_down,
    middle,
    gate_in,
    grads_out,
    result,
    gate_grad,
    q,
    k_ext,
    v_ext,
    k_t,
    key_sum,
    value_sum,
    halo_out,
    halo_in,
    gate_parts,
    gate_up_in,
    gate_down_in,
    out,
    into,
    total,
    hidden_block,
    r_send,
    r_recv,
    *sems,
):
    p = Place(line)
    gate_sems, loads, halo_send, halo_recv, stage, saves = sems[0:4], *sems[4:9]
    rows, width = result.shape
    slab = w_down.shape[2]
    count, part = q.shape
    scale = HEAD_DIM ** (-0.5)
    rows_of = lambda ref, j: ref.at[pl.ds(pl.multiple_of(j * rows, rows), rows)]
    gate_reduce = LineReduce(
        p, lambda d: gate_parts.at[d], gate_up_in, gate_down_in, *gate_sems
    )
    started = [
        pltpu.make_async_copy(gate_in, gate_parts, loads.at[0]),
        pltpu.make_async_copy(qkv.at[:, pl.ds(0, part)], q, loads.at[1]),
        pltpu.make_async_copy(
            qkv.at[:, pl.ds(part, part)], k_ext.at[pl.ds(WINDOW, count)], loads.at[2]
        ),
        pltpu.make_async_copy(
            qkv.at[:, pl.ds(2 * part, part)], v_ext.at[pl.ds(WINDOW, count)], loads.at[3]
        ),
        pltpu.make_async_copy(halo_kv.at[0], k_ext.at[pl.ds(0, WINDOW)], loads.at[4]),
        pltpu.make_async_copy(halo_kv.at[1], v_ext.at[pl.ds(0, WINDOW)], loads.at[5]),
        pltpu.make_async_copy(middle, total, loads.at[6]),
    ]
    halo = [
        remote(
            halo_out.at[i], halo_in.at[i], halo_send.at[i], halo_recv.at[i], (p.s - 1, p.h)
        )
        for i in range(2)
    ]
    order = (
        p.second + p.turn,
        p.across + p.turn,
        p.first,
        p.first + p.turn,
        p.across,
        p.core,
        p.h,
        p.second,
    )
    fetches = [
        pltpu.make_async_copy(rows_of(hidden, j), hidden_block.at[n % 2], stage.at[n % 2])
        for n, j in enumerate(order)
    ]
    copies = block_reduce(p, out, into, r_send, r_recv)

    def emit(n, target, *more):
        fetches[n].wait()
        if n + 1 < len(order):
            fetches[n + 1].start()

        @pl.loop(0, line)
        def _(d):
            cols = pl.ds(pl.multiple_of(d * slab, slab), slab)
            value = product(hidden_block[n % 2], w_down[d])
            for other in more:
                value = value + other[:, cols].astype(F32)
            target[:, cols] = value.astype(target.dtype)

    def tiles(first, last):
        @pl.loop(first, last)
        def _(tile):
            backward_tile(
                tile, q, k_ext, v_ext, k_t, floor, logs, inner, grad, key_sum, value_sum
            )

    for copy in started:
        copy.start()
    fetches[0].start()
    p.greet()
    started[0].wait()
    gate_reduce.start(0)
    clear_last(gate_reduce)
    emit(0, out.at[0])
    copies[0].start()
    emit(1, out.at[1])
    copies[1].start()
    copies[0].wait_recv()
    emit(2, out.at[2], into.at[0])
    copies[4].start()
    copies[0].wait_send()
    emit(3, out.at[0])
    copies[2].start()
    copies[1].wait_recv()
    emit(4, out.at[3], into.at[1])
    copies[5].start()
    copies[1].wait_send()
    emit(5, out.at[1])
    copies[3].start()
    for copy in started[1:]:
        copy.wait()

    @pl.loop(0, (WINDOW + count) // TILE)
    def _(i):
        at = pl.ds(pl.multiple_of(i * TILE, TILE), TILE)
        k_t[:, at] = k_ext[at, :].T
        key_sum[at, :] = jnp.zeros((TILE, part), F32)
        value_sum[at, :] = jnp.zeros((TILE, part), F32)

    ahead = WINDOW // TILE
    last = count // TILE
    tiles(0, ahead)

    @pl.when(p.s > 0)
    def _():
        @pl.loop(0, ahead)
        def _(i):
            at = pl.ds(pl.multiple_of(i * TILE, TILE), TILE)
            halo_out[0, at, :] = (key_sum[at, :] * scale).astype(BF16)
            halo_out[1, at, :] = value_sum[at, :].astype(BF16)

        halo[0].start()
        halo[1].start()

    gate_reduce.step(0)
    tiles(ahead, ahead + 4)
    copies[3].wait_recv()
    emit(6, total, into.at[3], total)
    copies[2].wait_recv()
    copies[5].wait_recv()
    emit(7, out.at[4], into.at[2], into.at[5])
    copies[6].start()
    gate_reduce.step(1)
    tiles(ahead + 4, last)

    @pl.when(p.s < line - 1)
    def _():
        halo[0].wait_recv()
        halo[1].wait_recv()

    @pl.loop(0, last)
    def _(i):
        here = pl.ds(pl.multiple_of(i * TILE, TILE), TILE)
        at = pl.ds(pl.multiple_of(i * TILE + WINDOW, TILE), TILE)
        key_value = key_sum[at, :] * scale
        value_value = value_sum[at, :]
        k_ext[here, :] = key_value.astype(BF16)
        v_ext[here, :] = value_value.astype(BF16)

    @pl.when(p.s < line - 1)
    def _():
        @pl.loop(0, ahead)
        def _(i):
            here = pl.ds(pl.multiple_of(i * TILE, TILE), TILE)
            near = pl.ds(pl.multiple_of(i * TILE + count, TILE), TILE)
            there = pl.ds(pl.multiple_of(i * TILE + count - WINDOW, TILE), TILE)
            k_ext[there, :] = (
                key_sum[near, :] * scale + halo_in[0, here, :].astype(F32)
            ).astype(BF16)
            v_ext[there, :] = (value_sum[near, :] + halo_in[1, here, :].astype(F32)).astype(BF16)

    save = [
        pltpu.make_async_copy(
            ref.at[pl.ds(0, count)], grads_out.at[:, pl.ds(i * part, part)], saves.at[i]
        )
        for i, ref in enumerate((q, k_ext, v_ext))
    ]
    for copy in save:
        copy.start()
    copies[4].wait_recv()
    copies[6].wait_recv()

    @pl.loop(0, line)
    def _(d):
        cols = pl.ds(pl.multiple_of(d * slab, slab), slab)
        value = total[:, cols] + into[4, :, cols].astype(F32) + into[6, :, cols].astype(F32)
        result[:, cols] = value.astype(BF16)

    gate_reduce.step(2)
    for first, stop in strips(gate_grad.shape[1], 128):
        gate_grad[:, first:stop] = gate_reduce.total(slice(first, stop)).T
    for i in range(2, 7):
        copies[i].wait_send()
    gate_reduce.finish()

    @pl.when(p.s > 0)
    def _():
        halo[0].wait_send()
        halo[1].wait_send()

    for copy in save:
        copy.wait()


def attend_back(line, qkv, halo_kv, floor, logs, grad, inner, hidden, w_down, middle, gate_parts):
    rows, width = middle.shape
    count = qkv.shape[0]
    part = qkv.shape[1] // 3
    units, slab = w_down.shape[1:]
    return pl.pallas_call(
        functools.partial(attend_back_kernel, line),
        out_shape=(
            jax.ShapeDtypeStruct((count, 3 * part), BF16),
            jax.ShapeDtypeStruct((rows, width), BF16),
            jax.ShapeDtypeStruct((slab, units), F32),
        ),
        in_specs=[any_spec()] * 2
        + [vmem_spec()] * 4
        + [any_spec(), vmem_spec(), any_spec(), any_spec()],
        out_specs=(any_spec(), vmem_spec(), vmem_spec()),
        scratch_shapes=[
            pltpu.VMEM((count, part), BF16),
            pltpu.VMEM((WINDOW + count, part), BF16),
            pltpu.VMEM((WINDOW + count, part), BF16),
            pltpu.VMEM((part, WINDOW + count), BF16),
            pltpu.VMEM((WINDOW + count, part), F32),
            pltpu.VMEM((WINDOW + count, part), F32),
            pltpu.VMEM((2, WINDOW, part), BF16),
            pltpu.VMEM((2, WINDOW, part), BF16),
            pltpu.VMEM((line, units, slab), BF16),
            pltpu.VMEM((line - 1, units, slab), BF16),
            pltpu.VMEM((line - 1, units, slab), BF16),
            pltpu.VMEM((5, rows, width), BF16),
            pltpu.VMEM((7, rows, width), BF16),
            pltpu.VMEM((rows, width), F32),
            pltpu.VMEM((2, rows, units), BF16),
            pltpu.SemaphoreType.DMA((7,)),
            pltpu.SemaphoreType.DMA((7,)),
            *line_sems(line),
            pltpu.SemaphoreType.DMA((7,)),
            pltpu.SemaphoreType.DMA((2,)),
            pltpu.SemaphoreType.DMA((2,)),
            pltpu.SemaphoreType.DMA((2,)),
            pltpu.SemaphoreType.DMA((3,)),
        ],
        compiler_params=pltpu.CompilerParams(
            collective_id=6, has_side_effects=True, vmem_limit_bytes=62 * MIB
        ),
        cost_estimate=pl.CostEstimate(
            flops=20 * 2**30, bytes_accessed=60 * MIB, transcendentals=0
        ),
    )(qkv, halo_kv, floor, logs, grad, inner, hidden, w_down, middle, gate_parts)


def finish_kernel(
    line,
    grads,
    weight,
    normed,
    tokens,
    gain,
    grad_middle,
    up_high,
    up_low,
    out_given,
    ffn_gain_part,
    input_grad,
    gain_sums,
    query_grad,
    key_grad,
    value_grad,
    out_grad,
    up_grad,
    turned,
    strip,
    parts,
    parts_up_in,
    parts_down_in,
    up_parts,
    up_up_in,
    up_down_in,
    out_parts,
    out_up_in,
    out_down_in,
    out,
    into,
    total,
    gain_line,
    gain_in,
    r_send,
    r_recv,
    *sems,
):
    p = Place(line)
    part_sems, up_sems, out_sems, gain_sems = sems[0:4], sems[4:8], sems[8:12], sems[12:16]
    loads, strip_sems, gain_send, gain_recv = sems[16:20]
    rows, width = tokens.shape
    slab = width // line
    part = query_grad.shape[1]
    cut = up_low.shape[1]
    part_reduce = LineReduce(p, lambda d: parts.at[d], parts_up_in, parts_down_in, *part_sems)
    up_reduce = LineReduce(p, lambda d: up_parts.at[d], up_up_in, up_down_in, *up_sems)
    out_reduce = LineReduce(p, lambda d: out_parts.at[d], out_up_in, out_down_in, *out_sems)
    started = [
        pltpu.make_async_copy(up_high, up_parts, loads.at[0]),
        pltpu.make_async_copy(out_given, out_parts, loads.at[1]),
        pltpu.make_async_copy(up_low, up_grad.at[:, pl.ds(0, cut)], loads.at[2]),
        pltpu.make_async_copy(grad_middle, input_grad, loads.at[3]),
    ]
    for copy in started:
        copy.start()
    p.greet()
    started[0].wait()
    up_reduce.start(0)
    started[1].wait()
    out_reduce.start(0)
    for reduce in (part_reduce, up_reduce, out_reduce):
        clear_last(reduce)
    copies = block_reduce(p, out, into, r_send, r_recv)

    def emit(j, target, *more):
        at = pl.ds(pl.multiple_of(j * rows, rows), rows)

        @pl.loop(0, line)
        def _(d):
            cols = pl.ds(pl.multiple_of(d * slab, slab), slab)
            value = product_nt(grads[at, :], weight[cols, :])
            for other in more:
                value = value + other[:, cols].astype(F32)
            target[:, cols] = value.astype(target.dtype)

    emit(p.second + p.turn, out.at[0])
    copies[0].start()
    emit(p.across + p.turn, out.at[1])
    copies[1].start()
    copies[0].wait_recv()
    emit(p.first, out.at[2], into.at[0])
    copies[4].start()
    copies[0].wait_send()
    emit(p.first + p.turn, out.at[0])
    copies[2].start()
    copies[1].wait_recv()
    emit(p.across, out.at[3], into.at[1])
    copies[5].start()
    copies[1].wait_send()
    emit(p.core, out.at[1])
    copies[3].start()
    turn_rows(grads, turned)
    up_reduce.step(0)
    out_reduce.step(0)
    weight_product(turned, normed, lambda d: parts.at[d], strip, strip_sems)
    part_reduce.start(0)
    copies[3].wait_recv()
    emit(p.h, total, into.at[3])
    up_reduce.step(1)
    out_reduce.step(1)
    copies[2].wait_recv()
    copies[5].wait_recv()
    emit(p.second, out.at[4], into.at[2], into.at[5])
    copies[6].start()
    up_reduce.step(2)
    out_reduce.step(2)
    part_reduce.step(0)
    started[2].wait()
    for first, last in strips(up_parts.shape[1], 128):
        up_grad[:, cut + first : cut + last] = up_reduce.total(slice(first, last)).T
    for first, last in strips(part, 128):
        out_grad[first:last, :] = out_reduce.total(slice(first, last))
    copies[4].wait_recv()
    copies[6].wait_recv()
    started[3].wait()
    gain_own = gain_line.at[p.s]
    gain_own[...] = jnp.zeros(gain_own.shape, F32)
    gain_own[1:2, :] = ffn_gain_part[...]
    step = 32

    @pl.loop(0, rows // step)
    def _(i):
        at = pl.ds(pl.multiple_of(i * step, step), step)
        grad = total[at] + into[4, at].astype(F32) + into[6, at].astype(F32)
        unit, inverse = normalize(tokens[at].astype(F32))
        gain_own[0:1, :] += jnp.sum(grad * unit, axis=0, keepdims=True)
        input_grad[at] += norm_back(unit, inverse, gain[...], grad)

    part_reduce.step(1)
    for i, head in enumerate((p.core, p.first, p.second)):
        copy = remote(gain_own, gain_in.at[i], gain_send.at[i], gain_recv.at[i], p.at(head))
        copy.start()
        copy.wait()
        gain_own[...] += gain_in[i]
    gain_gather = LineGather(p, lambda d: gain_line.at[d], *gain_sems)
    gain_gather.start(0)
    for t in range(line - 1):
        gain_gather.step(t)
    summed = gain_line[0]
    for d in range(1, line):
        summed = summed + gain_line[d]
    gain_sums[...] = summed
    part_reduce.step(2)
    for i, target in enumerate((query_grad, key_grad, value_grad)):
        for first, last in strips(part, 128):
            target[:, first:last] = part_reduce.total(
                slice(i * part + first, i * part + last)
            ).T
    for i in range(2, 7):
        copies[i].wait_send()
    gain_gather.finish()
    for reduce in (part_reduce, up_reduce, out_reduce):
        reduce.finish()


def finish(line, grads, weight, normed, tokens, gain, grad_middle, up_high, up_low, out_parts, ffn_gain_part):
    rows, width = tokens.shape
    full = grads.shape[0]
    part = grads.shape[1] // 3
    slab = width // line
    rest = up_high.shape[1]
    units = up_low.shape[1] + rest
    return pl.pallas_call(
        functools.partial(finish_kernel, line),
        out_shape=(
            jax.ShapeDtypeStruct((rows, width), F32),
            jax.ShapeDtypeStruct((8, width), F32),
            jax.ShapeDtypeStruct((slab, part), F32),
            jax.ShapeDtypeStruct((slab, part), F32),
            jax.ShapeDtypeStruct((slab, part), F32),
            jax.ShapeDtypeStruct((part, slab), F32),
            jax.ShapeDtypeStruct((slab, units), F32),
        ),
        in_specs=[
            vmem_spec(),
            vmem_spec(),
            any_spec(),
            vmem_spec(),
            vmem_spec(),
            any_spec(),
            any_spec(),
            any_spec(),
            any_spec(),
            vmem_spec(),
        ],
        out_specs=(vmem_spec(),) * 7,
        scratch_shapes=[
            pltpu.VMEM((3 * part, full), BF16),
            pltpu.VMEM((2, full, 256), BF16),
            pltpu.VMEM((line, 3 * part, slab), BF16),
            pltpu.VMEM((line - 1, 3 * part, slab), BF16),
            pltpu.VMEM((line - 1, 3 * part, slab), BF16),
            pltpu.VMEM((line, rest, slab), BF16),
            pltpu.VMEM((line - 1, rest, slab), BF16),
            pltpu.VMEM((line - 1, rest, slab), BF16),
            pltpu.VMEM((line, part, slab), BF16),
            pltpu.VMEM((line - 1, part, slab), BF16),
            pltpu.VMEM((line - 1, part, slab), BF16),
            pltpu.VMEM((5, rows, width), BF16),
            pltpu.VMEM((7, rows, width), BF16),
            pltpu.VMEM((rows, width), F32),
            pltpu.VMEM((line, 8, width), F32),
            pltpu.VMEM((3, 8, width), F32),
            pltpu.SemaphoreType.DMA((7,)),
            pltpu.SemaphoreType.DMA((7,)),
            *line_sems(line, 4),
            pltpu.SemaphoreType.DMA((4,)),
            pltpu.SemaphoreType.DMA((2,)),
            pltpu.SemaphoreType.DMA((3,)),
            pltpu.SemaphoreType.DMA((3,)),
        ],
        compiler_params=pltpu.CompilerParams(
            collective_id=7, has_side_effects=True, vmem_limit_bytes=62 * MIB
        ),
        cost_estimate=pl.CostEstimate(
            flops=20 * 2**30, bytes_accessed=60 * MIB, transcendentals=0
        ),
    )(
        grads,
        weight,
        normed,
        tokens,
        gain.reshape(1, width),
        grad_middle,
        up_high,
        up_low,
        out_parts,
        ffn_gain_part,
    )


def fused(
    tokens,
    segment,
    attn_gain,
    query_weight,
    key_weight,
    value_weight,
    out_weight,
    ffn_gain,
    gate_weight,
    up_weight,
    down_weight,
    cotangent,
):
    line = lax.axis_size("seq")
    normed_one, qkv, w_qkv, floor, gate_t, up_t = project(
        line,
        tokens,
        attn_gain,
        query_weight,
        key_weight,
        value_weight,
        segment,
        gate_weight,
        up_weight,
    )
    cut = gate_t.shape[0] // 256 * 128 + 128
    attended, logs, halo_kv, cot_full, w_out, gate_a = attend(
        line, qkv, floor, cotangent, out_weight, gate_t[:cut]
    )
    middle, gate_b, w_up = branch(line, attended, w_out, tokens, gate_t[cut:], up_t)
    normed_two, hidden, grad_gate, grad_up, grad_normed_two, w_down = feed(
        line, middle, ffn_gain, cot_full, gate_a, gate_b, w_up, down_weight
    )
    (
        grad_middle,
        ffn_gain_part,
        grad_attended,
        inner,
        down_grad,
        up_low,
        up_high,
        gate_parts,
        out_parts,
    ) = give_back(
        line,
        cut,
        grad_normed_two,
        middle,
        cotangent,
        ffn_gain,
        attended,
        w_out,
        hidden,
        grad_gate,
        grad_up,
        cot_full,
        normed_two,
    )
    grads, result, gate_grad = attend_back(
        line, qkv, halo_kv, floor, logs, grad_attended, inner, hidden, w_down, middle, gate_parts
    )
    input_grad, gain_sums, query_grad, key_grad, value_grad, out_grad, up_grad = finish(
        line,
        grads,
        w_qkv,
        normed_one,
        tokens,
        attn_gain,
        grad_middle,
        up_high,
        up_low,
        out_parts,
        ffn_gain_part,
    )
    share = tokens.shape[1] // (line * lax.axis_size("head"))
    place = (lax.axis_index("seq") * lax.axis_size("head") + lax.axis_index("head")) * share
    gain_grads = lax.dynamic_slice(gain_sums, (0, place), (2, share))
    return (
        result,
        input_grad,
        gain_grads[0],
        query_grad,
        key_grad,
        value_grad,
        out_grad,
        gain_grads[1],
        gate_grad,
        up_grad,
        down_grad,
    )


def solution(mesh):
    placed = (
        P(("seq", "head"), None),
        P("seq"),
        P(),
        P("seq", "head"),
        P("seq", "head"),
        P("seq", "head"),
        P("head", "seq"),
        P(),
        P("seq", "head"),
        P("seq", "head"),
        P("head", "seq"),
        P(("seq", "head"), None),
    )
    body = fused if mesh.shape["head"] == 8 else local
    return jax.shard_map(
        body,
        mesh=mesh,
        in_specs=placed,
        out_specs=(
            P(("seq", "head"), None),
            P(("seq", "head"), None),
            P(("seq", "head")),
            P("seq", "head"),
            P("seq", "head"),
            P("seq", "head"),
            P("head", "seq"),
            P(("seq", "head")),
            P("seq", "head"),
            P("seq", "head"),
            P("head", "seq"),
        ),
        check_vma=False,
    )
```

```python
import functools

import jax
import jax.numpy as jnp
from jax import lax
from jax.experimental import pallas as pl
from jax.experimental.pallas import tpu as pltpu
from jax.sharding import PartitionSpec as P

HEAD_DIM = 128
WINDOW = 1024


EPS = 1e-06
NEG = -1e30


def from_behind(value, axis, by):
    count = lax.axis_size(axis)
    pairs = [(i, i + by) for i in range(count) if 0 <= i + by < count]
    return lax.ppermute(value, axis, pairs)


def product(left, right):
    return jnp.dot(left, right, preferred_element_type=jnp.float32)


def product_tn(left, right):
    return lax.dot_general(
        left, right, (((0,), (0,)), ((), ())), preferred_element_type=jnp.float32
    )


def product_nt(left, right):
    return lax.dot_general(
        left, right, (((1,), (1,)), ((), ())), preferred_element_type=jnp.float32
    )


def normalize(rows):
    inverse = lax.rsqrt(jnp.mean(rows * rows, axis=-1, keepdims=True) + EPS)
    return (rows * inverse, inverse)


def norm_back(unit, inverse, gain, grad):
    scaled = grad * gain
    return inverse * (scaled - unit * jnp.mean(scaled * unit, axis=-1, keepdims=True))


def gather_rows(rows):
    return lax.all_gather(rows, "head", axis=0, tiled=True)


def block_scores(query_heads, key_heads, seg_query, seg_keys, valid, start, block):
    query_part = query_heads[start : start + block]
    key_part = key_heads[start : start + block + WINDOW]
    scores = jnp.einsum(
        "qhd,khd->hqk", query_part, key_part, preferred_element_type=jnp.float32
    ) * HEAD_DIM ** (-0.5)
    rows = jnp.arange(block)[:, None] + WINDOW
    cols = jnp.arange(block + WINDOW)[None, :]
    distance = rows - cols
    same_doc = (
        seg_query[start : start + block][:, None]
        == seg_keys[start : start + block + WINDOW][None, :]
    )
    visible = (
        (distance >= 0)
        & (distance <= WINDOW)
        & same_doc
        & valid[start : start + block + WINDOW][None, :]
    )
    return jnp.where(visible[None], scores, NEG)


def local(
    tokens,
    segment,
    attn_gain,
    query_weight,
    key_weight,
    value_weight,
    out_weight,
    ffn_gain,
    gate_weight,
    up_weight,
    down_weight,
    cotangent,
):
    own_rows = tokens.shape[0]
    group = own_rows * lax.axis_size("head")
    heads_here = query_weight.shape[1] // HEAD_DIM
    offset = lax.axis_index("head") * own_rows
    seq_index = lax.axis_index("seq")
    block = min(512, group)
    scale = HEAD_DIM ** (-0.5)
    w_query, w_key, w_value, w_out, w_gate, w_up, w_down = (
        lax.all_gather(query_weight, "seq", axis=0, tiled=True),
        lax.all_gather(key_weight, "seq", axis=0, tiled=True),
        lax.all_gather(value_weight, "seq", axis=0, tiled=True),
        lax.all_gather(out_weight, "seq", axis=1, tiled=True),
        lax.all_gather(gate_weight, "seq", axis=0, tiled=True),
        lax.all_gather(up_weight, "seq", axis=0, tiled=True),
        lax.all_gather(down_weight, "seq", axis=1, tiled=True),
    )
    inputs = tokens.astype(jnp.float32)
    unit_one, inverse_one = normalize(inputs)
    normed_full = gather_rows((unit_one * attn_gain).astype(jnp.bfloat16))
    queries = product(normed_full, w_query).astype(jnp.bfloat16)
    keys = product(normed_full, w_key).astype(jnp.bfloat16)
    values = product(normed_full, w_value).astype(jnp.bfloat16)
    halo_keys, halo_values, halo_segs = ([], [], [])
    hop = 1
    take = min(group, WINDOW - (hop - 1) * group)
    got_keys, got_values, got_segs = from_behind(
        (keys[group - take :], values[group - take :], segment[group - take :]), "seq", hop
    )
    halo_keys.append(got_keys)
    halo_values.append(got_values)
    halo_segs.append(got_segs)
    keys_ext = jnp.concatenate(halo_keys + [keys], axis=0)
    values_ext = jnp.concatenate(halo_values + [values], axis=0)
    segs_ext = jnp.concatenate(halo_segs + [segment], axis=0)
    positions = seq_index * group - WINDOW + jnp.arange(WINDOW + group)
    valid = positions >= 0
    query_heads = queries.reshape(group, heads_here, HEAD_DIM)
    key_heads = keys_ext.reshape(WINDOW + group, heads_here, HEAD_DIM)
    value_heads = values_ext.reshape(WINDOW + group, heads_here, HEAD_DIM)
    outputs, logsums = ([], [])
    for start in range(0, group, block):
        scores = block_scores(query_heads, key_heads, segment, segs_ext, valid, start, block)
        highest = jnp.max(scores, axis=-1, keepdims=True)
        weights = jnp.exp(scores - highest)
        total = jnp.sum(weights, axis=-1, keepdims=True)
        probs = (weights / total).astype(jnp.bfloat16)
        outputs.append(
            jnp.einsum(
                "hqk,khd->qhd",
                probs,
                value_heads[start : start + block + WINDOW],
                preferred_element_type=jnp.float32,
            )
        )
        logsums.append(highest + jnp.log(total))
    attended = (
        jnp.concatenate(outputs, axis=0).reshape(group, heads_here * HEAD_DIM).astype(jnp.bfloat16)
    )
    partial_out = product(attended, w_out)
    own_part = lax.dynamic_slice_in_dim(partial_out, offset, own_rows, 0)
    placed = lax.dynamic_update_slice_in_dim(partial_out, own_part + inputs, offset, 0)
    middle_full = lax.psum(placed, "head")
    middle = lax.dynamic_slice_in_dim(middle_full, offset, own_rows, 0)
    unit_full, inverse_full = normalize(middle_full)
    normed_two_full = (unit_full * ffn_gain).astype(jnp.bfloat16)
    unit_two, inverse_two = normalize(middle)
    gate = product(normed_two_full, w_gate)
    up = product(normed_two_full, w_up)
    sigmoid = jax.nn.sigmoid(gate)
    activated = gate * sigmoid
    hidden = (activated * up).astype(jnp.bfloat16)
    ffn_out = lax.psum_scatter(
        product(hidden, w_down).astype(jnp.bfloat16), "head", scatter_dimension=0, tiled=True
    ).astype(jnp.float32)
    result = middle + ffn_out
    grad_out = lax.all_gather(cotangent, "head", axis=0, tiled=True)
    grad_hidden = product_nt(grad_out, w_down)
    grad_gate = (grad_hidden * up * sigmoid * (1.0 + gate * (1.0 - sigmoid))).astype(jnp.bfloat16)
    grad_up = (grad_hidden * activated).astype(jnp.bfloat16)
    down_grad = product_tn(hidden, grad_out)
    gate_grad = product_tn(normed_two_full, grad_gate)
    up_grad = product_tn(normed_two_full, grad_up)
    grad_normed_two = lax.psum_scatter(
        (product_nt(grad_gate, w_gate) + product_nt(grad_up, w_up)).astype(jnp.bfloat16),
        "head",
        scatter_dimension=0,
        tiled=True,
    ).astype(jnp.float32)
    ffn_gain_part = jnp.sum(grad_normed_two * unit_two, axis=0)
    grad_middle = cotangent.astype(jnp.float32) + norm_back(
        unit_two, inverse_two, ffn_gain, grad_normed_two
    )
    grad_branch = lax.all_gather(grad_middle.astype(jnp.bfloat16), "head", axis=0, tiled=True)
    out_grad = product_tn(attended, grad_branch)
    grad_attended = product_nt(grad_branch, w_out).astype(jnp.bfloat16)
    grad_heads = grad_attended.reshape(group, heads_here, HEAD_DIM)
    grad_query_list = []
    grad_keys_ext = jnp.zeros((WINDOW + group, heads_here, HEAD_DIM), jnp.float32)
    grad_values_ext = jnp.zeros((WINDOW + group, heads_here, HEAD_DIM), jnp.float32)
    for number, start in enumerate(range(0, group, block)):
        scores = block_scores(query_heads, key_heads, segment, segs_ext, valid, start, block)
        probs = jnp.exp(scores - logsums[number])
        probs_low = probs.astype(jnp.bfloat16)
        key_part = key_heads[start : start + block + WINDOW]
        value_part = value_heads[start : start + block + WINDOW]
        query_part = query_heads[start : start + block]
        grad_part = grad_heads[start : start + block]
        grad_probs = jnp.einsum(
            "qhd,khd->hqk", grad_part, value_part, preferred_element_type=jnp.float32
        )
        inner = jnp.sum(probs * grad_probs, axis=-1, keepdims=True)
        grad_scores = (probs * (grad_probs - inner)).astype(jnp.bfloat16)
        grad_query_list.append(
            jnp.einsum("hqk,khd->qhd", grad_scores, key_part, preferred_element_type=jnp.float32)
            * scale
        )
        key_term = (
            jnp.einsum("hqk,qhd->khd", grad_scores, query_part, preferred_element_type=jnp.float32)
            * scale
        )
        value_term = jnp.einsum(
            "hqk,qhd->khd", probs_low, grad_part, preferred_element_type=jnp.float32
        )
        grad_keys_ext = grad_keys_ext.at[start : start + block + WINDOW].add(key_term)
        grad_values_ext = grad_values_ext.at[start : start + block + WINDOW].add(value_term)
    grad_keys_ext = grad_keys_ext.reshape(WINDOW + group, heads_here * HEAD_DIM)
    grad_values_ext = grad_values_ext.reshape(WINDOW + group, heads_here * HEAD_DIM)
    grad_keys = grad_keys_ext[WINDOW:]
    grad_values = grad_values_ext[WINDOW:]
    cursor = 0
    hop = 1
    take = min(group, WINDOW - (hop - 1) * group)
    back_keys = from_behind(
        grad_keys_ext[cursor : cursor + take].astype(jnp.bfloat16), "seq", -hop
    ).astype(jnp.float32)
    back_values = from_behind(
        grad_values_ext[cursor : cursor + take].astype(jnp.bfloat16), "seq", -hop
    ).astype(jnp.float32)
    grad_keys = grad_keys.at[group - take :].add(back_keys)
    grad_values = grad_values.at[group - take :].add(back_values)
    grad_queries = (
        jnp.concatenate(grad_query_list, axis=0)
        .reshape(group, heads_here * HEAD_DIM)
        .astype(jnp.bfloat16)
    )
    grad_keys = grad_keys.astype(jnp.bfloat16)
    grad_values = grad_values.astype(jnp.bfloat16)
    query_grad = product_tn(normed_full, grad_queries)
    key_grad = product_tn(normed_full, grad_keys)
    value_grad = product_tn(normed_full, grad_values)
    grad_normed_one = lax.psum_scatter(
        (
            product_nt(grad_queries, w_query)
            + product_nt(grad_keys, w_key)
            + product_nt(grad_values, w_value)
        ).astype(jnp.bfloat16),
        "head",
        scatter_dimension=0,
        tiled=True,
    ).astype(jnp.float32)
    attn_gain_part = jnp.sum(grad_normed_one * unit_one, axis=0)
    input_grad = grad_middle + norm_back(unit_one, inverse_one, attn_gain, grad_normed_one)
    summed = (
        lax.psum_scatter(
            query_grad.astype(jnp.bfloat16), "seq", scatter_dimension=0, tiled=True
        ).astype(jnp.float32),
        lax.psum_scatter(
            key_grad.astype(jnp.bfloat16), "seq", scatter_dimension=0, tiled=True
        ).astype(jnp.float32),
        lax.psum_scatter(
            value_grad.astype(jnp.bfloat16), "seq", scatter_dimension=0, tiled=True
        ).astype(jnp.float32),
        lax.psum_scatter(
            out_grad.astype(jnp.bfloat16), "seq", scatter_dimension=1, tiled=True
        ).astype(jnp.float32),
        lax.psum_scatter(
            gate_grad.astype(jnp.bfloat16), "seq", scatter_dimension=0, tiled=True
        ).astype(jnp.float32),
        lax.psum_scatter(
            up_grad.astype(jnp.bfloat16), "seq", scatter_dimension=0, tiled=True
        ).astype(jnp.float32),
        lax.psum_scatter(
            down_grad.astype(jnp.bfloat16), "seq", scatter_dimension=1, tiled=True
        ).astype(jnp.float32),
    )
    gain_grads = (
        lax.psum_scatter(attn_gain_part, ("seq", "head"), scatter_dimension=0, tiled=True),
        lax.psum_scatter(ffn_gain_part, ("seq", "head"), scatter_dimension=0, tiled=True),
    )
    return (
        result.astype(jnp.bfloat16),
        input_grad,
        gain_grads[0],
        summed[0],
        summed[1],
        summed[2],
        summed[3],
        gain_grads[1],
        summed[4],
        summed[5],
        summed[6],
    )


MESH = pl.DeviceIdType.MESH
BF16 = jnp.bfloat16
F32 = jnp.float32
MIB = 2**20


def remote(src, dst, send_sem, recv_sem, where):
    return pltpu.make_async_remote_copy(
        src_ref=src,
        dst_ref=dst,
        send_sem=send_sem,
        recv_sem=recv_sem,
        device_id=where,
        device_id_type=MESH,
    )


class Place:
    def __init__(self, line):
        s, h = lax.axis_index("seq"), lax.axis_index("head")
        core = lax.rem(h, 2)
        x = lax.rem(lax.div(h, 2), 2)
        y = lax.div(h, 4)
        self.s, self.h, self.line = s, h, line
        self.turn = 1 - 2 * core
        self.core = h + self.turn
        over_x, over_y = 2 - 4 * x, 4 - 8 * y
        self.first = h + over_x * (1 - core) + over_y * core
        self.second = h + over_y * (1 - core) + over_x * core
        self.across = h + over_x + over_y

    def at(self, head):
        return (self.s, head)

    def greet(self, along_seq=True):
        barrier = pltpu.get_barrier_semaphore()
        for head in (self.core, self.first, self.second):
            pl.semaphore_signal(barrier, inc=1, device_id=self.at(head), device_id_type=MESH)
        if along_seq:

            @pl.when(self.s > 0)
            def _():
                pl.semaphore_signal(
                    barrier, inc=1, device_id=(self.s - 1, self.h), device_id_type=MESH
                )

            @pl.when(self.s < self.line - 1)
            def _():
                pl.semaphore_signal(
                    barrier, inc=1, device_id=(self.s + 1, self.h), device_id_type=MESH
                )

            @pl.when((self.s > 0) & (self.s < self.line - 1))
            def _():
                pl.semaphore_wait(barrier, 5)

            @pl.when((self.s == 0) | (self.s == self.line - 1))
            def _():
                pl.semaphore_wait(barrier, 4)
        else:
            pl.semaphore_wait(barrier, 3)


class HeadGather:
    SEMS = 7

    def __init__(self, place, block, send, recv, own=None):
        p = place
        self.p = p
        plan = (
            (p.h, p.first, p.first),
            (p.h, p.second, p.second),
            (p.h, p.core, p.core),
            (p.first, p.second, p.across),
            (p.first, p.core, p.second + p.turn),
            (p.second, p.core, p.first + p.turn),
            (p.across, p.core, p.across + p.turn),
        )
        self.out = [
            remote(
                block(j) if own is None or i > 2 else own,
                block(j),
                send.at[i],
                recv.at[i],
                p.at(to),
            )
            for i, (j, to, _) in enumerate(plan)
        ]
        self.come = [
            remote(block(j), block(j), send.at[i], recv.at[i], p.at(to))
            for i, (_, to, j) in enumerate(plan)
        ]

    def start(self):
        for i in (0, 1, 2):
            self.out[i].start()

    def got_first(self):
        self.come[0].wait_recv()
        self.out[3].start()
        self.out[4].start()

    def got_second(self):
        self.come[1].wait_recv()
        self.out[5].start()

    def got_across(self):
        self.come[3].wait_recv()
        self.out[6].start()

    def got_core(self):
        self.come[2].wait_recv()

    def got_core_second(self):
        self.come[4].wait_recv()

    def got_core_first(self):
        self.come[5].wait_recv()

    def got_core_across(self):
        self.come[6].wait_recv()

    def finish(self):
        for copy in self.out:
            copy.wait_send()


class LineGather:
    def __init__(self, place, piece, up_send, up_recv, down_send, down_recv, own=None):
        self.p, self.piece, self.own = place, piece, own
        self.up = (up_send, up_recv)
        self.down = (down_send, down_recv)

    def _up(self, owner, t):
        p = self.p
        source = self.own if t == 0 and self.own is not None else self.piece(owner)
        return remote(
            source, self.piece(owner), self.up[0].at[t], self.up[1].at[t], (p.s + 1, p.h)
        )

    def _down(self, owner, t):
        p = self.p
        source = self.own if t == 0 and self.own is not None else self.piece(owner)
        return remote(
            source,
            self.piece(owner),
            self.down[0].at[t],
            self.down[1].at[t],
            (p.s - 1, p.h),
        )

    def start(self, t):
        p = self.p

        @pl.when((p.s < p.line - 1) & (p.s >= t))
        def _():
            self._up(p.s - t, t).start()

        @pl.when((p.s > 0) & (p.s + t < p.line))
        def _():
            self._down(p.s + t, t).start()

    def got(self, t):
        p = self.p

        @pl.when(p.s >= t + 1)
        def _():
            self._up(p.s - 1 - t, t).wait_recv()

        @pl.when(p.s + 1 + t < p.line)
        def _():
            self._down(p.s + 1 + t, t).wait_recv()

    def step(self, t):
        self.got(t)
        if t + 1 < self.p.line - 1:
            self.start(t + 1)

    def finish(self):
        p = self.p
        for t in range(p.line - 1):

            @pl.when((p.s < p.line - 1) & (p.s >= t))
            def _():
                self._up(p.s - t, t).wait_send()

            @pl.when((p.s > 0) & (p.s + t < p.line))
            def _():
                self._down(p.s + t, t).wait_send()


def line_sems(line, tensors=1):
    return [pltpu.SemaphoreType.DMA((line - 1,)) for _ in range(4 * tensors)]


def norm_rows(rows, gain):
    inverse = lax.rsqrt(jnp.mean(rows * rows, axis=-1, keepdims=True) + EPS)
    return rows * inverse * gain


def own_starts(segment):
    count = segment.shape[1]
    ids = segment[...]
    place = lax.broadcasted_iota(jnp.int32, (1, count), 1)
    starts = jnp.where((place > 0) & (ids != pltpu.roll(ids, 1, 1)), place, -1)
    shift = 1
    while shift < count:
        earlier = jnp.where(place >= shift, pltpu.roll(starts, shift, 1), -1)
        starts = jnp.maximum(starts, earlier)
        shift *= 2
    return starts


def any_spec():
    return pl.BlockSpec(memory_space=pl.ANY)


def vmem_spec():
    return pl.BlockSpec(memory_space=pltpu.VMEM)


LOG2E = 1.4426950408889634
TILE = 256
CHUNKS = WINDOW // TILE + 1


def tile_scores(tile, head, q, k_ext, floor):
    start = pl.multiple_of(tile * TILE, TILE)
    cols = slice(head * HEAD_DIM, (head + 1) * HEAD_DIM)
    queries = q[pl.ds(start, TILE), cols]
    row = lax.broadcasted_iota(jnp.int32, (TILE, TILE), 0)
    lane = lax.broadcasted_iota(jnp.int32, (TILE, TILE), 1)
    lowest = floor[:, pl.ds(start, TILE)] - start
    found = []
    for i in range(CHUNKS):
        keys = k_ext[pl.ds(start + i * TILE, TILE), cols]
        scores = product_nt(keys, queries)
        visible = row >= lowest - i * TILE
        if i == CHUNKS - 1:
            visible = visible & (row <= lane)
        found.append((scores, visible))
    return found


def forward_tile(tile, q, k_ext, v_t, floor, attended, logs):
    start = pl.multiple_of(tile * TILE, TILE)
    sharp = HEAD_DIM ** (-0.5) * LOG2E
    for head in range(q.shape[1] // HEAD_DIM):
        cols = slice(head * HEAD_DIM, (head + 1) * HEAD_DIM)
        found = [
            jnp.where(visible, scores, NEG)
            for scores, visible in tile_scores(tile, head, q, k_ext, floor)
        ]
        highest = functools.reduce(
            jnp.maximum, [jnp.max(scores, axis=0, keepdims=True) for scores in found]
        )
        total = jnp.zeros((1, TILE), F32)
        mixed = jnp.zeros((HEAD_DIM, TILE), F32)
        for i, scores in enumerate(found):
            weights = jnp.exp2((scores - highest) * sharp)
            total = total + jnp.sum(weights, axis=0, keepdims=True)
            mixed = mixed + product(
                v_t[cols, pl.ds(start + i * TILE, TILE)], weights.astype(BF16)
            )
        attended[pl.ds(start, TILE), cols] = (mixed / total).astype(BF16).T
        logs[head : head + 1, pl.ds(start, TILE)] = highest * sharp + jnp.log2(total)


def block_reduce(place, out, into, r_send, r_recv):
    p = place
    goes = (p.core, p.core, p.core, p.core, p.first, p.first, p.second)
    slots = (0, 1, 0, 1, 2, 3, 4)
    return [
        remote(out.at[slots[i]], into.at[i], r_send.at[i], r_recv.at[i], p.at(to))
        for i, to in enumerate(goes)
    ]


def forward_kernel(
    line,
    tokens,
    gain,
    wq,
    wk,
    wv,
    segment,
    cot,
    w_out,
    w_gate,
    w_up,
    normed_out,
    qkv_out,
    weight_out,
    floor,
    attended,
    logs,
    halo_out,
    cot_out,
    w_out_out,
    gate_full,
    up_full,
    middle,
    normed,
    weight,
    q,
    k_ext,
    v_ext,
    v_t,
    w_out_full,
    seg_halo,
    out,
    into,
    g_send,
    g_recv,
    c_send,
    c_recv,
    r_send,
    r_recv,
    halo_send,
    halo_recv,
    seg_sems,
    keep,
    *sems,
):
    p = Place(line)
    qkv_sems, out_sems, gate_sems, up_sems = sems[0:4], sems[4:8], sems[8:12], sems[12:16]
    rows, width = tokens.shape
    slab, part = wq.shape
    count = segment.shape[1]
    rows_of = lambda ref, j: ref.at[pl.ds(pl.multiple_of(j * rows, rows), rows)]
    slab_of = lambda d: weight.at[pl.ds(pl.multiple_of(d * slab, slab), slab)]
    weight_own = slab_of(p.s)
    weight_own[:, 0:part] = wq[...]
    weight_own[:, part : 2 * part] = wk[...]
    weight_own[:, 2 * part : 3 * part] = wv[...]
    seg_copy = remote(
        segment.at[:, pl.ds(count - WINDOW, WINDOW)],
        seg_halo,
        seg_sems.at[0],
        seg_sems.at[1],
        (p.s + 1, p.h),
    )
    halo = [
        remote(
            ext.at[pl.ds(count, WINDOW)],
            ext.at[pl.ds(0, WINDOW)],
            halo_send.at[i],
            halo_recv.at[i],
            (p.s + 1, p.h),
        )
        for i, ext in enumerate((k_ext, v_ext))
    ]
    gather = HeadGather(p, lambda j: rows_of(normed, j), g_send, g_recv)
    cot_gather = HeadGather(p, lambda j: rows_of(cot_out, j), c_send, c_recv, own=cot)
    qkv_gather = LineGather(p, slab_of, *qkv_sems)
    out_gather = LineGather(p, lambda d: w_out_full.at[d], *out_sems, own=w_out)
    gate_gather = LineGather(p, lambda d: gate_full.at[d], *gate_sems, own=w_gate)
    up_gather = LineGather(p, lambda d: up_full.at[d], *up_sems, own=w_up)
    p.greet()
    qkv_gather.start(0)

    @pl.when(p.s < line - 1)
    def _():
        seg_copy.start()

    mine = rows_of(normed, p.h)
    step = 32

    @pl.loop(0, rows // step)
    def _(i):
        at = pl.ds(pl.multiple_of(i * step, step), step)
        mine[at] = norm_rows(tokens[at].astype(F32), gain[...]).astype(BF16)

    gather.start()
    saved = []

    def save(source, target):
        copy = pltpu.make_async_copy(source, target, keep.at[len(saved)])
        copy.start()
        saved.append(copy)

    def save_block(j):
        save(rows_of(normed, j), rows_of(normed_out, j))

    save_block(p.h)
    save(cot, rows_of(cot_out, p.h))
    save(w_out, w_out_full.at[p.s])
    own_w_out = saved[-1]
    save(w_gate, gate_full.at[p.s])
    save(w_up, up_full.at[p.s])
    starts = own_starts(segment)

    @pl.when(p.s == 0)
    def _():
        k_ext[0:WINDOW, :] = jnp.zeros((WINDOW, part), BF16)
        v_ext[0:WINDOW, :] = jnp.zeros((WINDOW, part), BF16)

    @pl.when(p.s > 0)
    def _():
        seg_copy.wait_recv()

    before = jnp.sum(
        (seg_halo[...] == segment[:, 0:1]).astype(jnp.int32), axis=1, keepdims=True
    )
    before = jnp.where(p.s > 0, before, 0)
    floor[...] = jnp.maximum(
        lax.broadcasted_iota(jnp.int32, (1, count), 1),
        jnp.where(starts >= 0, starts + WINDOW, WINDOW - before),
    )
    gather.got_core()
    save_block(p.core)
    qkv_gather.step(0)
    gather.got_first()
    gather.got_second()
    cot_gather.start()
    save_block(p.first)
    save_block(p.second)
    qkv_gather.step(1)
    out_gather.start(0)
    gather.got_core_second()
    gather.got_core_first()
    save_block(p.second + p.turn)
    save_block(p.first + p.turn)
    qkv_gather.step(2)
    gather.got_across()
    save_block(p.across)
    gather.got_core_across()
    save_block(p.across + p.turn)
    save(weight, weight_out)

    def multiply(first, last):
        @pl.loop(first, last)
        def _(n):
            start = pl.multiple_of((count // rows - 1 - n) * rows, rows)
            value = product(normed[pl.ds(start, rows), :], weight[...]).astype(BF16)
            q[pl.ds(start, rows), :] = value[:, 0:part]
            k_ext[pl.ds(start + WINDOW, rows), :] = value[:, part : 2 * part]
            v_ext[pl.ds(start + WINDOW, rows), :] = value[:, 2 * part : 3 * part]

    late = (WINDOW + rows - 1) // rows
    multiply(0, late)

    @pl.when(p.s < line - 1)
    def _():
        halo[0].start()
        halo[1].start()

    out_gather.step(0)
    gate_gather.start(0)
    multiply(late, count // rows)
    save(q, qkv_out.at[:, pl.ds(0, part)])
    save(k_ext.at[pl.ds(WINDOW, count)], qkv_out.at[:, pl.ds(part, part)])
    save(v_ext.at[pl.ds(WINDOW, count)], qkv_out.at[:, pl.ds(2 * part, part)])

    def turn(first, last):
        @pl.loop(first, last)
        def _(i):
            at = pl.ds(pl.multiple_of(i * TILE, TILE), TILE)
            v_t[:, at] = v_ext[at, :].T

    def tiles(first, last):
        @pl.loop(first, last)
        def _(tile):
            forward_tile(tile, q, k_ext, v_t, floor, attended, logs)

    ahead = WINDOW // TILE
    turn(ahead, ahead + count // TILE)
    tiles(ahead, ahead + 1)
    out_gather.step(1)
    up_gather.start(0)
    tiles(ahead + 1, ahead + 4)
    cot_gather.got_core()
    cot_gather.got_first()
    cot_gather.got_second()
    tiles(ahead + 4, ahead + 5)
    out_gather.step(2)
    tiles(ahead + 5, count // TILE)
    gate_gather.step(0)

    @pl.when(p.s > 0)
    def _():
        halo[0].wait_recv()
        halo[1].wait_recv()

    turn(0, ahead)
    tiles(0, 2)
    cot_gather.got_core_second()
    cot_gather.got_core_first()
    cot_gather.got_across()
    tiles(2, ahead)
    up_gather.step(0)
    for i, ext in enumerate((k_ext, v_ext)):
        save(ext.at[pl.ds(0, WINDOW)], halo_out.at[i])
    own_w_out.wait()
    save(w_out_full, w_out_out)
    copies = block_reduce(p, out, into, r_send, r_recv)

    def emit(j, target, *more):
        start = pl.multiple_of(j * rows, rows)

        @pl.loop(0, line)
        def _(n):
            cols = pl.ds(pl.multiple_of(n * slab, slab), slab)
            value = product(attended[pl.ds(start, rows), :], w_out_full[n])
            for other in more:
                value = value + other[:, cols].astype(F32)
            target[:, cols] = value.astype(target.dtype)

    emit(p.second + p.turn, out.at[0])
    copies[0].start()
    emit(p.across + p.turn, out.at[1])
    copies[1].start()
    copies[0].wait_recv()
    emit(p.first, out.at[2], into.at[0])
    copies[4].start()
    copies[0].wait_send()
    emit(p.first + p.turn, out.at[0])
    copies[2].start()
    copies[1].wait_recv()
    emit(p.across, out.at[3], into.at[1])
    copies[5].start()
    copies[1].wait_send()
    emit(p.core, out.at[1])
    copies[3].start()
    gate_gather.step(1)
    copies[3].wait_recv()
    emit(p.h, middle, into.at[3], tokens)
    copies[2].wait_recv()
    cot_gather.got_core_across()
    copies[5].wait_recv()
    emit(p.second, out.at[4], into.at[2], into.at[5])
    copies[6].start()
    up_gather.step(1)
    gate_gather.step(2)
    copies[4].wait_recv()
    up_gather.step(2)
    copies[6].wait_recv()

    @pl.loop(0, line)
    def _(n):
        cols = pl.ds(pl.multiple_of(n * slab, slab), slab)
        middle[:, cols] += into[4, :, cols].astype(F32) + into[6, :, cols].astype(F32)

    for i in range(2, 7):
        copies[i].wait_send()
    gather.finish()
    cot_gather.finish()
    for each in (qkv_gather, out_gather, gate_gather, up_gather):
        each.finish()

    @pl.when(p.s < line - 1)
    def _():
        seg_copy.wait_send()
        halo[0].wait_send()
        halo[1].wait_send()

    for copy in saved:
        if copy is not own_w_out:
            copy.wait()


def forward(line, tokens, gain, wq, wk, wv, segment, cot, w_out, w_gate, w_up):
    rows, width = tokens.shape
    slab, part = wq.shape
    full = rows * 8
    units = w_gate.shape[0]
    heads = part // HEAD_DIM
    return pl.pallas_call(
        functools.partial(forward_kernel, line),
        out_shape=(
            jax.ShapeDtypeStruct((full, width), BF16),
            jax.ShapeDtypeStruct((full, 3 * part), BF16),
            jax.ShapeDtypeStruct((width, 3 * part), BF16),
            jax.ShapeDtypeStruct((1, full), jnp.int32),
            jax.ShapeDtypeStruct((full, part), BF16),
            jax.ShapeDtypeStruct((heads, full), F32),
            jax.ShapeDtypeStruct((2, WINDOW, part), BF16),
            jax.ShapeDtypeStruct((full, width), BF16),
            jax.ShapeDtypeStruct((line, part, slab), BF16),
            jax.ShapeDtypeStruct((line, units, slab), BF16),
            jax.ShapeDtypeStruct((line, units, slab), BF16),
            jax.ShapeDtypeStruct((rows, width), F32),
        ),
        in_specs=[vmem_spec()] * 10,
        out_specs=(
            any_spec(),
            any_spec(),
            any_spec(),
            vmem_spec(),
            vmem_spec(),
            vmem_spec(),
            any_spec(),
            any_spec(),
            any_spec(),
            any_spec(),
            any_spec(),
            vmem_spec(),
        ),
        scratch_shapes=[
            pltpu.VMEM((full, width), BF16),
            pltpu.VMEM((width, 3 * part), BF16),
            pltpu.VMEM((full, part), BF16),
            pltpu.VMEM((WINDOW + full, part), BF16),
            pltpu.VMEM((WINDOW + full, part), BF16),
            pltpu.VMEM((part, WINDOW + full), BF16),
            pltpu.VMEM((line, part, slab), BF16),
            pltpu.VMEM((1, WINDOW), jnp.int32),
            pltpu.VMEM((5, rows, width), BF16),
            pltpu.VMEM((7, rows, width), BF16),
            pltpu.SemaphoreType.DMA((7,)),
            pltpu.SemaphoreType.DMA((7,)),
            pltpu.SemaphoreType.DMA((7,)),
            pltpu.SemaphoreType.DMA((7,)),
            pltpu.SemaphoreType.DMA((7,)),
            pltpu.SemaphoreType.DMA((7,)),
            pltpu.SemaphoreType.DMA((2,)),
            pltpu.SemaphoreType.DMA((2,)),
            pltpu.SemaphoreType.DMA((2,)),
            pltpu.SemaphoreType.DMA((19,)),
            *line_sems(line, 4),
        ],
        compiler_params=pltpu.CompilerParams(
            collective_id=1, has_side_effects=True, vmem_limit_bytes=62 * MIB
        ),
        cost_estimate=pl.CostEstimate(
            flops=20 * 2**30, bytes_accessed=100 * MIB, transcendentals=0
        ),
    )(tokens, gain.reshape(1, width), wq, wk, wv, segment.reshape(1, full), cot, w_out, w_gate, w_up)


def strips(width, most=256):
    return [(start, min(start + most, width)) for start in range(0, width, most)]


def feed_kernel(
    line,
    middle,
    gain,
    cot,
    gate,
    up,
    down,
    normed_out,
    hidden_out,
    grad_gate_out,
    grad_up_out,
    grad_out,
    down_out,
    down_grad,
    normed,
    w_gate,
    w_up,
    w_down,
    gates,
    ups,
    cot_block,
    hidden,
    grad_gate,
    grad_up,
    down_parts,
    down_up_in,
    down_down_in,
    out,
    into,
    r_send,
    r_recv,
    g_send,
    g_recv,
    *sems,
):
    p = Place(line)
    down_sems, sum_sems, loads, saves, stage, strip_sems = sems[0:4], sems[4:8], *sems[8:12]
    rows, width = grad_out.shape
    units = w_down.shape[1]
    slab = w_down.shape[2]
    block = lambda j: normed.at[pl.ds(pl.multiple_of(j * rows, rows), rows)]
    rows_of = lambda ref, j: ref.at[pl.ds(pl.multiple_of(j * rows, rows), rows)]
    gather = HeadGather(p, block, g_send, g_recv)
    down_gather = LineGather(p, lambda d: w_down.at[d], *down_sems, own=down)
    p.greet()
    down_gather.start(0)
    started = [
        pltpu.make_async_copy(middle, grad_out, loads.at[0]),
        pltpu.make_async_copy(gate, w_gate, loads.at[1]),
        pltpu.make_async_copy(up, w_up, loads.at[3]),
        pltpu.make_async_copy(down, w_down.at[p.s], loads.at[4]),
    ]
    for copy in started:
        copy.start()
    started[0].wait()
    mine = block(p.h)
    step = 32

    @pl.loop(0, rows // step)
    def _(i):
        at = pl.ds(pl.multiple_of(i * step, step), step)
        mine[at] = norm_rows(grad_out[at], gain[...]).astype(BF16)

    gather.start()
    saved = []

    def save(j):
        copy = pltpu.make_async_copy(block(j), rows_of(normed_out, j), saves.at[len(saved)])
        copy.start()
        saved.append(copy)

    opened = (
        p.h,
        p.core,
        p.first,
        p.second + p.turn,
        p.across + p.turn,
        p.across,
        p.first + p.turn,
        p.second,
    )
    hidden_stores = [
        pltpu.make_async_copy(hidden.at[m % 2], rows_of(hidden_out, j), stage.at[m % 2])
        for m, j in enumerate(opened)
    ]

    def open_up(m, slot):
        start = pl.multiple_of(opened[m] * rows, rows)
        if m > 1:
            hidden_stores[m - 2].wait()
        for first, last in strips(units):
            found = []
            for weight in (w_gate, w_up):
                value = product_nt(normed[pl.ds(start, rows), 0:slab], weight[0, first:last, :])
                for d in range(1, line):
                    value = value + product_nt(
                        normed[pl.ds(start, rows), d * slab : (d + 1) * slab],
                        weight[d, first:last, :],
                    )
                found.append(value)
            value, lift = found
            gates[slot, :, first:last] = value.astype(BF16)
            ups[slot, :, first:last] = lift.astype(BF16)
            hidden[m % 2, :, first:last] = (value * jax.nn.sigmoid(value) * lift).astype(BF16)
        hidden_stores[m].start()

    order = (
        p.second + p.turn,
        p.first,
        p.across + p.turn,
        p.across,
        p.first + p.turn,
        p.second,
        p.core,
        p.h,
    )
    fetches = [
        pltpu.make_async_copy(rows_of(cot, j), cot_block, stage.at[6]) for j in order
    ]
    stores = [
        [
            pltpu.make_async_copy(
                held.at[n % 2], rows_of(home, j), stage.at[2 + 2 * (n % 2) + i]
            )
            for i, (held, home) in enumerate(
                ((grad_gate, grad_gate_out), (grad_up, grad_up_out))
            )
        ]
        for n, j in enumerate(order)
    ]

    def close(n, slot):
        fetches[n].wait()
        if n > 1:
            for copy in stores[n - 2]:
                copy.wait()
        turn = n % 2
        for first, last in strips(units):
            grad = product_nt(cot_block[:, 0:slab], w_down[0, first:last, :])
            for d in range(1, line):
                grad = grad + product_nt(
                    cot_block[:, d * slab : (d + 1) * slab], w_down[d, first:last, :]
                )
            gate = gates[slot, :, first:last].astype(F32)
            lift = ups[slot, :, first:last].astype(F32)
            sigmoid = jax.nn.sigmoid(gate)
            grad_up[turn, :, first:last] = (grad * gate * sigmoid).astype(BF16)
            grad_gate[turn, :, first:last] = (
                grad * lift * (sigmoid * (1.0 + gate * (1.0 - sigmoid)))
            ).astype(BF16)
        if n + 1 < len(order):
            fetches[n + 1].start()
        for copy in stores[n]:
            copy.start()

    def back(n, target, *more):
        turn = n % 2

        @pl.loop(0, line)
        def _(d):
            cols = pl.ds(pl.multiple_of(d * slab, slab), slab)
            value = product(grad_gate[turn], w_gate[d]) + product(grad_up[turn], w_up[d])
            for other in more:
                value = value + other[:, cols].astype(F32)
            target[:, cols] = value.astype(target.dtype)

    copies = block_reduce(p, out, into, r_send, r_recv)
    down_reduce = LineReduce(
        p, lambda d: down_parts.at[d], down_up_in, down_down_in, *sum_sems
    )
    wide = 256
    padded = hidden.shape[2]
    kept = slice(2 * wide, 2 * wide + units)
    hidden[:, :, units // 128 * 128 :] = jnp.zeros((2, rows, padded - units // 128 * 128), BF16)
    multiply = lambda *some: weight_product(
        lambda rows_in: product_tn(normed[:, kept], rows_in),
        cot,
        lambda d: down_parts.at[d],
        lambda k: normed.at[:, pl.ds(pl.multiple_of(k * wide, wide), wide)],
        wide,
        strip_sems,
        p,
        *some,
    )
    fetches[0].start()
    for copy in started[1:3]:
        copy.wait()
    save(p.h)
    open_up(0, 0)
    gather.got_core()
    save(p.core)
    open_up(1, 1)
    down_gather.step(0)
    gather.got_first()
    gather.got_second()
    save(p.first)
    save(p.second)
    down_gather.step(1)
    open_up(2, 2)
    gather.got_core_second()
    gather.got_core_first()
    save(p.second + p.turn)
    save(p.first + p.turn)
    open_up(3, 3)
    clear_last(down_reduce)
    down_gather.step(2)
    started[3].wait()
    down_save = pltpu.make_async_copy(w_down, down_out, loads.at[4])
    down_save.start()
    close(0, 3)
    back(0, out.at[0])
    copies[0].start()
    gather.got_across()
    save(p.across)
    close(1, 2)
    copies[0].wait_recv()
    back(1, out.at[2], into.at[0])
    copies[4].start()
    gather.got_core_across()
    save(p.across + p.turn)
    open_up(4, 2)
    open_up(5, 3)
    open_up(6, 4)
    open_up(7, 5)
    gather.finish()
    for copy in saved:
        copy.wait()
    for copy in hidden_stores[6:]:
        copy.wait()
    fill = pltpu.make_async_copy(hidden_out, normed.at[:, pl.ds(2 * wide, padded)], loads.at[5])
    fill.start()
    fill.wait()
    multiply(0, 1)
    down_reduce.start(0)
    close(2, 2)
    back(2, out.at[1])
    copies[1].start()
    close(3, 3)
    copies[1].wait_recv()
    back(3, out.at[3], into.at[1])
    copies[5].start()
    multiply(1, line)
    down_reduce.step(0)
    close(4, 4)
    copies[0].wait_send()
    back(4, out.at[0])
    copies[2].start()
    close(5, 5)
    copies[2].wait_recv()
    copies[5].wait_recv()
    back(5, out.at[4], into.at[2], into.at[5])
    copies[6].start()
    down_reduce.step(1)
    close(6, 1)
    copies[1].wait_send()
    back(6, out.at[1])
    copies[3].start()
    close(7, 0)
    copies[3].wait_recv()
    back(7, grad_out, into.at[3])
    copies[4].wait_recv()
    copies[6].wait_recv()

    @pl.loop(0, line)
    def _(d):
        cols = pl.ds(pl.multiple_of(d * slab, slab), slab)
        grad_out[:, cols] += into[4, :, cols].astype(F32) + into[6, :, cols].astype(F32)

    down_reduce.step(2)
    for first, last in strips(units, 128):
        down_grad[first:last, :] = down_reduce.total(slice(first, last))
    for i in range(2, 7):
        copies[i].wait_send()
    down_gather.finish()
    down_reduce.finish()
    for copy in stores[6] + stores[7]:
        copy.wait()
    down_save.wait()


def feed(line, middle, gain, cot, gate, up, down):
    rows, width = middle.shape
    units, slab = down.shape
    full = rows * 8
    padded = (units + 127) // 128 * 128
    return pl.pallas_call(
        functools.partial(feed_kernel, line),
        out_shape=(
            jax.ShapeDtypeStruct((full, width), BF16),
            jax.ShapeDtypeStruct((full, padded), BF16),
            jax.ShapeDtypeStruct((full, units), BF16),
            jax.ShapeDtypeStruct((full, units), BF16),
            jax.ShapeDtypeStruct((rows, width), F32),
            jax.ShapeDtypeStruct((line, units, slab), BF16),
            jax.ShapeDtypeStruct((units, slab), F32),
        ),
        in_specs=[any_spec(), vmem_spec()] + [any_spec()] * 4,
        out_specs=(
            any_spec(),
            any_spec(),
            any_spec(),
            any_spec(),
            vmem_spec(),
            any_spec(),
            vmem_spec(),
        ),
        scratch_shapes=[
            pltpu.VMEM((full, width), BF16),
            pltpu.VMEM((line, units, slab), BF16),
            pltpu.VMEM((line, units, slab), BF16),
            pltpu.VMEM((line, units, slab), BF16),
            pltpu.VMEM((6, rows, units), BF16),
            pltpu.VMEM((6, rows, units), BF16),
            pltpu.VMEM((rows, width), BF16),
            pltpu.VMEM((2, rows, padded), BF16),
            pltpu.VMEM((2, rows, units), BF16),
            pltpu.VMEM((2, rows, units), BF16),
            pltpu.VMEM((line, units, slab), BF16),
            pltpu.VMEM((line - 1, units, slab), BF16),
            pltpu.VMEM((line - 1, units, slab), BF16),
            pltpu.VMEM((5, rows, width), BF16),
            pltpu.VMEM((7, rows, width), BF16),
            pltpu.SemaphoreType.DMA((7,)),
            pltpu.SemaphoreType.DMA((7,)),
            pltpu.SemaphoreType.DMA((7,)),
            pltpu.SemaphoreType.DMA((7,)),
            *line_sems(line, 2),
            pltpu.SemaphoreType.DMA((6,)),
            pltpu.SemaphoreType.DMA((8,)),
            pltpu.SemaphoreType.DMA((7,)),
            pltpu.SemaphoreType.DMA((2,)),
        ],
        compiler_params=pltpu.CompilerParams(
            collective_id=2, has_side_effects=True, vmem_limit_bytes=63 * MIB
        ),
        cost_estimate=pl.CostEstimate(
            flops=50 * 2**30, bytes_accessed=80 * MIB, transcendentals=0
        ),
    )(middle, gain.reshape(1, width), cot, gate, up, down)


class LineReduce:
    def __init__(self, place, part, up_in, down_in, up_send, up_recv, down_send, down_recv):
        self.p, self.part = place, part
        self.up_in, self.down_in = up_in, down_in
        self.up = (up_send, up_recv)
        self.down = (down_send, down_recv)

    def _up(self, d, t):
        p = self.p
        return remote(
            self.part(d), self.up_in.at[t], self.up[0].at[t], self.up[1].at[t], (p.s + 1, p.h)
        )

    def _down(self, d, t):
        p = self.p
        return remote(
            self.part(d),
            self.down_in.at[t],
            self.down[0].at[t],
            self.down[1].at[t],
            (p.s - 1, p.h),
        )

    def _sends(self, t):
        p, last = self.p, self.p.line - 1
        return (
            ((p.s <= t) & (p.s < last), self._up, last - t + p.s),
            ((last - p.s <= t) & (p.s > 0), self._down, t - last + p.s),
        )

    def start(self, t):
        p, last = self.p, self.p.line - 1
        for number, (goes, copy, d) in enumerate(self._sends(t)):
            came = (self.up_in, self.down_in)[number]

            @pl.when(goes)
            def _():
                if t > 0:
                    inner = p.s > 0 if number == 0 else p.s < last

                    @pl.when(inner)
                    def _():
                        add_rows(self.part(d), came.at[t - 1])

                copy(d, t).start()

    def got(self, t):
        p, last = self.p, self.p.line - 1

        @pl.when((p.s >= 1) & (t >= p.s - 1))
        def _():
            self._up(0, t).wait_recv()

        @pl.when((p.s < last) & (t >= last - p.s - 1))
        def _():
            self._down(0, t).wait_recv()

    def step(self, t):
        self.got(t)
        if t + 1 < self.p.line - 1:
            self.start(t + 1)

    def end(self):
        p, last = self.p, self.p.line - 1

        @pl.when(p.s >= 1)
        def _():
            add_rows(self.part(p.s), self.up_in.at[last - 1])

        @pl.when(p.s < last)
        def _():
            add_rows(self.part(p.s), self.down_in.at[last - 1])

    def total(self, rows):
        p, last = self.p, self.p.line - 1
        value = self.part(p.s)[rows, :].astype(F32)
        value = value + jnp.where(p.s >= 1, self.up_in[last - 1, rows, :].astype(F32), 0.0)
        return value + jnp.where(p.s < last, self.down_in[last - 1, rows, :].astype(F32), 0.0)

    def finish(self):
        for t in range(self.p.line - 1):
            for goes, copy, d in self._sends(t):

                @pl.when(goes)
                def _():
                    copy(d, t).wait_send()


def add_rows(target, other):
    step = 16

    @pl.loop(0, target.shape[0] // step)
    def _(i):
        at = pl.ds(pl.multiple_of(i * step, step), step)
        target[at, :] = (target[at, :].astype(F32) + other[at, :].astype(F32)).astype(BF16)


def clear_last(reduce):
    p, last = reduce.p, reduce.p.line - 1

    @pl.when(p.s == 0)
    def _():
        reduce.up_in[last - 1] = jnp.zeros(reduce.up_in.shape[1:], BF16)

    @pl.when(p.s == last)
    def _():
        reduce.down_in[last - 1] = jnp.zeros(reduce.down_in.shape[1:], BF16)


def weight_product(apply, source, piece, strip, wide, sems, place, first, last):
    each = piece(0).shape[1] // wide
    begin, end = first * each, last * each

    def slab(n):
        d = lax.div(n, each)
        low = place.s < place.line // 2
        return jnp.where(low, place.line - 1 - d, d)

    def fetch(n):
        at = slab(n) * each + lax.rem(n, each)
        cols = pl.ds(pl.multiple_of(at * wide, wide), wide)
        return pltpu.make_async_copy(
            source.at[:, cols], strip(lax.rem(n, 2)), sems.at[lax.rem(n, 2)]
        )

    fetch(begin).start()

    @pl.loop(begin, end)
    def _(n):
        @pl.when(n + 1 < end)
        def _():
            fetch(n + 1).start()

        fetch(n).wait()
        cols = pl.ds(pl.multiple_of(lax.rem(n, each) * wide, wide), wide)
        piece(slab(n))[:, cols] = apply(strip(lax.rem(n, 2))[...]).astype(BF16)


def turn_rows(source, target):
    step = 256

    @pl.loop(0, source.shape[0] // step)
    def _(i):
        at = pl.ds(pl.multiple_of(i * step, step), step)
        for first, last in strips(source.shape[1], 128):
            target[first:last, at] = source[at, first:last].T


def return_kernel(
    line,
    grad_normed,
    middle,
    cot_own,
    gain,
    attended,
    w_out,
    grad_gate,
    grad_up,
    normed,
    grad_middle,
    gain_part,
    grad_attended,
    inner,
    up_grad,
    gate_parts,
    out_parts,
    branch,
    units_in,
    turned,
    strip,
    up_parts,
    other_parts,
    up_up_in,
    up_down_in,
    att_turned,
    out_sum,
    g_send,
    g_recv,
    *sems,
):
    p = Place(line)
    up_sems, loads, strips_sem, saves = sems[0:4], *sems[4:7]
    rows, width = grad_normed.shape
    slab = w_out.shape[2]
    part = attended.shape[1]
    block = lambda j: branch.at[pl.ds(pl.multiple_of(j * rows, rows), rows)]
    gather = HeadGather(p, block, g_send, g_recv)
    up_reduce = LineReduce(p, lambda d: up_parts.at[d], up_up_in, up_down_in, *up_sems)
    load = [
        pltpu.make_async_copy(source, units_in, loads.at[i])
        for i, source in enumerate((grad_up, grad_gate))
    ]
    load[0].start()
    p.greet()
    mine = block(p.h)
    gain_part[...] = jnp.zeros_like(gain_part)
    step = 32

    @pl.loop(0, rows // step)
    def _(i):
        at = pl.ds(pl.multiple_of(i * step, step), step)
        value = middle[at]
        inverse = lax.rsqrt(jnp.mean(value * value, axis=-1, keepdims=True) + EPS)
        unit = value * inverse
        grad = grad_normed[at]
        gain_part[...] += jnp.sum(grad * unit, axis=0, keepdims=True)
        result = cot_own[at].astype(F32) + norm_back(unit, inverse, gain[...], grad)
        grad_middle[at] = result
        mine[at] = result.astype(BF16)

    gather.start()
    clear_last(up_reduce)
    multiply = lambda parts, *some: weight_product(
        lambda rows_in: product(turned[...], rows_in),
        normed,
        lambda d: parts.at[d],
        strip.at.__getitem__,
        strip.shape[2],
        strips_sem,
        p,
        *some,
    )
    load[0].wait()
    turn_rows(units_in, turned)
    load[1].start()
    multiply(up_parts, 0, 1)
    up_reduce.start(0)
    multiply(up_parts, 1, line)
    gather.got_core()
    load[1].wait()
    turn_rows(units_in, turned)
    up_reduce.step(0)
    gather.got_first()
    gather.got_second()
    multiply(other_parts, 0, line)
    save_gate = pltpu.make_async_copy(other_parts, gate_parts, saves.at[1])
    save_gate.start()
    turn_rows(attended, att_turned)
    up_reduce.step(1)
    gather.got_core_second()
    gather.got_core_first()
    out_sum[...] = jnp.zeros_like(out_sum)

    def take(j):
        start = pl.multiple_of(j * rows, rows)
        at = pl.ds(start, rows)
        total = product_nt(branch[at, 0:slab], w_out[0])
        for d in range(1, line):
            total = total + product_nt(branch[at, d * slab : (d + 1) * slab], w_out[d])
        low = total.astype(BF16)
        grad_attended[at, :] = low
        for head in range(part // HEAD_DIM):
            cols = slice(head * HEAD_DIM, (head + 1) * HEAD_DIM)
            both = low[:, cols].astype(F32) * attended[at, cols].astype(F32)
            inner[head : head + 1, at] = jnp.sum(both.T, axis=0, keepdims=True)

        @pl.loop(0, line)
        def _(d):
            cols = pl.ds(pl.multiple_of(d * slab, slab), slab)
            out_sum[d] += product(att_turned[:, at], branch[at, cols])

    for j in (p.h, p.core, p.first, p.second):
        take(j)
    for j in (p.second + p.turn, p.first + p.turn):
        take(j)
    gather.got_across()
    take(p.across)
    gather.got_core_across()
    take(p.across + p.turn)
    for d in range(line):
        out_parts[d] = out_sum[d].astype(BF16)
    up_reduce.step(2)
    for first, last in strips(up_grad.shape[0], 128):
        up_grad[first:last, :] = up_reduce.total(slice(first, last))
    gather.finish()
    up_reduce.finish()
    save_gate.wait()


def give_back(
    line, grad_normed, middle, cot_own, gain, attended, w_out, grad_gate, grad_up, normed
):
    rows, width = middle.shape
    full, units = grad_up.shape
    part = attended.shape[1]
    slab = w_out.shape[2]
    heads = part // HEAD_DIM
    return pl.pallas_call(
        functools.partial(return_kernel, line),
        out_shape=(
            jax.ShapeDtypeStruct((rows, width), F32),
            jax.ShapeDtypeStruct((1, width), F32),
            jax.ShapeDtypeStruct((full, part), BF16),
            jax.ShapeDtypeStruct((heads, full), F32),
            jax.ShapeDtypeStruct((units, slab), F32),
            jax.ShapeDtypeStruct((line, units, slab), BF16),
            jax.ShapeDtypeStruct((line, part, slab), BF16),
        ),
        in_specs=[vmem_spec()] * 6 + [any_spec()] * 3,
        out_specs=(
            vmem_spec(),
            vmem_spec(),
            vmem_spec(),
            vmem_spec(),
            vmem_spec(),
            any_spec(),
            vmem_spec(),
        ),
        scratch_shapes=[
            pltpu.VMEM((full, width), BF16),
            pltpu.VMEM((full, units), BF16),
            pltpu.VMEM((units, full), BF16),
            pltpu.VMEM((2, full, 256), BF16),
            pltpu.VMEM((line, units, slab), BF16),
            pltpu.VMEM((line, units, slab), BF16),
            pltpu.VMEM((line - 1, units, slab), BF16),
            pltpu.VMEM((line - 1, units, slab), BF16),
            pltpu.VMEM((part, full), BF16),
            pltpu.VMEM((line, part, slab), F32),
            pltpu.SemaphoreType.DMA((7,)),
            pltpu.SemaphoreType.DMA((7,)),
            *line_sems(line),
            pltpu.SemaphoreType.DMA((2,)),
            pltpu.SemaphoreType.DMA((2,)),
            pltpu.SemaphoreType.DMA((2,)),
        ],
        compiler_params=pltpu.CompilerParams(
            collective_id=3, has_side_effects=True, vmem_limit_bytes=62 * MIB
        ),
        cost_estimate=pl.CostEstimate(
            flops=25 * 2**30, bytes_accessed=80 * MIB, transcendentals=0
        ),
    )(
        grad_normed,
        middle,
        cot_own,
        gain.reshape(1, width),
        attended,
        w_out,
        grad_gate,
        grad_up,
        normed,
    )


def backward_tile(tile, q, k_ext, v_ext, k_t, floor, logs, inner, grad, key_sum, value_sum):
    start = pl.multiple_of(tile * TILE, TILE)
    mine = pl.ds(start, TILE)
    scale = HEAD_DIM ** (-0.5)
    for head in range(q.shape[1] // HEAD_DIM):
        cols = slice(head * HEAD_DIM, (head + 1) * HEAD_DIM)
        queries = q[mine, cols]
        grads = grad[mine, cols]
        log = logs[head : head + 1, mine]
        middle = inner[head : head + 1, mine]
        turned = jnp.zeros((HEAD_DIM, TILE), F32)
        for i, (scores, visible) in enumerate(tile_scores(tile, head, q, k_ext, floor)):
            at = pl.ds(start + i * TILE, TILE)
            probs = jnp.where(visible, jnp.exp2(scores * (scale * LOG2E) - log), 0.0)
            grad_probs = product_nt(v_ext[at, cols], grads)
            grad_scores = (probs * (grad_probs - middle)).astype(BF16)
            value_sum[at, cols] += product(probs.astype(BF16), grads)
            key_sum[at, cols] += product(grad_scores, queries)
            turned = turned + product(k_t[cols, at], grad_scores)
        q[mine, cols] = (turned * scale).astype(BF16).T


def attend_back_kernel(
    line,
    qkv,
    halo_kv,
    floor,
    logs,
    grad,
    inner,
    hidden,
    w_down,
    middle,
    gate_in,
    grads_out,
    result,
    gate_grad,
    q,
    k_ext,
    v_ext,
    k_t,
    key_sum,
    value_sum,
    halo_out,
    halo_in,
    gate_parts,
    gate_up_in,
    gate_down_in,
    out,
    into,
    total,
    hidden_block,
    r_send,
    r_recv,
    *sems,
):
    p = Place(line)
    gate_sems, loads, halo_send, halo_recv, stage, saves = sems[0:4], *sems[4:9]
    rows, width = result.shape
    slab = w_down.shape[2]
    count, part = q.shape
    scale = HEAD_DIM ** (-0.5)
    rows_of = lambda ref, j: ref.at[pl.ds(pl.multiple_of(j * rows, rows), rows)]
    gate_reduce = LineReduce(
        p, lambda d: gate_parts.at[d], gate_up_in, gate_down_in, *gate_sems
    )
    started = [
        pltpu.make_async_copy(gate_in, gate_parts, loads.at[0]),
        pltpu.make_async_copy(qkv.at[:, pl.ds(0, part)], q, loads.at[1]),
        pltpu.make_async_copy(
            qkv.at[:, pl.ds(part, part)], k_ext.at[pl.ds(WINDOW, count)], loads.at[2]
        ),
        pltpu.make_async_copy(
            qkv.at[:, pl.ds(2 * part, part)], v_ext.at[pl.ds(WINDOW, count)], loads.at[3]
        ),
        pltpu.make_async_copy(halo_kv.at[0], k_ext.at[pl.ds(0, WINDOW)], loads.at[4]),
        pltpu.make_async_copy(halo_kv.at[1], v_ext.at[pl.ds(0, WINDOW)], loads.at[5]),
        pltpu.make_async_copy(middle, total, loads.at[6]),
    ]
    halo = [
        remote(
            halo_out.at[i], halo_in.at[i], halo_send.at[i], halo_recv.at[i], (p.s - 1, p.h)
        )
        for i in range(2)
    ]
    order = (
        p.second + p.turn,
        p.across + p.turn,
        p.first,
        p.first + p.turn,
        p.across,
        p.core,
        p.h,
        p.second,
    )
    fetches = [
        pltpu.make_async_copy(rows_of(hidden, j), hidden_block.at[n % 2], stage.at[n % 2])
        for n, j in enumerate(order)
    ]
    copies = block_reduce(p, out, into, r_send, r_recv)

    def emit(n, target, *more):
        fetches[n].wait()
        if n + 1 < len(order):
            fetches[n + 1].start()

        @pl.loop(0, line)
        def _(d):
            cols = pl.ds(pl.multiple_of(d * slab, slab), slab)
            value = product(hidden_block[n % 2][:, 0 : w_down.shape[1]], w_down[d])
            for other in more:
                value = value + other[:, cols].astype(F32)
            target[:, cols] = value.astype(target.dtype)

    def tiles(first, last):
        @pl.loop(first, last)
        def _(tile):
            backward_tile(
                tile, q, k_ext, v_ext, k_t, floor, logs, inner, grad, key_sum, value_sum
            )

    for copy in started:
        copy.start()
    fetches[0].start()
    p.greet()
    started[0].wait()
    gate_reduce.start(0)
    clear_last(gate_reduce)
    emit(0, out.at[0])
    copies[0].start()
    emit(1, out.at[1])
    copies[1].start()
    copies[0].wait_recv()
    emit(2, out.at[2], into.at[0])
    copies[4].start()
    copies[0].wait_send()
    emit(3, out.at[0])
    copies[2].start()
    copies[1].wait_recv()
    emit(4, out.at[3], into.at[1])
    copies[5].start()
    copies[1].wait_send()
    emit(5, out.at[1])
    copies[3].start()
    for copy in started[1:]:
        copy.wait()
    gate_reduce.step(0)

    @pl.loop(0, (WINDOW + count) // TILE)
    def _(i):
        at = pl.ds(pl.multiple_of(i * TILE, TILE), TILE)
        k_t[:, at] = k_ext[at, :].T
        key_sum[at, :] = jnp.zeros((TILE, part), F32)
        value_sum[at, :] = jnp.zeros((TILE, part), F32)

    ahead = WINDOW // TILE
    last = count // TILE
    tiles(0, ahead)

    @pl.when(p.s > 0)
    def _():
        @pl.loop(0, ahead)
        def _(i):
            at = pl.ds(pl.multiple_of(i * TILE, TILE), TILE)
            halo_out[0, at, :] = (key_sum[at, :] * scale).astype(BF16)
            halo_out[1, at, :] = value_sum[at, :].astype(BF16)

        halo[0].start()
        halo[1].start()

    gate_reduce.step(1)
    tiles(ahead, ahead + 4)
    copies[3].wait_recv()
    emit(6, total, into.at[3], total)
    copies[2].wait_recv()
    copies[5].wait_recv()
    emit(7, out.at[4], into.at[2], into.at[5])
    copies[6].start()
    tiles(ahead + 4, last)

    @pl.when(p.s < line - 1)
    def _():
        halo[0].wait_recv()
        halo[1].wait_recv()

    @pl.loop(0, last)
    def _(i):
        here = pl.ds(pl.multiple_of(i * TILE, TILE), TILE)
        at = pl.ds(pl.multiple_of(i * TILE + WINDOW, TILE), TILE)
        key_value = key_sum[at, :] * scale
        value_value = value_sum[at, :]
        k_ext[here, :] = key_value.astype(BF16)
        v_ext[here, :] = value_value.astype(BF16)

    @pl.when(p.s < line - 1)
    def _():
        @pl.loop(0, ahead)
        def _(i):
            here = pl.ds(pl.multiple_of(i * TILE, TILE), TILE)
            near = pl.ds(pl.multiple_of(i * TILE + count, TILE), TILE)
            there = pl.ds(pl.multiple_of(i * TILE + count - WINDOW, TILE), TILE)
            k_ext[there, :] = (
                key_sum[near, :] * scale + halo_in[0, here, :].astype(F32)
            ).astype(BF16)
            v_ext[there, :] = (value_sum[near, :] + halo_in[1, here, :].astype(F32)).astype(BF16)

    save = [
        pltpu.make_async_copy(
            ref.at[pl.ds(0, count)], grads_out.at[:, pl.ds(i * part, part)], saves.at[i]
        )
        for i, ref in enumerate((q, k_ext, v_ext))
    ]
    for copy in save:
        copy.start()
    copies[4].wait_recv()
    copies[6].wait_recv()

    @pl.loop(0, line)
    def _(d):
        cols = pl.ds(pl.multiple_of(d * slab, slab), slab)
        value = total[:, cols] + into[4, :, cols].astype(F32) + into[6, :, cols].astype(F32)
        result[:, cols] = value.astype(BF16)

    gate_reduce.step(2)
    for first, stop in strips(gate_grad.shape[0], 128):
        gate_grad[first:stop, :] = gate_reduce.total(slice(first, stop))
    for i in range(2, 7):
        copies[i].wait_send()
    gate_reduce.finish()

    @pl.when(p.s > 0)
    def _():
        halo[0].wait_send()
        halo[1].wait_send()

    for copy in save:
        copy.wait()


def attend_back(line, qkv, halo_kv, floor, logs, grad, inner, hidden, w_down, middle, gate_parts):
    rows, width = middle.shape
    count = qkv.shape[0]
    part = qkv.shape[1] // 3
    units, slab = w_down.shape[1:]
    return pl.pallas_call(
        functools.partial(attend_back_kernel, line),
        out_shape=(
            jax.ShapeDtypeStruct((count, 3 * part), BF16),
            jax.ShapeDtypeStruct((rows, width), BF16),
            jax.ShapeDtypeStruct((units, slab), F32),
        ),
        in_specs=[any_spec()] * 2
        + [vmem_spec()] * 4
        + [any_spec(), vmem_spec(), any_spec(), any_spec()],
        out_specs=(any_spec(), vmem_spec(), vmem_spec()),
        scratch_shapes=[
            pltpu.VMEM((count, part), BF16),
            pltpu.VMEM((WINDOW + count, part), BF16),
            pltpu.VMEM((WINDOW + count, part), BF16),
            pltpu.VMEM((part, WINDOW + count), BF16),
            pltpu.VMEM((WINDOW + count, part), F32),
            pltpu.VMEM((WINDOW + count, part), F32),
            pltpu.VMEM((2, WINDOW, part), BF16),
            pltpu.VMEM((2, WINDOW, part), BF16),
            pltpu.VMEM((line, units, slab), BF16),
            pltpu.VMEM((line - 1, units, slab), BF16),
            pltpu.VMEM((line - 1, units, slab), BF16),
            pltpu.VMEM((5, rows, width), BF16),
            pltpu.VMEM((7, rows, width), BF16),
            pltpu.VMEM((rows, width), F32),
            pltpu.VMEM((2, rows, hidden.shape[1]), BF16),
            pltpu.SemaphoreType.DMA((7,)),
            pltpu.SemaphoreType.DMA((7,)),
            *line_sems(line),
            pltpu.SemaphoreType.DMA((7,)),
            pltpu.SemaphoreType.DMA((2,)),
            pltpu.SemaphoreType.DMA((2,)),
            pltpu.SemaphoreType.DMA((2,)),
            pltpu.SemaphoreType.DMA((3,)),
        ],
        compiler_params=pltpu.CompilerParams(
            collective_id=4, has_side_effects=True, vmem_limit_bytes=62 * MIB
        ),
        cost_estimate=pl.CostEstimate(
            flops=20 * 2**30, bytes_accessed=60 * MIB, transcendentals=0
        ),
    )(qkv, halo_kv, floor, logs, grad, inner, hidden, w_down, middle, gate_parts)


def finish_kernel(
    line,
    grads,
    weight,
    normed,
    tokens,
    gain,
    grad_middle,
    out_given,
    ffn_gain_part,
    input_grad,
    gain_sums,
    query_grad,
    key_grad,
    value_grad,
    out_grad,
    turned,
    strip,
    parts,
    parts_up_in,
    parts_down_in,
    out_parts,
    out_up_in,
    out_down_in,
    out,
    into,
    total,
    gain_line,
    gain_in,
    r_send,
    r_recv,
    *sems,
):
    p = Place(line)
    part_sems, out_sems, gain_sems = sems[0:4], sems[4:8], sems[8:12]
    loads, strip_sems, gain_send, gain_recv = sems[12:16]
    rows, width = tokens.shape
    slab = width // line
    part = query_grad.shape[1]
    part_reduce = LineReduce(p, lambda d: parts.at[d], parts_up_in, parts_down_in, *part_sems)
    out_reduce = LineReduce(p, lambda d: out_parts.at[d], out_up_in, out_down_in, *out_sems)
    started = [
        pltpu.make_async_copy(out_given, out_parts, loads.at[0]),
        pltpu.make_async_copy(grad_middle, input_grad, loads.at[1]),
    ]
    for copy in started:
        copy.start()
    p.greet()
    started[0].wait()
    out_reduce.start(0)
    for reduce in (part_reduce, out_reduce):
        clear_last(reduce)
    copies = block_reduce(p, out, into, r_send, r_recv)

    def emit(j, target, *more):
        at = pl.ds(pl.multiple_of(j * rows, rows), rows)

        @pl.loop(0, line)
        def _(d):
            cols = pl.ds(pl.multiple_of(d * slab, slab), slab)
            value = product_nt(grads[at, :], weight[cols, :])
            for other in more:
                value = value + other[:, cols].astype(F32)
            target[:, cols] = value.astype(target.dtype)

    emit(p.second + p.turn, out.at[0])
    copies[0].start()
    emit(p.across + p.turn, out.at[1])
    copies[1].start()
    copies[0].wait_recv()
    emit(p.first, out.at[2], into.at[0])
    copies[4].start()
    copies[0].wait_send()
    emit(p.first + p.turn, out.at[0])
    copies[2].start()
    copies[1].wait_recv()
    emit(p.across, out.at[3], into.at[1])
    copies[5].start()
    copies[1].wait_send()
    emit(p.core, out.at[1])
    copies[3].start()
    turn_rows(grads, turned)
    multiply = lambda *some: weight_product(
        lambda rows_in: product(turned[...], rows_in),
        normed,
        lambda d: parts.at[d],
        strip.at.__getitem__,
        strip.shape[2],
        strip_sems,
        p,
        *some,
    )
    out_reduce.step(0)
    multiply(0, 1)
    part_reduce.start(0)
    multiply(1, line)
    out_reduce.step(1)
    copies[3].wait_recv()
    emit(p.h, total, into.at[3])
    part_reduce.step(0)
    copies[2].wait_recv()
    copies[5].wait_recv()
    emit(p.second, out.at[4], into.at[2], into.at[5])
    copies[6].start()
    out_reduce.step(2)
    for first, last in strips(part, 128):
        out_grad[first:last, :] = out_reduce.total(slice(first, last))
    copies[4].wait_recv()
    part_reduce.step(1)
    copies[6].wait_recv()
    started[1].wait()
    gain_own = gain_line.at[p.s]
    gain_own[...] = jnp.zeros(gain_own.shape, F32)
    gain_own[1:2, :] = ffn_gain_part[...]
    step = 32

    @pl.loop(0, rows // step)
    def _(i):
        at = pl.ds(pl.multiple_of(i * step, step), step)
        grad = total[at] + into[4, at].astype(F32) + into[6, at].astype(F32)
        unit, inverse = normalize(tokens[at].astype(F32))
        gain_own[0:1, :] += jnp.sum(grad * unit, axis=0, keepdims=True)
        input_grad[at] += norm_back(unit, inverse, gain[...], grad)

    for i, head in enumerate((p.core, p.first, p.second)):
        copy = remote(gain_own, gain_in.at[i], gain_send.at[i], gain_recv.at[i], p.at(head))
        copy.start()
        copy.wait()
        gain_own[...] += gain_in[i]
    gain_gather = LineGather(p, lambda d: gain_line.at[d], *gain_sems)
    gain_gather.start(0)
    for t in range(line - 1):
        gain_gather.step(t)
    summed = gain_line[0]
    for d in range(1, line):
        summed = summed + gain_line[d]
    gain_sums[...] = summed
    part_reduce.step(2)
    for i, target in enumerate((query_grad, key_grad, value_grad)):
        for first, last in strips(part, 128):
            target[:, first:last] = part_reduce.total(
                slice(i * part + first, i * part + last)
            ).T
    for i in range(2, 7):
        copies[i].wait_send()
    gain_gather.finish()
    for reduce in (part_reduce, out_reduce):
        reduce.finish()


def finish(line, grads, weight, normed, tokens, gain, grad_middle, out_parts, ffn_gain_part):
    rows, width = tokens.shape
    full = grads.shape[0]
    part = grads.shape[1] // 3
    slab = width // line
    return pl.pallas_call(
        functools.partial(finish_kernel, line),
        out_shape=(
            jax.ShapeDtypeStruct((rows, width), F32),
            jax.ShapeDtypeStruct((8, width), F32),
            jax.ShapeDtypeStruct((slab, part), F32),
            jax.ShapeDtypeStruct((slab, part), F32),
            jax.ShapeDtypeStruct((slab, part), F32),
            jax.ShapeDtypeStruct((part, slab), F32),
        ),
        in_specs=[
            vmem_spec(),
            vmem_spec(),
            any_spec(),
            vmem_spec(),
            vmem_spec(),
            any_spec(),
            any_spec(),
            vmem_spec(),
        ],
        out_specs=(vmem_spec(),) * 6,
        scratch_shapes=[
            pltpu.VMEM((3 * part, full), BF16),
            pltpu.VMEM((2, full, 256), BF16),
            pltpu.VMEM((line, 3 * part, slab), BF16),
            pltpu.VMEM((line - 1, 3 * part, slab), BF16),
            pltpu.VMEM((line - 1, 3 * part, slab), BF16),
            pltpu.VMEM((line, part, slab), BF16),
            pltpu.VMEM((line - 1, part, slab), BF16),
            pltpu.VMEM((line - 1, part, slab), BF16),
            pltpu.VMEM((5, rows, width), BF16),
            pltpu.VMEM((7, rows, width), BF16),
            pltpu.VMEM((rows, width), F32),
            pltpu.VMEM((line, 8, width), F32),
            pltpu.VMEM((3, 8, width), F32),
            pltpu.SemaphoreType.DMA((7,)),
            pltpu.SemaphoreType.DMA((7,)),
            *line_sems(line, 3),
            pltpu.SemaphoreType.DMA((2,)),
            pltpu.SemaphoreType.DMA((2,)),
            pltpu.SemaphoreType.DMA((3,)),
            pltpu.SemaphoreType.DMA((3,)),
        ],
        compiler_params=pltpu.CompilerParams(
            collective_id=5, has_side_effects=True, vmem_limit_bytes=62 * MIB
        ),
        cost_estimate=pl.CostEstimate(
            flops=20 * 2**30, bytes_accessed=60 * MIB, transcendentals=0
        ),
    )(
        grads,
        weight,
        normed,
        tokens,
        gain.reshape(1, width),
        grad_middle,
        out_parts,
        ffn_gain_part,
    )


def deliver_kernel(count, *refs):
    sources, targets, held = refs[:count], refs[count : 2 * count], refs[2 * count : 3 * count]
    sems = refs[3 * count]
    loads = [
        pltpu.make_async_copy(source, keep, sems.at[i])
        for i, (source, keep) in enumerate(zip(sources, held))
    ]
    stores = [
        pltpu.make_async_copy(keep, target, sems.at[count + i])
        for i, (keep, target) in enumerate(zip(held, targets))
    ]
    for copy in loads:
        copy.start()
    for load, store in zip(loads, stores):
        load.wait()
        store.start()
    for copy in stores:
        copy.wait()


def deliver(*arrays):
    count = len(arrays)
    return pl.pallas_call(
        functools.partial(deliver_kernel, count),
        out_shape=tuple(jax.ShapeDtypeStruct(a.shape, a.dtype) for a in arrays),
        in_specs=[any_spec()] * count,
        out_specs=(any_spec(),) * count,
        scratch_shapes=[pltpu.VMEM(a.shape, a.dtype) for a in arrays]
        + [pltpu.SemaphoreType.DMA((2 * count,))],
        compiler_params=pltpu.CompilerParams(vmem_limit_bytes=62 * MIB),
    )(*arrays)


def fused(
    tokens,
    segment,
    attn_gain,
    query_weight,
    key_weight,
    value_weight,
    out_weight,
    ffn_gain,
    gate_weight,
    up_weight,
    down_weight,
    cotangent,
):
    line = lax.axis_size("seq")
    (
        normed_one,
        qkv,
        w_qkv,
        floor,
        attended,
        logs,
        halo_kv,
        cot_full,
        w_out,
        w_gate,
        w_up,
        middle,
    ) = forward(
        line,
        tokens,
        attn_gain,
        query_weight,
        key_weight,
        value_weight,
        segment,
        cotangent,
        out_weight,
        gate_weight.T,
        up_weight.T,
    )
    normed_two, hidden, grad_gate, grad_up, grad_normed_two, w_down, down_grad = feed(
        line, middle, ffn_gain, cot_full, w_gate, w_up, down_weight
    )
    grad_middle, ffn_gain_part, grad_attended, inner, up_grad, gate_parts, out_parts = give_back(
        line,
        grad_normed_two,
        middle,
        cotangent,
        ffn_gain,
        attended,
        w_out,
        grad_gate,
        grad_up,
        normed_two,
    )
    grads, result, gate_grad = attend_back(
        line, qkv, halo_kv, floor, logs, grad_attended, inner, hidden, w_down, middle, gate_parts
    )
    input_grad, gain_sums, query_grad, key_grad, value_grad, out_grad = finish(
        line,
        grads,
        w_qkv,
        normed_one,
        tokens,
        attn_gain,
        grad_middle,
        out_parts,
        ffn_gain_part,
    )
    (
        result,
        input_grad,
        query_grad,
        key_grad,
        value_grad,
        out_grad,
        gate_grad,
        up_grad,
        down_grad,
    ) = deliver(
        result,
        input_grad,
        query_grad,
        key_grad,
        value_grad,
        out_grad,
        gate_grad,
        up_grad,
        down_grad,
    )
    share = tokens.shape[1] // (line * lax.axis_size("head"))
    place = (lax.axis_index("seq") * lax.axis_size("head") + lax.axis_index("head")) * share
    gain_grads = lax.dynamic_slice(gain_sums, (0, place), (2, share))
    return (
        result,
        input_grad,
        gain_grads[0],
        query_grad,
        key_grad,
        value_grad,
        out_grad,
        gain_grads[1],
        gate_grad.T,
        up_grad.T,
        down_grad,
    )


def solution(mesh):
    placed = (
        P(("seq", "head"), None),
        P("seq"),
        P(),
        P("seq", "head"),
        P("seq", "head"),
        P("seq", "head"),
        P("head", "seq"),
        P(),
        P("seq", "head"),
        P("seq", "head"),
        P("head", "seq"),
        P(("seq", "head"), None),
    )
    body = fused if mesh.shape["head"] == 8 else local
    return jax.shard_map(
        body,
        mesh=mesh,
        in_specs=placed,
        out_specs=(
            P(("seq", "head"), None),
            P(("seq", "head"), None),
            P(("seq", "head")),
            P("seq", "head"),
            P("seq", "head"),
            P("seq", "head"),
            P("head", "seq"),
            P(("seq", "head")),
            P("seq", "head"),
            P("seq", "head"),
            P("head", "seq"),
        ),
        check_vma=False,
    )
```

```python
import functools

import jax
import jax.numpy as jnp
from jax import lax
from jax.experimental import pallas as pl
from jax.experimental.pallas import tpu as pltpu
from jax.sharding import PartitionSpec as P

HEAD_DIM = 128
WINDOW = 1024


EPS = 1e-06
NEG = -1e30


def from_behind(value, axis, by):
    count = lax.axis_size(axis)
    pairs = [(i, i + by) for i in range(count) if 0 <= i + by < count]
    return lax.ppermute(value, axis, pairs)


def product(left, right):
    return jnp.dot(left, right, preferred_element_type=jnp.float32)


def product_tn(left, right):
    return lax.dot_general(
        left, right, (((0,), (0,)), ((), ())), preferred_element_type=jnp.float32
    )


def product_nt(left, right):
    return lax.dot_general(
        left, right, (((1,), (1,)), ((), ())), preferred_element_type=jnp.float32
    )


def normalize(rows):
    inverse = lax.rsqrt(jnp.mean(rows * rows, axis=-1, keepdims=True) + EPS)
    return (rows * inverse, inverse)


def norm_back(unit, inverse, gain, grad):
    scaled = grad * gain
    return inverse * (scaled - unit * jnp.mean(scaled * unit, axis=-1, keepdims=True))


def gather_rows(rows):
    return lax.all_gather(rows, "head", axis=0, tiled=True)


def block_scores(query_heads, key_heads, seg_query, seg_keys, valid, start, block):
    query_part = query_heads[start : start + block]
    key_part = key_heads[start : start + block + WINDOW]
    scores = jnp.einsum(
        "qhd,khd->hqk", query_part, key_part, preferred_element_type=jnp.float32
    ) * HEAD_DIM ** (-0.5)
    rows = jnp.arange(block)[:, None] + WINDOW
    cols = jnp.arange(block + WINDOW)[None, :]
    distance = rows - cols
    same_doc = (
        seg_query[start : start + block][:, None]
        == seg_keys[start : start + block + WINDOW][None, :]
    )
    visible = (
        (distance >= 0)
        & (distance <= WINDOW)
        & same_doc
        & valid[start : start + block + WINDOW][None, :]
    )
    return jnp.where(visible[None], scores, NEG)


def local(
    tokens,
    segment,
    attn_gain,
    query_weight,
    key_weight,
    value_weight,
    out_weight,
    ffn_gain,
    gate_weight,
    up_weight,
    down_weight,
    cotangent,
):
    own_rows = tokens.shape[0]
    group = own_rows * lax.axis_size("head")
    heads_here = query_weight.shape[1] // HEAD_DIM
    offset = lax.axis_index("head") * own_rows
    seq_index = lax.axis_index("seq")
    block = min(512, group)
    scale = HEAD_DIM ** (-0.5)
    w_query, w_key, w_value, w_out, w_gate, w_up, w_down = (
        lax.all_gather(query_weight, "seq", axis=0, tiled=True),
        lax.all_gather(key_weight, "seq", axis=0, tiled=True),
        lax.all_gather(value_weight, "seq", axis=0, tiled=True),
        lax.all_gather(out_weight, "seq", axis=1, tiled=True),
        lax.all_gather(gate_weight, "seq", axis=0, tiled=True),
        lax.all_gather(up_weight, "seq", axis=0, tiled=True),
        lax.all_gather(down_weight, "seq", axis=1, tiled=True),
    )
    inputs = tokens.astype(jnp.float32)
    unit_one, inverse_one = normalize(inputs)
    normed_full = gather_rows((unit_one * attn_gain).astype(jnp.bfloat16))
    queries = product(normed_full, w_query).astype(jnp.bfloat16)
    keys = product(normed_full, w_key).astype(jnp.bfloat16)
    values = product(normed_full, w_value).astype(jnp.bfloat16)
    halo_keys, halo_values, halo_segs = ([], [], [])
    hop = 1
    take = min(group, WINDOW - (hop - 1) * group)
    got_keys, got_values, got_segs = from_behind(
        (keys[group - take :], values[group - take :], segment[group - take :]), "seq", hop
    )
    halo_keys.append(got_keys)
    halo_values.append(got_values)
    halo_segs.append(got_segs)
    keys_ext = jnp.concatenate(halo_keys + [keys], axis=0)
    values_ext = jnp.concatenate(halo_values + [values], axis=0)
    segs_ext = jnp.concatenate(halo_segs + [segment], axis=0)
    positions = seq_index * group - WINDOW + jnp.arange(WINDOW + group)
    valid = positions >= 0
    query_heads = queries.reshape(group, heads_here, HEAD_DIM)
    key_heads = keys_ext.reshape(WINDOW + group, heads_here, HEAD_DIM)
    value_heads = values_ext.reshape(WINDOW + group, heads_here, HEAD_DIM)
    outputs, logsums = ([], [])
    for start in range(0, group, block):
        scores = block_scores(query_heads, key_heads, segment, segs_ext, valid, start, block)
        highest = jnp.max(scores, axis=-1, keepdims=True)
        weights = jnp.exp(scores - highest)
        total = jnp.sum(weights, axis=-1, keepdims=True)
        probs = (weights / total).astype(jnp.bfloat16)
        outputs.append(
            jnp.einsum(
                "hqk,khd->qhd",
                probs,
                value_heads[start : start + block + WINDOW],
                preferred_element_type=jnp.float32,
            )
        )
        logsums.append(highest + jnp.log(total))
    attended = (
        jnp.concatenate(outputs, axis=0).reshape(group, heads_here * HEAD_DIM).astype(jnp.bfloat16)
    )
    partial_out = product(attended, w_out)
    own_part = lax.dynamic_slice_in_dim(partial_out, offset, own_rows, 0)
    placed = lax.dynamic_update_slice_in_dim(partial_out, own_part + inputs, offset, 0)
    middle_full = lax.psum(placed, "head")
    middle = lax.dynamic_slice_in_dim(middle_full, offset, own_rows, 0)
    unit_full, inverse_full = normalize(middle_full)
    normed_two_full = (unit_full * ffn_gain).astype(jnp.bfloat16)
    unit_two, inverse_two = normalize(middle)
    gate = product(normed_two_full, w_gate)
    up = product(normed_two_full, w_up)
    sigmoid = jax.nn.sigmoid(gate)
    activated = gate * sigmoid
    hidden = (activated * up).astype(jnp.bfloat16)
    ffn_out = lax.psum_scatter(
        product(hidden, w_down).astype(jnp.bfloat16), "head", scatter_dimension=0, tiled=True
    ).astype(jnp.float32)
    result = middle + ffn_out
    grad_out = lax.all_gather(cotangent, "head", axis=0, tiled=True)
    grad_hidden = product_nt(grad_out, w_down)
    grad_gate = (grad_hidden * up * sigmoid * (1.0 + gate * (1.0 - sigmoid))).astype(jnp.bfloat16)
    grad_up = (grad_hidden * activated).astype(jnp.bfloat16)
    down_grad = product_tn(hidden, grad_out)
    gate_grad = product_tn(normed_two_full, grad_gate)
    up_grad = product_tn(normed_two_full, grad_up)
    grad_normed_two = lax.psum_scatter(
        (product_nt(grad_gate, w_gate) + product_nt(grad_up, w_up)).astype(jnp.bfloat16),
        "head",
        scatter_dimension=0,
        tiled=True,
    ).astype(jnp.float32)
    ffn_gain_part = jnp.sum(grad_normed_two * unit_two, axis=0)
    grad_middle = cotangent.astype(jnp.float32) + norm_back(
        unit_two, inverse_two, ffn_gain, grad_normed_two
    )
    grad_branch = lax.all_gather(grad_middle.astype(jnp.bfloat16), "head", axis=0, tiled=True)
    out_grad = product_tn(attended, grad_branch)
    grad_attended = product_nt(grad_branch, w_out).astype(jnp.bfloat16)
    grad_heads = grad_attended.reshape(group, heads_here, HEAD_DIM)
    grad_query_list = []
    grad_keys_ext = jnp.zeros((WINDOW + group, heads_here, HEAD_DIM), jnp.float32)
    grad_values_ext = jnp.zeros((WINDOW + group, heads_here, HEAD_DIM), jnp.float32)
    for number, start in enumerate(range(0, group, block)):
        scores = block_scores(query_heads, key_heads, segment, segs_ext, valid, start, block)
        probs = jnp.exp(scores - logsums[number])
        probs_low = probs.astype(jnp.bfloat16)
        key_part = key_heads[start : start + block + WINDOW]
        value_part = value_heads[start : start + block + WINDOW]
        query_part = query_heads[start : start + block]
        grad_part = grad_heads[start : start + block]
        grad_probs = jnp.einsum(
            "qhd,khd->hqk", grad_part, value_part, preferred_element_type=jnp.float32
        )
        inner = jnp.sum(probs * grad_probs, axis=-1, keepdims=True)
        grad_scores = (probs * (grad_probs - inner)).astype(jnp.bfloat16)
        grad_query_list.append(
            jnp.einsum("hqk,khd->qhd", grad_scores, key_part, preferred_element_type=jnp.float32)
            * scale
        )
        key_term = (
            jnp.einsum("hqk,qhd->khd", grad_scores, query_part, preferred_element_type=jnp.float32)
            * scale
        )
        value_term = jnp.einsum(
            "hqk,qhd->khd", probs_low, grad_part, preferred_element_type=jnp.float32
        )
        grad_keys_ext = grad_keys_ext.at[start : start + block + WINDOW].add(key_term)
        grad_values_ext = grad_values_ext.at[start : start + block + WINDOW].add(value_term)
    grad_keys_ext = grad_keys_ext.reshape(WINDOW + group, heads_here * HEAD_DIM)
    grad_values_ext = grad_values_ext.reshape(WINDOW + group, heads_here * HEAD_DIM)
    grad_keys = grad_keys_ext[WINDOW:]
    grad_values = grad_values_ext[WINDOW:]
    cursor = 0
    hop = 1
    take = min(group, WINDOW - (hop - 1) * group)
    back_keys = from_behind(
        grad_keys_ext[cursor : cursor + take].astype(jnp.bfloat16), "seq", -hop
    ).astype(jnp.float32)
    back_values = from_behind(
        grad_values_ext[cursor : cursor + take].astype(jnp.bfloat16), "seq", -hop
    ).astype(jnp.float32)
    grad_keys = grad_keys.at[group - take :].add(back_keys)
    grad_values = grad_values.at[group - take :].add(back_values)
    grad_queries = (
        jnp.concatenate(grad_query_list, axis=0)
        .reshape(group, heads_here * HEAD_DIM)
        .astype(jnp.bfloat16)
    )
    grad_keys = grad_keys.astype(jnp.bfloat16)
    grad_values = grad_values.astype(jnp.bfloat16)
    query_grad = product_tn(normed_full, grad_queries)
    key_grad = product_tn(normed_full, grad_keys)
    value_grad = product_tn(normed_full, grad_values)
    grad_normed_one = lax.psum_scatter(
        (
            product_nt(grad_queries, w_query)
            + product_nt(grad_keys, w_key)
            + product_nt(grad_values, w_value)
        ).astype(jnp.bfloat16),
        "head",
        scatter_dimension=0,
        tiled=True,
    ).astype(jnp.float32)
    attn_gain_part = jnp.sum(grad_normed_one * unit_one, axis=0)
    input_grad = grad_middle + norm_back(unit_one, inverse_one, attn_gain, grad_normed_one)
    summed = (
        lax.psum_scatter(
            query_grad.astype(jnp.bfloat16), "seq", scatter_dimension=0, tiled=True
        ).astype(jnp.float32),
        lax.psum_scatter(
            key_grad.astype(jnp.bfloat16), "seq", scatter_dimension=0, tiled=True
        ).astype(jnp.float32),
        lax.psum_scatter(
            value_grad.astype(jnp.bfloat16), "seq", scatter_dimension=0, tiled=True
        ).astype(jnp.float32),
        lax.psum_scatter(
            out_grad.astype(jnp.bfloat16), "seq", scatter_dimension=1, tiled=True
        ).astype(jnp.float32),
        lax.psum_scatter(
            gate_grad.astype(jnp.bfloat16), "seq", scatter_dimension=0, tiled=True
        ).astype(jnp.float32),
        lax.psum_scatter(
            up_grad.astype(jnp.bfloat16), "seq", scatter_dimension=0, tiled=True
        ).astype(jnp.float32),
        lax.psum_scatter(
            down_grad.astype(jnp.bfloat16), "seq", scatter_dimension=1, tiled=True
        ).astype(jnp.float32),
    )
    gain_grads = (
        lax.psum_scatter(attn_gain_part, ("seq", "head"), scatter_dimension=0, tiled=True),
        lax.psum_scatter(ffn_gain_part, ("seq", "head"), scatter_dimension=0, tiled=True),
    )
    return (
        result.astype(jnp.bfloat16),
        input_grad,
        gain_grads[0],
        summed[0],
        summed[1],
        summed[2],
        summed[3],
        gain_grads[1],
        summed[4],
        summed[5],
        summed[6],
    )


MESH = pl.DeviceIdType.MESH
BF16 = jnp.bfloat16
F32 = jnp.float32
MIB = 2**20


def remote(src, dst, send_sem, recv_sem, where):
    return pltpu.make_async_remote_copy(
        src_ref=src,
        dst_ref=dst,
        send_sem=send_sem,
        recv_sem=recv_sem,
        device_id=where,
        device_id_type=MESH,
    )


class Place:
    def __init__(self, line):
        s, h = lax.axis_index("seq"), lax.axis_index("head")
        core = lax.rem(h, 2)
        x = lax.rem(lax.div(h, 2), 2)
        y = lax.div(h, 4)
        self.s, self.h, self.line = s, h, line
        self.turn = 1 - 2 * core
        self.core = h + self.turn
        over_x, over_y = 2 - 4 * x, 4 - 8 * y
        self.first = h + over_x * (1 - core) + over_y * core
        self.second = h + over_y * (1 - core) + over_x * core
        self.across = h + over_x + over_y

    def at(self, head):
        return (self.s, head)

    def greet(self, along_seq=True):
        barrier = pltpu.get_barrier_semaphore()
        for head in (self.core, self.first, self.second):
            pl.semaphore_signal(barrier, inc=1, device_id=self.at(head), device_id_type=MESH)
        if along_seq:

            @pl.when(self.s > 0)
            def _():
                pl.semaphore_signal(
                    barrier, inc=1, device_id=(self.s - 1, self.h), device_id_type=MESH
                )

            @pl.when(self.s < self.line - 1)
            def _():
                pl.semaphore_signal(
                    barrier, inc=1, device_id=(self.s + 1, self.h), device_id_type=MESH
                )

            @pl.when((self.s > 0) & (self.s < self.line - 1))
            def _():
                pl.semaphore_wait(barrier, 5)

            @pl.when((self.s == 0) | (self.s == self.line - 1))
            def _():
                pl.semaphore_wait(barrier, 4)
        else:
            pl.semaphore_wait(barrier, 3)


def greet_line(place):
    p = place
    barrier = pltpu.get_barrier_semaphore()
    for head in (p.core, p.first, p.second):
        pl.semaphore_signal(barrier, inc=1, device_id=p.at(head), device_id_type=MESH)
    for k in range(1, p.line):
        pl.semaphore_signal(
            barrier, inc=1, device_id=(lax.rem(p.s + k, p.line), p.h), device_id_type=MESH
        )
    pl.semaphore_wait(barrier, 2 + p.line)


class HeadGather:
    SEMS = 7

    def __init__(self, place, block, send, recv, own=None):
        p = place
        self.p = p
        plan = (
            (p.h, p.first, p.first),
            (p.h, p.second, p.second),
            (p.h, p.core, p.core),
            (p.first, p.second, p.across),
            (p.first, p.core, p.second + p.turn),
            (p.second, p.core, p.first + p.turn),
            (p.across, p.core, p.across + p.turn),
        )
        self.out = [
            remote(
                block(j) if own is None or i > 2 else own,
                block(j),
                send.at[i],
                recv.at[i],
                p.at(to),
            )
            for i, (j, to, _) in enumerate(plan)
        ]
        self.come = [
            remote(block(j), block(j), send.at[i], recv.at[i], p.at(to))
            for i, (_, to, j) in enumerate(plan)
        ]

    def start(self):
        for i in (0, 1, 2):
            self.out[i].start()

    def got_first(self):
        self.come[0].wait_recv()
        self.out[3].start()
        self.out[4].start()

    def got_second(self):
        self.come[1].wait_recv()
        self.out[5].start()

    def got_across(self):
        self.come[3].wait_recv()
        self.out[6].start()

    def got_core(self):
        self.come[2].wait_recv()

    def got_core_second(self):
        self.come[4].wait_recv()

    def got_core_first(self):
        self.come[5].wait_recv()

    def got_core_across(self):
        self.come[6].wait_recv()

    def finish(self):
        for copy in self.out:
            copy.wait_send()


class LineGather:
    def __init__(self, place, piece, up_send, up_recv, down_send, down_recv, own=None):
        self.p, self.piece, self.own = place, piece, own
        self.up = (up_send, up_recv)
        self.down = (down_send, down_recv)

    def _up(self, owner, t):
        p = self.p
        source = self.own if t == 0 and self.own is not None else self.piece(owner)
        return remote(
            source, self.piece(owner), self.up[0].at[t], self.up[1].at[t], (p.s + 1, p.h)
        )

    def _down(self, owner, t):
        p = self.p
        source = self.own if t == 0 and self.own is not None else self.piece(owner)
        return remote(
            source,
            self.piece(owner),
            self.down[0].at[t],
            self.down[1].at[t],
            (p.s - 1, p.h),
        )

    def start(self, t):
        p = self.p

        @pl.when((p.s < p.line - 1) & (p.s >= t))
        def _():
            self._up(p.s - t, t).start()

        @pl.when((p.s > 0) & (p.s + t < p.line))
        def _():
            self._down(p.s + t, t).start()

    def got(self, t):
        p = self.p

        @pl.when(p.s >= t + 1)
        def _():
            self._up(p.s - 1 - t, t).wait_recv()

        @pl.when(p.s + 1 + t < p.line)
        def _():
            self._down(p.s + 1 + t, t).wait_recv()

    def step(self, t):
        self.got(t)
        if t + 1 < self.p.line - 1:
            self.start(t + 1)

    def finish(self):
        p = self.p
        for t in range(p.line - 1):

            @pl.when((p.s < p.line - 1) & (p.s >= t))
            def _():
                self._up(p.s - t, t).wait_send()

            @pl.when((p.s > 0) & (p.s + t < p.line))
            def _():
                self._down(p.s + t, t).wait_send()


def line_sems(line, tensors=1):
    return [pltpu.SemaphoreType.DMA((line - 1,)) for _ in range(4 * tensors)]


def norm_rows(rows, gain):
    inverse = lax.rsqrt(jnp.mean(rows * rows, axis=-1, keepdims=True) + EPS)
    return rows * inverse * gain


def own_starts(segment):
    count = segment.shape[1]
    ids = segment[...]
    place = lax.broadcasted_iota(jnp.int32, (1, count), 1)
    starts = jnp.where((place > 0) & (ids != pltpu.roll(ids, 1, 1)), place, -1)
    shift = 1
    while shift < count:
        earlier = jnp.where(place >= shift, pltpu.roll(starts, shift, 1), -1)
        starts = jnp.maximum(starts, earlier)
        shift *= 2
    return starts


def any_spec():
    return pl.BlockSpec(memory_space=pl.ANY)


def vmem_spec():
    return pl.BlockSpec(memory_space=pltpu.VMEM)


LOG2E = 1.4426950408889634
TILE = 256
CHUNKS = WINDOW // TILE + 1


def tile_scores(tile, head, q, k_ext, floor):
    start = pl.multiple_of(tile * TILE, TILE)
    cols = slice(head * HEAD_DIM, (head + 1) * HEAD_DIM)
    queries = q[pl.ds(start, TILE), cols]
    row = lax.broadcasted_iota(jnp.int32, (TILE, TILE), 0)
    lane = lax.broadcasted_iota(jnp.int32, (TILE, TILE), 1)
    lowest = floor[:, pl.ds(start, TILE)] - start
    found = []
    for i in range(CHUNKS):
        keys = k_ext[pl.ds(start + i * TILE, TILE), cols]
        scores = product_nt(keys, queries)
        visible = row >= lowest - i * TILE
        if i == CHUNKS - 1:
            visible = visible & (row <= lane)
        found.append((scores, visible))
    return found


def forward_tile(tile, q, k_ext, v_t, floor, attended, logs):
    start = pl.multiple_of(tile * TILE, TILE)
    sharp = HEAD_DIM ** (-0.5) * LOG2E
    for head in range(q.shape[1] // HEAD_DIM):
        cols = slice(head * HEAD_DIM, (head + 1) * HEAD_DIM)
        found = [
            jnp.where(visible, scores, NEG)
            for scores, visible in tile_scores(tile, head, q, k_ext, floor)
        ]
        highest = functools.reduce(
            jnp.maximum, [jnp.max(scores, axis=0, keepdims=True) for scores in found]
        )
        total = jnp.zeros((1, TILE), F32)
        mixed = jnp.zeros((HEAD_DIM, TILE), F32)
        for i, scores in enumerate(found):
            weights = jnp.exp2((scores - highest) * sharp)
            total = total + jnp.sum(weights, axis=0, keepdims=True)
            mixed = mixed + product(
                v_t[cols, pl.ds(start + i * TILE, TILE)], weights.astype(BF16)
            )
        attended[pl.ds(start, TILE), cols] = (mixed / total).astype(BF16).T
        logs[head : head + 1, pl.ds(start, TILE)] = highest * sharp + jnp.log2(total)


def block_reduce(place, out, into, r_send, r_recv):
    p = place
    goes = (p.core, p.core, p.core, p.core, p.first, p.first, p.second)
    slots = (0, 1, 0, 1, 2, 3, 4)
    return [
        remote(out.at[slots[i]], into.at[i], r_send.at[i], r_recv.at[i], p.at(to))
        for i, to in enumerate(goes)
    ]


def forward_kernel(
    line,
    tokens,
    gain,
    wq,
    wk,
    wv,
    segment,
    cot,
    w_out,
    w_gate,
    w_up,
    normed_out,
    qkv_out,
    weight_out,
    floor,
    attended,
    logs,
    halo_out,
    cot_out,
    w_out_out,
    gate_full,
    up_full,
    middle,
    normed,
    weight,
    q,
    k_ext,
    v_ext,
    v_t,
    w_out_full,
    seg_halo,
    out,
    into,
    g_send,
    g_recv,
    c_send,
    c_recv,
    r_send,
    r_recv,
    halo_send,
    halo_recv,
    seg_sems,
    keep,
    *sems,
):
    p = Place(line)
    qkv_sems, out_sems, gate_sems, up_sems = sems[0:4], sems[4:8], sems[8:12], sems[12:16]
    rows, width = tokens.shape
    slab, part = wq.shape
    count = segment.shape[1]
    rows_of = lambda ref, j: ref.at[pl.ds(pl.multiple_of(j * rows, rows), rows)]
    slab_of = lambda d: weight.at[pl.ds(pl.multiple_of(d * slab, slab), slab)]
    weight_own = slab_of(p.s)
    weight_own[:, 0:part] = wq[...]
    weight_own[:, part : 2 * part] = wk[...]
    weight_own[:, 2 * part : 3 * part] = wv[...]
    seg_copy = remote(
        segment.at[:, pl.ds(count - WINDOW, WINDOW)],
        seg_halo,
        seg_sems.at[0],
        seg_sems.at[1],
        (p.s + 1, p.h),
    )
    halo = [
        remote(
            ext.at[pl.ds(count, WINDOW)],
            ext.at[pl.ds(0, WINDOW)],
            halo_send.at[i],
            halo_recv.at[i],
            (p.s + 1, p.h),
        )
        for i, ext in enumerate((k_ext, v_ext))
    ]
    gather = HeadGather(p, lambda j: rows_of(normed, j), g_send, g_recv)
    cot_gather = HeadGather(p, lambda j: rows_of(cot_out, j), c_send, c_recv, own=cot)
    qkv_gather = LineGather(p, slab_of, *qkv_sems)
    out_gather = LineGather(p, lambda d: w_out_full.at[d], *out_sems, own=w_out)
    gate_gather = LineGather(p, lambda d: gate_full.at[d], *gate_sems, own=w_gate)
    up_gather = LineGather(p, lambda d: up_full.at[d], *up_sems, own=w_up)
    p.greet()
    qkv_gather.start(0)

    @pl.when(p.s < line - 1)
    def _():
        seg_copy.start()

    mine = rows_of(normed, p.h)
    step = 32

    @pl.loop(0, rows // step)
    def _(i):
        at = pl.ds(pl.multiple_of(i * step, step), step)
        mine[at] = norm_rows(tokens[at].astype(F32), gain[...]).astype(BF16)

    gather.start()
    saved = []

    def save(source, target):
        copy = pltpu.make_async_copy(source, target, keep.at[len(saved)])
        copy.start()
        saved.append(copy)

    def save_block(j):
        save(rows_of(normed, j), rows_of(normed_out, j))

    save_block(p.h)
    save(cot, rows_of(cot_out, p.h))
    save(w_out, w_out_full.at[p.s])
    own_w_out = saved[-1]
    save(w_gate, gate_full.at[p.s])
    save(w_up, up_full.at[p.s])
    starts = own_starts(segment)

    @pl.when(p.s == 0)
    def _():
        k_ext[0:WINDOW, :] = jnp.zeros((WINDOW, part), BF16)
        v_ext[0:WINDOW, :] = jnp.zeros((WINDOW, part), BF16)

    @pl.when(p.s > 0)
    def _():
        seg_copy.wait_recv()

    before = jnp.sum(
        (seg_halo[...] == segment[:, 0:1]).astype(jnp.int32), axis=1, keepdims=True
    )
    before = jnp.where(p.s > 0, before, 0)
    floor[...] = jnp.maximum(
        lax.broadcasted_iota(jnp.int32, (1, count), 1),
        jnp.where(starts >= 0, starts + WINDOW, WINDOW - before),
    )
    gather.got_core()
    save_block(p.core)
    qkv_gather.step(0)
    gather.got_first()
    gather.got_second()
    cot_gather.start()
    save_block(p.first)
    save_block(p.second)
    qkv_gather.step(1)
    out_gather.start(0)
    gather.got_core_second()
    gather.got_core_first()
    save_block(p.second + p.turn)
    save_block(p.first + p.turn)
    qkv_gather.step(2)
    gather.got_across()
    save_block(p.across)
    gather.got_core_across()
    save_block(p.across + p.turn)
    save(weight, weight_out)

    def multiply(first, last):
        @pl.loop(first, last)
        def _(n):
            start = pl.multiple_of((count // rows - 1 - n) * rows, rows)
            value = product(normed[pl.ds(start, rows), :], weight[...]).astype(BF16)
            q[pl.ds(start, rows), :] = value[:, 0:part]
            k_ext[pl.ds(start + WINDOW, rows), :] = value[:, part : 2 * part]
            v_ext[pl.ds(start + WINDOW, rows), :] = value[:, 2 * part : 3 * part]

    late = (WINDOW + rows - 1) // rows
    multiply(0, late)

    @pl.when(p.s < line - 1)
    def _():
        halo[0].start()
        halo[1].start()

    multiply(late, count // rows)
    multiply(late, count // rows)
    out_gather.step(0)
    gate_gather.start(0)
    save(q, qkv_out.at[:, pl.ds(0, part)])
    save(k_ext.at[pl.ds(WINDOW, count)], qkv_out.at[:, pl.ds(part, part)])
    save(v_ext.at[pl.ds(WINDOW, count)], qkv_out.at[:, pl.ds(2 * part, part)])

    def turn(first, last):
        @pl.loop(first, last)
        def _(i):
            at = pl.ds(pl.multiple_of(i * TILE, TILE), TILE)
            v_t[:, at] = v_ext[at, :].T

    def tiles(first, last):
        @pl.loop(first, last)
        def _(tile):
            forward_tile(tile, q, k_ext, v_t, floor, attended, logs)

    ahead = WINDOW // TILE
    turn(ahead, ahead + count // TILE)
    tiles(ahead, ahead + 5)
    cot_gather.got_core()
    cot_gather.got_first()
    cot_gather.got_second()
    out_gather.step(1)
    up_gather.start(0)
    tiles(ahead + 5, count // TILE)

    @pl.when(p.s > 0)
    def _():
        halo[0].wait_recv()
        halo[1].wait_recv()

    turn(0, ahead)
    tiles(0, 2)
    cot_gather.got_core_second()
    cot_gather.got_core_first()
    cot_gather.got_across()
    gate_gather.step(0)
    tiles(2, ahead)
    out_gather.step(2)
    for i, ext in enumerate((k_ext, v_ext)):
        save(ext.at[pl.ds(0, WINDOW)], halo_out.at[i])
    own_w_out.wait()
    save(w_out_full, w_out_out)
    copies = block_reduce(p, out, into, r_send, r_recv)

    def emit(j, target, *more):
        start = pl.multiple_of(j * rows, rows)

        for n in range(line):
            cols = slice(n * slab, (n + 1) * slab)
            value = product(attended[pl.ds(start, rows), :], w_out_full[n])
            for other in more:
                value = value + other[:, cols].astype(F32)
            target[:, cols] = value.astype(target.dtype)

    emit(p.second + p.turn, out.at[0])
    copies[0].start()
    emit(p.across + p.turn, out.at[1])
    copies[1].start()
    copies[0].wait_recv()
    emit(p.first, out.at[2], into.at[0])
    copies[4].start()
    copies[0].wait_send()
    emit(p.first + p.turn, out.at[0])
    copies[2].start()
    copies[1].wait_recv()
    emit(p.across, out.at[3], into.at[1])
    copies[5].start()
    copies[1].wait_send()
    emit(p.core, out.at[1])
    copies[3].start()
    copies[3].wait_recv()
    emit(p.h, middle, into.at[3], tokens)
    up_gather.step(0)
    gate_gather.step(1)
    copies[2].wait_recv()
    cot_gather.got_core_across()
    up_gather.step(1)
    copies[5].wait_recv()
    emit(p.second, out.at[4], into.at[2], into.at[5])
    copies[6].start()
    gate_gather.step(2)
    copies[4].wait_recv()
    up_gather.step(2)
    copies[6].wait_recv()

    @pl.loop(0, line)
    def _(n):
        cols = pl.ds(pl.multiple_of(n * slab, slab), slab)
        middle[:, cols] += into[4, :, cols].astype(F32) + into[6, :, cols].astype(F32)

    for i in range(2, 7):
        copies[i].wait_send()
    gather.finish()
    cot_gather.finish()
    for each in (qkv_gather, out_gather, gate_gather, up_gather):
        each.finish()

    @pl.when(p.s < line - 1)
    def _():
        seg_copy.wait_send()
        halo[0].wait_send()
        halo[1].wait_send()

    for copy in saved:
        if copy is not own_w_out:
            copy.wait()


def forward(line, tokens, gain, wq, wk, wv, segment, cot, w_out, w_gate, w_up):
    rows, width = tokens.shape
    slab, part = wq.shape
    full = rows * 8
    units = w_gate.shape[0]
    heads = part // HEAD_DIM
    return pl.pallas_call(
        functools.partial(forward_kernel, line),
        out_shape=(
            jax.ShapeDtypeStruct((full, width), BF16),
            jax.ShapeDtypeStruct((full, 3 * part), BF16),
            jax.ShapeDtypeStruct((width, 3 * part), BF16),
            jax.ShapeDtypeStruct((1, full), jnp.int32),
            jax.ShapeDtypeStruct((full, part), BF16),
            jax.ShapeDtypeStruct((heads, full), F32),
            jax.ShapeDtypeStruct((2, WINDOW, part), BF16),
            jax.ShapeDtypeStruct((full, width), BF16),
            jax.ShapeDtypeStruct((line, part, slab), BF16),
            jax.ShapeDtypeStruct((line, units, slab), BF16),
            jax.ShapeDtypeStruct((line, units, slab), BF16),
            jax.ShapeDtypeStruct((rows, width), F32),
        ),
        in_specs=[vmem_spec()] * 10,
        out_specs=(
            any_spec(),
            any_spec(),
            any_spec(),
            vmem_spec(),
            vmem_spec(),
            vmem_spec(),
            any_spec(),
            any_spec(),
            any_spec(),
            any_spec(),
            any_spec(),
            vmem_spec(),
        ),
        scratch_shapes=[
            pltpu.VMEM((full, width), BF16),
            pltpu.VMEM((width, 3 * part), BF16),
            pltpu.VMEM((full, part), BF16),
            pltpu.VMEM((WINDOW + full, part), BF16),
            pltpu.VMEM((WINDOW + full, part), BF16),
            pltpu.VMEM((part, WINDOW + full), BF16),
            pltpu.VMEM((line, part, slab), BF16),
            pltpu.VMEM((1, WINDOW), jnp.int32),
            pltpu.VMEM((5, rows, width), BF16),
            pltpu.VMEM((7, rows, width), BF16),
            pltpu.SemaphoreType.DMA((7,)),
            pltpu.SemaphoreType.DMA((7,)),
            pltpu.SemaphoreType.DMA((7,)),
            pltpu.SemaphoreType.DMA((7,)),
            pltpu.SemaphoreType.DMA((7,)),
            pltpu.SemaphoreType.DMA((7,)),
            pltpu.SemaphoreType.DMA((2,)),
            pltpu.SemaphoreType.DMA((2,)),
            pltpu.SemaphoreType.DMA((2,)),
            pltpu.SemaphoreType.DMA((19,)),
            *line_sems(line, 4),
        ],
        compiler_params=pltpu.CompilerParams(
            collective_id=1, has_side_effects=True, vmem_limit_bytes=62 * MIB
        ),
        cost_estimate=pl.CostEstimate(
            flops=20 * 2**30, bytes_accessed=100 * MIB, transcendentals=0
        ),
    )(tokens, gain.reshape(1, width), wq, wk, wv, segment.reshape(1, full), cot, w_out, w_gate, w_up)


def sigmoid_of(value):
    return 0.5 * jnp.tanh(0.5 * value) + 0.5


def strips(width, most=256):
    return [(start, min(start + most, width)) for start in range(0, width, most)]


def feed_kernel(
    line,
    middle,
    gain,
    cot,
    gate,
    up,
    down,
    normed_out,
    hidden_out,
    grad_gate_out,
    grad_up_out,
    grad_out,
    down_out,
    down_grad,
    normed,
    w_gate,
    w_up,
    w_down,
    gates,
    ups,
    cot_block,
    hidden,
    grad_gate,
    grad_up,
    down_parts,
    down_up_in,
    down_down_in,
    out,
    into,
    r_send,
    r_recv,
    g_send,
    g_recv,
    *sems,
):
    p = Place(line)
    down_sems, sum_sems, loads, saves, stage, strip_sems = sems[0:4], sems[4:8], *sems[8:12]
    rows, width = grad_out.shape
    units = w_down.shape[1]
    slab = w_down.shape[2]
    block = lambda j: normed.at[pl.ds(pl.multiple_of(j * rows, rows), rows)]
    rows_of = lambda ref, j: ref.at[pl.ds(pl.multiple_of(j * rows, rows), rows)]
    gather = HeadGather(p, block, g_send, g_recv)
    down_gather = LineGather(p, lambda d: w_down.at[d], *down_sems, own=down)
    p.greet()
    down_gather.start(0)
    started = [
        pltpu.make_async_copy(middle, grad_out, loads.at[0]),
        pltpu.make_async_copy(gate, w_gate, loads.at[1]),
        pltpu.make_async_copy(up, w_up, loads.at[3]),
        pltpu.make_async_copy(down, w_down.at[p.s], loads.at[4]),
    ]
    for copy in started:
        copy.start()
    started[0].wait()
    mine = block(p.h)
    step = 32

    @pl.loop(0, rows // step)
    def _(i):
        at = pl.ds(pl.multiple_of(i * step, step), step)
        mine[at] = norm_rows(grad_out[at], gain[...]).astype(BF16)

    gather.start()
    saved = []

    def save(j):
        copy = pltpu.make_async_copy(block(j), rows_of(normed_out, j), saves.at[len(saved)])
        copy.start()
        saved.append(copy)

    opened = (
        p.h,
        p.core,
        p.first,
        p.second + p.turn,
        p.first + p.turn,
        p.second,
        p.across + p.turn,
        p.across,
    )
    hidden_stores = [
        pltpu.make_async_copy(hidden.at[m % 2], rows_of(hidden_out, j), stage.at[m % 2])
        for m, j in enumerate(opened)
    ]

    def open_up(m, slot):
        start = pl.multiple_of(opened[m] * rows, rows)
        if m > 1:
            hidden_stores[m - 2].wait()
        for first, last in strips(units):
            found = []
            for weight in (w_gate, w_up):
                value = product_nt(normed[pl.ds(start, rows), 0:slab], weight[0, first:last, :])
                for d in range(1, line):
                    value = value + product_nt(
                        normed[pl.ds(start, rows), d * slab : (d + 1) * slab],
                        weight[d, first:last, :],
                    )
                found.append(value)
            value, lift = found
            gates[slot, :, first:last] = value.astype(BF16)
            ups[slot, :, first:last] = lift.astype(BF16)
            hidden[m % 2, :, first:last] = (value * sigmoid_of(value) * lift).astype(BF16)
        hidden_stores[m].start()

    order = (
        p.second + p.turn,
        p.first,
        p.across + p.turn,
        p.across,
        p.first + p.turn,
        p.second,
        p.core,
        p.h,
    )
    fetches = [
        pltpu.make_async_copy(rows_of(cot, j), cot_block, stage.at[6]) for j in order
    ]
    stores = [
        [
            pltpu.make_async_copy(
                held.at[n % 2], rows_of(home, j), stage.at[2 + 2 * (n % 2) + i]
            )
            for i, (held, home) in enumerate(
                ((grad_gate, grad_gate_out), (grad_up, grad_up_out))
            )
        ]
        for n, j in enumerate(order)
    ]

    def close(n, slot):
        fetches[n].wait()
        if n > 1:
            for copy in stores[n - 2]:
                copy.wait()
        turn = n % 2
        for first, last in strips(units):
            grad = product_nt(cot_block[:, 0:slab], w_down[0, first:last, :])
            for d in range(1, line):
                grad = grad + product_nt(
                    cot_block[:, d * slab : (d + 1) * slab], w_down[d, first:last, :]
                )
            gate = gates[slot, :, first:last].astype(F32)
            lift = ups[slot, :, first:last].astype(F32)
            sigmoid = sigmoid_of(gate)
            grad_up[turn, :, first:last] = (grad * gate * sigmoid).astype(BF16)
            grad_gate[turn, :, first:last] = (
                grad * lift * (sigmoid * (1.0 + gate * (1.0 - sigmoid)))
            ).astype(BF16)
        if n + 1 < len(order):
            fetches[n + 1].start()
        for copy in stores[n]:
            copy.start()

    def back(n, target, *more):
        turn = n % 2

        for d in range(line):
            cols = slice(d * slab, (d + 1) * slab)
            value = product(grad_gate[turn], w_gate[d]) + product(grad_up[turn], w_up[d])
            for other in more:
                value = value + other[:, cols].astype(F32)
            target[:, cols] = value.astype(target.dtype)

    copies = block_reduce(p, out, into, r_send, r_recv)
    down_reduce = LineReduce(
        p, lambda d: down_parts.at[d], down_up_in, down_down_in, *sum_sems
    )
    wide = slab
    padded = hidden.shape[2]
    kept = slice(2 * wide, 2 * wide + units)
    hidden[:, :, units // 128 * 128 :] = jnp.zeros((2, rows, padded - units // 128 * 128), BF16)
    multiply = lambda *some: weight_product(
        lambda rows_in: product_tn(normed[:, kept], rows_in),
        cot,
        lambda d: down_parts.at[d],
        lambda k: normed.at[:, pl.ds(pl.multiple_of(k * wide, wide), wide)],
        wide,
        strip_sems,
        p,
        *some,
    )
    fetches[0].start()
    for copy in started[1:3]:
        copy.wait()
    save(p.h)
    open_up(0, 0)
    gather.got_core()
    save(p.core)
    open_up(1, 1)
    down_gather.step(0)
    gather.got_first()
    gather.got_second()
    save(p.first)
    save(p.second)
    down_gather.step(1)
    open_up(2, 2)
    gather.got_core_second()
    gather.got_core_first()
    save(p.second + p.turn)
    save(p.first + p.turn)
    open_up(3, 3)
    open_up(4, 4)
    open_up(5, 5)
    clear_last(down_reduce)
    down_gather.step(2)
    started[3].wait()
    down_save = pltpu.make_async_copy(w_down, down_out, loads.at[4])
    down_save.start()
    close(0, 3)
    back(0, out.at[0])
    copies[0].start()
    gather.got_across()
    save(p.across)
    close(1, 2)
    copies[0].wait_recv()
    back(1, out.at[2], into.at[0])
    copies[4].start()
    gather.got_core_across()
    save(p.across + p.turn)
    open_up(6, 2)
    open_up(7, 3)
    gather.finish()
    for copy in saved:
        copy.wait()
    for copy in hidden_stores[6:]:
        copy.wait()
    fill = pltpu.make_async_copy(hidden_out, normed.at[:, pl.ds(2 * wide, padded)], loads.at[5])
    fill.start()
    fill.wait()
    multiply(0, 1)
    down_reduce.start(0)
    multiply(1, 2)
    close(2, 2)
    back(2, out.at[1])
    copies[1].start()
    close(3, 3)
    copies[1].wait_recv()
    back(3, out.at[3], into.at[1])
    copies[5].start()
    down_reduce.step(0)
    multiply(2, line)
    close(4, 4)
    copies[0].wait_send()
    back(4, out.at[0])
    copies[2].start()
    close(5, 5)
    copies[2].wait_recv()
    copies[5].wait_recv()
    back(5, out.at[4], into.at[2], into.at[5])
    copies[6].start()
    down_reduce.step(1)
    close(6, 1)
    copies[1].wait_send()
    back(6, out.at[1])
    copies[3].start()
    close(7, 0)
    copies[3].wait_recv()
    back(7, grad_out, into.at[3])
    copies[4].wait_recv()
    copies[6].wait_recv()

    @pl.loop(0, line)
    def _(d):
        cols = pl.ds(pl.multiple_of(d * slab, slab), slab)
        grad_out[:, cols] += into[4, :, cols].astype(F32) + into[6, :, cols].astype(F32)

    down_reduce.step(2)
    for first, last in strips(units, 128):
        down_grad[first:last, :] = down_reduce.total(slice(first, last))
    for i in range(2, 7):
        copies[i].wait_send()
    down_gather.finish()
    down_reduce.finish()
    for copy in stores[6] + stores[7]:
        copy.wait()
    down_save.wait()


def feed(line, middle, gain, cot, gate, up, down):
    rows, width = middle.shape
    units, slab = down.shape
    full = rows * 8
    padded = (units + 127) // 128 * 128
    return pl.pallas_call(
        functools.partial(feed_kernel, line),
        out_shape=(
            jax.ShapeDtypeStruct((full, width), BF16),
            jax.ShapeDtypeStruct((full, padded), BF16),
            jax.ShapeDtypeStruct((full, units), BF16),
            jax.ShapeDtypeStruct((full, units), BF16),
            jax.ShapeDtypeStruct((rows, width), F32),
            jax.ShapeDtypeStruct((line, units, slab), BF16),
            jax.ShapeDtypeStruct((units, slab), F32),
        ),
        in_specs=[any_spec(), vmem_spec()] + [any_spec()] * 4,
        out_specs=(
            any_spec(),
            any_spec(),
            any_spec(),
            any_spec(),
            vmem_spec(),
            any_spec(),
            vmem_spec(),
        ),
        scratch_shapes=[
            pltpu.VMEM((full, width), BF16),
            pltpu.VMEM((line, units, slab), BF16),
            pltpu.VMEM((line, units, slab), BF16),
            pltpu.VMEM((line, units, slab), BF16),
            pltpu.VMEM((6, rows, units), BF16),
            pltpu.VMEM((6, rows, units), BF16),
            pltpu.VMEM((rows, width), BF16),
            pltpu.VMEM((2, rows, padded), BF16),
            pltpu.VMEM((2, rows, units), BF16),
            pltpu.VMEM((2, rows, units), BF16),
            pltpu.VMEM((line, units, slab), BF16),
            pltpu.VMEM((line - 1, units, slab), BF16),
            pltpu.VMEM((line - 1, units, slab), BF16),
            pltpu.VMEM((5, rows, width), BF16),
            pltpu.VMEM((7, rows, width), BF16),
            pltpu.SemaphoreType.DMA((7,)),
            pltpu.SemaphoreType.DMA((7,)),
            pltpu.SemaphoreType.DMA((7,)),
            pltpu.SemaphoreType.DMA((7,)),
            *line_sems(line, 2),
            pltpu.SemaphoreType.DMA((6,)),
            pltpu.SemaphoreType.DMA((8,)),
            pltpu.SemaphoreType.DMA((7,)),
            pltpu.SemaphoreType.DMA((2,)),
        ],
        compiler_params=pltpu.CompilerParams(
            collective_id=2, has_side_effects=True, vmem_limit_bytes=63 * MIB
        ),
        cost_estimate=pl.CostEstimate(
            flops=50 * 2**30, bytes_accessed=80 * MIB, transcendentals=0
        ),
    )(middle, gain.reshape(1, width), cot, gate, up, down)


class LineReduce:
    def __init__(self, place, part, up_in, down_in, up_send, up_recv, down_send, down_recv):
        self.p, self.part = place, part
        self.up_in, self.down_in = up_in, down_in
        self.up = (up_send, up_recv)
        self.down = (down_send, down_recv)

    def _up(self, d, t):
        p = self.p
        return remote(
            self.part(d), self.up_in.at[t], self.up[0].at[t], self.up[1].at[t], (p.s + 1, p.h)
        )

    def _down(self, d, t):
        p = self.p
        return remote(
            self.part(d),
            self.down_in.at[t],
            self.down[0].at[t],
            self.down[1].at[t],
            (p.s - 1, p.h),
        )

    def _sends(self, t):
        p, last = self.p, self.p.line - 1
        return (
            ((p.s <= t) & (p.s < last), self._up, last - t + p.s),
            ((last - p.s <= t) & (p.s > 0), self._down, t - last + p.s),
        )

    def start(self, t):
        p, last = self.p, self.p.line - 1
        for number, (goes, copy, d) in enumerate(self._sends(t)):
            came = (self.up_in, self.down_in)[number]

            @pl.when(goes)
            def _():
                if t > 0:
                    inner = p.s > 0 if number == 0 else p.s < last

                    @pl.when(inner)
                    def _():
                        add_rows(self.part(d), came.at[t - 1])

                copy(d, t).start()

    def got(self, t):
        p, last = self.p, self.p.line - 1

        @pl.when((p.s >= 1) & (t >= p.s - 1))
        def _():
            self._up(0, t).wait_recv()

        @pl.when((p.s < last) & (t >= last - p.s - 1))
        def _():
            self._down(0, t).wait_recv()

    def step(self, t):
        self.got(t)
        if t + 1 < self.p.line - 1:
            self.start(t + 1)

    def end(self):
        p, last = self.p, self.p.line - 1

        @pl.when(p.s >= 1)
        def _():
            add_rows(self.part(p.s), self.up_in.at[last - 1])

        @pl.when(p.s < last)
        def _():
            add_rows(self.part(p.s), self.down_in.at[last - 1])

    def total(self, rows):
        p, last = self.p, self.p.line - 1
        value = self.part(p.s)[rows, :].astype(F32)
        value = value + jnp.where(p.s >= 1, self.up_in[last - 1, rows, :].astype(F32), 0.0)
        return value + jnp.where(p.s < last, self.down_in[last - 1, rows, :].astype(F32), 0.0)

    def finish(self):
        for t in range(self.p.line - 1):
            for goes, copy, d in self._sends(t):

                @pl.when(goes)
                def _():
                    copy(d, t).wait_send()


def add_rows(target, other):
    step = 16

    @pl.loop(0, target.shape[0] // step)
    def _(i):
        at = pl.ds(pl.multiple_of(i * step, step), step)
        target[at, :] = (target[at, :].astype(F32) + other[at, :].astype(F32)).astype(BF16)


def clear_last(reduce):
    p, last = reduce.p, reduce.p.line - 1

    @pl.when(p.s == 0)
    def _():
        reduce.up_in[last - 1] = jnp.zeros(reduce.up_in.shape[1:], BF16)

    @pl.when(p.s == last)
    def _():
        reduce.down_in[last - 1] = jnp.zeros(reduce.down_in.shape[1:], BF16)


def weight_product(apply, source, piece, strip, wide, sems, place, first, last):
    each = piece(0).shape[1] // wide
    begin, end = first * each, last * each

    def slab(n):
        d = lax.div(n, each)
        low = place.s < place.line // 2
        return jnp.where(low, place.line - 1 - d, d)

    def fetch(n):
        at = slab(n) * each + lax.rem(n, each)
        cols = pl.ds(pl.multiple_of(at * wide, wide), wide)
        return pltpu.make_async_copy(
            source.at[:, cols], strip(lax.rem(n, 2)), sems.at[lax.rem(n, 2)]
        )

    fetch(begin).start()

    @pl.loop(begin, end)
    def _(n):
        @pl.when(n + 1 < end)
        def _():
            fetch(n + 1).start()

        fetch(n).wait()
        cols = pl.ds(pl.multiple_of(lax.rem(n, each) * wide, wide), wide)
        piece(slab(n))[:, cols] = apply(strip(lax.rem(n, 2))[...]).astype(BF16)


def turn_rows(source, target):
    step = 256

    @pl.loop(0, source.shape[0] // step)
    def _(i):
        at = pl.ds(pl.multiple_of(i * step, step), step)
        for first, last in strips(source.shape[1], 128):
            target[first:last, at] = source[at, first:last].T


def return_kernel(
    line,
    grad_given,
    middle_given,
    cot_given,
    gain,
    attended_given,
    w_out_given,
    grad_gate,
    grad_up,
    normed,
    grad_middle_out,
    gain_part,
    grad_attended,
    inner,
    up_grad,
    gate_parts,
    out_parts,
    branch,
    units_in,
    strip,
    up_parts,
    other_parts,
    up_up_in,
    up_down_in,
    att_turned,
    out_sum,
    grad_normed,
    middle,
    cot_own,
    attended,
    w_out,
    grad_middle,
    g_send,
    g_recv,
    *sems,
):
    p = Place(line)
    up_sems, loads, strips_sem, saves, early, kept = sems[0:4], *sems[4:9]
    rows, width = grad_normed.shape
    slab = w_out.shape[2]
    part = attended.shape[1]
    block = lambda j: branch.at[pl.ds(pl.multiple_of(j * rows, rows), rows)]
    gather = HeadGather(p, block, g_send, g_recv)
    up_reduce = LineReduce(p, lambda d: up_parts.at[d], up_up_in, up_down_in, *up_sems)
    load = [
        pltpu.make_async_copy(source, units_in, loads.at[i])
        for i, source in enumerate((grad_up, grad_gate))
    ]
    pieces = 4
    piece_rows = rows // pieces
    piece_at = [pl.ds(i * piece_rows, piece_rows) for i in range(pieces)]
    arriving = [
        [
            pltpu.make_async_copy(source.at[at], target.at[at], early.at[3 * i + k])
            for k, (source, target) in enumerate(
                ((grad_given, grad_normed), (middle_given, middle), (cot_given, cot_own))
            )
        ]
        for i, at in enumerate(piece_at)
    ]
    leaving = [
        pltpu.make_async_copy(grad_middle.at[at], grad_middle_out.at[at], kept.at[i])
        for i, at in enumerate(piece_at)
    ]
    later = [
        pltpu.make_async_copy(attended_given, attended, early.at[3 * pieces]),
        pltpu.make_async_copy(w_out_given, w_out, early.at[3 * pieces + 1]),
    ]
    for group in arriving:
        for copy in group:
            copy.start()
    load[0].start()
    for copy in later:
        copy.start()
    p.greet()
    mine = block(p.h)
    gain_part[...] = jnp.zeros_like(gain_part)
    step = 32

    def piece_back(number, i):
        at = pl.ds(pl.multiple_of(number * piece_rows + i * step, step), step)
        value = middle[at]
        inverse = lax.rsqrt(jnp.mean(value * value, axis=-1, keepdims=True) + EPS)
        unit = value * inverse
        grad = grad_normed[at]
        gain_part[...] += jnp.sum(grad * unit, axis=0, keepdims=True)
        result = cot_own[at].astype(F32) + norm_back(unit, inverse, gain[...], grad)
        grad_middle[at] = result
        mine[at] = result.astype(BF16)

    for number in range(pieces):
        for copy in arriving[number]:
            copy.wait()
        pl.loop(0, piece_rows // step)(functools.partial(piece_back, number))
        leaving[number].start()

    gather.start()
    clear_last(up_reduce)
    multiply = lambda parts, *some: weight_product(
        lambda rows_in: product_tn(units_in[...], rows_in),
        normed,
        lambda d: parts.at[d],
        strip.at.__getitem__,
        strip.shape[2],
        strips_sem,
        p,
        *some,
    )
    load[0].wait()
    multiply(up_parts, 0, 1)
    up_reduce.start(0)
    multiply(up_parts, 1, line)
    load[1].start()
    gather.got_core()
    load[1].wait()
    up_reduce.step(0)
    gather.got_first()
    gather.got_second()
    multiply(other_parts, 0, line)
    save_gate = pltpu.make_async_copy(other_parts, gate_parts, saves.at[1])
    save_gate.start()
    for copy in later:
        copy.wait()
    turn_rows(attended, att_turned)
    up_reduce.step(1)
    gather.got_core_second()
    gather.got_core_first()
    out_sum[...] = jnp.zeros_like(out_sum)

    def take(j):
        start = pl.multiple_of(j * rows, rows)
        at = pl.ds(start, rows)
        total = product_nt(branch[at, 0:slab], w_out[0])
        for d in range(1, line):
            total = total + product_nt(branch[at, d * slab : (d + 1) * slab], w_out[d])
        low = total.astype(BF16)
        grad_attended[at, :] = low
        for head in range(part // HEAD_DIM):
            cols = slice(head * HEAD_DIM, (head + 1) * HEAD_DIM)
            both = low[:, cols].astype(F32) * attended[at, cols].astype(F32)
            inner[head : head + 1, at] = jnp.sum(both.T, axis=0, keepdims=True)

        @pl.loop(0, line)
        def _(d):
            cols = pl.ds(pl.multiple_of(d * slab, slab), slab)
            out_sum[d] += product(att_turned[:, at], branch[at, cols])

    for j in (p.h, p.core, p.first, p.second):
        take(j)
    for j in (p.second + p.turn, p.first + p.turn):
        take(j)
    gather.got_across()
    take(p.across)
    gather.got_core_across()
    take(p.across + p.turn)
    for d in range(line):
        out_parts[d] = out_sum[d].astype(BF16)
    up_reduce.step(2)
    for first, last in strips(up_grad.shape[0], 128):
        up_grad[first:last, :] = up_reduce.total(slice(first, last))
    gather.finish()
    up_reduce.finish()
    save_gate.wait()
    for copy in leaving:
        copy.wait()


def give_back(
    line, grad_normed, middle, cot_own, gain, attended, w_out, grad_gate, grad_up, normed
):
    rows, width = middle.shape
    full, units = grad_up.shape
    part = attended.shape[1]
    slab = w_out.shape[2]
    heads = part // HEAD_DIM
    return pl.pallas_call(
        functools.partial(return_kernel, line),
        out_shape=(
            jax.ShapeDtypeStruct((rows, width), F32),
            jax.ShapeDtypeStruct((1, width), F32),
            jax.ShapeDtypeStruct((full, part), BF16),
            jax.ShapeDtypeStruct((heads, full), F32),
            jax.ShapeDtypeStruct((units, slab), F32),
            jax.ShapeDtypeStruct((line, units, slab), BF16),
            jax.ShapeDtypeStruct((line, part, slab), BF16),
        ),
        in_specs=[any_spec()] * 3 + [vmem_spec()] + [any_spec()] * 5,
        out_specs=(
            any_spec(),
            vmem_spec(),
            vmem_spec(),
            vmem_spec(),
            vmem_spec(),
            any_spec(),
            vmem_spec(),
        ),
        scratch_shapes=[
            pltpu.VMEM((full, width), BF16),
            pltpu.VMEM((full, units), BF16),
            pltpu.VMEM((2, full, slab), BF16),
            pltpu.VMEM((line, units, slab), BF16),
            pltpu.VMEM((line, units, slab), BF16),
            pltpu.VMEM((line - 1, units, slab), BF16),
            pltpu.VMEM((line - 1, units, slab), BF16),
            pltpu.VMEM((part, full), BF16),
            pltpu.VMEM((line, part, slab), F32),
            pltpu.VMEM((rows, width), F32),
            pltpu.VMEM((rows, width), F32),
            pltpu.VMEM((rows, width), BF16),
            pltpu.VMEM((full, part), BF16),
            pltpu.VMEM((line, part, slab), BF16),
            pltpu.VMEM((rows, width), F32),
            pltpu.SemaphoreType.DMA((7,)),
            pltpu.SemaphoreType.DMA((7,)),
            *line_sems(line),
            pltpu.SemaphoreType.DMA((2,)),
            pltpu.SemaphoreType.DMA((2,)),
            pltpu.SemaphoreType.DMA((2,)),
            pltpu.SemaphoreType.DMA((14,)),
            pltpu.SemaphoreType.DMA((4,)),
        ],
        compiler_params=pltpu.CompilerParams(
            collective_id=3, has_side_effects=True, vmem_limit_bytes=62 * MIB
        ),
        cost_estimate=pl.CostEstimate(
            flops=25 * 2**30, bytes_accessed=80 * MIB, transcendentals=0
        ),
    )(
        grad_normed,
        middle,
        cot_own,
        gain.reshape(1, width),
        attended,
        w_out,
        grad_gate,
        grad_up,
        normed,
    )


def backward_tile(tile, q, k_ext, v_ext, k_t, floor, logs, inner, grad, key_sum, value_sum):
    start = pl.multiple_of(tile * TILE, TILE)
    mine = pl.ds(start, TILE)
    scale = HEAD_DIM ** (-0.5)
    for head in range(q.shape[1] // HEAD_DIM):
        cols = slice(head * HEAD_DIM, (head + 1) * HEAD_DIM)
        queries = q[mine, cols]
        grads = grad[mine, cols]
        log = logs[head : head + 1, mine]
        middle = inner[head : head + 1, mine]
        turned = jnp.zeros((HEAD_DIM, TILE), F32)
        for i, (scores, visible) in enumerate(tile_scores(tile, head, q, k_ext, floor)):
            at = pl.ds(start + i * TILE, TILE)
            probs = jnp.where(visible, jnp.exp2(scores * (scale * LOG2E) - log), 0.0)
            grad_probs = product_nt(v_ext[at, cols], grads)
            grad_scores = (probs * (grad_probs - middle)).astype(BF16)
            value_sum[at, cols] += product(probs.astype(BF16), grads)
            key_sum[at, cols] += product(grad_scores, queries)
            turned = turned + product(k_t[cols, at], grad_scores)
        q[mine, cols] = (turned * scale).astype(BF16).T


def attend_back_kernel(
    line,
    qkv,
    halo_kv,
    floor,
    logs,
    grad_given,
    inner,
    hidden,
    w_down_given,
    middle,
    gate_in,
    grads_out,
    result,
    gate_grad,
    q,
    k_ext,
    v_ext,
    k_t,
    key_sum,
    value_sum,
    halo_out,
    halo_in,
    gate_parts,
    gate_up_in,
    gate_down_in,
    out,
    into,
    total,
    hidden_block,
    grad,
    w_down,
    r_send,
    r_recv,
    *sems,
):
    p = Place(line)
    gate_sems, loads, halo_send, halo_recv, stage, saves = sems[0:4], *sems[4:9]
    rows, width = result.shape
    slab = w_down.shape[2]
    count, part = q.shape
    scale = HEAD_DIM ** (-0.5)
    rows_of = lambda ref, j: ref.at[pl.ds(pl.multiple_of(j * rows, rows), rows)]
    gate_reduce = LineReduce(
        p, lambda d: gate_parts.at[d], gate_up_in, gate_down_in, *gate_sems
    )
    started = [
        pltpu.make_async_copy(gate_in, gate_parts, loads.at[0]),
        pltpu.make_async_copy(qkv.at[:, pl.ds(0, part)], q, loads.at[1]),
        pltpu.make_async_copy(
            qkv.at[:, pl.ds(part, part)], k_ext.at[pl.ds(WINDOW, count)], loads.at[2]
        ),
        pltpu.make_async_copy(
            qkv.at[:, pl.ds(2 * part, part)], v_ext.at[pl.ds(WINDOW, count)], loads.at[3]
        ),
        pltpu.make_async_copy(halo_kv.at[0], k_ext.at[pl.ds(0, WINDOW)], loads.at[4]),
        pltpu.make_async_copy(halo_kv.at[1], v_ext.at[pl.ds(0, WINDOW)], loads.at[5]),
        pltpu.make_async_copy(middle, total, loads.at[6]),
        pltpu.make_async_copy(grad_given, grad, loads.at[7]),
    ]
    down_load = pltpu.make_async_copy(w_down_given, w_down, loads.at[8])
    halo = [
        remote(
            halo_out.at[i], halo_in.at[i], halo_send.at[i], halo_recv.at[i], (p.s - 1, p.h)
        )
        for i in range(2)
    ]
    order = (
        p.second + p.turn,
        p.across + p.turn,
        p.first,
        p.first + p.turn,
        p.across,
        p.core,
        p.h,
        p.second,
    )
    fetches = [
        pltpu.make_async_copy(rows_of(hidden, j), hidden_block.at[n % 2], stage.at[n % 2])
        for n, j in enumerate(order)
    ]
    copies = block_reduce(p, out, into, r_send, r_recv)

    def emit(n, target, *more):
        fetches[n].wait()
        if n + 1 < len(order):
            fetches[n + 1].start()

        for d in range(line):
            cols = slice(d * slab, (d + 1) * slab)
            value = product(hidden_block[n % 2][:, 0 : w_down.shape[1]], w_down[d])
            for other in more:
                value = value + other[:, cols].astype(F32)
            target[:, cols] = value.astype(target.dtype)

    def tiles(first, last):
        @pl.loop(first, last)
        def _(tile):
            backward_tile(
                tile, q, k_ext, v_ext, k_t, floor, logs, inner, grad, key_sum, value_sum
            )

    down_load.start()
    fetches[0].start()
    for copy in started:
        copy.start()
    p.greet()
    started[0].wait()
    gate_reduce.start(0)
    clear_last(gate_reduce)
    down_load.wait()
    emit(0, out.at[0])
    copies[0].start()
    emit(1, out.at[1])
    copies[1].start()
    copies[0].wait_recv()
    emit(2, out.at[2], into.at[0])
    copies[4].start()
    copies[0].wait_send()
    emit(3, out.at[0])
    copies[2].start()
    copies[1].wait_recv()
    emit(4, out.at[3], into.at[1])
    copies[5].start()
    copies[1].wait_send()
    emit(5, out.at[1])
    copies[3].start()
    for copy in started[1:]:
        copy.wait()
    gate_reduce.step(0)

    @pl.loop(0, (WINDOW + count) // TILE)
    def _(i):
        at = pl.ds(pl.multiple_of(i * TILE, TILE), TILE)
        k_t[:, at] = k_ext[at, :].T
        key_sum[at, :] = jnp.zeros((TILE, part), F32)
        value_sum[at, :] = jnp.zeros((TILE, part), F32)

    ahead = WINDOW // TILE
    last = count // TILE
    tiles(0, ahead)

    @pl.when(p.s > 0)
    def _():
        @pl.loop(0, ahead)
        def _(i):
            at = pl.ds(pl.multiple_of(i * TILE, TILE), TILE)
            halo_out[0, at, :] = (key_sum[at, :] * scale).astype(BF16)
            halo_out[1, at, :] = value_sum[at, :].astype(BF16)

        halo[0].start()
        halo[1].start()

    gate_reduce.step(1)
    tiles(ahead, ahead + 4)
    copies[3].wait_recv()
    emit(6, total, into.at[3], total)
    copies[2].wait_recv()
    copies[5].wait_recv()
    emit(7, out.at[4], into.at[2], into.at[5])
    copies[6].start()
    tiles(ahead + 4, last)

    @pl.when(p.s < line - 1)
    def _():
        halo[0].wait_recv()
        halo[1].wait_recv()

    @pl.loop(0, last)
    def _(i):
        here = pl.ds(pl.multiple_of(i * TILE, TILE), TILE)
        at = pl.ds(pl.multiple_of(i * TILE + WINDOW, TILE), TILE)
        key_value = key_sum[at, :] * scale
        value_value = value_sum[at, :]
        k_ext[here, :] = key_value.astype(BF16)
        v_ext[here, :] = value_value.astype(BF16)

    @pl.when(p.s < line - 1)
    def _():
        @pl.loop(0, ahead)
        def _(i):
            here = pl.ds(pl.multiple_of(i * TILE, TILE), TILE)
            near = pl.ds(pl.multiple_of(i * TILE + count, TILE), TILE)
            there = pl.ds(pl.multiple_of(i * TILE + count - WINDOW, TILE), TILE)
            k_ext[there, :] = (
                key_sum[near, :] * scale + halo_in[0, here, :].astype(F32)
            ).astype(BF16)
            v_ext[there, :] = (value_sum[near, :] + halo_in[1, here, :].astype(F32)).astype(BF16)

    save = [
        pltpu.make_async_copy(
            ref.at[pl.ds(0, count)], grads_out.at[:, pl.ds(i * part, part)], saves.at[i]
        )
        for i, ref in enumerate((q, k_ext, v_ext))
    ]
    for copy in save:
        copy.start()
    copies[4].wait_recv()
    copies[6].wait_recv()

    @pl.loop(0, line)
    def _(d):
        cols = pl.ds(pl.multiple_of(d * slab, slab), slab)
        value = total[:, cols] + into[4, :, cols].astype(F32) + into[6, :, cols].astype(F32)
        result[:, cols] = value.astype(BF16)

    gate_reduce.step(2)
    for first, stop in strips(gate_grad.shape[0], 128):
        gate_grad[first:stop, :] = gate_reduce.total(slice(first, stop))
    for i in range(2, 7):
        copies[i].wait_send()
    gate_reduce.finish()

    @pl.when(p.s > 0)
    def _():
        halo[0].wait_send()
        halo[1].wait_send()

    for copy in save:
        copy.wait()


def attend_back(line, qkv, halo_kv, floor, logs, grad, inner, hidden, w_down, middle, gate_parts):
    rows, width = middle.shape
    count = qkv.shape[0]
    part = qkv.shape[1] // 3
    units, slab = w_down.shape[1:]
    return pl.pallas_call(
        functools.partial(attend_back_kernel, line),
        out_shape=(
            jax.ShapeDtypeStruct((count, 3 * part), BF16),
            jax.ShapeDtypeStruct((rows, width), BF16),
            jax.ShapeDtypeStruct((units, slab), F32),
        ),
        in_specs=[any_spec()] * 2
        + [vmem_spec(), vmem_spec(), any_spec(), vmem_spec()]
        + [any_spec()] * 4,
        out_specs=(any_spec(), vmem_spec(), vmem_spec()),
        scratch_shapes=[
            pltpu.VMEM((count, part), BF16),
            pltpu.VMEM((WINDOW + count, part), BF16),
            pltpu.VMEM((WINDOW + count, part), BF16),
            pltpu.VMEM((part, WINDOW + count), BF16),
            pltpu.VMEM((WINDOW + count, part), F32),
            pltpu.VMEM((WINDOW + count, part), F32),
            pltpu.VMEM((2, WINDOW, part), BF16),
            pltpu.VMEM((2, WINDOW, part), BF16),
            pltpu.VMEM((line, units, slab), BF16),
            pltpu.VMEM((line - 1, units, slab), BF16),
            pltpu.VMEM((line - 1, units, slab), BF16),
            pltpu.VMEM((5, rows, width), BF16),
            pltpu.VMEM((7, rows, width), BF16),
            pltpu.VMEM((rows, width), F32),
            pltpu.VMEM((2, rows, hidden.shape[1]), BF16),
            pltpu.VMEM((count, part), BF16),
            pltpu.VMEM((line, units, slab), BF16),
            pltpu.SemaphoreType.DMA((7,)),
            pltpu.SemaphoreType.DMA((7,)),
            *line_sems(line),
            pltpu.SemaphoreType.DMA((9,)),
            pltpu.SemaphoreType.DMA((2,)),
            pltpu.SemaphoreType.DMA((2,)),
            pltpu.SemaphoreType.DMA((2,)),
            pltpu.SemaphoreType.DMA((3,)),
        ],
        compiler_params=pltpu.CompilerParams(
            collective_id=4, has_side_effects=True, vmem_limit_bytes=62 * MIB
        ),
        cost_estimate=pl.CostEstimate(
            flops=20 * 2**30, bytes_accessed=60 * MIB, transcendentals=0
        ),
    )(qkv, halo_kv, floor, logs, grad, inner, hidden, w_down, middle, gate_parts)


def finish_kernel(
    line,
    grads_given,
    weight_given,
    normed,
    tokens_given,
    gain,
    grad_middle,
    out_given,
    ffn_gain_part,
    input_grad,
    gain_sums,
    query_grad,
    key_grad,
    value_grad,
    out_grad,
    strip,
    parts,
    parts_up_in,
    parts_down_in,
    out_parts,
    out_up_in,
    out_down_in,
    out,
    into,
    total,
    gain_line,
    gain_in,
    grads_in,
    weight_in,
    tokens_in,
    r_send,
    r_recv,
    *sems,
):
    p = Place(line)
    part_sems, out_sems = sems[0:4], sems[4:8]
    loads, strip_sems, gain_send, gain_recv, line_send, line_recv, block_sems = sems[8:15]
    grads, weight, tokens = grads_in, weight_in, tokens_in
    rows, width = tokens.shape
    slab = width // line
    part = query_grad.shape[1]
    part_reduce = LineReduce(p, lambda d: parts.at[d], parts_up_in, parts_down_in, *part_sems)
    out_reduce = LineReduce(p, lambda d: out_parts.at[d], out_up_in, out_down_in, *out_sems)
    started = [
        pltpu.make_async_copy(out_given, out_parts, loads.at[0]),
        pltpu.make_async_copy(grad_middle, input_grad, loads.at[1]),
    ]
    turns = (
        p.second + p.turn,
        p.across + p.turn,
        p.first,
        p.first + p.turn,
        p.across,
        p.core,
        p.h,
        p.second,
    )
    blocks = []
    for n, j in enumerate(turns):
        at = pl.ds(pl.multiple_of(j * rows, rows), rows)
        blocks.append(pltpu.make_async_copy(grads_given.at[at], grads.at[at], block_sems.at[n]))
    weight_load = pltpu.make_async_copy(weight_given, weight, loads.at[2])
    tokens_load = pltpu.make_async_copy(tokens_given, tokens, loads.at[3])
    weight_load.start()
    blocks[0].start()
    started[0].start()
    for copy in blocks[1:] + [started[1], tokens_load]:
        copy.start()
    greet_line(p)
    started[0].wait()
    out_reduce.start(0)
    for reduce in (part_reduce, out_reduce):
        clear_last(reduce)
    copies = block_reduce(p, out, into, r_send, r_recv)

    def emit(j, target, *more):
        at = pl.ds(pl.multiple_of(j * rows, rows), rows)

        for d in range(line):
            cols = slice(d * slab, (d + 1) * slab)
            value = product_nt(grads[at, :], weight[cols, :])
            for other in more:
                value = value + other[:, cols].astype(F32)
            target[:, cols] = value.astype(target.dtype)

    weight_load.wait()
    blocks[0].wait()
    emit(p.second + p.turn, out.at[0])
    copies[0].start()
    blocks[1].wait()
    emit(p.across + p.turn, out.at[1])
    copies[1].start()
    copies[0].wait_recv()
    blocks[2].wait()
    emit(p.first, out.at[2], into.at[0])
    copies[4].start()
    copies[0].wait_send()
    blocks[3].wait()
    emit(p.first + p.turn, out.at[0])
    copies[2].start()
    copies[1].wait_recv()
    blocks[4].wait()
    emit(p.across, out.at[3], into.at[1])
    copies[5].start()
    copies[1].wait_send()
    blocks[5].wait()
    emit(p.core, out.at[1])
    copies[3].start()
    blocks[6].wait()
    blocks[7].wait()
    multiply = lambda *some: weight_product(
        lambda rows_in: product_tn(grads[...], rows_in),
        normed,
        lambda d: parts.at[d],
        strip.at.__getitem__,
        strip.shape[2],
        strip_sems,
        p,
        *some,
    )
    out_reduce.step(0)
    multiply(0, 1)
    part_reduce.start(0)
    multiply(1, line)
    out_reduce.step(1)
    copies[3].wait_recv()
    emit(p.h, total, into.at[3])
    part_reduce.step(0)
    copies[2].wait_recv()
    copies[5].wait_recv()
    emit(p.second, out.at[4], into.at[2], into.at[5])
    copies[6].start()
    out_reduce.step(2)
    for first, last in strips(part, 128):
        out_grad[first:last, :] = out_reduce.total(slice(first, last))
    copies[4].wait_recv()
    part_reduce.step(1)
    copies[6].wait_recv()
    started[1].wait()
    tokens_load.wait()
    gain_own = gain_line.at[p.s]
    gain_own[...] = jnp.zeros(gain_own.shape, F32)
    gain_own[1:2, :] = ffn_gain_part[...]
    step = 32

    @pl.loop(0, rows // step)
    def _(i):
        at = pl.ds(pl.multiple_of(i * step, step), step)
        grad = total[at] + into[4, at].astype(F32) + into[6, at].astype(F32)
        unit, inverse = normalize(tokens[at].astype(F32))
        gain_own[0:1, :] += jnp.sum(grad * unit, axis=0, keepdims=True)
        input_grad[at] += norm_back(unit, inverse, gain[...], grad)

    for i, head in enumerate((p.core, p.first, p.second)):
        copy = remote(gain_own, gain_in.at[i], gain_send.at[i], gain_recv.at[i], p.at(head))
        copy.start()
        copy.wait()
        gain_own[...] += gain_in[i]
    spread = [
        remote(
            gain_own,
            gain_own,
            line_send.at[k - 1],
            line_recv.at[k - 1],
            (lax.rem(p.s + k, line), p.h),
        )
        for k in range(1, line)
    ]
    came = [
        remote(
            gain_line.at[lax.rem(p.s + line - k, line)],
            gain_line.at[lax.rem(p.s + line - k, line)],
            line_send.at[k - 1],
            line_recv.at[k - 1],
            (lax.rem(p.s + k, line), p.h),
        )
        for k in range(1, line)
    ]
    for copy in spread:
        copy.start()
    for copy in came:
        copy.wait_recv()
    summed = gain_line[0]
    for d in range(1, line):
        summed = summed + gain_line[d]
    gain_sums[...] = summed
    part_reduce.step(2)
    for i, target in enumerate((query_grad, key_grad, value_grad)):
        for first, last in strips(part, 128):
            target[:, first:last] = part_reduce.total(
                slice(i * part + first, i * part + last)
            ).T
    for i in range(2, 7):
        copies[i].wait_send()
    for copy in spread:
        copy.wait_send()
    for reduce in (part_reduce, out_reduce):
        reduce.finish()


def finish(line, grads, weight, normed, tokens, gain, grad_middle, out_parts, ffn_gain_part):
    rows, width = tokens.shape
    full = grads.shape[0]
    part = grads.shape[1] // 3
    slab = width // line
    return pl.pallas_call(
        functools.partial(finish_kernel, line),
        out_shape=(
            jax.ShapeDtypeStruct((rows, width), F32),
            jax.ShapeDtypeStruct((2, width), F32),
            jax.ShapeDtypeStruct((slab, part), F32),
            jax.ShapeDtypeStruct((slab, part), F32),
            jax.ShapeDtypeStruct((slab, part), F32),
            jax.ShapeDtypeStruct((part, slab), F32),
        ),
        in_specs=[
            any_spec(),
            any_spec(),
            any_spec(),
            any_spec(),
            vmem_spec(),
            any_spec(),
            any_spec(),
            vmem_spec(),
        ],
        out_specs=(vmem_spec(),) * 6,
        scratch_shapes=[
            pltpu.VMEM((2, full, slab), BF16),
            pltpu.VMEM((line, 3 * part, slab), BF16),
            pltpu.VMEM((line - 1, 3 * part, slab), BF16),
            pltpu.VMEM((line - 1, 3 * part, slab), BF16),
            pltpu.VMEM((line, part, slab), BF16),
            pltpu.VMEM((line - 1, part, slab), BF16),
            pltpu.VMEM((line - 1, part, slab), BF16),
            pltpu.VMEM((5, rows, width), BF16),
            pltpu.VMEM((7, rows, width), BF16),
            pltpu.VMEM((rows, width), F32),
            pltpu.VMEM((line, 2, width), F32),
            pltpu.VMEM((3, 2, width), F32),
            pltpu.VMEM(grads.shape, BF16),
            pltpu.VMEM(weight.shape, BF16),
            pltpu.VMEM((rows, width), BF16),
            pltpu.SemaphoreType.DMA((7,)),
            pltpu.SemaphoreType.DMA((7,)),
            *line_sems(line, 2),
            pltpu.SemaphoreType.DMA((4,)),
            pltpu.SemaphoreType.DMA((2,)),
            pltpu.SemaphoreType.DMA((3,)),
            pltpu.SemaphoreType.DMA((3,)),
            pltpu.SemaphoreType.DMA((line - 1,)),
            pltpu.SemaphoreType.DMA((line - 1,)),
            pltpu.SemaphoreType.DMA((8,)),
        ],
        compiler_params=pltpu.CompilerParams(
            collective_id=5, has_side_effects=True, vmem_limit_bytes=62 * MIB
        ),
        cost_estimate=pl.CostEstimate(
            flops=20 * 2**30, bytes_accessed=60 * MIB, transcendentals=0
        ),
    )(
        grads,
        weight,
        normed,
        tokens,
        gain.reshape(1, width),
        grad_middle,
        out_parts,
        ffn_gain_part,
    )


def deliver_kernel(count, *refs):
    sources, targets, held = refs[:count], refs[count : 2 * count], refs[2 * count : 3 * count]
    sems = refs[3 * count]
    loads = [
        pltpu.make_async_copy(source, keep, sems.at[i])
        for i, (source, keep) in enumerate(zip(sources, held))
    ]
    stores = [
        pltpu.make_async_copy(keep, target, sems.at[count + i])
        for i, (keep, target) in enumerate(zip(held, targets))
    ]
    for copy in loads:
        copy.start()
    for load, store in zip(loads, stores):
        load.wait()
        store.start()
    for copy in stores:
        copy.wait()


def deliver(*arrays):
    count = len(arrays)
    return pl.pallas_call(
        functools.partial(deliver_kernel, count),
        out_shape=tuple(jax.ShapeDtypeStruct(a.shape, a.dtype) for a in arrays),
        in_specs=[any_spec()] * count,
        out_specs=(any_spec(),) * count,
        scratch_shapes=[pltpu.VMEM(a.shape, a.dtype) for a in arrays]
        + [pltpu.SemaphoreType.DMA((2 * count,))],
        compiler_params=pltpu.CompilerParams(vmem_limit_bytes=62 * MIB),
    )(*arrays)


def fused(
    tokens,
    segment,
    attn_gain,
    query_weight,
    key_weight,
    value_weight,
    out_weight,
    ffn_gain,
    gate_weight,
    up_weight,
    down_weight,
    cotangent,
):
    line = lax.axis_size("seq")
    (
        normed_one,
        qkv,
        w_qkv,
        floor,
        attended,
        logs,
        halo_kv,
        cot_full,
        w_out,
        w_gate,
        w_up,
        middle,
    ) = forward(
        line,
        tokens,
        attn_gain,
        query_weight,
        key_weight,
        value_weight,
        segment,
        cotangent,
        out_weight,
        gate_weight.T,
        up_weight.T,
    )
    normed_two, hidden, grad_gate, grad_up, grad_normed_two, w_down, down_grad = feed(
        line, middle, ffn_gain, cot_full, w_gate, w_up, down_weight
    )
    grad_middle, ffn_gain_part, grad_attended, inner, up_grad, gate_parts, out_parts = give_back(
        line,
        grad_normed_two,
        middle,
        cotangent,
        ffn_gain,
        attended,
        w_out,
        grad_gate,
        grad_up,
        normed_two,
    )
    grads, result, gate_grad = attend_back(
        line, qkv, halo_kv, floor, logs, grad_attended, inner, hidden, w_down, middle, gate_parts
    )
    input_grad, gain_sums, query_grad, key_grad, value_grad, out_grad = finish(
        line,
        grads,
        w_qkv,
        normed_one,
        tokens,
        attn_gain,
        grad_middle,
        out_parts,
        ffn_gain_part,
    )
    (
        result,
        input_grad,
        query_grad,
        key_grad,
        value_grad,
        out_grad,
        gate_grad,
        up_grad,
        down_grad,
    ) = deliver(
        result,
        input_grad,
        query_grad,
        key_grad,
        value_grad,
        out_grad,
        gate_grad,
        up_grad,
        down_grad,
    )
    share = tokens.shape[1] // (line * lax.axis_size("head"))
    place = (lax.axis_index("seq") * lax.axis_size("head") + lax.axis_index("head")) * share
    gain_grads = lax.dynamic_slice(gain_sums, (0, place), (2, share))
    return (
        result,
        input_grad,
        gain_grads[0],
        query_grad,
        key_grad,
        value_grad,
        out_grad,
        gain_grads[1],
        gate_grad.T,
        up_grad.T,
        down_grad,
    )


def solution(mesh):
    placed = (
        P(("seq", "head"), None),
        P("seq"),
        P(),
        P("seq", "head"),
        P("seq", "head"),
        P("seq", "head"),
        P("head", "seq"),
        P(),
        P("seq", "head"),
        P("seq", "head"),
        P("head", "seq"),
        P(("seq", "head"), None),
    )
    body = fused if mesh.shape["head"] == 8 else local
    return jax.shard_map(
        body,
        mesh=mesh,
        in_specs=placed,
        out_specs=(
            P(("seq", "head"), None),
            P(("seq", "head"), None),
            P(("seq", "head")),
            P("seq", "head"),
            P("seq", "head"),
            P("seq", "head"),
            P("head", "seq"),
            P(("seq", "head")),
            P("seq", "head"),
            P("seq", "head"),
            P("head", "seq"),
        ),
        check_vma=False,
    )
```

```python
import functools

import jax
import jax.numpy as jnp
from jax import lax
from jax.experimental import pallas as pl
from jax.experimental.pallas import tpu as pltpu
from jax.sharding import PartitionSpec as P

HEAD_DIM = 128
WINDOW = 1024


EPS = 1e-06
NEG = -1e30


def from_behind(value, axis, by):
    count = lax.axis_size(axis)
    pairs = [(i, i + by) for i in range(count) if 0 <= i + by < count]
    return lax.ppermute(value, axis, pairs)


def product(left, right):
    return jnp.dot(left, right, preferred_element_type=jnp.float32)


def product_tn(left, right):
    return lax.dot_general(
        left, right, (((0,), (0,)), ((), ())), preferred_element_type=jnp.float32
    )


def product_nt(left, right):
    return lax.dot_general(
        left, right, (((1,), (1,)), ((), ())), preferred_element_type=jnp.float32
    )


def normalize(rows):
    inverse = lax.rsqrt(jnp.mean(rows * rows, axis=-1, keepdims=True) + EPS)
    return (rows * inverse, inverse)


def norm_back(unit, inverse, gain, grad):
    scaled = grad * gain
    return inverse * (scaled - unit * jnp.mean(scaled * unit, axis=-1, keepdims=True))


def gather_rows(rows):
    return lax.all_gather(rows, "head", axis=0, tiled=True)


def block_scores(query_heads, key_heads, seg_query, seg_keys, valid, start, block):
    query_part = query_heads[start : start + block]
    key_part = key_heads[start : start + block + WINDOW]
    scores = jnp.einsum(
        "qhd,khd->hqk", query_part, key_part, preferred_element_type=jnp.float32
    ) * HEAD_DIM ** (-0.5)
    rows = jnp.arange(block)[:, None] + WINDOW
    cols = jnp.arange(block + WINDOW)[None, :]
    distance = rows - cols
    same_doc = (
        seg_query[start : start + block][:, None]
        == seg_keys[start : start + block + WINDOW][None, :]
    )
    visible = (
        (distance >= 0)
        & (distance <= WINDOW)
        & same_doc
        & valid[start : start + block + WINDOW][None, :]
    )
    return jnp.where(visible[None], scores, NEG)


def local(
    tokens,
    segment,
    attn_gain,
    query_weight,
    key_weight,
    value_weight,
    out_weight,
    ffn_gain,
    gate_weight,
    up_weight,
    down_weight,
    cotangent,
):
    own_rows = tokens.shape[0]
    group = own_rows * lax.axis_size("head")
    heads_here = query_weight.shape[1] // HEAD_DIM
    offset = lax.axis_index("head") * own_rows
    seq_index = lax.axis_index("seq")
    block = min(512, group)
    scale = HEAD_DIM ** (-0.5)
    w_query, w_key, w_value, w_out, w_gate, w_up, w_down = (
        lax.all_gather(query_weight, "seq", axis=0, tiled=True),
        lax.all_gather(key_weight, "seq", axis=0, tiled=True),
        lax.all_gather(value_weight, "seq", axis=0, tiled=True),
        lax.all_gather(out_weight, "seq", axis=1, tiled=True),
        lax.all_gather(gate_weight, "seq", axis=0, tiled=True),
        lax.all_gather(up_weight, "seq", axis=0, tiled=True),
        lax.all_gather(down_weight, "seq", axis=1, tiled=True),
    )
    inputs = tokens.astype(jnp.float32)
    unit_one, inverse_one = normalize(inputs)
    normed_full = gather_rows((unit_one * attn_gain).astype(jnp.bfloat16))
    queries = product(normed_full, w_query).astype(jnp.bfloat16)
    keys = product(normed_full, w_key).astype(jnp.bfloat16)
    values = product(normed_full, w_value).astype(jnp.bfloat16)
    halo_keys, halo_values, halo_segs = ([], [], [])
    hop = 1
    take = min(group, WINDOW - (hop - 1) * group)
    got_keys, got_values, got_segs = from_behind(
        (keys[group - take :], values[group - take :], segment[group - take :]), "seq", hop
    )
    halo_keys.append(got_keys)
    halo_values.append(got_values)
    halo_segs.append(got_segs)
    keys_ext = jnp.concatenate(halo_keys + [keys], axis=0)
    values_ext = jnp.concatenate(halo_values + [values], axis=0)
    segs_ext = jnp.concatenate(halo_segs + [segment], axis=0)
    positions = seq_index * group - WINDOW + jnp.arange(WINDOW + group)
    valid = positions >= 0
    query_heads = queries.reshape(group, heads_here, HEAD_DIM)
    key_heads = keys_ext.reshape(WINDOW + group, heads_here, HEAD_DIM)
    value_heads = values_ext.reshape(WINDOW + group, heads_here, HEAD_DIM)
    outputs, logsums = ([], [])
    for start in range(0, group, block):
        scores = block_scores(query_heads, key_heads, segment, segs_ext, valid, start, block)
        highest = jnp.max(scores, axis=-1, keepdims=True)
        weights = jnp.exp(scores - highest)
        total = jnp.sum(weights, axis=-1, keepdims=True)
        probs = (weights / total).astype(jnp.bfloat16)
        outputs.append(
            jnp.einsum(
                "hqk,khd->qhd",
                probs,
                value_heads[start : start + block + WINDOW],
                preferred_element_type=jnp.float32,
            )
        )
        logsums.append(highest + jnp.log(total))
    attended = (
        jnp.concatenate(outputs, axis=0).reshape(group, heads_here * HEAD_DIM).astype(jnp.bfloat16)
    )
    partial_out = product(attended, w_out)
    own_part = lax.dynamic_slice_in_dim(partial_out, offset, own_rows, 0)
    placed = lax.dynamic_update_slice_in_dim(partial_out, own_part + inputs, offset, 0)
    middle_full = lax.psum(placed, "head")
    middle = lax.dynamic_slice_in_dim(middle_full, offset, own_rows, 0)
    unit_full, inverse_full = normalize(middle_full)
    normed_two_full = (unit_full * ffn_gain).astype(jnp.bfloat16)
    unit_two, inverse_two = normalize(middle)
    gate = product(normed_two_full, w_gate)
    up = product(normed_two_full, w_up)
    sigmoid = jax.nn.sigmoid(gate)
    activated = gate * sigmoid
    hidden = (activated * up).astype(jnp.bfloat16)
    ffn_out = lax.psum_scatter(
        product(hidden, w_down).astype(jnp.bfloat16), "head", scatter_dimension=0, tiled=True
    ).astype(jnp.float32)
    result = middle + ffn_out
    grad_out = lax.all_gather(cotangent, "head", axis=0, tiled=True)
    grad_hidden = product_nt(grad_out, w_down)
    grad_gate = (grad_hidden * up * sigmoid * (1.0 + gate * (1.0 - sigmoid))).astype(jnp.bfloat16)
    grad_up = (grad_hidden * activated).astype(jnp.bfloat16)
    down_grad = product_tn(hidden, grad_out)
    gate_grad = product_tn(normed_two_full, grad_gate)
    up_grad = product_tn(normed_two_full, grad_up)
    grad_normed_two = lax.psum_scatter(
        (product_nt(grad_gate, w_gate) + product_nt(grad_up, w_up)).astype(jnp.bfloat16),
        "head",
        scatter_dimension=0,
        tiled=True,
    ).astype(jnp.float32)
    ffn_gain_part = jnp.sum(grad_normed_two * unit_two, axis=0)
    grad_middle = cotangent.astype(jnp.float32) + norm_back(
        unit_two, inverse_two, ffn_gain, grad_normed_two
    )
    grad_branch = lax.all_gather(grad_middle.astype(jnp.bfloat16), "head", axis=0, tiled=True)
    out_grad = product_tn(attended, grad_branch)
    grad_attended = product_nt(grad_branch, w_out).astype(jnp.bfloat16)
    grad_heads = grad_attended.reshape(group, heads_here, HEAD_DIM)
    grad_query_list = []
    grad_keys_ext = jnp.zeros((WINDOW + group, heads_here, HEAD_DIM), jnp.float32)
    grad_values_ext = jnp.zeros((WINDOW + group, heads_here, HEAD_DIM), jnp.float32)
    for number, start in enumerate(range(0, group, block)):
        scores = block_scores(query_heads, key_heads, segment, segs_ext, valid, start, block)
        probs = jnp.exp(scores - logsums[number])
        probs_low = probs.astype(jnp.bfloat16)
        key_part = key_heads[start : start + block + WINDOW]
        value_part = value_heads[start : start + block + WINDOW]
        query_part = query_heads[start : start + block]
        grad_part = grad_heads[start : start + block]
        grad_probs = jnp.einsum(
            "qhd,khd->hqk", grad_part, value_part, preferred_element_type=jnp.float32
        )
        inner = jnp.sum(probs * grad_probs, axis=-1, keepdims=True)
        grad_scores = (probs * (grad_probs - inner)).astype(jnp.bfloat16)
        grad_query_list.append(
            jnp.einsum("hqk,khd->qhd", grad_scores, key_part, preferred_element_type=jnp.float32)
            * scale
        )
        key_term = (
            jnp.einsum("hqk,qhd->khd", grad_scores, query_part, preferred_element_type=jnp.float32)
            * scale
        )
        value_term = jnp.einsum(
            "hqk,qhd->khd", probs_low, grad_part, preferred_element_type=jnp.float32
        )
        grad_keys_ext = grad_keys_ext.at[start : start + block + WINDOW].add(key_term)
        grad_values_ext = grad_values_ext.at[start : start + block + WINDOW].add(value_term)
    grad_keys_ext = grad_keys_ext.reshape(WINDOW + group, heads_here * HEAD_DIM)
    grad_values_ext = grad_values_ext.reshape(WINDOW + group, heads_here * HEAD_DIM)
    grad_keys = grad_keys_ext[WINDOW:]
    grad_values = grad_values_ext[WINDOW:]
    cursor = 0
    hop = 1
    take = min(group, WINDOW - (hop - 1) * group)
    back_keys = from_behind(
        grad_keys_ext[cursor : cursor + take].astype(jnp.bfloat16), "seq", -hop
    ).astype(jnp.float32)
    back_values = from_behind(
        grad_values_ext[cursor : cursor + take].astype(jnp.bfloat16), "seq", -hop
    ).astype(jnp.float32)
    grad_keys = grad_keys.at[group - take :].add(back_keys)
    grad_values = grad_values.at[group - take :].add(back_values)
    grad_queries = (
        jnp.concatenate(grad_query_list, axis=0)
        .reshape(group, heads_here * HEAD_DIM)
        .astype(jnp.bfloat16)
    )
    grad_keys = grad_keys.astype(jnp.bfloat16)
    grad_values = grad_values.astype(jnp.bfloat16)
    query_grad = product_tn(normed_full, grad_queries)
    key_grad = product_tn(normed_full, grad_keys)
    value_grad = product_tn(normed_full, grad_values)
    grad_normed_one = lax.psum_scatter(
        (
            product_nt(grad_queries, w_query)
            + product_nt(grad_keys, w_key)
            + product_nt(grad_values, w_value)
        ).astype(jnp.bfloat16),
        "head",
        scatter_dimension=0,
        tiled=True,
    ).astype(jnp.float32)
    attn_gain_part = jnp.sum(grad_normed_one * unit_one, axis=0)
    input_grad = grad_middle + norm_back(unit_one, inverse_one, attn_gain, grad_normed_one)
    summed = (
        lax.psum_scatter(
            query_grad.astype(jnp.bfloat16), "seq", scatter_dimension=0, tiled=True
        ).astype(jnp.float32),
        lax.psum_scatter(
            key_grad.astype(jnp.bfloat16), "seq", scatter_dimension=0, tiled=True
        ).astype(jnp.float32),
        lax.psum_scatter(
            value_grad.astype(jnp.bfloat16), "seq", scatter_dimension=0, tiled=True
        ).astype(jnp.float32),
        lax.psum_scatter(
            out_grad.astype(jnp.bfloat16), "seq", scatter_dimension=1, tiled=True
        ).astype(jnp.float32),
        lax.psum_scatter(
            gate_grad.astype(jnp.bfloat16), "seq", scatter_dimension=0, tiled=True
        ).astype(jnp.float32),
        lax.psum_scatter(
            up_grad.astype(jnp.bfloat16), "seq", scatter_dimension=0, tiled=True
        ).astype(jnp.float32),
        lax.psum_scatter(
            down_grad.astype(jnp.bfloat16), "seq", scatter_dimension=1, tiled=True
        ).astype(jnp.float32),
    )
    gain_grads = (
        lax.psum_scatter(attn_gain_part, ("seq", "head"), scatter_dimension=0, tiled=True),
        lax.psum_scatter(ffn_gain_part, ("seq", "head"), scatter_dimension=0, tiled=True),
    )
    return (
        result.astype(jnp.bfloat16),
        input_grad,
        gain_grads[0],
        summed[0],
        summed[1],
        summed[2],
        summed[3],
        gain_grads[1],
        summed[4],
        summed[5],
        summed[6],
    )


MESH = pl.DeviceIdType.MESH
BF16 = jnp.bfloat16
F32 = jnp.float32
MIB = 2**20


def remote(src, dst, send_sem, recv_sem, where):
    return pltpu.make_async_remote_copy(
        src_ref=src,
        dst_ref=dst,
        send_sem=send_sem,
        recv_sem=recv_sem,
        device_id=where,
        device_id_type=MESH,
    )


class Place:
    def __init__(self, line):
        s, h = lax.axis_index("seq"), lax.axis_index("head")
        core = lax.rem(h, 2)
        x = lax.rem(lax.div(h, 2), 2)
        y = lax.div(h, 4)
        self.s, self.h, self.line = s, h, line
        self.turn = 1 - 2 * core
        self.core = h + self.turn
        over_x, over_y = 2 - 4 * x, 4 - 8 * y
        self.first = h + over_x * (1 - core) + over_y * core
        self.second = h + over_y * (1 - core) + over_x * core
        self.across = h + over_x + over_y

    def at(self, head):
        return (self.s, head)

    def greet(self, along_seq=True):
        barrier = pltpu.get_barrier_semaphore()
        for head in (self.core, self.first, self.second):
            pl.semaphore_signal(barrier, inc=1, device_id=self.at(head), device_id_type=MESH)
        if along_seq:

            @pl.when(self.s > 0)
            def _():
                pl.semaphore_signal(
                    barrier, inc=1, device_id=(self.s - 1, self.h), device_id_type=MESH
                )

            @pl.when(self.s < self.line - 1)
            def _():
                pl.semaphore_signal(
                    barrier, inc=1, device_id=(self.s + 1, self.h), device_id_type=MESH
                )

            @pl.when((self.s > 0) & (self.s < self.line - 1))
            def _():
                pl.semaphore_wait(barrier, 5)

            @pl.when((self.s == 0) | (self.s == self.line - 1))
            def _():
                pl.semaphore_wait(barrier, 4)
        else:
            pl.semaphore_wait(barrier, 3)


def greet_line(place):
    p = place
    barrier = pltpu.get_barrier_semaphore()
    for head in (p.core, p.first, p.second):
        pl.semaphore_signal(barrier, inc=1, device_id=p.at(head), device_id_type=MESH)
    for k in range(1, p.line):
        pl.semaphore_signal(
            barrier, inc=1, device_id=(lax.rem(p.s + k, p.line), p.h), device_id_type=MESH
        )
    pl.semaphore_wait(barrier, 2 + p.line)


class HeadGather:
    SEMS = 7

    def __init__(self, place, block, send, recv, own=None):
        p = place
        self.p = p
        plan = (
            (p.h, p.first, p.first),
            (p.h, p.second, p.second),
            (p.h, p.core, p.core),
            (p.first, p.second, p.across),
            (p.first, p.core, p.second + p.turn),
            (p.second, p.core, p.first + p.turn),
            (p.across, p.core, p.across + p.turn),
        )
        self.out = [
            remote(
                block(j) if own is None or i > 2 else own,
                block(j),
                send.at[i],
                recv.at[i],
                p.at(to),
            )
            for i, (j, to, _) in enumerate(plan)
        ]
        self.come = [
            remote(block(j), block(j), send.at[i], recv.at[i], p.at(to))
            for i, (_, to, j) in enumerate(plan)
        ]

    def start(self):
        for i in (0, 1, 2):
            self.out[i].start()

    def got_first(self):
        self.come[0].wait_recv()
        self.out[3].start()
        self.out[4].start()

    def got_second(self):
        self.come[1].wait_recv()
        self.out[5].start()

    def got_across(self):
        self.come[3].wait_recv()
        self.out[6].start()

    def got_core(self):
        self.come[2].wait_recv()

    def got_core_second(self):
        self.come[4].wait_recv()

    def got_core_first(self):
        self.come[5].wait_recv()

    def got_core_across(self):
        self.come[6].wait_recv()

    def finish(self):
        for copy in self.out:
            copy.wait_send()


class LineGather:
    def __init__(self, place, piece, up_send, up_recv, down_send, down_recv, own=None):
        self.p, self.piece, self.own = place, piece, own
        self.up = (up_send, up_recv)
        self.down = (down_send, down_recv)

    def _up(self, owner, t):
        p = self.p
        source = self.own if t == 0 and self.own is not None else self.piece(owner)
        return remote(
            source, self.piece(owner), self.up[0].at[t], self.up[1].at[t], (p.s + 1, p.h)
        )

    def _down(self, owner, t):
        p = self.p
        source = self.own if t == 0 and self.own is not None else self.piece(owner)
        return remote(
            source,
            self.piece(owner),
            self.down[0].at[t],
            self.down[1].at[t],
            (p.s - 1, p.h),
        )

    def start(self, t):
        p = self.p

        @pl.when((p.s < p.line - 1) & (p.s >= t))
        def _():
            self._up(p.s - t, t).start()

        @pl.when((p.s > 0) & (p.s + t < p.line))
        def _():
            self._down(p.s + t, t).start()

    def got(self, t):
        p = self.p

        @pl.when(p.s >= t + 1)
        def _():
            self._up(p.s - 1 - t, t).wait_recv()

        @pl.when(p.s + 1 + t < p.line)
        def _():
            self._down(p.s + 1 + t, t).wait_recv()

    def step(self, t):
        self.got(t)
        if t + 1 < self.p.line - 1:
            self.start(t + 1)

    def finish(self):
        p = self.p
        for t in range(p.line - 1):

            @pl.when((p.s < p.line - 1) & (p.s >= t))
            def _():
                self._up(p.s - t, t).wait_send()

            @pl.when((p.s > 0) & (p.s + t < p.line))
            def _():
                self._down(p.s + t, t).wait_send()


def line_sems(line, tensors=1):
    return [pltpu.SemaphoreType.DMA((line - 1,)) for _ in range(4 * tensors)]


def norm_rows(rows, gain):
    inverse = lax.rsqrt(jnp.mean(rows * rows, axis=-1, keepdims=True) + EPS)
    return rows * inverse * gain


def own_starts(segment):
    count = segment.shape[1]
    ids = segment[...]
    place = lax.broadcasted_iota(jnp.int32, (1, count), 1)
    starts = jnp.where((place > 0) & (ids != pltpu.roll(ids, 1, 1)), place, -1)
    shift = 1
    while shift < count:
        earlier = jnp.where(place >= shift, pltpu.roll(starts, shift, 1), -1)
        starts = jnp.maximum(starts, earlier)
        shift *= 2
    return starts


def any_spec():
    return pl.BlockSpec(memory_space=pl.ANY)


def vmem_spec():
    return pl.BlockSpec(memory_space=pltpu.VMEM)


LOG2E = 1.4426950408889634
TILE = 256
CHUNKS = WINDOW // TILE + 1


def tile_scores(tile, head, q, k_ext, floor):
    start = pl.multiple_of(tile * TILE, TILE)
    cols = slice(head * HEAD_DIM, (head + 1) * HEAD_DIM)
    queries = q[pl.ds(start, TILE), cols]
    row = lax.broadcasted_iota(jnp.int32, (TILE, TILE), 0)
    lane = lax.broadcasted_iota(jnp.int32, (TILE, TILE), 1)
    lowest = floor[:, pl.ds(start, TILE)] - start
    found = []
    for i in range(CHUNKS):
        keys = k_ext[pl.ds(start + i * TILE, TILE), cols]
        scores = product_nt(keys, queries)
        visible = row >= lowest - i * TILE
        if i == CHUNKS - 1:
            visible = visible & (row <= lane)
        found.append((scores, visible))
    return found


def forward_tile(tile, q, k_ext, v_t, floor, attended, logs):
    start = pl.multiple_of(tile * TILE, TILE)
    sharp = HEAD_DIM ** (-0.5) * LOG2E
    for head in range(q.shape[1] // HEAD_DIM):
        cols = slice(head * HEAD_DIM, (head + 1) * HEAD_DIM)
        found = [
            jnp.where(visible, scores, NEG)
            for scores, visible in tile_scores(tile, head, q, k_ext, floor)
        ]
        highest = functools.reduce(
            jnp.maximum, [jnp.max(scores, axis=0, keepdims=True) for scores in found]
        )
        total = jnp.zeros((1, TILE), F32)
        mixed = jnp.zeros((HEAD_DIM, TILE), F32)
        for i, scores in enumerate(found):
            weights = jnp.exp2((scores - highest) * sharp)
            total = total + jnp.sum(weights, axis=0, keepdims=True)
            mixed = mixed + product(
                v_t[cols, pl.ds(start + i * TILE, TILE)], weights.astype(BF16)
            )
        attended[pl.ds(start, TILE), cols] = (mixed / total).astype(BF16).T
        logs[head : head + 1, pl.ds(start, TILE)] = highest * sharp + jnp.log2(total)


def block_reduce(place, out, into, r_send, r_recv):
    p = place
    goes = (p.core, p.core, p.core, p.core, p.first, p.first, p.second)
    slots = (0, 1, 0, 1, 2, 3, 4)
    return [
        remote(out.at[slots[i]], into.at[i], r_send.at[i], r_recv.at[i], p.at(to))
        for i, to in enumerate(goes)
    ]


def forward_kernel(
    line,
    tokens,
    gain,
    wq,
    wk,
    wv,
    segment,
    cot,
    w_out,
    w_gate,
    w_up,
    normed_out,
    qkv_out,
    weight_out,
    floor,
    attended,
    logs,
    halo_out,
    cot_out,
    w_out_out,
    gate_full,
    up_full,
    middle,
    normed,
    weight,
    q,
    k_ext,
    v_ext,
    v_t,
    w_out_full,
    seg_halo,
    out,
    into,
    g_send,
    g_recv,
    c_send,
    c_recv,
    r_send,
    r_recv,
    halo_send,
    halo_recv,
    seg_sems,
    keep,
    *sems,
):
    p = Place(line)
    qkv_sems, out_sems, gate_sems, up_sems = sems[0:4], sems[4:8], sems[8:12], sems[12:16]
    rows, width = tokens.shape
    slab, part = wq.shape
    count = segment.shape[1]
    rows_of = lambda ref, j: ref.at[pl.ds(pl.multiple_of(j * rows, rows), rows)]
    slab_of = lambda d: weight.at[pl.ds(pl.multiple_of(d * slab, slab), slab)]
    weight_own = slab_of(p.s)
    weight_own[:, 0:part] = wq[...]
    weight_own[:, part : 2 * part] = wk[...]
    weight_own[:, 2 * part : 3 * part] = wv[...]
    seg_copy = remote(
        segment.at[:, pl.ds(count - WINDOW, WINDOW)],
        seg_halo,
        seg_sems.at[0],
        seg_sems.at[1],
        (p.s + 1, p.h),
    )
    halo = [
        remote(
            ext.at[pl.ds(count, WINDOW)],
            ext.at[pl.ds(0, WINDOW)],
            halo_send.at[i],
            halo_recv.at[i],
            (p.s + 1, p.h),
        )
        for i, ext in enumerate((k_ext, v_ext))
    ]
    gather = HeadGather(p, lambda j: rows_of(normed, j), g_send, g_recv)
    cot_gather = HeadGather(p, lambda j: rows_of(cot_out, j), c_send, c_recv, own=cot)
    qkv_gather = LineGather(p, slab_of, *qkv_sems)
    out_gather = LineGather(p, lambda d: w_out_full.at[d], *out_sems, own=w_out)
    gate_gather = LineGather(p, lambda d: gate_full.at[d], *gate_sems, own=w_gate)
    up_gather = LineGather(p, lambda d: up_full.at[d], *up_sems, own=w_up)
    p.greet()
    qkv_gather.start(0)

    @pl.when(p.s < line - 1)
    def _():
        seg_copy.start()

    mine = rows_of(normed, p.h)
    step = 32

    @pl.loop(0, rows // step)
    def _(i):
        at = pl.ds(pl.multiple_of(i * step, step), step)
        mine[at] = norm_rows(tokens[at].astype(F32), gain[...]).astype(BF16)

    gather.start()
    saved = []

    def save(source, target):
        copy = pltpu.make_async_copy(source, target, keep.at[len(saved)])
        copy.start()
        saved.append(copy)

    def save_block(j):
        save(rows_of(normed, j), rows_of(normed_out, j))

    save_block(p.h)
    save(cot, rows_of(cot_out, p.h))
    save(w_out, w_out_full.at[p.s])
    own_w_out = saved[-1]
    save(w_gate, gate_full.at[p.s])
    save(w_up, up_full.at[p.s])
    starts = own_starts(segment)

    @pl.when(p.s == 0)
    def _():
        k_ext[0:WINDOW, :] = jnp.zeros((WINDOW, part), BF16)
        v_ext[0:WINDOW, :] = jnp.zeros((WINDOW, part), BF16)

    @pl.when(p.s > 0)
    def _():
        seg_copy.wait_recv()

    before = jnp.sum(
        (seg_halo[...] == segment[:, 0:1]).astype(jnp.int32), axis=1, keepdims=True
    )
    before = jnp.where(p.s > 0, before, 0)
    floor[...] = jnp.maximum(
        lax.broadcasted_iota(jnp.int32, (1, count), 1),
        jnp.where(starts >= 0, starts + WINDOW, WINDOW - before),
    )
    gather.got_core()
    save_block(p.core)
    qkv_gather.step(0)
    gather.got_first()
    gather.got_second()
    cot_gather.start()
    save_block(p.first)
    save_block(p.second)
    qkv_gather.step(1)
    out_gather.start(0)
    gather.got_core_second()
    gather.got_core_first()
    save_block(p.second + p.turn)
    save_block(p.first + p.turn)
    qkv_gather.step(2)
    gather.got_across()
    save_block(p.across)
    gather.got_core_across()
    save_block(p.across + p.turn)
    save(weight, weight_out)

    def multiply(first, last):
        @pl.loop(first, last)
        def _(n):
            start = pl.multiple_of((count // rows - 1 - n) * rows, rows)
            value = product(normed[pl.ds(start, rows), :], weight[...]).astype(BF16)
            q[pl.ds(start, rows), :] = value[:, 0:part]
            k_ext[pl.ds(start + WINDOW, rows), :] = value[:, part : 2 * part]
            v_ext[pl.ds(start + WINDOW, rows), :] = value[:, 2 * part : 3 * part]

    late = (WINDOW + rows - 1) // rows
    multiply(0, late)

    @pl.when(p.s < line - 1)
    def _():
        halo[0].start()
        halo[1].start()

    multiply(late, count // rows)
    multiply(late, count // rows)
    out_gather.step(0)
    gate_gather.start(0)
    save(q, qkv_out.at[:, pl.ds(0, part)])
    save(k_ext.at[pl.ds(WINDOW, count)], qkv_out.at[:, pl.ds(part, part)])
    save(v_ext.at[pl.ds(WINDOW, count)], qkv_out.at[:, pl.ds(2 * part, part)])

    def turn(first, last):
        @pl.loop(first, last)
        def _(i):
            at = pl.ds(pl.multiple_of(i * TILE, TILE), TILE)
            v_t[:, at] = v_ext[at, :].T

    def tiles(first, last):
        @pl.loop(first, last)
        def _(tile):
            forward_tile(tile, q, k_ext, v_t, floor, attended, logs)

    ahead = WINDOW // TILE
    turn(ahead, ahead + count // TILE)
    tiles(ahead, ahead + 5)
    cot_gather.got_core()
    cot_gather.got_first()
    cot_gather.got_second()
    out_gather.step(1)
    up_gather.start(0)
    tiles(ahead + 5, count // TILE)

    @pl.when(p.s > 0)
    def _():
        halo[0].wait_recv()
        halo[1].wait_recv()

    turn(0, ahead)
    tiles(0, 2)
    cot_gather.got_core_second()
    cot_gather.got_core_first()
    cot_gather.got_across()
    gate_gather.step(0)
    tiles(2, ahead)
    out_gather.step(2)
    for i, ext in enumerate((k_ext, v_ext)):
        save(ext.at[pl.ds(0, WINDOW)], halo_out.at[i])
    own_w_out.wait()
    save(w_out_full, w_out_out)
    copies = block_reduce(p, out, into, r_send, r_recv)

    def emit(j, target, *more):
        start = pl.multiple_of(j * rows, rows)

        for n in range(line):
            cols = slice(n * slab, (n + 1) * slab)
            value = product(attended[pl.ds(start, rows), :], w_out_full[n])
            for other in more:
                value = value + other[:, cols].astype(F32)
            target[:, cols] = value.astype(target.dtype)

    emit(p.second + p.turn, out.at[0])
    copies[0].start()
    emit(p.across + p.turn, out.at[1])
    copies[1].start()
    copies[0].wait_recv()
    emit(p.first, out.at[2], into.at[0])
    copies[4].start()
    copies[0].wait_send()
    emit(p.first + p.turn, out.at[0])
    copies[2].start()
    copies[1].wait_recv()
    emit(p.across, out.at[3], into.at[1])
    copies[5].start()
    copies[1].wait_send()
    emit(p.core, out.at[1])
    copies[3].start()
    copies[3].wait_recv()
    emit(p.h, middle, into.at[3], tokens)
    up_gather.step(0)
    gate_gather.step(1)
    copies[2].wait_recv()
    cot_gather.got_core_across()
    up_gather.step(1)
    copies[5].wait_recv()
    emit(p.second, out.at[4], into.at[2], into.at[5])
    copies[6].start()
    gate_gather.step(2)
    copies[4].wait_recv()
    up_gather.step(2)
    copies[6].wait_recv()

    @pl.loop(0, line)
    def _(n):
        cols = pl.ds(pl.multiple_of(n * slab, slab), slab)
        middle[:, cols] += into[4, :, cols].astype(F32) + into[6, :, cols].astype(F32)

    for i in range(2, 7):
        copies[i].wait_send()
    gather.finish()
    cot_gather.finish()
    for each in (qkv_gather, out_gather, gate_gather, up_gather):
        each.finish()

    @pl.when(p.s < line - 1)
    def _():
        seg_copy.wait_send()
        halo[0].wait_send()
        halo[1].wait_send()

    for copy in saved:
        if copy is not own_w_out:
            copy.wait()


def forward(line, tokens, gain, wq, wk, wv, segment, cot, w_out, w_gate, w_up):
    rows, width = tokens.shape
    slab, part = wq.shape
    full = rows * 8
    units = w_gate.shape[0]
    heads = part // HEAD_DIM
    return pl.pallas_call(
        functools.partial(forward_kernel, line),
        out_shape=(
            jax.ShapeDtypeStruct((full, width), BF16),
            jax.ShapeDtypeStruct((full, 3 * part), BF16),
            jax.ShapeDtypeStruct((width, 3 * part), BF16),
            jax.ShapeDtypeStruct((1, full), jnp.int32),
            jax.ShapeDtypeStruct((full, part), BF16),
            jax.ShapeDtypeStruct((heads, full), F32),
            jax.ShapeDtypeStruct((2, WINDOW, part), BF16),
            jax.ShapeDtypeStruct((full, width), BF16),
            jax.ShapeDtypeStruct((line, part, slab), BF16),
            jax.ShapeDtypeStruct((line, units, slab), BF16),
            jax.ShapeDtypeStruct((line, units, slab), BF16),
            jax.ShapeDtypeStruct((rows, width), F32),
        ),
        in_specs=[vmem_spec()] * 10,
        out_specs=(
            any_spec(),
            any_spec(),
            any_spec(),
            vmem_spec(),
            vmem_spec(),
            vmem_spec(),
            any_spec(),
            any_spec(),
            any_spec(),
            any_spec(),
            any_spec(),
            vmem_spec(),
        ),
        scratch_shapes=[
            pltpu.VMEM((full, width), BF16),
            pltpu.VMEM((width, 3 * part), BF16),
            pltpu.VMEM((full, part), BF16),
            pltpu.VMEM((WINDOW + full, part), BF16),
            pltpu.VMEM((WINDOW + full, part), BF16),
            pltpu.VMEM((part, WINDOW + full), BF16),
            pltpu.VMEM((line, part, slab), BF16),
            pltpu.VMEM((1, WINDOW), jnp.int32),
            pltpu.VMEM((5, rows, width), BF16),
            pltpu.VMEM((7, rows, width), BF16),
            pltpu.SemaphoreType.DMA((7,)),
            pltpu.SemaphoreType.DMA((7,)),
            pltpu.SemaphoreType.DMA((7,)),
            pltpu.SemaphoreType.DMA((7,)),
            pltpu.SemaphoreType.DMA((7,)),
            pltpu.SemaphoreType.DMA((7,)),
            pltpu.SemaphoreType.DMA((2,)),
            pltpu.SemaphoreType.DMA((2,)),
            pltpu.SemaphoreType.DMA((2,)),
            pltpu.SemaphoreType.DMA((19,)),
            *line_sems(line, 4),
        ],
        compiler_params=pltpu.CompilerParams(
            collective_id=1, has_side_effects=True, vmem_limit_bytes=62 * MIB
        ),
        cost_estimate=pl.CostEstimate(
            flops=20 * 2**30, bytes_accessed=100 * MIB, transcendentals=0
        ),
    )(tokens, gain.reshape(1, width), wq, wk, wv, segment.reshape(1, full), cot, w_out, w_gate, w_up)


def sigmoid_of(value):
    return 0.5 * jnp.tanh(0.5 * value) + 0.5


def strips(width, most=256):
    return [(start, min(start + most, width)) for start in range(0, width, most)]


def feed_kernel(
    line,
    middle,
    gain,
    cot,
    gate,
    up,
    down,
    normed_out,
    hidden_out,
    grad_gate_out,
    grad_up_out,
    grad_out,
    down_out,
    down_grad,
    normed,
    w_gate,
    w_up,
    w_down,
    gates,
    ups,
    cot_block,
    hidden,
    grad_gate,
    grad_up,
    down_parts,
    down_up_in,
    down_down_in,
    out,
    into,
    r_send,
    r_recv,
    g_send,
    g_recv,
    *sems,
):
    p = Place(line)
    down_sems, sum_sems, loads, saves, stage, strip_sems = sems[0:4], sems[4:8], *sems[8:12]
    rows, width = grad_out.shape
    units = w_down.shape[1]
    slab = w_down.shape[2]
    block = lambda j: normed.at[pl.ds(pl.multiple_of(j * rows, rows), rows)]
    rows_of = lambda ref, j: ref.at[pl.ds(pl.multiple_of(j * rows, rows), rows)]
    gather = HeadGather(p, block, g_send, g_recv)
    down_gather = LineGather(p, lambda d: w_down.at[d], *down_sems, own=down)
    p.greet()
    down_gather.start(0)
    started = [
        pltpu.make_async_copy(middle, grad_out, loads.at[0]),
        pltpu.make_async_copy(gate, w_gate, loads.at[1]),
        pltpu.make_async_copy(up, w_up, loads.at[3]),
        pltpu.make_async_copy(down, w_down.at[p.s], loads.at[4]),
    ]
    for copy in started:
        copy.start()
    started[0].wait()
    mine = block(p.h)
    step = 32

    @pl.loop(0, rows // step)
    def _(i):
        at = pl.ds(pl.multiple_of(i * step, step), step)
        mine[at] = norm_rows(grad_out[at], gain[...]).astype(BF16)

    gather.out[0].start()
    gather.out[2].start()
    saved = []

    def save(j):
        copy = pltpu.make_async_copy(block(j), rows_of(normed_out, j), saves.at[len(saved)])
        copy.start()
        saved.append(copy)

    opened = (
        p.h,
        p.core,
        p.first,
        p.second + p.turn,
        p.first + p.turn,
        p.second,
        p.across + p.turn,
        p.across,
    )
    hidden_stores = [
        pltpu.make_async_copy(hidden.at[m % 2], rows_of(hidden_out, j), stage.at[m % 2])
        for m, j in enumerate(opened)
    ]

    def open_up(m, slot):
        start = pl.multiple_of(opened[m] * rows, rows)
        if m > 1:
            hidden_stores[m - 2].wait()
        for first, last in strips(units):
            found = []
            for weight in (w_gate, w_up):
                value = product_nt(normed[pl.ds(start, rows), 0:slab], weight[0, first:last, :])
                for d in range(1, line):
                    value = value + product_nt(
                        normed[pl.ds(start, rows), d * slab : (d + 1) * slab],
                        weight[d, first:last, :],
                    )
                found.append(value)
            value, lift = found
            gates[slot, :, first:last] = value.astype(BF16)
            ups[slot, :, first:last] = lift.astype(BF16)
            hidden[m % 2, :, first:last] = (value * sigmoid_of(value) * lift).astype(BF16)
        hidden_stores[m].start()

    order = (
        p.second + p.turn,
        p.first,
        p.across + p.turn,
        p.across,
        p.first + p.turn,
        p.second,
        p.core,
        p.h,
    )
    fetches = [
        pltpu.make_async_copy(rows_of(cot, j), cot_block, stage.at[6]) for j in order
    ]
    stores = [
        [
            pltpu.make_async_copy(
                held.at[n % 2], rows_of(home, j), stage.at[2 + 2 * (n % 2) + i]
            )
            for i, (held, home) in enumerate(
                ((grad_gate, grad_gate_out), (grad_up, grad_up_out))
            )
        ]
        for n, j in enumerate(order)
    ]

    def close(n, slot):
        fetches[n].wait()
        if n > 1:
            for copy in stores[n - 2]:
                copy.wait()
        turn = n % 2
        for first, last in strips(units):
            grad = product_nt(cot_block[:, 0:slab], w_down[0, first:last, :])
            for d in range(1, line):
                grad = grad + product_nt(
                    cot_block[:, d * slab : (d + 1) * slab], w_down[d, first:last, :]
                )
            gate = gates[slot, :, first:last].astype(F32)
            lift = ups[slot, :, first:last].astype(F32)
            sigmoid = sigmoid_of(gate)
            grad_up[turn, :, first:last] = (grad * gate * sigmoid).astype(BF16)
            grad_gate[turn, :, first:last] = (
                grad * lift * (sigmoid * (1.0 + gate * (1.0 - sigmoid)))
            ).astype(BF16)
        if n + 1 < len(order):
            fetches[n + 1].start()
        for copy in stores[n]:
            copy.start()

    def back(n, target, *more):
        turn = n % 2

        for d in range(line):
            cols = slice(d * slab, (d + 1) * slab)
            value = product(grad_gate[turn], w_gate[d]) + product(grad_up[turn], w_up[d])
            for other in more:
                value = value + other[:, cols].astype(F32)
            target[:, cols] = value.astype(target.dtype)

    copies = block_reduce(p, out, into, r_send, r_recv)
    down_reduce = LineReduce(
        p, lambda d: down_parts.at[d], down_up_in, down_down_in, *sum_sems
    )
    wide = slab
    padded = hidden.shape[2]
    kept = slice(2 * wide, 2 * wide + units)
    hidden[:, :, units // 128 * 128 :] = jnp.zeros((2, rows, padded - units // 128 * 128), BF16)
    multiply = lambda *some: weight_product(
        lambda rows_in: product_tn(normed[:, kept], rows_in),
        cot,
        lambda d: down_parts.at[d],
        lambda k: normed.at[:, pl.ds(pl.multiple_of(k * wide, wide), wide)],
        wide,
        strip_sems,
        p,
        *some,
    )
    fetches[0].start()
    for copy in started[1:3]:
        copy.wait()
    save(p.h)
    open_up(0, 0)
    gather.got_core()
    save(p.core)
    open_up(1, 1)
    gather.out[0].wait_send()
    gather.out[1].start()
    gather.got_first()
    save(p.first)
    down_gather.step(0)
    open_up(2, 2)
    gather.got_core_second()
    save(p.second + p.turn)
    open_up(3, 3)
    down_gather.step(1)
    gather.got_second()
    save(p.second)
    gather.got_core_first()
    save(p.first + p.turn)
    open_up(4, 4)
    open_up(5, 5)
    clear_last(down_reduce)
    down_gather.step(2)
    started[3].wait()
    down_save = pltpu.make_async_copy(w_down, down_out, loads.at[4])
    down_save.start()
    close(0, 3)
    back(0, out.at[0])
    copies[0].start()
    gather.got_across()
    save(p.across)
    close(1, 2)
    copies[0].wait_recv()
    back(1, out.at[2], into.at[0])
    copies[4].start()
    gather.got_core_across()
    save(p.across + p.turn)
    open_up(6, 2)
    open_up(7, 3)
    for copy in gather.out[1:]:
        copy.wait_send()
    for copy in saved:
        copy.wait()
    for copy in hidden_stores[6:]:
        copy.wait()
    fill = pltpu.make_async_copy(hidden_out, normed.at[:, pl.ds(2 * wide, padded)], loads.at[5])
    fill.start()
    fill.wait()
    multiply(0, 1)
    down_reduce.start(0)
    multiply(1, 2)
    close(2, 2)
    back(2, out.at[1])
    copies[1].start()
    close(3, 3)
    copies[1].wait_recv()
    back(3, out.at[3], into.at[1])
    copies[5].start()
    down_reduce.step(0)
    multiply(2, line)
    close(4, 4)
    copies[0].wait_send()
    back(4, out.at[0])
    copies[2].start()
    close(5, 5)
    copies[2].wait_recv()
    copies[5].wait_recv()
    back(5, out.at[4], into.at[2], into.at[5])
    copies[6].start()
    down_reduce.step(1)
    close(6, 1)
    copies[1].wait_send()
    back(6, out.at[1])
    copies[3].start()
    close(7, 0)
    copies[3].wait_recv()
    back(7, grad_out, into.at[3])
    copies[4].wait_recv()
    copies[6].wait_recv()

    @pl.loop(0, line)
    def _(d):
        cols = pl.ds(pl.multiple_of(d * slab, slab), slab)
        grad_out[:, cols] += into[4, :, cols].astype(F32) + into[6, :, cols].astype(F32)

    down_reduce.step(2)
    for first, last in strips(units, 128):
        down_grad[first:last, :] = down_reduce.total(slice(first, last))
    for i in range(2, 7):
        copies[i].wait_send()
    down_gather.finish()
    down_reduce.finish()
    for copy in stores[6] + stores[7]:
        copy.wait()
    down_save.wait()


def feed(line, middle, gain, cot, gate, up, down):
    rows, width = middle.shape
    units, slab = down.shape
    full = rows * 8
    padded = (units + 127) // 128 * 128
    return pl.pallas_call(
        functools.partial(feed_kernel, line),
        out_shape=(
            jax.ShapeDtypeStruct((full, width), BF16),
            jax.ShapeDtypeStruct((full, padded), BF16),
            jax.ShapeDtypeStruct((full, units), BF16),
            jax.ShapeDtypeStruct((full, units), BF16),
            jax.ShapeDtypeStruct((rows, width), F32),
            jax.ShapeDtypeStruct((line, units, slab), BF16),
            jax.ShapeDtypeStruct((units, slab), F32),
        ),
        in_specs=[any_spec(), vmem_spec()] + [any_spec()] * 4,
        out_specs=(
            any_spec(),
            any_spec(),
            any_spec(),
            any_spec(),
            vmem_spec(),
            any_spec(),
            vmem_spec(),
        ),
        scratch_shapes=[
            pltpu.VMEM((full, width), BF16),
            pltpu.VMEM((line, units, slab), BF16),
            pltpu.VMEM((line, units, slab), BF16),
            pltpu.VMEM((line, units, slab), BF16),
            pltpu.VMEM((6, rows, units), BF16),
            pltpu.VMEM((6, rows, units), BF16),
            pltpu.VMEM((rows, width), BF16),
            pltpu.VMEM((2, rows, padded), BF16),
            pltpu.VMEM((2, rows, units), BF16),
            pltpu.VMEM((2, rows, units), BF16),
            pltpu.VMEM((line, units, slab), BF16),
            pltpu.VMEM((line - 1, units, slab), BF16),
            pltpu.VMEM((line - 1, units, slab), BF16),
            pltpu.VMEM((5, rows, width), BF16),
            pltpu.VMEM((7, rows, width), BF16),
            pltpu.SemaphoreType.DMA((7,)),
            pltpu.SemaphoreType.DMA((7,)),
            pltpu.SemaphoreType.DMA((7,)),
            pltpu.SemaphoreType.DMA((7,)),
            *line_sems(line, 2),
            pltpu.SemaphoreType.DMA((6,)),
            pltpu.SemaphoreType.DMA((8,)),
            pltpu.SemaphoreType.DMA((7,)),
            pltpu.SemaphoreType.DMA((2,)),
        ],
        compiler_params=pltpu.CompilerParams(
            collective_id=2, has_side_effects=True, vmem_limit_bytes=63 * MIB
        ),
        cost_estimate=pl.CostEstimate(
            flops=50 * 2**30, bytes_accessed=80 * MIB, transcendentals=0
        ),
    )(middle, gain.reshape(1, width), cot, gate, up, down)


class LineReduce:
    def __init__(self, place, part, up_in, down_in, up_send, up_recv, down_send, down_recv):
        self.p, self.part = place, part
        self.up_in, self.down_in = up_in, down_in
        self.up = (up_send, up_recv)
        self.down = (down_send, down_recv)

    def _up(self, d, t):
        p = self.p
        return remote(
            self.part(d), self.up_in.at[t], self.up[0].at[t], self.up[1].at[t], (p.s + 1, p.h)
        )

    def _down(self, d, t):
        p = self.p
        return remote(
            self.part(d),
            self.down_in.at[t],
            self.down[0].at[t],
            self.down[1].at[t],
            (p.s - 1, p.h),
        )

    def _sends(self, t):
        p, last = self.p, self.p.line - 1
        return (
            ((p.s <= t) & (p.s < last), self._up, last - t + p.s),
            ((last - p.s <= t) & (p.s > 0), self._down, t - last + p.s),
        )

    def start(self, t):
        p, last = self.p, self.p.line - 1
        for number, (goes, copy, d) in enumerate(self._sends(t)):
            came = (self.up_in, self.down_in)[number]

            @pl.when(goes)
            def _():
                if t > 0:
                    inner = p.s > 0 if number == 0 else p.s < last

                    @pl.when(inner)
                    def _():
                        add_rows(self.part(d), came.at[t - 1])

                copy(d, t).start()

    def got(self, t):
        p, last = self.p, self.p.line - 1

        @pl.when((p.s >= 1) & (t >= p.s - 1))
        def _():
            self._up(0, t).wait_recv()

        @pl.when((p.s < last) & (t >= last - p.s - 1))
        def _():
            self._down(0, t).wait_recv()

    def step(self, t):
        self.got(t)
        if t + 1 < self.p.line - 1:
            self.start(t + 1)

    def end(self):
        p, last = self.p, self.p.line - 1

        @pl.when(p.s >= 1)
        def _():
            add_rows(self.part(p.s), self.up_in.at[last - 1])

        @pl.when(p.s < last)
        def _():
            add_rows(self.part(p.s), self.down_in.at[last - 1])

    def total(self, rows):
        p, last = self.p, self.p.line - 1
        value = self.part(p.s)[rows, :].astype(F32)
        value = value + jnp.where(p.s >= 1, self.up_in[last - 1, rows, :].astype(F32), 0.0)
        return value + jnp.where(p.s < last, self.down_in[last - 1, rows, :].astype(F32), 0.0)

    def finish(self):
        for t in range(self.p.line - 1):
            for goes, copy, d in self._sends(t):

                @pl.when(goes)
                def _():
                    copy(d, t).wait_send()


def add_rows(target, other):
    step = 16

    @pl.loop(0, target.shape[0] // step)
    def _(i):
        at = pl.ds(pl.multiple_of(i * step, step), step)
        target[at, :] = (target[at, :].astype(F32) + other[at, :].astype(F32)).astype(BF16)


def clear_last(reduce):
    p, last = reduce.p, reduce.p.line - 1

    @pl.when(p.s == 0)
    def _():
        reduce.up_in[last - 1] = jnp.zeros(reduce.up_in.shape[1:], BF16)

    @pl.when(p.s == last)
    def _():
        reduce.down_in[last - 1] = jnp.zeros(reduce.down_in.shape[1:], BF16)


def weight_product(apply, source, piece, strip, wide, sems, place, first, last):
    each = piece(0).shape[1] // wide
    begin, end = first * each, last * each

    def slab(n):
        d = lax.div(n, each)
        low = place.s < place.line // 2
        return jnp.where(low, place.line - 1 - d, d)

    def fetch(n):
        at = slab(n) * each + lax.rem(n, each)
        cols = pl.ds(pl.multiple_of(at * wide, wide), wide)
        return pltpu.make_async_copy(
            source.at[:, cols], strip(lax.rem(n, 2)), sems.at[lax.rem(n, 2)]
        )

    fetch(begin).start()

    @pl.loop(begin, end)
    def _(n):
        @pl.when(n + 1 < end)
        def _():
            fetch(n + 1).start()

        fetch(n).wait()
        cols = pl.ds(pl.multiple_of(lax.rem(n, each) * wide, wide), wide)
        piece(slab(n))[:, cols] = apply(strip(lax.rem(n, 2))[...]).astype(BF16)


def turn_rows(source, target):
    step = 256

    @pl.loop(0, source.shape[0] // step)
    def _(i):
        at = pl.ds(pl.multiple_of(i * step, step), step)
        for first, last in strips(source.shape[1], 128):
            target[first:last, at] = source[at, first:last].T


def return_kernel(
    line,
    grad_given,
    middle_given,
    cot_given,
    gain,
    attended_given,
    w_out_given,
    grad_gate,
    grad_up,
    normed,
    grad_middle_out,
    gain_part,
    grad_attended,
    inner,
    up_grad,
    gate_parts,
    out_parts,
    branch,
    units_in,
    strip,
    up_parts,
    other_parts,
    up_up_in,
    up_down_in,
    att_turned,
    out_sum,
    grad_normed,
    middle,
    cot_own,
    attended,
    w_out,
    grad_middle,
    g_send,
    g_recv,
    *sems,
):
    p = Place(line)
    up_sems, loads, strips_sem, saves, early, kept = sems[0:4], *sems[4:9]
    rows, width = grad_normed.shape
    slab = w_out.shape[2]
    part = attended.shape[1]
    block = lambda j: branch.at[pl.ds(pl.multiple_of(j * rows, rows), rows)]
    gather = HeadGather(p, block, g_send, g_recv)
    up_reduce = LineReduce(p, lambda d: up_parts.at[d], up_up_in, up_down_in, *up_sems)
    load = [
        pltpu.make_async_copy(source, units_in, loads.at[i])
        for i, source in enumerate((grad_up, grad_gate))
    ]
    pieces = 4
    piece_rows = rows // pieces
    piece_at = [pl.ds(i * piece_rows, piece_rows) for i in range(pieces)]
    arriving = [
        [
            pltpu.make_async_copy(source.at[at], target.at[at], early.at[3 * i + k])
            for k, (source, target) in enumerate(
                ((grad_given, grad_normed), (middle_given, middle), (cot_given, cot_own))
            )
        ]
        for i, at in enumerate(piece_at)
    ]
    leaving = [
        pltpu.make_async_copy(grad_middle.at[at], grad_middle_out.at[at], kept.at[i])
        for i, at in enumerate(piece_at)
    ]
    later = [
        pltpu.make_async_copy(attended_given, attended, early.at[3 * pieces]),
        pltpu.make_async_copy(w_out_given, w_out, early.at[3 * pieces + 1]),
    ]
    for group in arriving:
        for copy in group:
            copy.start()
    load[0].start()
    for copy in later:
        copy.start()
    p.greet()
    mine = block(p.h)
    gain_part[...] = jnp.zeros_like(gain_part)
    step = 32

    def piece_back(number, i):
        at = pl.ds(pl.multiple_of(number * piece_rows + i * step, step), step)
        value = middle[at]
        inverse = lax.rsqrt(jnp.mean(value * value, axis=-1, keepdims=True) + EPS)
        unit = value * inverse
        grad = grad_normed[at]
        gain_part[...] += jnp.sum(grad * unit, axis=0, keepdims=True)
        result = cot_own[at].astype(F32) + norm_back(unit, inverse, gain[...], grad)
        grad_middle[at] = result
        mine[at] = result.astype(BF16)

    for number in range(pieces):
        for copy in arriving[number]:
            copy.wait()
        pl.loop(0, piece_rows // step)(functools.partial(piece_back, number))
        leaving[number].start()

    gather.start()
    clear_last(up_reduce)
    multiply = lambda parts, *some: weight_product(
        lambda rows_in: product_tn(units_in[...], rows_in),
        normed,
        lambda d: parts.at[d],
        strip.at.__getitem__,
        strip.shape[2],
        strips_sem,
        p,
        *some,
    )
    load[0].wait()
    multiply(up_parts, 0, 1)
    up_reduce.start(0)
    multiply(up_parts, 1, line)
    load[1].start()
    gather.got_core()
    load[1].wait()
    up_reduce.step(0)
    gather.got_first()
    gather.got_second()
    multiply(other_parts, 0, line)
    save_gate = pltpu.make_async_copy(other_parts, gate_parts, saves.at[1])
    save_gate.start()
    for copy in later:
        copy.wait()
    turn_rows(attended, att_turned)
    up_reduce.step(1)
    gather.got_core_second()
    gather.got_core_first()
    out_sum[...] = jnp.zeros_like(out_sum)

    def take(j):
        start = pl.multiple_of(j * rows, rows)
        at = pl.ds(start, rows)
        total = product_nt(branch[at, 0:slab], w_out[0])
        for d in range(1, line):
            total = total + product_nt(branch[at, d * slab : (d + 1) * slab], w_out[d])
        low = total.astype(BF16)
        grad_attended[at, :] = low
        for head in range(part // HEAD_DIM):
            cols = slice(head * HEAD_DIM, (head + 1) * HEAD_DIM)
            both = low[:, cols].astype(F32) * attended[at, cols].astype(F32)
            inner[head : head + 1, at] = jnp.sum(both.T, axis=0, keepdims=True)

        @pl.loop(0, line)
        def _(d):
            cols = pl.ds(pl.multiple_of(d * slab, slab), slab)
            out_sum[d] += product(att_turned[:, at], branch[at, cols])

    for j in (p.h, p.core, p.first, p.second):
        take(j)
    for j in (p.second + p.turn, p.first + p.turn):
        take(j)
    gather.got_across()
    take(p.across)
    gather.got_core_across()
    take(p.across + p.turn)
    for d in range(line):
        out_parts[d] = out_sum[d].astype(BF16)
    up_reduce.step(2)
    for first, last in strips(up_grad.shape[0], 128):
        up_grad[first:last, :] = up_reduce.total(slice(first, last))
    gather.finish()
    up_reduce.finish()
    save_gate.wait()
    for copy in leaving:
        copy.wait()


def give_back(
    line, grad_normed, middle, cot_own, gain, attended, w_out, grad_gate, grad_up, normed
):
    rows, width = middle.shape
    full, units = grad_up.shape
    part = attended.shape[1]
    slab = w_out.shape[2]
    heads = part // HEAD_DIM
    return pl.pallas_call(
        functools.partial(return_kernel, line),
        out_shape=(
            jax.ShapeDtypeStruct((rows, width), F32),
            jax.ShapeDtypeStruct((1, width), F32),
            jax.ShapeDtypeStruct((full, part), BF16),
            jax.ShapeDtypeStruct((heads, full), F32),
            jax.ShapeDtypeStruct((units, slab), F32),
            jax.ShapeDtypeStruct((line, units, slab), BF16),
            jax.ShapeDtypeStruct((line, part, slab), BF16),
        ),
        in_specs=[any_spec()] * 3 + [vmem_spec()] + [any_spec()] * 5,
        out_specs=(
            any_spec(),
            vmem_spec(),
            vmem_spec(),
            vmem_spec(),
            vmem_spec(),
            any_spec(),
            vmem_spec(),
        ),
        scratch_shapes=[
            pltpu.VMEM((full, width), BF16),
            pltpu.VMEM((full, units), BF16),
            pltpu.VMEM((2, full, slab), BF16),
            pltpu.VMEM((line, units, slab), BF16),
            pltpu.VMEM((line, units, slab), BF16),
            pltpu.VMEM((line - 1, units, slab), BF16),
            pltpu.VMEM((line - 1, units, slab), BF16),
            pltpu.VMEM((part, full), BF16),
            pltpu.VMEM((line, part, slab), F32),
            pltpu.VMEM((rows, width), F32),
            pltpu.VMEM((rows, width), F32),
            pltpu.VMEM((rows, width), BF16),
            pltpu.VMEM((full, part), BF16),
            pltpu.VMEM((line, part, slab), BF16),
            pltpu.VMEM((rows, width), F32),
            pltpu.SemaphoreType.DMA((7,)),
            pltpu.SemaphoreType.DMA((7,)),
            *line_sems(line),
            pltpu.SemaphoreType.DMA((2,)),
            pltpu.SemaphoreType.DMA((2,)),
            pltpu.SemaphoreType.DMA((2,)),
            pltpu.SemaphoreType.DMA((14,)),
            pltpu.SemaphoreType.DMA((4,)),
        ],
        compiler_params=pltpu.CompilerParams(
            collective_id=3, has_side_effects=True, vmem_limit_bytes=62 * MIB
        ),
        cost_estimate=pl.CostEstimate(
            flops=25 * 2**30, bytes_accessed=80 * MIB, transcendentals=0
        ),
    )(
        grad_normed,
        middle,
        cot_own,
        gain.reshape(1, width),
        attended,
        w_out,
        grad_gate,
        grad_up,
        normed,
    )


def backward_tile(tile, q, k_ext, v_ext, k_t, floor, logs, inner, grad, key_sum, value_sum):
    start = pl.multiple_of(tile * TILE, TILE)
    mine = pl.ds(start, TILE)
    scale = HEAD_DIM ** (-0.5)
    for head in range(q.shape[1] // HEAD_DIM):
        cols = slice(head * HEAD_DIM, (head + 1) * HEAD_DIM)
        queries = q[mine, cols]
        grads = grad[mine, cols]
        log = logs[head : head + 1, mine]
        middle = inner[head : head + 1, mine]
        turned = jnp.zeros((HEAD_DIM, TILE), F32)
        for i, (scores, visible) in enumerate(tile_scores(tile, head, q, k_ext, floor)):
            at = pl.ds(start + i * TILE, TILE)
            probs = jnp.where(visible, jnp.exp2(scores * (scale * LOG2E) - log), 0.0)
            grad_probs = product_nt(v_ext[at, cols], grads)
            grad_scores = (probs * (grad_probs - middle)).astype(BF16)
            value_sum[at, cols] += product(probs.astype(BF16), grads)
            key_sum[at, cols] += product(grad_scores, queries)
            turned = turned + product(k_t[cols, at], grad_scores)
        q[mine, cols] = (turned * scale).astype(BF16).T


def attend_back_kernel(
    line,
    qkv,
    halo_kv,
    floor,
    logs,
    grad_given,
    inner,
    hidden,
    w_down_given,
    middle,
    gate_in,
    grads_out,
    result,
    gate_grad,
    q,
    k_ext,
    v_ext,
    k_t,
    key_sum,
    value_sum,
    halo_out,
    halo_in,
    gate_parts,
    gate_up_in,
    gate_down_in,
    out,
    into,
    total,
    hidden_block,
    grad,
    w_down,
    r_send,
    r_recv,
    *sems,
):
    p = Place(line)
    gate_sems, loads, halo_send, halo_recv, stage, saves = sems[0:4], *sems[4:9]
    rows, width = result.shape
    slab = w_down.shape[2]
    count, part = q.shape
    scale = HEAD_DIM ** (-0.5)
    rows_of = lambda ref, j: ref.at[pl.ds(pl.multiple_of(j * rows, rows), rows)]
    gate_reduce = LineReduce(
        p, lambda d: gate_parts.at[d], gate_up_in, gate_down_in, *gate_sems
    )
    started = [
        pltpu.make_async_copy(gate_in, gate_parts, loads.at[0]),
        pltpu.make_async_copy(qkv.at[:, pl.ds(0, part)], q, loads.at[1]),
        pltpu.make_async_copy(
            qkv.at[:, pl.ds(part, part)], k_ext.at[pl.ds(WINDOW, count)], loads.at[2]
        ),
        pltpu.make_async_copy(
            qkv.at[:, pl.ds(2 * part, part)], v_ext.at[pl.ds(WINDOW, count)], loads.at[3]
        ),
        pltpu.make_async_copy(halo_kv.at[0], k_ext.at[pl.ds(0, WINDOW)], loads.at[4]),
        pltpu.make_async_copy(halo_kv.at[1], v_ext.at[pl.ds(0, WINDOW)], loads.at[5]),
        pltpu.make_async_copy(middle, total, loads.at[6]),
        pltpu.make_async_copy(grad_given, grad, loads.at[7]),
    ]
    down_load = pltpu.make_async_copy(w_down_given, w_down, loads.at[8])
    halo = [
        remote(
            halo_out.at[i], halo_in.at[i], halo_send.at[i], halo_recv.at[i], (p.s - 1, p.h)
        )
        for i in range(2)
    ]
    order = (
        p.second + p.turn,
        p.across + p.turn,
        p.first,
        p.first + p.turn,
        p.across,
        p.core,
        p.h,
        p.second,
    )
    fetches = [
        pltpu.make_async_copy(rows_of(hidden, j), hidden_block.at[n % 2], stage.at[n % 2])
        for n, j in enumerate(order)
    ]
    copies = block_reduce(p, out, into, r_send, r_recv)

    def emit(n, target, *more):
        fetches[n].wait()
        if n + 1 < len(order):
            fetches[n + 1].start()

        for d in range(line):
            cols = slice(d * slab, (d + 1) * slab)
            value = product(hidden_block[n % 2][:, 0 : w_down.shape[1]], w_down[d])
            for other in more:
                value = value + other[:, cols].astype(F32)
            target[:, cols] = value.astype(target.dtype)

    def tiles(first, last):
        @pl.loop(first, last)
        def _(tile):
            backward_tile(
                tile, q, k_ext, v_ext, k_t, floor, logs, inner, grad, key_sum, value_sum
            )

    down_load.start()
    fetches[0].start()
    for copy in started:
        copy.start()
    p.greet()
    started[0].wait()
    gate_reduce.start(0)
    clear_last(gate_reduce)
    down_load.wait()
    emit(0, out.at[0])
    copies[0].start()
    emit(1, out.at[1])
    copies[1].start()
    copies[0].wait_recv()
    emit(2, out.at[2], into.at[0])
    copies[4].start()
    copies[0].wait_send()
    emit(3, out.at[0])
    copies[2].start()
    copies[1].wait_recv()
    emit(4, out.at[3], into.at[1])
    copies[5].start()
    copies[1].wait_send()
    emit(5, out.at[1])
    copies[3].start()
    for copy in started[1:]:
        copy.wait()
    gate_reduce.step(0)

    @pl.loop(0, (WINDOW + count) // TILE)
    def _(i):
        at = pl.ds(pl.multiple_of(i * TILE, TILE), TILE)
        k_t[:, at] = k_ext[at, :].T
        key_sum[at, :] = jnp.zeros((TILE, part), F32)
        value_sum[at, :] = jnp.zeros((TILE, part), F32)

    ahead = WINDOW // TILE
    last = count // TILE
    tiles(0, ahead)

    @pl.when(p.s > 0)
    def _():
        @pl.loop(0, ahead)
        def _(i):
            at = pl.ds(pl.multiple_of(i * TILE, TILE), TILE)
            halo_out[0, at, :] = (key_sum[at, :] * scale).astype(BF16)
            halo_out[1, at, :] = value_sum[at, :].astype(BF16)

        halo[0].start()
        halo[1].start()

    gate_reduce.step(1)
    tiles(ahead, ahead + 4)
    copies[3].wait_recv()
    emit(6, total, into.at[3], total)
    copies[2].wait_recv()
    copies[5].wait_recv()
    emit(7, out.at[4], into.at[2], into.at[5])
    copies[6].start()
    tiles(ahead + 4, last)

    @pl.when(p.s < line - 1)
    def _():
        halo[0].wait_recv()
        halo[1].wait_recv()

    @pl.loop(0, last)
    def _(i):
        here = pl.ds(pl.multiple_of(i * TILE, TILE), TILE)
        at = pl.ds(pl.multiple_of(i * TILE + WINDOW, TILE), TILE)
        key_value = key_sum[at, :] * scale
        value_value = value_sum[at, :]
        k_ext[here, :] = key_value.astype(BF16)
        v_ext[here, :] = value_value.astype(BF16)

    @pl.when(p.s < line - 1)
    def _():
        @pl.loop(0, ahead)
        def _(i):
            here = pl.ds(pl.multiple_of(i * TILE, TILE), TILE)
            near = pl.ds(pl.multiple_of(i * TILE + count, TILE), TILE)
            there = pl.ds(pl.multiple_of(i * TILE + count - WINDOW, TILE), TILE)
            k_ext[there, :] = (
                key_sum[near, :] * scale + halo_in[0, here, :].astype(F32)
            ).astype(BF16)
            v_ext[there, :] = (value_sum[near, :] + halo_in[1, here, :].astype(F32)).astype(BF16)

    save = [
        pltpu.make_async_copy(
            ref.at[pl.ds(0, count)], grads_out.at[:, pl.ds(i * part, part)], saves.at[i]
        )
        for i, ref in enumerate((q, k_ext, v_ext))
    ]
    for copy in save:
        copy.start()
    copies[4].wait_recv()
    copies[6].wait_recv()

    @pl.loop(0, line)
    def _(d):
        cols = pl.ds(pl.multiple_of(d * slab, slab), slab)
        value = total[:, cols] + into[4, :, cols].astype(F32) + into[6, :, cols].astype(F32)
        result[:, cols] = value.astype(BF16)

    gate_reduce.step(2)
    for first, stop in strips(gate_grad.shape[0], 128):
        gate_grad[first:stop, :] = gate_reduce.total(slice(first, stop))
    for i in range(2, 7):
        copies[i].wait_send()
    gate_reduce.finish()

    @pl.when(p.s > 0)
    def _():
        halo[0].wait_send()
        halo[1].wait_send()

    for copy in save:
        copy.wait()


def attend_back(line, qkv, halo_kv, floor, logs, grad, inner, hidden, w_down, middle, gate_parts):
    rows, width = middle.shape
    count = qkv.shape[0]
    part = qkv.shape[1] // 3
    units, slab = w_down.shape[1:]
    return pl.pallas_call(
        functools.partial(attend_back_kernel, line),
        out_shape=(
            jax.ShapeDtypeStruct((count, 3 * part), BF16),
            jax.ShapeDtypeStruct((rows, width), BF16),
            jax.ShapeDtypeStruct((units, slab), F32),
        ),
        in_specs=[any_spec()] * 2
        + [vmem_spec(), vmem_spec(), any_spec(), vmem_spec()]
        + [any_spec()] * 4,
        out_specs=(any_spec(), vmem_spec(), vmem_spec()),
        scratch_shapes=[
            pltpu.VMEM((count, part), BF16),
            pltpu.VMEM((WINDOW + count, part), BF16),
            pltpu.VMEM((WINDOW + count, part), BF16),
            pltpu.VMEM((part, WINDOW + count), BF16),
            pltpu.VMEM((WINDOW + count, part), F32),
            pltpu.VMEM((WINDOW + count, part), F32),
            pltpu.VMEM((2, WINDOW, part), BF16),
            pltpu.VMEM((2, WINDOW, part), BF16),
            pltpu.VMEM((line, units, slab), BF16),
            pltpu.VMEM((line - 1, units, slab), BF16),
            pltpu.VMEM((line - 1, units, slab), BF16),
            pltpu.VMEM((5, rows, width), BF16),
            pltpu.VMEM((7, rows, width), BF16),
            pltpu.VMEM((rows, width), F32),
            pltpu.VMEM((2, rows, hidden.shape[1]), BF16),
            pltpu.VMEM((count, part), BF16),
            pltpu.VMEM((line, units, slab), BF16),
            pltpu.SemaphoreType.DMA((7,)),
            pltpu.SemaphoreType.DMA((7,)),
            *line_sems(line),
            pltpu.SemaphoreType.DMA((9,)),
            pltpu.SemaphoreType.DMA((2,)),
            pltpu.SemaphoreType.DMA((2,)),
            pltpu.SemaphoreType.DMA((2,)),
            pltpu.SemaphoreType.DMA((3,)),
        ],
        compiler_params=pltpu.CompilerParams(
            collective_id=4, has_side_effects=True, vmem_limit_bytes=62 * MIB
        ),
        cost_estimate=pl.CostEstimate(
            flops=20 * 2**30, bytes_accessed=60 * MIB, transcendentals=0
        ),
    )(qkv, halo_kv, floor, logs, grad, inner, hidden, w_down, middle, gate_parts)


def finish_kernel(
    line,
    grads_given,
    weight_given,
    normed,
    tokens_given,
    gain,
    grad_middle,
    out_given,
    ffn_gain_part,
    input_grad,
    gain_sums,
    query_grad,
    key_grad,
    value_grad,
    out_grad,
    strip,
    parts,
    parts_up_in,
    parts_down_in,
    out_parts,
    out_up_in,
    out_down_in,
    out,
    into,
    total,
    gain_line,
    gain_in,
    grads_in,
    weight_in,
    tokens_in,
    r_send,
    r_recv,
    *sems,
):
    p = Place(line)
    part_sems, out_sems = sems[0:4], sems[4:8]
    loads, strip_sems, gain_send, gain_recv, line_send, line_recv, block_sems = sems[8:15]
    grads, weight, tokens = grads_in, weight_in, tokens_in
    rows, width = tokens.shape
    slab = width // line
    part = query_grad.shape[1]
    part_reduce = LineReduce(p, lambda d: parts.at[d], parts_up_in, parts_down_in, *part_sems)
    out_reduce = LineReduce(p, lambda d: out_parts.at[d], out_up_in, out_down_in, *out_sems)
    started = [
        pltpu.make_async_copy(out_given, out_parts, loads.at[0]),
        pltpu.make_async_copy(grad_middle, input_grad, loads.at[1]),
    ]
    turns = (
        p.second + p.turn,
        p.across + p.turn,
        p.first,
        p.first + p.turn,
        p.across,
        p.core,
        p.h,
        p.second,
    )
    blocks = []
    for n, j in enumerate(turns):
        at = pl.ds(pl.multiple_of(j * rows, rows), rows)
        blocks.append(pltpu.make_async_copy(grads_given.at[at], grads.at[at], block_sems.at[n]))
    weight_load = pltpu.make_async_copy(weight_given, weight, loads.at[2])
    tokens_load = pltpu.make_async_copy(tokens_given, tokens, loads.at[3])
    weight_load.start()
    blocks[0].start()
    started[0].start()
    for copy in blocks[1:] + [started[1], tokens_load]:
        copy.start()
    greet_line(p)
    started[0].wait()
    out_reduce.start(0)
    for reduce in (part_reduce, out_reduce):
        clear_last(reduce)
    copies = block_reduce(p, out, into, r_send, r_recv)

    def emit(j, target, *more):
        at = pl.ds(pl.multiple_of(j * rows, rows), rows)

        for d in range(line):
            cols = slice(d * slab, (d + 1) * slab)
            value = product_nt(grads[at, :], weight[cols, :])
            for other in more:
                value = value + other[:, cols].astype(F32)
            target[:, cols] = value.astype(target.dtype)

    weight_load.wait()
    blocks[0].wait()
    emit(p.second + p.turn, out.at[0])
    copies[0].start()
    blocks[1].wait()
    emit(p.across + p.turn, out.at[1])
    copies[1].start()
    copies[0].wait_recv()
    blocks[2].wait()
    emit(p.first, out.at[2], into.at[0])
    copies[4].start()
    copies[0].wait_send()
    blocks[3].wait()
    emit(p.first + p.turn, out.at[0])
    copies[2].start()
    copies[1].wait_recv()
    blocks[4].wait()
    emit(p.across, out.at[3], into.at[1])
    copies[5].start()
    copies[1].wait_send()
    blocks[5].wait()
    emit(p.core, out.at[1])
    copies[3].start()
    blocks[6].wait()
    blocks[7].wait()
    multiply = lambda *some: weight_product(
        lambda rows_in: product_tn(grads[...], rows_in),
        normed,
        lambda d: parts.at[d],
        strip.at.__getitem__,
        strip.shape[2],
        strip_sems,
        p,
        *some,
    )
    out_reduce.step(0)
    multiply(0, 1)
    part_reduce.start(0)
    multiply(1, line)
    out_reduce.step(1)
    copies[3].wait_recv()
    emit(p.h, total, into.at[3])
    part_reduce.step(0)
    copies[2].wait_recv()
    copies[5].wait_recv()
    emit(p.second, out.at[4], into.at[2], into.at[5])
    copies[6].start()
    out_reduce.step(2)
    for first, last in strips(part, 128):
        out_grad[first:last, :] = out_reduce.total(slice(first, last))
    copies[4].wait_recv()
    part_reduce.step(1)
    copies[6].wait_recv()
    started[1].wait()
    tokens_load.wait()
    gain_own = gain_line.at[p.s]
    gain_own[...] = jnp.zeros(gain_own.shape, F32)
    gain_own[1:2, :] = ffn_gain_part[...]
    step = 32

    @pl.loop(0, rows // step)
    def _(i):
        at = pl.ds(pl.multiple_of(i * step, step), step)
        grad = total[at] + into[4, at].astype(F32) + into[6, at].astype(F32)
        unit, inverse = normalize(tokens[at].astype(F32))
        gain_own[0:1, :] += jnp.sum(grad * unit, axis=0, keepdims=True)
        input_grad[at] += norm_back(unit, inverse, gain[...], grad)

    for i, head in enumerate((p.core, p.first, p.second)):
        copy = remote(gain_own, gain_in.at[i], gain_send.at[i], gain_recv.at[i], p.at(head))
        copy.start()
        copy.wait()
        gain_own[...] += gain_in[i]
    spread = [
        remote(
            gain_own,
            gain_own,
            line_send.at[k - 1],
            line_recv.at[k - 1],
            (lax.rem(p.s + k, line), p.h),
        )
        for k in range(1, line)
    ]
    came = [
        remote(
            gain_line.at[lax.rem(p.s + line - k, line)],
            gain_line.at[lax.rem(p.s + line - k, line)],
            line_send.at[k - 1],
            line_recv.at[k - 1],
            (lax.rem(p.s + k, line), p.h),
        )
        for k in range(1, line)
    ]
    for copy in spread:
        copy.start()
    for copy in came:
        copy.wait_recv()
    summed = gain_line[0]
    for d in range(1, line):
        summed = summed + gain_line[d]
    gain_sums[...] = summed
    part_reduce.step(2)
    for i, target in enumerate((query_grad, key_grad, value_grad)):
        for first, last in strips(part, 128):
            target[:, first:last] = part_reduce.total(
                slice(i * part + first, i * part + last)
            ).T
    for i in range(2, 7):
        copies[i].wait_send()
    for copy in spread:
        copy.wait_send()
    for reduce in (part_reduce, out_reduce):
        reduce.finish()


def finish(line, grads, weight, normed, tokens, gain, grad_middle, out_parts, ffn_gain_part):
    rows, width = tokens.shape
    full = grads.shape[0]
    part = grads.shape[1] // 3
    slab = width // line
    return pl.pallas_call(
        functools.partial(finish_kernel, line),
        out_shape=(
            jax.ShapeDtypeStruct((rows, width), F32),
            jax.ShapeDtypeStruct((2, width), F32),
            jax.ShapeDtypeStruct((slab, part), F32),
            jax.ShapeDtypeStruct((slab, part), F32),
            jax.ShapeDtypeStruct((slab, part), F32),
            jax.ShapeDtypeStruct((part, slab), F32),
        ),
        in_specs=[
            any_spec(),
            any_spec(),
            any_spec(),
            any_spec(),
            vmem_spec(),
            any_spec(),
            any_spec(),
            vmem_spec(),
        ],
        out_specs=(vmem_spec(),) * 6,
        scratch_shapes=[
            pltpu.VMEM((2, full, slab), BF16),
            pltpu.VMEM((line, 3 * part, slab), BF16),
            pltpu.VMEM((line - 1, 3 * part, slab), BF16),
            pltpu.VMEM((line - 1, 3 * part, slab), BF16),
            pltpu.VMEM((line, part, slab), BF16),
            pltpu.VMEM((line - 1, part, slab), BF16),
            pltpu.VMEM((line - 1, part, slab), BF16),
            pltpu.VMEM((5, rows, width), BF16),
            pltpu.VMEM((7, rows, width), BF16),
            pltpu.VMEM((rows, width), F32),
            pltpu.VMEM((line, 2, width), F32),
            pltpu.VMEM((3, 2, width), F32),
            pltpu.VMEM(grads.shape, BF16),
            pltpu.VMEM(weight.shape, BF16),
            pltpu.VMEM((rows, width), BF16),
            pltpu.SemaphoreType.DMA((7,)),
            pltpu.SemaphoreType.DMA((7,)),
            *line_sems(line, 2),
            pltpu.SemaphoreType.DMA((4,)),
            pltpu.SemaphoreType.DMA((2,)),
            pltpu.SemaphoreType.DMA((3,)),
            pltpu.SemaphoreType.DMA((3,)),
            pltpu.SemaphoreType.DMA((line - 1,)),
            pltpu.SemaphoreType.DMA((line - 1,)),
            pltpu.SemaphoreType.DMA((8,)),
        ],
        compiler_params=pltpu.CompilerParams(
            collective_id=5, has_side_effects=True, vmem_limit_bytes=62 * MIB
        ),
        cost_estimate=pl.CostEstimate(
            flops=20 * 2**30, bytes_accessed=60 * MIB, transcendentals=0
        ),
    )(
        grads,
        weight,
        normed,
        tokens,
        gain.reshape(1, width),
        grad_middle,
        out_parts,
        ffn_gain_part,
    )


def deliver_kernel(count, *refs):
    sources, targets, held = refs[:count], refs[count : 2 * count], refs[2 * count : 3 * count]
    sems = refs[3 * count]
    loads = [
        pltpu.make_async_copy(source, keep, sems.at[i])
        for i, (source, keep) in enumerate(zip(sources, held))
    ]
    stores = [
        pltpu.make_async_copy(keep, target, sems.at[count + i])
        for i, (keep, target) in enumerate(zip(held, targets))
    ]
    for copy in loads:
        copy.start()
    for load, store in zip(loads, stores):
        load.wait()
        store.start()
    for copy in stores:
        copy.wait()


def deliver(*arrays):
    count = len(arrays)
    return pl.pallas_call(
        functools.partial(deliver_kernel, count),
        out_shape=tuple(jax.ShapeDtypeStruct(a.shape, a.dtype) for a in arrays),
        in_specs=[any_spec()] * count,
        out_specs=(any_spec(),) * count,
        scratch_shapes=[pltpu.VMEM(a.shape, a.dtype) for a in arrays]
        + [pltpu.SemaphoreType.DMA((2 * count,))],
        compiler_params=pltpu.CompilerParams(vmem_limit_bytes=62 * MIB),
    )(*arrays)


def fused(
    tokens,
    segment,
    attn_gain,
    query_weight,
    key_weight,
    value_weight,
    out_weight,
    ffn_gain,
    gate_weight,
    up_weight,
    down_weight,
    cotangent,
):
    line = lax.axis_size("seq")
    (
        normed_one,
        qkv,
        w_qkv,
        floor,
        attended,
        logs,
        halo_kv,
        cot_full,
        w_out,
        w_gate,
        w_up,
        middle,
    ) = forward(
        line,
        tokens,
        attn_gain,
        query_weight,
        key_weight,
        value_weight,
        segment,
        cotangent,
        out_weight,
        gate_weight.T,
        up_weight.T,
    )
    normed_two, hidden, grad_gate, grad_up, grad_normed_two, w_down, down_grad = feed(
        line, middle, ffn_gain, cot_full, w_gate, w_up, down_weight
    )
    grad_middle, ffn_gain_part, grad_attended, inner, up_grad, gate_parts, out_parts = give_back(
        line,
        grad_normed_two,
        middle,
        cotangent,
        ffn_gain,
        attended,
        w_out,
        grad_gate,
        grad_up,
        normed_two,
    )
    grads, result, gate_grad = attend_back(
        line, qkv, halo_kv, floor, logs, grad_attended, inner, hidden, w_down, middle, gate_parts
    )
    input_grad, gain_sums, query_grad, key_grad, value_grad, out_grad = finish(
        line,
        grads,
        w_qkv,
        normed_one,
        tokens,
        attn_gain,
        grad_middle,
        out_parts,
        ffn_gain_part,
    )
    (
        result,
        input_grad,
        query_grad,
        key_grad,
        value_grad,
        out_grad,
        gate_grad,
        up_grad,
        down_grad,
    ) = deliver(
        result,
        input_grad,
        query_grad,
        key_grad,
        value_grad,
        out_grad,
        gate_grad,
        up_grad,
        down_grad,
    )
    share = tokens.shape[1] // (line * lax.axis_size("head"))
    place = (lax.axis_index("seq") * lax.axis_size("head") + lax.axis_index("head")) * share
    gain_grads = lax.dynamic_slice(gain_sums, (0, place), (2, share))
    return (
        result,
        input_grad,
        gain_grads[0],
        query_grad,
        key_grad,
        value_grad,
        out_grad,
        gain_grads[1],
        gate_grad.T,
        up_grad.T,
        down_grad,
    )


def solution(mesh):
    placed = (
        P(("seq", "head"), None),
        P("seq"),
        P(),
        P("seq", "head"),
        P("seq", "head"),
        P("seq", "head"),
        P("head", "seq"),
        P(),
        P("seq", "head"),
        P("seq", "head"),
        P("head", "seq"),
        P(("seq", "head"), None),
    )
    body = fused if mesh.shape["head"] == 8 else local
    return jax.shard_map(
        body,
        mesh=mesh,
        in_specs=placed,
        out_specs=(
            P(("seq", "head"), None),
            P(("seq", "head"), None),
            P(("seq", "head")),
            P("seq", "head"),
            P("seq", "head"),
            P("seq", "head"),
            P("head", "seq"),
            P(("seq", "head")),
            P("seq", "head"),
            P("seq", "head"),
            P("head", "seq"),
        ),
        check_vma=False,
    )
```

```python
import functools

import jax
import jax.numpy as jnp
from jax import lax
from jax.experimental import pallas as pl
from jax.experimental.pallas import tpu as pltpu
from jax.sharding import PartitionSpec as P

HEAD_DIM = 128
WINDOW = 1024


EPS = 1e-06
NEG = -1e30


def from_behind(value, axis, by):
    count = lax.axis_size(axis)
    pairs = [(i, i + by) for i in range(count) if 0 <= i + by < count]
    return lax.ppermute(value, axis, pairs)


def product(left, right):
    return jnp.dot(left, right, preferred_element_type=jnp.float32)


def product_tn(left, right):
    return lax.dot_general(
        left, right, (((0,), (0,)), ((), ())), preferred_element_type=jnp.float32
    )


def product_nt(left, right):
    return lax.dot_general(
        left, right, (((1,), (1,)), ((), ())), preferred_element_type=jnp.float32
    )


def normalize(rows):
    inverse = lax.rsqrt(jnp.mean(rows * rows, axis=-1, keepdims=True) + EPS)
    return (rows * inverse, inverse)


def norm_back(unit, inverse, gain, grad):
    scaled = grad * gain
    return inverse * (scaled - unit * jnp.mean(scaled * unit, axis=-1, keepdims=True))


def gather_rows(rows):
    return lax.all_gather(rows, "head", axis=0, tiled=True)


def block_scores(query_heads, key_heads, seg_query, seg_keys, valid, start, block):
    query_part = query_heads[start : start + block]
    key_part = key_heads[start : start + block + WINDOW]
    scores = jnp.einsum(
        "qhd,khd->hqk", query_part, key_part, preferred_element_type=jnp.float32
    ) * HEAD_DIM ** (-0.5)
    rows = jnp.arange(block)[:, None] + WINDOW
    cols = jnp.arange(block + WINDOW)[None, :]
    distance = rows - cols
    same_doc = (
        seg_query[start : start + block][:, None]
        == seg_keys[start : start + block + WINDOW][None, :]
    )
    visible = (
        (distance >= 0)
        & (distance <= WINDOW)
        & same_doc
        & valid[start : start + block + WINDOW][None, :]
    )
    return jnp.where(visible[None], scores, NEG)


def local(
    tokens,
    segment,
    attn_gain,
    query_weight,
    key_weight,
    value_weight,
    out_weight,
    ffn_gain,
    gate_weight,
    up_weight,
    down_weight,
    cotangent,
):
    own_rows = tokens.shape[0]
    group = own_rows * lax.axis_size("head")
    heads_here = query_weight.shape[1] // HEAD_DIM
    offset = lax.axis_index("head") * own_rows
    seq_index = lax.axis_index("seq")
    block = min(512, group)
    scale = HEAD_DIM ** (-0.5)
    w_query, w_key, w_value, w_out, w_gate, w_up, w_down = (
        lax.all_gather(query_weight, "seq", axis=0, tiled=True),
        lax.all_gather(key_weight, "seq", axis=0, tiled=True),
        lax.all_gather(value_weight, "seq", axis=0, tiled=True),
        lax.all_gather(out_weight, "seq", axis=1, tiled=True),
        lax.all_gather(gate_weight, "seq", axis=0, tiled=True),
        lax.all_gather(up_weight, "seq", axis=0, tiled=True),
        lax.all_gather(down_weight, "seq", axis=1, tiled=True),
    )
    inputs = tokens.astype(jnp.float32)
    unit_one, inverse_one = normalize(inputs)
    normed_full = gather_rows((unit_one * attn_gain).astype(jnp.bfloat16))
    queries = product(normed_full, w_query).astype(jnp.bfloat16)
    keys = product(normed_full, w_key).astype(jnp.bfloat16)
    values = product(normed_full, w_value).astype(jnp.bfloat16)
    halo_keys, halo_values, halo_segs = ([], [], [])
    hop = 1
    take = min(group, WINDOW - (hop - 1) * group)
    got_keys, got_values, got_segs = from_behind(
        (keys[group - take :], values[group - take :], segment[group - take :]), "seq", hop
    )
    halo_keys.append(got_keys)
    halo_values.append(got_values)
    halo_segs.append(got_segs)
    keys_ext = jnp.concatenate(halo_keys + [keys], axis=0)
    values_ext = jnp.concatenate(halo_values + [values], axis=0)
    segs_ext = jnp.concatenate(halo_segs + [segment], axis=0)
    positions = seq_index * group - WINDOW + jnp.arange(WINDOW + group)
    valid = positions >= 0
    query_heads = queries.reshape(group, heads_here, HEAD_DIM)
    key_heads = keys_ext.reshape(WINDOW + group, heads_here, HEAD_DIM)
    value_heads = values_ext.reshape(WINDOW + group, heads_here, HEAD_DIM)
    outputs, logsums = ([], [])
    for start in range(0, group, block):
        scores = block_scores(query_heads, key_heads, segment, segs_ext, valid, start, block)
        highest = jnp.max(scores, axis=-1, keepdims=True)
        weights = jnp.exp(scores - highest)
        total = jnp.sum(weights, axis=-1, keepdims=True)
        probs = (weights / total).astype(jnp.bfloat16)
        outputs.append(
            jnp.einsum(
                "hqk,khd->qhd",
                probs,
                value_heads[start : start + block + WINDOW],
                preferred_element_type=jnp.float32,
            )
        )
        logsums.append(highest + jnp.log(total))
    attended = (
        jnp.concatenate(outputs, axis=0).reshape(group, heads_here * HEAD_DIM).astype(jnp.bfloat16)
    )
    partial_out = product(attended, w_out)
    own_part = lax.dynamic_slice_in_dim(partial_out, offset, own_rows, 0)
    placed = lax.dynamic_update_slice_in_dim(partial_out, own_part + inputs, offset, 0)
    middle_full = lax.psum(placed, "head")
    middle = lax.dynamic_slice_in_dim(middle_full, offset, own_rows, 0)
    unit_full, inverse_full = normalize(middle_full)
    normed_two_full = (unit_full * ffn_gain).astype(jnp.bfloat16)
    unit_two, inverse_two = normalize(middle)
    gate = product(normed_two_full, w_gate)
    up = product(normed_two_full, w_up)
    sigmoid = jax.nn.sigmoid(gate)
    activated = gate * sigmoid
    hidden = (activated * up).astype(jnp.bfloat16)
    ffn_out = lax.psum_scatter(
        product(hidden, w_down).astype(jnp.bfloat16), "head", scatter_dimension=0, tiled=True
    ).astype(jnp.float32)
    result = middle + ffn_out
    grad_out = lax.all_gather(cotangent, "head", axis=0, tiled=True)
    grad_hidden = product_nt(grad_out, w_down)
    grad_gate = (grad_hidden * up * sigmoid * (1.0 + gate * (1.0 - sigmoid))).astype(jnp.bfloat16)
    grad_up = (grad_hidden * activated).astype(jnp.bfloat16)
    down_grad = product_tn(hidden, grad_out)
    gate_grad = product_tn(normed_two_full, grad_gate)
    up_grad = product_tn(normed_two_full, grad_up)
    grad_normed_two = lax.psum_scatter(
        (product_nt(grad_gate, w_gate) + product_nt(grad_up, w_up)).astype(jnp.bfloat16),
        "head",
        scatter_dimension=0,
        tiled=True,
    ).astype(jnp.float32)
    ffn_gain_part = jnp.sum(grad_normed_two * unit_two, axis=0)
    grad_middle = cotangent.astype(jnp.float32) + norm_back(
        unit_two, inverse_two, ffn_gain, grad_normed_two
    )
    grad_branch = lax.all_gather(grad_middle.astype(jnp.bfloat16), "head", axis=0, tiled=True)
    out_grad = product_tn(attended, grad_branch)
    grad_attended = product_nt(grad_branch, w_out).astype(jnp.bfloat16)
    grad_heads = grad_attended.reshape(group, heads_here, HEAD_DIM)
    grad_query_list = []
    grad_keys_ext = jnp.zeros((WINDOW + group, heads_here, HEAD_DIM), jnp.float32)
    grad_values_ext = jnp.zeros((WINDOW + group, heads_here, HEAD_DIM), jnp.float32)
    for number, start in enumerate(range(0, group, block)):
        scores = block_scores(query_heads, key_heads, segment, segs_ext, valid, start, block)
        probs = jnp.exp(scores - logsums[number])
        probs_low = probs.astype(jnp.bfloat16)
        key_part = key_heads[start : start + block + WINDOW]
        value_part = value_heads[start : start + block + WINDOW]
        query_part = query_heads[start : start + block]
        grad_part = grad_heads[start : start + block]
        grad_probs = jnp.einsum(
            "qhd,khd->hqk", grad_part, value_part, preferred_element_type=jnp.float32
        )
        inner = jnp.sum(probs * grad_probs, axis=-1, keepdims=True)
        grad_scores = (probs * (grad_probs - inner)).astype(jnp.bfloat16)
        grad_query_list.append(
            jnp.einsum("hqk,khd->qhd", grad_scores, key_part, preferred_element_type=jnp.float32)
            * scale
        )
        key_term = (
            jnp.einsum("hqk,qhd->khd", grad_scores, query_part, preferred_element_type=jnp.float32)
            * scale
        )
        value_term = jnp.einsum(
            "hqk,qhd->khd", probs_low, grad_part, preferred_element_type=jnp.float32
        )
        grad_keys_ext = grad_keys_ext.at[start : start + block + WINDOW].add(key_term)
        grad_values_ext = grad_values_ext.at[start : start + block + WINDOW].add(value_term)
    grad_keys_ext = grad_keys_ext.reshape(WINDOW + group, heads_here * HEAD_DIM)
    grad_values_ext = grad_values_ext.reshape(WINDOW + group, heads_here * HEAD_DIM)
    grad_keys = grad_keys_ext[WINDOW:]
    grad_values = grad_values_ext[WINDOW:]
    cursor = 0
    hop = 1
    take = min(group, WINDOW - (hop - 1) * group)
    back_keys = from_behind(
        grad_keys_ext[cursor : cursor + take].astype(jnp.bfloat16), "seq", -hop
    ).astype(jnp.float32)
    back_values = from_behind(
        grad_values_ext[cursor : cursor + take].astype(jnp.bfloat16), "seq", -hop
    ).astype(jnp.float32)
    grad_keys = grad_keys.at[group - take :].add(back_keys)
    grad_values = grad_values.at[group - take :].add(back_values)
    grad_queries = (
        jnp.concatenate(grad_query_list, axis=0)
        .reshape(group, heads_here * HEAD_DIM)
        .astype(jnp.bfloat16)
    )
    grad_keys = grad_keys.astype(jnp.bfloat16)
    grad_values = grad_values.astype(jnp.bfloat16)
    query_grad = product_tn(normed_full, grad_queries)
    key_grad = product_tn(normed_full, grad_keys)
    value_grad = product_tn(normed_full, grad_values)
    grad_normed_one = lax.psum_scatter(
        (
            product_nt(grad_queries, w_query)
            + product_nt(grad_keys, w_key)
            + product_nt(grad_values, w_value)
        ).astype(jnp.bfloat16),
        "head",
        scatter_dimension=0,
        tiled=True,
    ).astype(jnp.float32)
    attn_gain_part = jnp.sum(grad_normed_one * unit_one, axis=0)
    input_grad = grad_middle + norm_back(unit_one, inverse_one, attn_gain, grad_normed_one)
    summed = (
        lax.psum_scatter(
            query_grad.astype(jnp.bfloat16), "seq", scatter_dimension=0, tiled=True
        ).astype(jnp.float32),
        lax.psum_scatter(
            key_grad.astype(jnp.bfloat16), "seq", scatter_dimension=0, tiled=True
        ).astype(jnp.float32),
        lax.psum_scatter(
            value_grad.astype(jnp.bfloat16), "seq", scatter_dimension=0, tiled=True
        ).astype(jnp.float32),
        lax.psum_scatter(
            out_grad.astype(jnp.bfloat16), "seq", scatter_dimension=1, tiled=True
        ).astype(jnp.float32),
        lax.psum_scatter(
            gate_grad.astype(jnp.bfloat16), "seq", scatter_dimension=0, tiled=True
        ).astype(jnp.float32),
        lax.psum_scatter(
            up_grad.astype(jnp.bfloat16), "seq", scatter_dimension=0, tiled=True
        ).astype(jnp.float32),
        lax.psum_scatter(
            down_grad.astype(jnp.bfloat16), "seq", scatter_dimension=1, tiled=True
        ).astype(jnp.float32),
    )
    gain_grads = (
        lax.psum_scatter(attn_gain_part, ("seq", "head"), scatter_dimension=0, tiled=True),
        lax.psum_scatter(ffn_gain_part, ("seq", "head"), scatter_dimension=0, tiled=True),
    )
    return (
        result.astype(jnp.bfloat16),
        input_grad,
        gain_grads[0],
        summed[0],
        summed[1],
        summed[2],
        summed[3],
        gain_grads[1],
        summed[4],
        summed[5],
        summed[6],
    )


MESH = pl.DeviceIdType.MESH
BF16 = jnp.bfloat16
F32 = jnp.float32
MIB = 2**20


def remote(src, dst, send_sem, recv_sem, where):
    return pltpu.make_async_remote_copy(
        src_ref=src,
        dst_ref=dst,
        send_sem=send_sem,
        recv_sem=recv_sem,
        device_id=where,
        device_id_type=MESH,
    )


class Place:
    def __init__(self, line):
        s, h = lax.axis_index("seq"), lax.axis_index("head")
        core = lax.rem(h, 2)
        x = lax.rem(lax.div(h, 2), 2)
        y = lax.div(h, 4)
        self.s, self.h, self.line = s, h, line
        self.turn = 1 - 2 * core
        self.core = h + self.turn
        over_x, over_y = 2 - 4 * x, 4 - 8 * y
        self.first = h + over_x * (1 - core) + over_y * core
        self.second = h + over_y * (1 - core) + over_x * core
        self.across = h + over_x + over_y

    def at(self, head):
        return (self.s, head)

    def greet(self, along_seq=True):
        barrier = pltpu.get_barrier_semaphore()
        for head in (self.core, self.first, self.second):
            pl.semaphore_signal(barrier, inc=1, device_id=self.at(head), device_id_type=MESH)
        if along_seq:

            @pl.when(self.s > 0)
            def _():
                pl.semaphore_signal(
                    barrier, inc=1, device_id=(self.s - 1, self.h), device_id_type=MESH
                )

            @pl.when(self.s < self.line - 1)
            def _():
                pl.semaphore_signal(
                    barrier, inc=1, device_id=(self.s + 1, self.h), device_id_type=MESH
                )

            @pl.when((self.s > 0) & (self.s < self.line - 1))
            def _():
                pl.semaphore_wait(barrier, 5)

            @pl.when((self.s == 0) | (self.s == self.line - 1))
            def _():
                pl.semaphore_wait(barrier, 4)
        else:
            pl.semaphore_wait(barrier, 3)


def greet_line(place):
    p = place
    barrier = pltpu.get_barrier_semaphore()
    for head in (p.core, p.first, p.second):
        pl.semaphore_signal(barrier, inc=1, device_id=p.at(head), device_id_type=MESH)
    for k in range(1, p.line):
        pl.semaphore_signal(
            barrier, inc=1, device_id=(lax.rem(p.s + k, p.line), p.h), device_id_type=MESH
        )
    pl.semaphore_wait(barrier, 2 + p.line)


class HeadGather:
    SEMS = 7

    def __init__(self, place, block, send, recv, own=None):
        p = place
        self.p = p
        plan = (
            (p.h, p.first, p.first),
            (p.h, p.second, p.second),
            (p.h, p.core, p.core),
            (p.first, p.second, p.across),
            (p.first, p.core, p.second + p.turn),
            (p.second, p.core, p.first + p.turn),
            (p.across, p.core, p.across + p.turn),
        )
        self.out = [
            remote(
                block(j) if own is None or i > 2 else own,
                block(j),
                send.at[i],
                recv.at[i],
                p.at(to),
            )
            for i, (j, to, _) in enumerate(plan)
        ]
        self.come = [
            remote(block(j), block(j), send.at[i], recv.at[i], p.at(to))
            for i, (_, to, j) in enumerate(plan)
        ]

    def start(self):
        for i in (0, 1, 2):
            self.out[i].start()

    def got_first(self):
        self.come[0].wait_recv()
        self.out[3].start()
        self.out[4].start()

    def got_second(self):
        self.come[1].wait_recv()
        self.out[5].start()

    def got_across(self):
        self.come[3].wait_recv()
        self.out[6].start()

    def got_core(self):
        self.come[2].wait_recv()

    def got_core_second(self):
        self.come[4].wait_recv()

    def got_core_first(self):
        self.come[5].wait_recv()

    def got_core_across(self):
        self.come[6].wait_recv()

    def finish(self):
        for copy in self.out:
            copy.wait_send()


class LineGather:
    def __init__(self, place, piece, up_send, up_recv, down_send, down_recv, own=None):
        self.p, self.piece, self.own = place, piece, own
        self.up = (up_send, up_recv)
        self.down = (down_send, down_recv)

    def _up(self, owner, t):
        p = self.p
        source = self.own if t == 0 and self.own is not None else self.piece(owner)
        return remote(
            source, self.piece(owner), self.up[0].at[t], self.up[1].at[t], (p.s + 1, p.h)
        )

    def _down(self, owner, t):
        p = self.p
        source = self.own if t == 0 and self.own is not None else self.piece(owner)
        return remote(
            source,
            self.piece(owner),
            self.down[0].at[t],
            self.down[1].at[t],
            (p.s - 1, p.h),
        )

    def start(self, t):
        p = self.p

        @pl.when((p.s < p.line - 1) & (p.s >= t))
        def _():
            self._up(p.s - t, t).start()

        @pl.when((p.s > 0) & (p.s + t < p.line))
        def _():
            self._down(p.s + t, t).start()

    def got(self, t):
        p = self.p

        @pl.when(p.s >= t + 1)
        def _():
            self._up(p.s - 1 - t, t).wait_recv()

        @pl.when(p.s + 1 + t < p.line)
        def _():
            self._down(p.s + 1 + t, t).wait_recv()

    def step(self, t):
        self.got(t)
        if t + 1 < self.p.line - 1:
            self.start(t + 1)

    def finish(self):
        p = self.p
        for t in range(p.line - 1):

            @pl.when((p.s < p.line - 1) & (p.s >= t))
            def _():
                self._up(p.s - t, t).wait_send()

            @pl.when((p.s > 0) & (p.s + t < p.line))
            def _():
                self._down(p.s + t, t).wait_send()


def line_sems(line, tensors=1):
    return [pltpu.SemaphoreType.DMA((line - 1,)) for _ in range(4 * tensors)]


def norm_rows(rows, gain):
    inverse = lax.rsqrt(jnp.mean(rows * rows, axis=-1, keepdims=True) + EPS)
    return rows * inverse * gain


def own_starts(segment):
    count = segment.shape[1]
    ids = segment[...]
    place = lax.broadcasted_iota(jnp.int32, (1, count), 1)
    starts = jnp.where((place > 0) & (ids != pltpu.roll(ids, 1, 1)), place, -1)
    shift = 1
    while shift < count:
        earlier = jnp.where(place >= shift, pltpu.roll(starts, shift, 1), -1)
        starts = jnp.maximum(starts, earlier)
        shift *= 2
    return starts


def any_spec():
    return pl.BlockSpec(memory_space=pl.ANY)


def vmem_spec():
    return pl.BlockSpec(memory_space=pltpu.VMEM)


LOG2E = 1.4426950408889634
TILE = 256
CHUNKS = WINDOW // TILE + 1


def tile_scores(tile, head, q, k_ext, floor):
    start = pl.multiple_of(tile * TILE, TILE)
    cols = slice(head * HEAD_DIM, (head + 1) * HEAD_DIM)
    queries = q[pl.ds(start, TILE), cols]
    row = lax.broadcasted_iota(jnp.int32, (TILE, TILE), 0)
    lane = lax.broadcasted_iota(jnp.int32, (TILE, TILE), 1)
    lowest = floor[:, pl.ds(start, TILE)] - start
    found = []
    for i in range(CHUNKS):
        keys = k_ext[pl.ds(start + i * TILE, TILE), cols]
        scores = product_nt(keys, queries)
        visible = row >= lowest - i * TILE
        if i == CHUNKS - 1:
            visible = visible & (row <= lane)
        found.append((scores, visible))
    return found


def forward_tile(tile, q, k_ext, v_t, floor, attended, logs):
    start = pl.multiple_of(tile * TILE, TILE)
    sharp = HEAD_DIM ** (-0.5) * LOG2E
    for head in range(q.shape[1] // HEAD_DIM):
        cols = slice(head * HEAD_DIM, (head + 1) * HEAD_DIM)
        found = [
            jnp.where(visible, scores, NEG)
            for scores, visible in tile_scores(tile, head, q, k_ext, floor)
        ]
        highest = functools.reduce(
            jnp.maximum, [jnp.max(scores, axis=0, keepdims=True) for scores in found]
        )
        total = jnp.zeros((1, TILE), F32)
        mixed = jnp.zeros((HEAD_DIM, TILE), F32)
        for i, scores in enumerate(found):
            weights = jnp.exp2((scores - highest) * sharp)
            total = total + jnp.sum(weights, axis=0, keepdims=True)
            mixed = mixed + product(
                v_t[cols, pl.ds(start + i * TILE, TILE)], weights.astype(BF16)
            )
        attended[pl.ds(start, TILE), cols] = (mixed / total).astype(BF16).T
        logs[head : head + 1, pl.ds(start, TILE)] = highest * sharp + jnp.log2(total)


def block_reduce(place, out, into, r_send, r_recv):
    p = place
    goes = (p.core, p.core, p.core, p.core, p.first, p.first, p.second)
    slots = (0, 1, 0, 1, 2, 3, 4)
    return [
        remote(out.at[slots[i]], into.at[i], r_send.at[i], r_recv.at[i], p.at(to))
        for i, to in enumerate(goes)
    ]


def forward_kernel(
    line,
    tokens,
    gain,
    wq,
    wk,
    wv,
    segment,
    cot,
    w_out,
    w_gate,
    w_up,
    normed_out,
    qkv_out,
    weight_out,
    floor,
    attended,
    logs,
    halo_out,
    cot_out,
    w_out_out,
    gate_full,
    up_full,
    middle,
    normed,
    weight,
    q,
    k_ext,
    v_ext,
    v_t,
    w_out_full,
    seg_halo,
    out,
    into,
    g_send,
    g_recv,
    c_send,
    c_recv,
    r_send,
    r_recv,
    halo_send,
    halo_recv,
    seg_sems,
    keep,
    *sems,
):
    p = Place(line)
    qkv_sems, out_sems, gate_sems, up_sems = sems[0:4], sems[4:8], sems[8:12], sems[12:16]
    rows, width = tokens.shape
    slab, part = wq.shape
    count = segment.shape[1]
    rows_of = lambda ref, j: ref.at[pl.ds(pl.multiple_of(j * rows, rows), rows)]
    slab_of = lambda d: weight.at[pl.ds(pl.multiple_of(d * slab, slab), slab)]
    weight_own = slab_of(p.s)
    weight_own[:, 0:part] = wq[...]
    weight_own[:, part : 2 * part] = wk[...]
    weight_own[:, 2 * part : 3 * part] = wv[...]
    seg_copy = remote(
        segment.at[:, pl.ds(count - WINDOW, WINDOW)],
        seg_halo,
        seg_sems.at[0],
        seg_sems.at[1],
        (p.s + 1, p.h),
    )
    halo = [
        remote(
            ext.at[pl.ds(count, WINDOW)],
            ext.at[pl.ds(0, WINDOW)],
            halo_send.at[i],
            halo_recv.at[i],
            (p.s + 1, p.h),
        )
        for i, ext in enumerate((k_ext, v_ext))
    ]
    gather = HeadGather(p, lambda j: rows_of(normed, j), g_send, g_recv)
    cot_gather = HeadGather(p, lambda j: rows_of(cot_out, j), c_send, c_recv, own=cot)
    qkv_gather = LineGather(p, slab_of, *qkv_sems)
    out_gather = LineGather(p, lambda d: w_out_full.at[d], *out_sems, own=w_out)
    gate_gather = LineGather(p, lambda d: gate_full.at[d], *gate_sems, own=w_gate)
    up_gather = LineGather(p, lambda d: up_full.at[d], *up_sems, own=w_up)
    p.greet()
    qkv_gather.start(0)

    @pl.when(p.s < line - 1)
    def _():
        seg_copy.start()

    mine = rows_of(normed, p.h)
    step = 32

    @pl.loop(0, rows // step)
    def _(i):
        at = pl.ds(pl.multiple_of(i * step, step), step)
        mine[at] = norm_rows(tokens[at].astype(F32), gain[...]).astype(BF16)

    gather.start()
    saved = []

    def save(source, target):
        copy = pltpu.make_async_copy(source, target, keep.at[len(saved)])
        copy.start()
        saved.append(copy)

    def save_block(j):
        save(rows_of(normed, j), rows_of(normed_out, j))

    save_block(p.h)
    save(cot, rows_of(cot_out, p.h))
    save(w_out, w_out_full.at[p.s])
    own_w_out = saved[-1]
    save(w_gate, gate_full.at[p.s])
    save(w_up, up_full.at[p.s])
    starts = own_starts(segment)

    @pl.when(p.s == 0)
    def _():
        k_ext[0:WINDOW, :] = jnp.zeros((WINDOW, part), BF16)
        v_ext[0:WINDOW, :] = jnp.zeros((WINDOW, part), BF16)

    @pl.when(p.s > 0)
    def _():
        seg_copy.wait_recv()

    before = jnp.sum(
        (seg_halo[...] == segment[:, 0:1]).astype(jnp.int32), axis=1, keepdims=True
    )
    before = jnp.where(p.s > 0, before, 0)
    floor[...] = jnp.maximum(
        lax.broadcasted_iota(jnp.int32, (1, count), 1),
        jnp.where(starts >= 0, starts + WINDOW, WINDOW - before),
    )
    gather.got_core()
    save_block(p.core)
    qkv_gather.step(0)
    gather.got_first()
    gather.got_second()
    cot_gather.start()
    save_block(p.first)
    save_block(p.second)
    qkv_gather.step(1)
    out_gather.start(0)
    gather.got_core_second()
    gather.got_core_first()
    save_block(p.second + p.turn)
    save_block(p.first + p.turn)
    qkv_gather.step(2)
    gather.got_across()
    save_block(p.across)
    gather.got_core_across()
    save_block(p.across + p.turn)
    save(weight, weight_out)

    def multiply(first, last):
        @pl.loop(first, last)
        def _(n):
            start = pl.multiple_of((count // rows - 1 - n) * rows, rows)
            value = product(normed[pl.ds(start, rows), :], weight[...]).astype(BF16)
            q[pl.ds(start, rows), :] = value[:, 0:part]
            k_ext[pl.ds(start + WINDOW, rows), :] = value[:, part : 2 * part]
            v_ext[pl.ds(start + WINDOW, rows), :] = value[:, 2 * part : 3 * part]

    late = (WINDOW + rows - 1) // rows
    multiply(0, late)

    @pl.when(p.s < line - 1)
    def _():
        halo[0].start()
        halo[1].start()

    multiply(late, count // rows)
    multiply(late, count // rows)
    out_gather.step(0)
    gate_gather.start(0)
    save(q, qkv_out.at[:, pl.ds(0, part)])
    save(k_ext.at[pl.ds(WINDOW, count)], qkv_out.at[:, pl.ds(part, part)])
    save(v_ext.at[pl.ds(WINDOW, count)], qkv_out.at[:, pl.ds(2 * part, part)])

    def turn(first, last):
        @pl.loop(first, last)
        def _(i):
            at = pl.ds(pl.multiple_of(i * TILE, TILE), TILE)
            v_t[:, at] = v_ext[at, :].T

    def tiles(first, last):
        @pl.loop(first, last)
        def _(tile):
            forward_tile(tile, q, k_ext, v_t, floor, attended, logs)

    ahead = WINDOW // TILE
    turn(ahead, ahead + count // TILE)
    tiles(ahead, ahead + 5)
    cot_gather.got_core()
    cot_gather.got_first()
    cot_gather.got_second()
    out_gather.step(1)
    up_gather.start(0)
    tiles(ahead + 5, count // TILE)

    @pl.when(p.s > 0)
    def _():
        halo[0].wait_recv()
        halo[1].wait_recv()

    turn(0, ahead)
    tiles(0, 2)
    cot_gather.got_core_second()
    cot_gather.got_core_first()
    cot_gather.got_across()
    gate_gather.step(0)
    tiles(2, ahead)
    out_gather.step(2)
    for i, ext in enumerate((k_ext, v_ext)):
        save(ext.at[pl.ds(0, WINDOW)], halo_out.at[i])
    own_w_out.wait()
    save(w_out_full, w_out_out)
    copies = block_reduce(p, out, into, r_send, r_recv)

    def emit(j, target, *more):
        start = pl.multiple_of(j * rows, rows)

        for n in range(line):
            cols = slice(n * slab, (n + 1) * slab)
            value = product(attended[pl.ds(start, rows), :], w_out_full[n])
            for other in more:
                value = value + other[:, cols].astype(F32)
            target[:, cols] = value.astype(target.dtype)

    emit(p.second + p.turn, out.at[0])
    copies[0].start()
    emit(p.across + p.turn, out.at[1])
    copies[1].start()
    copies[0].wait_recv()
    emit(p.first, out.at[2], into.at[0])
    copies[4].start()
    copies[0].wait_send()
    emit(p.first + p.turn, out.at[0])
    copies[2].start()
    copies[1].wait_recv()
    emit(p.across, out.at[3], into.at[1])
    copies[5].start()
    copies[1].wait_send()
    emit(p.core, out.at[1])
    copies[3].start()
    copies[3].wait_recv()
    emit(p.h, middle, into.at[3], tokens)
    up_gather.step(0)
    gate_gather.step(1)
    copies[2].wait_recv()
    cot_gather.got_core_across()
    up_gather.step(1)
    copies[5].wait_recv()
    emit(p.second, out.at[4], into.at[2], into.at[5])
    copies[6].start()
    gate_gather.step(2)
    copies[4].wait_recv()
    up_gather.step(2)
    copies[6].wait_recv()

    @pl.loop(0, line)
    def _(n):
        cols = pl.ds(pl.multiple_of(n * slab, slab), slab)
        middle[:, cols] += into[4, :, cols].astype(F32) + into[6, :, cols].astype(F32)

    for i in range(2, 7):
        copies[i].wait_send()
    gather.finish()
    cot_gather.finish()
    for each in (qkv_gather, out_gather, gate_gather, up_gather):
        each.finish()

    @pl.when(p.s < line - 1)
    def _():
        seg_copy.wait_send()
        halo[0].wait_send()
        halo[1].wait_send()

    for copy in saved:
        if copy is not own_w_out:
            copy.wait()


def forward(line, tokens, gain, wq, wk, wv, segment, cot, w_out, w_gate, w_up):
    rows, width = tokens.shape
    slab, part = wq.shape
    full = rows * 8
    units = w_gate.shape[0]
    heads = part // HEAD_DIM
    return pl.pallas_call(
        functools.partial(forward_kernel, line),
        out_shape=(
            jax.ShapeDtypeStruct((full, width), BF16),
            jax.ShapeDtypeStruct((full, 3 * part), BF16),
            jax.ShapeDtypeStruct((width, 3 * part), BF16),
            jax.ShapeDtypeStruct((1, full), jnp.int32),
            jax.ShapeDtypeStruct((full, part), BF16),
            jax.ShapeDtypeStruct((heads, full), F32),
            jax.ShapeDtypeStruct((2, WINDOW, part), BF16),
            jax.ShapeDtypeStruct((full, width), BF16),
            jax.ShapeDtypeStruct((line, part, slab), BF16),
            jax.ShapeDtypeStruct((line, units, slab), BF16),
            jax.ShapeDtypeStruct((line, units, slab), BF16),
            jax.ShapeDtypeStruct((rows, width), F32),
        ),
        in_specs=[vmem_spec()] * 10,
        out_specs=(
            any_spec(),
            any_spec(),
            any_spec(),
            vmem_spec(),
            vmem_spec(),
            vmem_spec(),
            any_spec(),
            any_spec(),
            any_spec(),
            any_spec(),
            any_spec(),
            vmem_spec(),
        ),
        scratch_shapes=[
            pltpu.VMEM((full, width), BF16),
            pltpu.VMEM((width, 3 * part), BF16),
            pltpu.VMEM((full, part), BF16),
            pltpu.VMEM((WINDOW + full, part), BF16),
            pltpu.VMEM((WINDOW + full, part), BF16),
            pltpu.VMEM((part, WINDOW + full), BF16),
            pltpu.VMEM((line, part, slab), BF16),
            pltpu.VMEM((1, WINDOW), jnp.int32),
            pltpu.VMEM((5, rows, width), BF16),
            pltpu.VMEM((7, rows, width), BF16),
            pltpu.SemaphoreType.DMA((7,)),
            pltpu.SemaphoreType.DMA((7,)),
            pltpu.SemaphoreType.DMA((7,)),
            pltpu.SemaphoreType.DMA((7,)),
            pltpu.SemaphoreType.DMA((7,)),
            pltpu.SemaphoreType.DMA((7,)),
            pltpu.SemaphoreType.DMA((2,)),
            pltpu.SemaphoreType.DMA((2,)),
            pltpu.SemaphoreType.DMA((2,)),
            pltpu.SemaphoreType.DMA((19,)),
            *line_sems(line, 4),
        ],
        compiler_params=pltpu.CompilerParams(
            collective_id=1, has_side_effects=True, vmem_limit_bytes=62 * MIB
        ),
        cost_estimate=pl.CostEstimate(
            flops=20 * 2**30, bytes_accessed=100 * MIB, transcendentals=0
        ),
    )(tokens, gain.reshape(1, width), wq, wk, wv, segment.reshape(1, full), cot, w_out, w_gate, w_up)


def sigmoid_of(value):
    return 0.5 * jnp.tanh(0.5 * value) + 0.5


def strips(width, most=256):
    return [(start, min(start + most, width)) for start in range(0, width, most)]


def feed_kernel(
    line,
    middle,
    gain,
    cot,
    gate,
    up,
    down,
    normed_out,
    hidden_out,
    grad_gate_out,
    grad_up_out,
    grad_out,
    down_out,
    down_grad,
    normed,
    w_gate,
    w_up,
    w_down,
    gates,
    ups,
    cot_block,
    hidden,
    grad_gate,
    grad_up,
    down_parts,
    down_up_in,
    down_down_in,
    out,
    into,
    r_send,
    r_recv,
    g_send,
    g_recv,
    *sems,
):
    p = Place(line)
    down_sems, sum_sems, loads, saves, stage, strip_sems = sems[0:4], sems[4:8], *sems[8:12]
    rows, width = grad_out.shape
    units = w_down.shape[1]
    slab = w_down.shape[2]
    block = lambda j: normed.at[pl.ds(pl.multiple_of(j * rows, rows), rows)]
    rows_of = lambda ref, j: ref.at[pl.ds(pl.multiple_of(j * rows, rows), rows)]
    gather = HeadGather(p, block, g_send, g_recv)
    down_gather = LineGather(p, lambda d: w_down.at[d], *down_sems, own=down)
    p.greet()
    down_gather.start(0)
    started = [
        pltpu.make_async_copy(middle, grad_out, loads.at[0]),
        pltpu.make_async_copy(gate, w_gate, loads.at[1]),
        pltpu.make_async_copy(up, w_up, loads.at[3]),
        pltpu.make_async_copy(down, w_down.at[p.s], loads.at[4]),
    ]
    for copy in started:
        copy.start()
    started[0].wait()
    mine = block(p.h)
    step = 32

    @pl.loop(0, rows // step)
    def _(i):
        at = pl.ds(pl.multiple_of(i * step, step), step)
        mine[at] = norm_rows(grad_out[at], gain[...]).astype(BF16)

    gather.out[0].start()
    gather.out[2].start()
    saved = []

    def save(j):
        copy = pltpu.make_async_copy(block(j), rows_of(normed_out, j), saves.at[len(saved)])
        copy.start()
        saved.append(copy)

    opened = (
        p.h,
        p.core,
        p.first,
        p.second + p.turn,
        p.first + p.turn,
        p.second,
        p.across + p.turn,
        p.across,
    )
    hidden_stores = [
        pltpu.make_async_copy(hidden.at[m % 2], rows_of(hidden_out, j), stage.at[m % 2])
        for m, j in enumerate(opened)
    ]

    def open_up(m, slot):
        start = pl.multiple_of(opened[m] * rows, rows)
        if m > 1:
            hidden_stores[m - 2].wait()
        for first, last in strips(units):
            found = []
            for weight in (w_gate, w_up):
                value = product_nt(normed[pl.ds(start, rows), 0:slab], weight[0, first:last, :])
                for d in range(1, line):
                    value = value + product_nt(
                        normed[pl.ds(start, rows), d * slab : (d + 1) * slab],
                        weight[d, first:last, :],
                    )
                found.append(value)
            value, lift = found
            gates[slot, :, first:last] = value.astype(BF16)
            ups[slot, :, first:last] = lift.astype(BF16)
            hidden[m % 2, :, first:last] = (value * sigmoid_of(value) * lift).astype(BF16)
        hidden_stores[m].start()

    order = (
        p.second + p.turn,
        p.first,
        p.across + p.turn,
        p.across,
        p.first + p.turn,
        p.second,
        p.core,
        p.h,
    )
    fetches = [
        pltpu.make_async_copy(rows_of(cot, j), cot_block, stage.at[6]) for j in order
    ]
    stores = [
        [
            pltpu.make_async_copy(
                held.at[n % 2], rows_of(home, j), stage.at[2 + 2 * (n % 2) + i]
            )
            for i, (held, home) in enumerate(
                ((grad_gate, grad_gate_out), (grad_up, grad_up_out))
            )
        ]
        for n, j in enumerate(order)
    ]

    def close(n, slot):
        fetches[n].wait()
        if n > 1:
            for copy in stores[n - 2]:
                copy.wait()
        turn = n % 2
        for first, last in strips(units):
            grad = product_nt(cot_block[:, 0:slab], w_down[0, first:last, :])
            for d in range(1, line):
                grad = grad + product_nt(
                    cot_block[:, d * slab : (d + 1) * slab], w_down[d, first:last, :]
                )
            gate = gates[slot, :, first:last].astype(F32)
            lift = ups[slot, :, first:last].astype(F32)
            sigmoid = sigmoid_of(gate)
            grad_up[turn, :, first:last] = (grad * gate * sigmoid).astype(BF16)
            grad_gate[turn, :, first:last] = (
                grad * lift * (sigmoid * (1.0 + gate * (1.0 - sigmoid)))
            ).astype(BF16)
        if n + 1 < len(order):
            fetches[n + 1].start()
        for copy in stores[n]:
            copy.start()

    def back(n, target, *more):
        turn = n % 2

        for d in range(line):
            cols = slice(d * slab, (d + 1) * slab)
            value = product(grad_gate[turn], w_gate[d]) + product(grad_up[turn], w_up[d])
            for other in more:
                value = value + other[:, cols].astype(F32)
            target[:, cols] = value.astype(target.dtype)

    copies = block_reduce(p, out, into, r_send, r_recv)
    down_reduce = LineReduce(
        p, lambda d: down_parts.at[d], down_up_in, down_down_in, *sum_sems
    )
    wide = slab
    padded = hidden.shape[2]
    kept = slice(2 * wide, 2 * wide + units)
    hidden[:, :, units // 128 * 128 :] = jnp.zeros((2, rows, padded - units // 128 * 128), BF16)
    multiply = lambda *some: weight_product(
        lambda rows_in: product_tn(normed[:, kept], rows_in),
        cot,
        lambda d: down_parts.at[d],
        lambda k: normed.at[:, pl.ds(pl.multiple_of(k * wide, wide), wide)],
        wide,
        strip_sems,
        p,
        *some,
    )
    fetches[0].start()
    for copy in started[1:3]:
        copy.wait()
    save(p.h)
    open_up(0, 0)
    gather.got_core()
    save(p.core)
    open_up(1, 1)
    gather.out[0].wait_send()
    gather.out[1].start()
    gather.got_first()
    save(p.first)
    down_gather.step(0)
    open_up(2, 2)
    gather.got_core_second()
    save(p.second + p.turn)
    open_up(3, 3)
    down_gather.step(1)
    gather.got_second()
    save(p.second)
    gather.got_core_first()
    save(p.first + p.turn)
    open_up(4, 4)
    open_up(5, 5)
    clear_last(down_reduce)
    down_gather.step(2)
    started[3].wait()
    down_save = pltpu.make_async_copy(w_down, down_out, loads.at[4])
    down_save.start()
    close(0, 3)
    back(0, out.at[0])
    copies[0].start()
    gather.got_across()
    save(p.across)
    close(1, 2)
    copies[0].wait_recv()
    back(1, out.at[2], into.at[0])
    copies[4].start()
    gather.got_core_across()
    save(p.across + p.turn)
    open_up(6, 2)
    open_up(7, 3)
    for copy in gather.out[1:]:
        copy.wait_send()
    for copy in saved:
        copy.wait()
    for copy in hidden_stores[6:]:
        copy.wait()
    fill = pltpu.make_async_copy(hidden_out, normed.at[:, pl.ds(2 * wide, padded)], loads.at[5])
    fill.start()
    fill.wait()
    multiply(0, 1)
    down_reduce.start(0)
    multiply(1, 2)
    close(2, 2)
    back(2, out.at[1])
    copies[1].start()
    close(3, 3)
    copies[1].wait_recv()
    back(3, out.at[3], into.at[1])
    copies[5].start()
    down_reduce.step(0)
    multiply(2, line)
    close(4, 4)
    copies[0].wait_send()
    back(4, out.at[0])
    copies[2].start()
    close(5, 5)
    copies[2].wait_recv()
    copies[5].wait_recv()
    back(5, out.at[4], into.at[2], into.at[5])
    copies[6].start()
    down_reduce.step(1)
    close(6, 1)
    copies[1].wait_send()
    back(6, out.at[1])
    copies[3].start()
    close(7, 0)
    copies[3].wait_recv()
    back(7, grad_out, into.at[3])
    copies[4].wait_recv()
    copies[6].wait_recv()

    @pl.loop(0, line)
    def _(d):
        cols = pl.ds(pl.multiple_of(d * slab, slab), slab)
        grad_out[:, cols] += into[4, :, cols].astype(F32) + into[6, :, cols].astype(F32)

    down_reduce.step(2)
    for first, last in strips(units, 128):
        down_grad[first:last, :] = down_reduce.total(slice(first, last))
    for i in range(2, 7):
        copies[i].wait_send()
    down_gather.finish()
    down_reduce.finish()
    for copy in stores[6] + stores[7]:
        copy.wait()
    down_save.wait()


def feed(line, middle, gain, cot, gate, up, down):
    rows, width = middle.shape
    units, slab = down.shape
    full = rows * 8
    padded = (units + 127) // 128 * 128
    return pl.pallas_call(
        functools.partial(feed_kernel, line),
        out_shape=(
            jax.ShapeDtypeStruct((full, width), BF16),
            jax.ShapeDtypeStruct((full, padded), BF16),
            jax.ShapeDtypeStruct((full, units), BF16),
            jax.ShapeDtypeStruct((full, units), BF16),
            jax.ShapeDtypeStruct((rows, width), F32),
            jax.ShapeDtypeStruct((line, units, slab), BF16),
            jax.ShapeDtypeStruct((units, slab), F32),
        ),
        in_specs=[any_spec(), vmem_spec()] + [any_spec()] * 4,
        out_specs=(
            any_spec(),
            any_spec(),
            any_spec(),
            any_spec(),
            vmem_spec(),
            any_spec(),
            vmem_spec(),
        ),
        scratch_shapes=[
            pltpu.VMEM((full, width), BF16),
            pltpu.VMEM((line, units, slab), BF16),
            pltpu.VMEM((line, units, slab), BF16),
            pltpu.VMEM((line, units, slab), BF16),
            pltpu.VMEM((6, rows, units), BF16),
            pltpu.VMEM((6, rows, units), BF16),
            pltpu.VMEM((rows, width), BF16),
            pltpu.VMEM((2, rows, padded), BF16),
            pltpu.VMEM((2, rows, units), BF16),
            pltpu.VMEM((2, rows, units), BF16),
            pltpu.VMEM((line, units, slab), BF16),
            pltpu.VMEM((line - 1, units, slab), BF16),
            pltpu.VMEM((line - 1, units, slab), BF16),
            pltpu.VMEM((5, rows, width), BF16),
            pltpu.VMEM((7, rows, width), BF16),
            pltpu.SemaphoreType.DMA((7,)),
            pltpu.SemaphoreType.DMA((7,)),
            pltpu.SemaphoreType.DMA((7,)),
            pltpu.SemaphoreType.DMA((7,)),
            *line_sems(line, 2),
            pltpu.SemaphoreType.DMA((6,)),
            pltpu.SemaphoreType.DMA((8,)),
            pltpu.SemaphoreType.DMA((7,)),
            pltpu.SemaphoreType.DMA((2,)),
        ],
        compiler_params=pltpu.CompilerParams(
            collective_id=2, has_side_effects=True, vmem_limit_bytes=63 * MIB
        ),
        cost_estimate=pl.CostEstimate(
            flops=50 * 2**30, bytes_accessed=80 * MIB, transcendentals=0
        ),
    )(middle, gain.reshape(1, width), cot, gate, up, down)


class LineReduce:
    def __init__(self, place, part, up_in, down_in, up_send, up_recv, down_send, down_recv):
        self.p, self.part = place, part
        self.up_in, self.down_in = up_in, down_in
        self.up = (up_send, up_recv)
        self.down = (down_send, down_recv)

    def _up(self, d, t):
        p = self.p
        return remote(
            self.part(d), self.up_in.at[t], self.up[0].at[t], self.up[1].at[t], (p.s + 1, p.h)
        )

    def _down(self, d, t):
        p = self.p
        return remote(
            self.part(d),
            self.down_in.at[t],
            self.down[0].at[t],
            self.down[1].at[t],
            (p.s - 1, p.h),
        )

    def _sends(self, t):
        p, last = self.p, self.p.line - 1
        return (
            ((p.s <= t) & (p.s < last), self._up, last - t + p.s),
            ((last - p.s <= t) & (p.s > 0), self._down, t - last + p.s),
        )

    def start(self, t):
        p, last = self.p, self.p.line - 1
        for number, (goes, copy, d) in enumerate(self._sends(t)):
            came = (self.up_in, self.down_in)[number]

            @pl.when(goes)
            def _():
                if t > 0:
                    inner = p.s > 0 if number == 0 else p.s < last

                    @pl.when(inner)
                    def _():
                        add_rows(self.part(d), came.at[t - 1])

                copy(d, t).start()

    def got(self, t):
        p, last = self.p, self.p.line - 1

        @pl.when((p.s >= 1) & (t >= p.s - 1))
        def _():
            self._up(0, t).wait_recv()

        @pl.when((p.s < last) & (t >= last - p.s - 1))
        def _():
            self._down(0, t).wait_recv()

    def step(self, t):
        self.got(t)
        if t + 1 < self.p.line - 1:
            self.start(t + 1)

    def end(self):
        p, last = self.p, self.p.line - 1

        @pl.when(p.s >= 1)
        def _():
            add_rows(self.part(p.s), self.up_in.at[last - 1])

        @pl.when(p.s < last)
        def _():
            add_rows(self.part(p.s), self.down_in.at[last - 1])

    def total(self, rows):
        p, last = self.p, self.p.line - 1
        value = self.part(p.s)[rows, :].astype(F32)
        value = value + jnp.where(p.s >= 1, self.up_in[last - 1, rows, :].astype(F32), 0.0)
        return value + jnp.where(p.s < last, self.down_in[last - 1, rows, :].astype(F32), 0.0)

    def finish(self):
        for t in range(self.p.line - 1):
            for goes, copy, d in self._sends(t):

                @pl.when(goes)
                def _():
                    copy(d, t).wait_send()


def add_rows(target, other):
    step = 16

    @pl.loop(0, target.shape[0] // step)
    def _(i):
        at = pl.ds(pl.multiple_of(i * step, step), step)
        target[at, :] = (target[at, :].astype(F32) + other[at, :].astype(F32)).astype(BF16)


def clear_last(reduce):
    p, last = reduce.p, reduce.p.line - 1

    @pl.when(p.s == 0)
    def _():
        reduce.up_in[last - 1] = jnp.zeros(reduce.up_in.shape[1:], BF16)

    @pl.when(p.s == last)
    def _():
        reduce.down_in[last - 1] = jnp.zeros(reduce.down_in.shape[1:], BF16)


def weight_product(apply, source, piece, strip, wide, sems, place, first, last):
    each = piece(0).shape[1] // wide
    begin, end = first * each, last * each

    def slab(n):
        d = lax.div(n, each)
        low = place.s < place.line // 2
        return jnp.where(low, place.line - 1 - d, d)

    def fetch(n):
        at = slab(n) * each + lax.rem(n, each)
        cols = pl.ds(pl.multiple_of(at * wide, wide), wide)
        return pltpu.make_async_copy(
            source.at[:, cols], strip(lax.rem(n, 2)), sems.at[lax.rem(n, 2)]
        )

    fetch(begin).start()

    @pl.loop(begin, end)
    def _(n):
        @pl.when(n + 1 < end)
        def _():
            fetch(n + 1).start()

        fetch(n).wait()
        cols = pl.ds(pl.multiple_of(lax.rem(n, each) * wide, wide), wide)
        piece(slab(n))[:, cols] = apply(strip(lax.rem(n, 2))[...]).astype(BF16)


def turn_rows(source, target):
    step = 256

    @pl.loop(0, source.shape[0] // step)
    def _(i):
        at = pl.ds(pl.multiple_of(i * step, step), step)
        for first, last in strips(source.shape[1], 128):
            target[first:last, at] = source[at, first:last].T


def return_kernel(
    line,
    grad_given,
    middle_given,
    cot_given,
    gain,
    attended_given,
    w_out_given,
    grad_gate,
    grad_up,
    normed,
    grad_middle_out,
    gain_part,
    grad_attended,
    inner,
    up_grad,
    gate_parts,
    out_parts,
    branch,
    units_in,
    strip,
    up_parts,
    other_parts,
    up_up_in,
    up_down_in,
    att_turned,
    out_sum,
    grad_normed,
    middle,
    cot_own,
    attended,
    w_out,
    grad_middle,
    g_send,
    g_recv,
    *sems,
):
    p = Place(line)
    up_sems, loads, strips_sem, saves, early, kept = sems[0:4], *sems[4:9]
    rows, width = grad_normed.shape
    slab = w_out.shape[2]
    part = attended.shape[1]
    block = lambda j: branch.at[pl.ds(pl.multiple_of(j * rows, rows), rows)]
    gather = HeadGather(p, block, g_send, g_recv)
    up_reduce = LineReduce(p, lambda d: up_parts.at[d], up_up_in, up_down_in, *up_sems)
    load = [
        pltpu.make_async_copy(source, units_in, loads.at[i])
        for i, source in enumerate((grad_up, grad_gate))
    ]
    pieces = 4
    piece_rows = rows // pieces
    piece_at = [pl.ds(i * piece_rows, piece_rows) for i in range(pieces)]
    arriving = [
        [
            pltpu.make_async_copy(source.at[at], target.at[at], early.at[3 * i + k])
            for k, (source, target) in enumerate(
                ((grad_given, grad_normed), (middle_given, middle), (cot_given, cot_own))
            )
        ]
        for i, at in enumerate(piece_at)
    ]
    leaving = [
        pltpu.make_async_copy(grad_middle.at[at], grad_middle_out.at[at], kept.at[i])
        for i, at in enumerate(piece_at)
    ]
    later = [
        pltpu.make_async_copy(attended_given, attended, early.at[3 * pieces]),
        pltpu.make_async_copy(w_out_given, w_out, early.at[3 * pieces + 1]),
    ]
    for group in arriving:
        for copy in group:
            copy.start()
    load[0].start()
    for copy in later:
        copy.start()
    p.greet()
    mine = block(p.h)
    gain_part[...] = jnp.zeros_like(gain_part)
    step = 32

    def piece_back(number, i):
        at = pl.ds(pl.multiple_of(number * piece_rows + i * step, step), step)
        value = middle[at]
        inverse = lax.rsqrt(jnp.mean(value * value, axis=-1, keepdims=True) + EPS)
        unit = value * inverse
        grad = grad_normed[at]
        gain_part[...] += jnp.sum(grad * unit, axis=0, keepdims=True)
        result = cot_own[at].astype(F32) + norm_back(unit, inverse, gain[...], grad)
        grad_middle[at] = result
        mine[at] = result.astype(BF16)

    for number in range(pieces):
        for copy in arriving[number]:
            copy.wait()
        pl.loop(0, piece_rows // step)(functools.partial(piece_back, number))
        leaving[number].start()

    gather.start()
    clear_last(up_reduce)
    multiply = lambda parts, *some: weight_product(
        lambda rows_in: product_tn(units_in[...], rows_in),
        normed,
        lambda d: parts.at[d],
        strip.at.__getitem__,
        strip.shape[2],
        strips_sem,
        p,
        *some,
    )
    load[0].wait()
    multiply(up_parts, 0, 1)
    up_reduce.start(0)
    multiply(up_parts, 1, line)
    load[1].start()
    gather.got_core()
    load[1].wait()
    up_reduce.step(0)
    gather.got_first()
    gather.got_second()
    multiply(other_parts, 0, line)
    save_gate = pltpu.make_async_copy(other_parts, gate_parts, saves.at[1])
    save_gate.start()
    for copy in later:
        copy.wait()
    turn_rows(attended, att_turned)
    up_reduce.step(1)
    gather.got_core_second()
    gather.got_core_first()
    out_sum[...] = jnp.zeros_like(out_sum)

    def take(j):
        start = pl.multiple_of(j * rows, rows)
        at = pl.ds(start, rows)
        total = product_nt(branch[at, 0:slab], w_out[0])
        for d in range(1, line):
            total = total + product_nt(branch[at, d * slab : (d + 1) * slab], w_out[d])
        low = total.astype(BF16)
        grad_attended[at, :] = low
        for head in range(part // HEAD_DIM):
            cols = slice(head * HEAD_DIM, (head + 1) * HEAD_DIM)
            both = low[:, cols].astype(F32) * attended[at, cols].astype(F32)
            inner[head : head + 1, at] = jnp.sum(both.T, axis=0, keepdims=True)

        @pl.loop(0, line)
        def _(d):
            cols = pl.ds(pl.multiple_of(d * slab, slab), slab)
            out_sum[d] += product(att_turned[:, at], branch[at, cols])

    for j in (p.h, p.core, p.first, p.second):
        take(j)
    for j in (p.second + p.turn, p.first + p.turn):
        take(j)
    gather.got_across()
    take(p.across)
    gather.got_core_across()
    take(p.across + p.turn)
    for d in range(line):
        out_parts[d] = out_sum[d].astype(BF16)
    up_reduce.step(2)
    for first, last in strips(up_grad.shape[0], 128):
        up_grad[first:last, :] = up_reduce.total(slice(first, last))
    gather.finish()
    up_reduce.finish()
    save_gate.wait()
    for copy in leaving:
        copy.wait()


def give_back(
    line, grad_normed, middle, cot_own, gain, attended, w_out, grad_gate, grad_up, normed
):
    rows, width = middle.shape
    full, units = grad_up.shape
    part = attended.shape[1]
    slab = w_out.shape[2]
    heads = part // HEAD_DIM
    return pl.pallas_call(
        functools.partial(return_kernel, line),
        out_shape=(
            jax.ShapeDtypeStruct((rows, width), F32),
            jax.ShapeDtypeStruct((1, width), F32),
            jax.ShapeDtypeStruct((full, part), BF16),
            jax.ShapeDtypeStruct((heads, full), F32),
            jax.ShapeDtypeStruct((units, slab), F32),
            jax.ShapeDtypeStruct((line, units, slab), BF16),
            jax.ShapeDtypeStruct((line, part, slab), BF16),
        ),
        in_specs=[any_spec()] * 3 + [vmem_spec()] + [any_spec()] * 5,
        out_specs=(
            any_spec(),
            vmem_spec(),
            vmem_spec(),
            vmem_spec(),
            vmem_spec(),
            any_spec(),
            vmem_spec(),
        ),
        scratch_shapes=[
            pltpu.VMEM((full, width), BF16),
            pltpu.VMEM((full, units), BF16),
            pltpu.VMEM((2, full, slab), BF16),
            pltpu.VMEM((line, units, slab), BF16),
            pltpu.VMEM((line, units, slab), BF16),
            pltpu.VMEM((line - 1, units, slab), BF16),
            pltpu.VMEM((line - 1, units, slab), BF16),
            pltpu.VMEM((part, full), BF16),
            pltpu.VMEM((line, part, slab), F32),
            pltpu.VMEM((rows, width), F32),
            pltpu.VMEM((rows, width), F32),
            pltpu.VMEM((rows, width), BF16),
            pltpu.VMEM((full, part), BF16),
            pltpu.VMEM((line, part, slab), BF16),
            pltpu.VMEM((rows, width), F32),
            pltpu.SemaphoreType.DMA((7,)),
            pltpu.SemaphoreType.DMA((7,)),
            *line_sems(line),
            pltpu.SemaphoreType.DMA((2,)),
            pltpu.SemaphoreType.DMA((2,)),
            pltpu.SemaphoreType.DMA((2,)),
            pltpu.SemaphoreType.DMA((14,)),
            pltpu.SemaphoreType.DMA((4,)),
        ],
        compiler_params=pltpu.CompilerParams(
            collective_id=3, has_side_effects=True, vmem_limit_bytes=62 * MIB
        ),
        cost_estimate=pl.CostEstimate(
            flops=25 * 2**30, bytes_accessed=80 * MIB, transcendentals=0
        ),
    )(
        grad_normed,
        middle,
        cot_own,
        gain.reshape(1, width),
        attended,
        w_out,
        grad_gate,
        grad_up,
        normed,
    )


def backward_tile(tile, q, k_ext, v_ext, k_t, floor, logs, inner, grad, key_sum, value_sum):
    start = pl.multiple_of(tile * TILE, TILE)
    mine = pl.ds(start, TILE)
    scale = HEAD_DIM ** (-0.5)
    for head in range(q.shape[1] // HEAD_DIM):
        cols = slice(head * HEAD_DIM, (head + 1) * HEAD_DIM)
        queries = q[mine, cols]
        grads = grad[mine, cols]
        log = logs[head : head + 1, mine]
        middle = inner[head : head + 1, mine]
        turned = jnp.zeros((HEAD_DIM, TILE), F32)
        for i, (scores, visible) in enumerate(tile_scores(tile, head, q, k_ext, floor)):
            at = pl.ds(start + i * TILE, TILE)
            probs = jnp.where(visible, jnp.exp2(scores * (scale * LOG2E) - log), 0.0)
            grad_probs = product_nt(v_ext[at, cols], grads)
            grad_scores = (probs * (grad_probs - middle)).astype(BF16)
            value_sum[at, cols] += product(probs.astype(BF16), grads)
            key_sum[at, cols] += product(grad_scores, queries)
            turned = turned + product(k_t[cols, at], grad_scores)
        q[mine, cols] = (turned * scale).astype(BF16).T


def attend_back_kernel(
    line,
    qkv,
    halo_kv,
    floor,
    logs,
    grad_given,
    inner,
    hidden,
    w_down_given,
    middle,
    gate_in,
    grads_out,
    result,
    gate_grad,
    q,
    k_ext,
    v_ext,
    k_t,
    key_sum,
    value_sum,
    halo_out,
    halo_in,
    gate_parts,
    gate_up_in,
    gate_down_in,
    out,
    into,
    total,
    hidden_block,
    grad,
    w_down,
    r_send,
    r_recv,
    *sems,
):
    p = Place(line)
    gate_sems, loads, halo_send, halo_recv, stage, saves = sems[0:4], *sems[4:9]
    rows, width = result.shape
    slab = w_down.shape[2]
    count, part = q.shape
    scale = HEAD_DIM ** (-0.5)
    rows_of = lambda ref, j: ref.at[pl.ds(pl.multiple_of(j * rows, rows), rows)]
    gate_reduce = LineReduce(
        p, lambda d: gate_parts.at[d], gate_up_in, gate_down_in, *gate_sems
    )
    started = [
        pltpu.make_async_copy(gate_in, gate_parts, loads.at[0]),
        pltpu.make_async_copy(qkv.at[:, pl.ds(0, part)], q, loads.at[1]),
        pltpu.make_async_copy(
            qkv.at[:, pl.ds(part, part)], k_ext.at[pl.ds(WINDOW, count)], loads.at[2]
        ),
        pltpu.make_async_copy(
            qkv.at[:, pl.ds(2 * part, part)], v_ext.at[pl.ds(WINDOW, count)], loads.at[3]
        ),
        pltpu.make_async_copy(halo_kv.at[0], k_ext.at[pl.ds(0, WINDOW)], loads.at[4]),
        pltpu.make_async_copy(halo_kv.at[1], v_ext.at[pl.ds(0, WINDOW)], loads.at[5]),
        pltpu.make_async_copy(middle, total, loads.at[6]),
        pltpu.make_async_copy(grad_given, grad, loads.at[7]),
    ]
    down_load = pltpu.make_async_copy(w_down_given, w_down, loads.at[8])
    halo = [
        remote(
            halo_out.at[i], halo_in.at[i], halo_send.at[i], halo_recv.at[i], (p.s - 1, p.h)
        )
        for i in range(2)
    ]
    order = (
        p.second + p.turn,
        p.across + p.turn,
        p.first,
        p.first + p.turn,
        p.across,
        p.core,
        p.h,
        p.second,
    )
    fetches = [
        pltpu.make_async_copy(rows_of(hidden, j), hidden_block.at[n % 2], stage.at[n % 2])
        for n, j in enumerate(order)
    ]
    copies = block_reduce(p, out, into, r_send, r_recv)

    def emit(n, target, *more):
        fetches[n].wait()
        if n + 1 < len(order):
            fetches[n + 1].start()

        for d in range(line):
            cols = slice(d * slab, (d + 1) * slab)
            value = product(hidden_block[n % 2][:, 0 : w_down.shape[1]], w_down[d])
            for other in more:
                value = value + other[:, cols].astype(F32)
            target[:, cols] = value.astype(target.dtype)

    def tiles(first, last):
        @pl.loop(first, last)
        def _(tile):
            backward_tile(
                tile, q, k_ext, v_ext, k_t, floor, logs, inner, grad, key_sum, value_sum
            )

    down_load.start()
    fetches[0].start()
    for copy in started:
        copy.start()
    p.greet()
    started[0].wait()
    gate_reduce.start(0)
    clear_last(gate_reduce)
    down_load.wait()
    emit(0, out.at[0])
    copies[0].start()
    emit(1, out.at[1])
    copies[1].start()
    copies[0].wait_recv()
    emit(2, out.at[2], into.at[0])
    copies[4].start()
    copies[0].wait_send()
    emit(3, out.at[0])
    copies[2].start()
    copies[1].wait_recv()
    emit(4, out.at[3], into.at[1])
    copies[5].start()
    copies[1].wait_send()
    emit(5, out.at[1])
    copies[3].start()
    for copy in started[1:]:
        copy.wait()
    gate_reduce.step(0)

    @pl.loop(0, (WINDOW + count) // TILE)
    def _(i):
        at = pl.ds(pl.multiple_of(i * TILE, TILE), TILE)
        k_t[:, at] = k_ext[at, :].T
        key_sum[at, :] = jnp.zeros((TILE, part), F32)
        value_sum[at, :] = jnp.zeros((TILE, part), F32)

    ahead = WINDOW // TILE
    last = count // TILE
    tiles(0, ahead)

    @pl.when(p.s > 0)
    def _():
        @pl.loop(0, ahead)
        def _(i):
            at = pl.ds(pl.multiple_of(i * TILE, TILE), TILE)
            halo_out[0, at, :] = (key_sum[at, :] * scale).astype(BF16)
            halo_out[1, at, :] = value_sum[at, :].astype(BF16)

        halo[0].start()
        halo[1].start()

    gate_reduce.step(1)
    tiles(ahead, ahead + 4)
    copies[3].wait_recv()
    emit(6, total, into.at[3], total)
    copies[2].wait_recv()
    copies[5].wait_recv()
    emit(7, out.at[4], into.at[2], into.at[5])
    copies[6].start()
    tiles(ahead + 4, last)

    @pl.when(p.s < line - 1)
    def _():
        halo[0].wait_recv()
        halo[1].wait_recv()

    @pl.loop(0, last)
    def _(i):
        here = pl.ds(pl.multiple_of(i * TILE, TILE), TILE)
        at = pl.ds(pl.multiple_of(i * TILE + WINDOW, TILE), TILE)
        key_value = key_sum[at, :] * scale
        value_value = value_sum[at, :]
        k_ext[here, :] = key_value.astype(BF16)
        v_ext[here, :] = value_value.astype(BF16)

    @pl.when(p.s < line - 1)
    def _():
        @pl.loop(0, ahead)
        def _(i):
            here = pl.ds(pl.multiple_of(i * TILE, TILE), TILE)
            near = pl.ds(pl.multiple_of(i * TILE + count, TILE), TILE)
            there = pl.ds(pl.multiple_of(i * TILE + count - WINDOW, TILE), TILE)
            k_ext[there, :] = (
                key_sum[near, :] * scale + halo_in[0, here, :].astype(F32)
            ).astype(BF16)
            v_ext[there, :] = (value_sum[near, :] + halo_in[1, here, :].astype(F32)).astype(BF16)

    save = [
        pltpu.make_async_copy(
            ref.at[pl.ds(0, count)], grads_out.at[:, pl.ds(i * part, part)], saves.at[i]
        )
        for i, ref in enumerate((q, k_ext, v_ext))
    ]
    for copy in save:
        copy.start()
    copies[4].wait_recv()
    copies[6].wait_recv()

    @pl.loop(0, line)
    def _(d):
        cols = pl.ds(pl.multiple_of(d * slab, slab), slab)
        value = total[:, cols] + into[4, :, cols].astype(F32) + into[6, :, cols].astype(F32)
        result[:, cols] = value.astype(BF16)

    gate_reduce.step(2)
    for first, stop in strips(gate_grad.shape[0], 128):
        gate_grad[first:stop, :] = gate_reduce.total(slice(first, stop))
    for i in range(2, 7):
        copies[i].wait_send()
    gate_reduce.finish()

    @pl.when(p.s > 0)
    def _():
        halo[0].wait_send()
        halo[1].wait_send()

    for copy in save:
        copy.wait()


def attend_back(line, qkv, halo_kv, floor, logs, grad, inner, hidden, w_down, middle, gate_parts):
    rows, width = middle.shape
    count = qkv.shape[0]
    part = qkv.shape[1] // 3
    units, slab = w_down.shape[1:]
    return pl.pallas_call(
        functools.partial(attend_back_kernel, line),
        out_shape=(
            jax.ShapeDtypeStruct((count, 3 * part), BF16),
            jax.ShapeDtypeStruct((rows, width), BF16),
            jax.ShapeDtypeStruct((units, slab), F32),
        ),
        in_specs=[any_spec()] * 2
        + [vmem_spec(), vmem_spec(), any_spec(), vmem_spec()]
        + [any_spec()] * 4,
        out_specs=(any_spec(), vmem_spec(), vmem_spec()),
        scratch_shapes=[
            pltpu.VMEM((count, part), BF16),
            pltpu.VMEM((WINDOW + count, part), BF16),
            pltpu.VMEM((WINDOW + count, part), BF16),
            pltpu.VMEM((part, WINDOW + count), BF16),
            pltpu.VMEM((WINDOW + count, part), F32),
            pltpu.VMEM((WINDOW + count, part), F32),
            pltpu.VMEM((2, WINDOW, part), BF16),
            pltpu.VMEM((2, WINDOW, part), BF16),
            pltpu.VMEM((line, units, slab), BF16),
            pltpu.VMEM((line - 1, units, slab), BF16),
            pltpu.VMEM((line - 1, units, slab), BF16),
            pltpu.VMEM((5, rows, width), BF16),
            pltpu.VMEM((7, rows, width), BF16),
            pltpu.VMEM((rows, width), F32),
            pltpu.VMEM((2, rows, hidden.shape[1]), BF16),
            pltpu.VMEM((count, part), BF16),
            pltpu.VMEM((line, units, slab), BF16),
            pltpu.SemaphoreType.DMA((7,)),
            pltpu.SemaphoreType.DMA((7,)),
            *line_sems(line),
            pltpu.SemaphoreType.DMA((9,)),
            pltpu.SemaphoreType.DMA((2,)),
            pltpu.SemaphoreType.DMA((2,)),
            pltpu.SemaphoreType.DMA((2,)),
            pltpu.SemaphoreType.DMA((3,)),
        ],
        compiler_params=pltpu.CompilerParams(
            collective_id=4, has_side_effects=True, vmem_limit_bytes=62 * MIB
        ),
        cost_estimate=pl.CostEstimate(
            flops=20 * 2**30, bytes_accessed=60 * MIB, transcendentals=0
        ),
    )(qkv, halo_kv, floor, logs, grad, inner, hidden, w_down, middle, gate_parts)


def finish_kernel(
    line,
    grads_given,
    weight_given,
    normed,
    tokens_given,
    gain,
    grad_middle,
    out_given,
    ffn_gain_part,
    input_grad,
    gain_sums,
    query_grad,
    key_grad,
    value_grad,
    out_grad,
    strip,
    parts,
    parts_up_in,
    parts_down_in,
    out_parts,
    out_up_in,
    out_down_in,
    out,
    into,
    total,
    gain_line,
    gain_in,
    grads_in,
    weight_in,
    tokens_in,
    r_send,
    r_recv,
    *sems,
):
    p = Place(line)
    part_sems, out_sems = sems[0:4], sems[4:8]
    loads, strip_sems, gain_send, gain_recv, line_send, line_recv, block_sems = sems[8:15]
    grads, weight, tokens = grads_in, weight_in, tokens_in
    rows, width = tokens.shape
    slab = width // line
    part = query_grad.shape[1]
    part_reduce = LineReduce(p, lambda d: parts.at[d], parts_up_in, parts_down_in, *part_sems)
    out_reduce = LineReduce(p, lambda d: out_parts.at[d], out_up_in, out_down_in, *out_sems)
    started = [
        pltpu.make_async_copy(out_given, out_parts, loads.at[0]),
        pltpu.make_async_copy(grad_middle, input_grad, loads.at[1]),
    ]
    turns = (
        p.second + p.turn,
        p.across + p.turn,
        p.first,
        p.first + p.turn,
        p.across,
        p.core,
        p.h,
        p.second,
    )
    blocks = []
    for n, j in enumerate(turns):
        at = pl.ds(pl.multiple_of(j * rows, rows), rows)
        blocks.append(pltpu.make_async_copy(grads_given.at[at], grads.at[at], block_sems.at[n]))
    weight_load = pltpu.make_async_copy(weight_given, weight, loads.at[2])
    tokens_load = pltpu.make_async_copy(tokens_given, tokens, loads.at[3])
    weight_load.start()
    blocks[0].start()
    started[0].start()
    for copy in blocks[1:] + [started[1], tokens_load]:
        copy.start()
    greet_line(p)
    started[0].wait()
    out_reduce.start(0)
    for reduce in (part_reduce, out_reduce):
        clear_last(reduce)
    copies = block_reduce(p, out, into, r_send, r_recv)

    def emit(j, target, *more):
        at = pl.ds(pl.multiple_of(j * rows, rows), rows)

        for d in range(line):
            cols = slice(d * slab, (d + 1) * slab)
            value = product_nt(grads[at, :], weight[cols, :])
            for other in more:
                value = value + other[:, cols].astype(F32)
            target[:, cols] = value.astype(target.dtype)

    weight_load.wait()
    blocks[0].wait()
    emit(p.second + p.turn, out.at[0])
    copies[0].start()
    blocks[1].wait()
    emit(p.across + p.turn, out.at[1])
    copies[1].start()
    copies[0].wait_recv()
    blocks[2].wait()
    emit(p.first, out.at[2], into.at[0])
    copies[4].start()
    copies[0].wait_send()
    blocks[3].wait()
    emit(p.first + p.turn, out.at[0])
    copies[2].start()
    copies[1].wait_recv()
    blocks[4].wait()
    emit(p.across, out.at[3], into.at[1])
    copies[5].start()
    copies[1].wait_send()
    blocks[5].wait()
    emit(p.core, out.at[1])
    copies[3].start()
    blocks[6].wait()
    blocks[7].wait()
    multiply = lambda *some: weight_product(
        lambda rows_in: product_tn(grads[...], rows_in),
        normed,
        lambda d: parts.at[d],
        strip.at.__getitem__,
        strip.shape[2],
        strip_sems,
        p,
        *some,
    )
    out_reduce.step(0)
    multiply(0, 1)
    part_reduce.start(0)
    multiply(1, line)
    out_reduce.step(1)
    copies[3].wait_recv()
    emit(p.h, total, into.at[3])
    part_reduce.step(0)
    copies[2].wait_recv()
    copies[5].wait_recv()
    emit(p.second, out.at[4], into.at[2], into.at[5])
    copies[6].start()
    part_reduce.step(1)
    out_reduce.step(2)
    for first, last in strips(part, 128):
        out_grad[first:last, :] = out_reduce.total(slice(first, last))
    copies[4].wait_recv()
    copies[6].wait_recv()
    started[1].wait()
    tokens_load.wait()
    gain_own = gain_line.at[p.s]
    gain_own[...] = jnp.zeros(gain_own.shape, F32)
    gain_own[1:2, :] = ffn_gain_part[...]
    step = 32

    @pl.loop(0, rows // step)
    def _(i):
        at = pl.ds(pl.multiple_of(i * step, step), step)
        grad = total[at] + into[4, at].astype(F32) + into[6, at].astype(F32)
        unit, inverse = normalize(tokens[at].astype(F32))
        gain_own[0:1, :] += jnp.sum(grad * unit, axis=0, keepdims=True)
        input_grad[at] += norm_back(unit, inverse, gain[...], grad)

    for i, head in enumerate((p.core, p.first, p.second)):
        copy = remote(gain_own, gain_in.at[i], gain_send.at[i], gain_recv.at[i], p.at(head))
        copy.start()
        copy.wait()
        gain_own[...] += gain_in[i]
    spread = [
        remote(
            gain_own,
            gain_own,
            line_send.at[k - 1],
            line_recv.at[k - 1],
            (lax.rem(p.s + k, line), p.h),
        )
        for k in range(1, line)
    ]
    came = [
        remote(
            gain_line.at[lax.rem(p.s + line - k, line)],
            gain_line.at[lax.rem(p.s + line - k, line)],
            line_send.at[k - 1],
            line_recv.at[k - 1],
            (lax.rem(p.s + k, line), p.h),
        )
        for k in range(1, line)
    ]
    for copy in spread:
        copy.start()
    for copy in came:
        copy.wait_recv()
    summed = gain_line[0]
    for d in range(1, line):
        summed = summed + gain_line[d]
    gain_sums[...] = summed
    part_reduce.step(2)
    for i, target in enumerate((query_grad, key_grad, value_grad)):
        for first, last in strips(part, 128):
            target[:, first:last] = part_reduce.total(
                slice(i * part + first, i * part + last)
            ).T
    for i in range(2, 7):
        copies[i].wait_send()
    for copy in spread:
        copy.wait_send()
    for reduce in (part_reduce, out_reduce):
        reduce.finish()


def finish(line, grads, weight, normed, tokens, gain, grad_middle, out_parts, ffn_gain_part):
    rows, width = tokens.shape
    full = grads.shape[0]
    part = grads.shape[1] // 3
    slab = width // line
    return pl.pallas_call(
        functools.partial(finish_kernel, line),
        out_shape=(
            jax.ShapeDtypeStruct((rows, width), F32),
            jax.ShapeDtypeStruct((2, width), F32),
            jax.ShapeDtypeStruct((slab, part), F32),
            jax.ShapeDtypeStruct((slab, part), F32),
            jax.ShapeDtypeStruct((slab, part), F32),
            jax.ShapeDtypeStruct((part, slab), F32),
        ),
        in_specs=[
            any_spec(),
            any_spec(),
            any_spec(),
            any_spec(),
            vmem_spec(),
            any_spec(),
            any_spec(),
            vmem_spec(),
        ],
        out_specs=(vmem_spec(),) * 6,
        scratch_shapes=[
            pltpu.VMEM((2, full, slab), BF16),
            pltpu.VMEM((line, 3 * part, slab), BF16),
            pltpu.VMEM((line - 1, 3 * part, slab), BF16),
            pltpu.VMEM((line - 1, 3 * part, slab), BF16),
            pltpu.VMEM((line, part, slab), BF16),
            pltpu.VMEM((line - 1, part, slab), BF16),
            pltpu.VMEM((line - 1, part, slab), BF16),
            pltpu.VMEM((5, rows, width), BF16),
            pltpu.VMEM((7, rows, width), BF16),
            pltpu.VMEM((rows, width), F32),
            pltpu.VMEM((line, 2, width), F32),
            pltpu.VMEM((3, 2, width), F32),
            pltpu.VMEM(grads.shape, BF16),
            pltpu.VMEM(weight.shape, BF16),
            pltpu.VMEM((rows, width), BF16),
            pltpu.SemaphoreType.DMA((7,)),
            pltpu.SemaphoreType.DMA((7,)),
            *line_sems(line, 2),
            pltpu.SemaphoreType.DMA((4,)),
            pltpu.SemaphoreType.DMA((2,)),
            pltpu.SemaphoreType.DMA((3,)),
            pltpu.SemaphoreType.DMA((3,)),
            pltpu.SemaphoreType.DMA((line - 1,)),
            pltpu.SemaphoreType.DMA((line - 1,)),
            pltpu.SemaphoreType.DMA((8,)),
        ],
        compiler_params=pltpu.CompilerParams(
            collective_id=5, has_side_effects=True, vmem_limit_bytes=62 * MIB
        ),
        cost_estimate=pl.CostEstimate(
            flops=20 * 2**30, bytes_accessed=60 * MIB, transcendentals=0
        ),
    )(
        grads,
        weight,
        normed,
        tokens,
        gain.reshape(1, width),
        grad_middle,
        out_parts,
        ffn_gain_part,
    )


def deliver_kernel(count, *refs):
    sources, targets, held = refs[:count], refs[count : 2 * count], refs[2 * count : 3 * count]
    sems = refs[3 * count]
    loads = [
        pltpu.make_async_copy(source, keep, sems.at[i])
        for i, (source, keep) in enumerate(zip(sources, held))
    ]
    stores = [
        pltpu.make_async_copy(keep, target, sems.at[count + i])
        for i, (keep, target) in enumerate(zip(held, targets))
    ]
    for copy in loads:
        copy.start()
    for load, store in zip(loads, stores):
        load.wait()
        store.start()
    for copy in stores:
        copy.wait()


def deliver(*arrays):
    count = len(arrays)
    return pl.pallas_call(
        functools.partial(deliver_kernel, count),
        out_shape=tuple(jax.ShapeDtypeStruct(a.shape, a.dtype) for a in arrays),
        in_specs=[any_spec()] * count,
        out_specs=(any_spec(),) * count,
        scratch_shapes=[pltpu.VMEM(a.shape, a.dtype) for a in arrays]
        + [pltpu.SemaphoreType.DMA((2 * count,))],
        compiler_params=pltpu.CompilerParams(vmem_limit_bytes=62 * MIB),
    )(*arrays)


def fused(
    tokens,
    segment,
    attn_gain,
    query_weight,
    key_weight,
    value_weight,
    out_weight,
    ffn_gain,
    gate_weight,
    up_weight,
    down_weight,
    cotangent,
):
    line = lax.axis_size("seq")
    (
        normed_one,
        qkv,
        w_qkv,
        floor,
        attended,
        logs,
        halo_kv,
        cot_full,
        w_out,
        w_gate,
        w_up,
        middle,
    ) = forward(
        line,
        tokens,
        attn_gain,
        query_weight,
        key_weight,
        value_weight,
        segment,
        cotangent,
        out_weight,
        gate_weight.T,
        up_weight.T,
    )
    normed_two, hidden, grad_gate, grad_up, grad_normed_two, w_down, down_grad = feed(
        line, middle, ffn_gain, cot_full, w_gate, w_up, down_weight
    )
    grad_middle, ffn_gain_part, grad_attended, inner, up_grad, gate_parts, out_parts = give_back(
        line,
        grad_normed_two,
        middle,
        cotangent,
        ffn_gain,
        attended,
        w_out,
        grad_gate,
        grad_up,
        normed_two,
    )
    grads, result, gate_grad = attend_back(
        line, qkv, halo_kv, floor, logs, grad_attended, inner, hidden, w_down, middle, gate_parts
    )
    input_grad, gain_sums, query_grad, key_grad, value_grad, out_grad = finish(
        line,
        grads,
        w_qkv,
        normed_one,
        tokens,
        attn_gain,
        grad_middle,
        out_parts,
        ffn_gain_part,
    )
    (
        result,
        input_grad,
        query_grad,
        key_grad,
        value_grad,
        out_grad,
        gate_grad,
        up_grad,
        down_grad,
    ) = deliver(
        result,
        input_grad,
        query_grad,
        key_grad,
        value_grad,
        out_grad,
        gate_grad,
        up_grad,
        down_grad,
    )
    share = tokens.shape[1] // (line * lax.axis_size("head"))
    place = (lax.axis_index("seq") * lax.axis_size("head") + lax.axis_index("head")) * share
    gain_grads = lax.dynamic_slice(gain_sums, (0, place), (2, share))
    return (
        result,
        input_grad,
        gain_grads[0],
        query_grad,
        key_grad,
        value_grad,
        out_grad,
        gain_grads[1],
        gate_grad.T,
        up_grad.T,
        down_grad,
    )


def solution(mesh):
    placed = (
        P(("seq", "head"), None),
        P("seq"),
        P(),
        P("seq", "head"),
        P("seq", "head"),
        P("seq", "head"),
        P("head", "seq"),
        P(),
        P("seq", "head"),
        P("seq", "head"),
        P("head", "seq"),
        P(("seq", "head"), None),
    )
    body = fused if mesh.shape["head"] == 8 else local
    return jax.shard_map(
        body,
        mesh=mesh,
        in_specs=placed,
        out_specs=(
            P(("seq", "head"), None),
            P(("seq", "head"), None),
            P(("seq", "head")),
            P("seq", "head"),
            P("seq", "head"),
            P("seq", "head"),
            P("head", "seq"),
            P(("seq", "head")),
            P("seq", "head"),
            P("seq", "head"),
            P("head", "seq"),
        ),
        check_vma=False,
    )
```
